32 devices in a mesh: batch: 16 (over z, y, core), head: 2 (over x).
Axes of the slice: x: 2, y: 2, z: 4, core: 2. Of those that a mesh axis runs over, the one named last changes fastest.
Arguments:
- inputs: bfloat16 [4, 32, 392, 768], P(None, ('batch', 'head')), may hold values from -6 to 6
- qkv_weight: bfloat16 [768, 8, 288], P(None, 'head'), may hold values from -0.21875 to 0.21875
- proj_weight: bfloat16 [8, 96, 768], P('head'), may hold values from -0.21875 to 0.21875
- pool_weight: bfloat16 [8, 4, 96], P('head'), may hold values from 0.29882812 to 0.8984375
- gain_one: float32 [768], replicated, may hold values from 0.5 to 1.5
- gain_two: float32 [768], replicated, may hold values from 0.5 to 1.5
- hidden_weight: bfloat16 [768, 3072], P(('batch', 'head')), may hold values from -0.21875 to 0.21875
- output_weight: bfloat16 [3072, 768], P(('batch', 'head')), may hold values from -0.109375 to 0.109375
- memory: bfloat16 [4, 32, 392, 8, 192], P(None, 'batch', None, 'head'), may hold values from -6 to 6
- clip_index: int32 [4, 32], P(None, 'batch'), may hold values from 0 to 11
- cotangent: bfloat16 [4, 32, 392, 768], P(None, ('batch', 'head')), may hold values from -6 to 6
Outputs:
- outputs: bfloat16 [4, 32, 392, 768], P(None, ('batch', 'head'))
- d_inputs: bfloat16 [4, 32, 392, 768], P(None, ('batch', 'head'))
- d_qkv_weight: float32 [768, 8, 288], P(None, 'head')
- d_proj_weight: float32 [8, 96, 768], P('head')
- d_pool_weight: float32 [8, 4, 96], P('head')
- d_gain_one: float32 [768], P(('batch', 'head'))
- d_gain_two: float32 [768], P(('batch', 'head'))
- d_hidden_weight: float32 [768, 3072], P(('batch', 'head'))
- d_output_weight: float32 [3072, 768], P(('batch', 'head'))
The draws below stay inside these ranges and needn't reach their ends.
Inputs may be any that keep to these rules, and one draw needn't show every extreme that they name: `clip_index`: each clip's position in its video of 1 to 12 clips; memory slot r of a clip holds real data only when its index exceeds r, and other slots hold arbitrary values.
All inputs are finite; a program needn't handle non-finite values.
Results may differ from the reference program's by a relative error of at most 0.02.
Values may be sent and summed in bfloat16 or wider, within the bound.
A program may use at most 384 MiB of HBM per device.

```python
import jax
import jax.numpy as jnp
from jax import lax

D = 768
FF = 3072
HEADS = 8
HD = 96
FRAMES = 8
MICRO = 4
TPC = 392
PTOK = 196
MTOK = 392
KEYS = 588
CLIPS = 32
N_HEAD = 2


def plant(values, stream_key, low, high):
    index_at = [jax.random.randint(jax.random.fold_in(stream_key, axis), (), 0, length) for axis, length in enumerate(values.shape)]
    longest = values.shape.index(max(values.shape))
    next_to = index_at[:longest] + [(index_at[longest] + 1) % values.shape[longest]] + index_at[longest + 1:]
    return values.at[tuple(index_at)].set(low).at[tuple(next_to)].set(high)


def spiked(drawn, own_key, source, target, blocks, factor):
    owner, partner = [(jnp.arange(drawn.shape[dim]) // (drawn.shape[dim] // blocks)).reshape([-1 if axis == dim else 1 for axis in range(drawn.ndim)]) for dim in (source, target)]
    chosen = jax.random.permutation(own_key, blocks)[partner]
    strong = (owner == chosen) | (owner == (partner + blocks // 2) % blocks)
    return jnp.where(strong, factor * drawn, drawn)


def block_scale(rng, dims, shards, least, largest):
    gain, own = 1.0, jax.random.fold_in(rng, 6)
    for axis_at, shards_of in shards:
        steps = jnp.exp(jax.random.uniform(jax.random.fold_in(own, axis_at), (shards_of,), jnp.float32, least / len(shards), largest / len(shards)))
        gain = gain * jnp.repeat(steps, dims[axis_at] // shards_of).reshape([-1 if axis == axis_at else 1 for axis in range(len(dims))])
    return gain


def bell_draw(key, dims, deviation, limit, pieces=(), kind=jnp.bfloat16):
    values = deviation * jax.random.normal(key, dims, jnp.float32)
    if pieces:
        values = values * block_scale(key, dims, pieces, -0.22, 0.18)
    return jnp.clip(values, -limit, limit).astype(kind)


def gaussian_with(rng, extent, spread, reach, shards, heavy, held_as=jnp.bfloat16):
    entries = spread * jax.random.normal(rng, extent, jnp.float32)
    if shards:
        entries = entries * block_scale(rng, extent, shards, -0.22, 0.18)
    return jnp.clip(spiked(entries, jax.random.fold_in(rng, 3), *heavy), -reach, reach).astype(held_as)


def setup_inputs(seed: int = 0) -> dict:
    arg_keys = jax.random.split(jax.random.key(seed), 12)
    return {
        "inputs": bell_draw(arg_keys[0], (MICRO, CLIPS, TPC, D), 1.0, 6.0, ((1, 32),)),
        "qkv_weight": bell_draw(arg_keys[1], (D, HEADS, 3 * HD), D ** -0.5, 0.21875, ((1, 2),)),
        "proj_weight": bell_draw(arg_keys[2], (HEADS, HD, D), D ** -0.5, 0.21875, ((0, 2),)),
        "pool_weight": jnp.clip(0.29882812 + 0.5996094 * jax.random.uniform(arg_keys[3], (HEADS, 4, HD), jnp.float32) ** block_scale(arg_keys[3], (HEADS, 4, HD), ((0, 2),), -0.2, 0.2), 0.29882812, 0.8984375).astype(jnp.bfloat16),
        "gain_one": jnp.clip(1.0 + 0.1 * jax.random.normal(arg_keys[4], (D,), jnp.float32), 0.5, 1.5),
        "gain_two": jnp.clip(1.0 + 0.1 * jax.random.normal(arg_keys[5], (D,), jnp.float32), 0.5, 1.5),
        "hidden_weight": bell_draw(arg_keys[6], (D, FF), D ** -0.5, 0.21875, ((0, 32),)),
        "output_weight": bell_draw(arg_keys[7], (FF, D), FF ** -0.5, 0.109375, ((0, 32),)),
        "memory": bell_draw(arg_keys[8], (MICRO, CLIPS, MTOK, HEADS, 2 * HD), 1.0, 6.0, ((1, 16), (3, 2))),
        "clip_index": plant(jax.random.randint(arg_keys[9], (MICRO, CLIPS), 0, 12), jax.random.fold_in(arg_keys[9], 1), 0, 11).astype(jnp.int32),
        "cotangent": gaussian_with(arg_keys[10], (MICRO, CLIPS, TPC, D), 1.0, 6.0, ((1, 32),), (1, 3, 32, 2.75)),
    }


@jax.custom_vjp
def low(v):
    return lax.optimization_barrier(v.astype(jnp.bfloat16)).astype(jnp.float32)

@jax.custom_vjp
def low_back(v):
    return v

def low_keep(v):
    return (low(v), None)

def low_pass(kept, grad):
    return (grad,)

def back_keep(v):
    return (v, None)

def back_low(kept, grad):
    return (low(grad),)
low.defvjp(low_keep, low_pass)
low_back.defvjp(back_keep, back_low)
norm_eps = 1e-06

def layer_norm(values, gain_vector):
    average = lax.optimization_barrier(jnp.mean(values, axis=-1, keepdims=True))
    centered = values - average
    variance = lax.optimization_barrier(jnp.mean(centered * centered, axis=-1, keepdims=True))
    return centered * lax.rsqrt(variance + norm_eps) * gain_vector

def pool_pairs(raw_rows, first_tap, second_tap):
    clip_total, token_total, head_total, head_width = raw_rows.shape
    paired = raw_rows.reshape(clip_total, FRAMES // 2, 2, token_total // FRAMES, head_total, head_width)
    merged = first_tap * paired[:, :, 0] + second_tap * paired[:, :, 1]
    return merged.reshape(clip_total, token_total // 2, head_total, head_width)

def key_mask(indices):
    position = lax.broadcasted_iota(jnp.int32, indices.shape + (KEYS,), indices.ndim)
    return indices[..., None] > position // PTOK - 1

def block_forward(block_in, block_memory, block_mask, qkv_all, proj_all, pool_all, gain_first, gain_second, hidden_all, output_all):
    highest = lax.Precision.HIGHEST
    clip_total = block_in.shape[0]
    normed_one = low(layer_norm(block_in, gain_first))
    packed = low_back(jnp.einsum('ctd,dhe->cthe', normed_one, qkv_all, precision=highest))
    queries = packed[..., :HD]
    query_low = low(queries)
    pooled_keys = low(pool_pairs(packed[..., HD:2 * HD], pool_all[:, 0], pool_all[:, 1]))
    pooled_values = low(pool_pairs(packed[..., 2 * HD:], pool_all[:, 2], pool_all[:, 3]))
    key_all = jnp.concatenate([pooled_keys, block_memory[..., :HD]], axis=1)
    value_all = jnp.concatenate([pooled_values, block_memory[..., HD:]], axis=1)
    scores = low_back(jnp.einsum('cqhe,ckhe->chqk', query_low, key_all, precision=highest) * HD ** (-0.5))
    scores = jnp.where(block_mask[:, None, None, :], scores, -1000000000.0)
    attention = low(jax.nn.softmax(scores, axis=-1))
    attended = low(low_back(jnp.einsum('chqk,ckhe->cqhe', attention, value_all, precision=highest) + queries))
    groups = N_HEAD
    grouped = attended.reshape(clip_total, TPC, groups, HEADS // groups * HD)
    weights = proj_all.reshape(groups, HEADS // groups * HD, D)
    partial_sums = jnp.einsum('ctgf,gfd->gctd', grouped, weights, precision=highest)
    branch = low_back(lax.optimization_barrier(jnp.sum(low(partial_sums), axis=0)))
    middle = block_in + branch
    normed_two = low(layer_norm(middle, gain_second))
    hidden = low_back(jnp.einsum('ctd,df->ctf', normed_two, hidden_all, precision=highest))
    active = low(jax.nn.gelu(hidden, approximate=False))
    return middle + jnp.einsum('ctf,fd->ctd', active, output_all, precision=highest)

def reference(inputs, qkv_weight, proj_weight, pool_weight, gain_one, gain_two, hidden_weight, output_weight, memory, clip_index, cotangent):
    block_size = 8
    clip_total = MICRO * CLIPS

    def to_blocks(array):
        return array.reshape((clip_total // block_size, block_size) + array.shape[2:])
    inputs_blocks = to_blocks(inputs.astype(jnp.float32))
    memory_blocks = to_blocks(memory.astype(jnp.float32))
    mask_blocks = to_blocks(key_mask(clip_index))
    cotangent_blocks = to_blocks(cotangent.astype(jnp.float32))

    def forward_all(inputs_all, qkv_all, proj_all, pool_all, gain_first, gain_second, hidden_all, output_all):

        def one_block(members):
            block_in, block_memory, block_mask = members
            return block_forward(block_in, block_memory, block_mask, qkv_all, proj_all, pool_all, gain_first, gain_second, hidden_all, output_all)
        return lax.map(jax.checkpoint(one_block), (inputs_all, memory_blocks, mask_blocks))
    result, backward_pull = jax.vjp(forward_all, inputs_blocks, qkv_weight.astype(jnp.float32), proj_weight.astype(jnp.float32), pool_weight.astype(jnp.float32), gain_one, gain_two, hidden_weight.astype(jnp.float32), output_weight.astype(jnp.float32))
    gradients = backward_pull(cotangent_blocks)
    outputs = result.reshape(inputs.shape).astype(jnp.bfloat16)
    d_inputs = gradients[0].reshape(inputs.shape).astype(jnp.bfloat16)
    return (outputs, d_inputs, gradients[1], gradients[2], gradients[3], gradients[4], gradients[5], gradients[6], gradients[7])
```

```python
import functools
import math

import jax
import jax.numpy as jnp
from jax import lax
from jax.experimental import pallas as pl
from jax.experimental.pallas import tpu as pltpu
from jax.sharding import PartitionSpec as P

HD = 96
WIDE = 128
FRAMES = 8
TPC = 392
PTOK = 196
SPOT = TPC // FRAMES
HALF = 200
ROWS = 2 * HALF
MAIN = 384
REST = TPC - MAIN
SIDE = 256
PAIR = 2
PIECES = 3 * PAIR

NORM_EPS = 1e-06
NEG = -1e30
LOG2E = 1.4426950408889634
SCORE = HD ** (-0.5)

F32 = jnp.float32
BF16 = jnp.bfloat16


def dot(a, b):
    return lax.dot_general(a, b, (((1,), (0,)), ((), ())), preferred_element_type=F32)


def dot_nt(a, b):
    return lax.dot_general(a, b, (((1,), (1,)), ((), ())), preferred_element_type=F32)


def dot_tn(a, b):
    return lax.dot_general(a, b, (((0,), (0,)), ((), ())), preferred_element_type=F32)


def reorder(shape, row_dim):
    rows = lax.broadcasted_iota(jnp.int32, shape, row_dim)
    tokens = lax.broadcasted_iota(jnp.int32, shape, 1 - row_dim)
    odd = (rows >= HALF).astype(jnp.int32)
    spot = rows - HALF * odd
    frame = sum((spot >= SPOT * step).astype(jnp.int32) for step in range(1, FRAMES // 2))
    return ((tokens == spot + SPOT * (frame + odd)) & (spot < PTOK)).astype(BF16)


def norm_parts(values):
    average = jnp.mean(values, axis=-1, keepdims=True)
    centered = values - average
    spread = lax.rsqrt(jnp.mean(centered * centered, axis=-1, keepdims=True) + NORM_EPS)
    return centered * spread, spread


def norm_pull(values, gain, grad):
    unit, spread = norm_parts(values)
    scaled = grad * gain
    inner = jnp.mean(scaled * unit, axis=-1, keepdims=True)
    pulled = spread * (scaled - jnp.mean(scaled, axis=-1, keepdims=True) - unit * inner)
    return pulled, jnp.sum(grad * unit, axis=0, keepdims=True)


def value_columns(memory_t):
    return jnp.concatenate([memory_t[HD:], jnp.zeros((WIDE - HD, memory_t.shape[1]), BF16)], axis=0)


def forward_kernel(
    x_ref, w_ref, mem_ref, tail_ref, side_ref, main_ref, taps_ref, proj_ref, gain_one_ref, gain_two_ref,
    packed_ref, keys_ref, att_ref, log_ref, normed_ref, middle_ref, normed_two_ref,
    x_rows, normed_rows, branch,
):
    pair, clip = pl.program_id(0), pl.program_id(1)
    here = pl.ds(clip, 1)

    @pl.when(pair == 0)
    def _():
        rows = dot(reorder((ROWS, TPC), 0), x_ref[0])
        x_rows[here] = rows.astype(BF16)[None]
        unit, _ = norm_parts(rows)
        normed_rows[here] = (unit * gain_one_ref[...]).astype(BF16)[None]

    normed = normed_rows[here][0]
    normed_ref[0] = normed
    packed = dot_nt(normed, w_ref[0])
    packed_ref[0, 0] = packed.astype(BF16)
    logs = []
    outs = []
    for head in range(PAIR):
        base = 3 * WIDE * head
        query = packed[:, base : base + WIDE]
        key = packed[:, base + WIDE : base + 2 * WIDE]
        value = packed[:, base + 2 * WIDE : base + 3 * WIDE]
        query_low = query.astype(BF16)
        taps = taps_ref[0, head]
        zeros = jnp.zeros((SIDE - HALF - REST, WIDE), F32)
        pooled_key = taps[0:1] * key[:HALF] + taps[1:2] * key[HALF:]
        pooled_value = taps[2:3] * value[:HALF] + taps[3:4] * value[HALF:]
        side_key = jnp.concatenate([pooled_key, tail_ref[0, head, 0], zeros], axis=0).astype(BF16)
        side_value = jnp.concatenate([pooled_value, tail_ref[0, head, 1], zeros], axis=0).astype(BF16)
        keys_ref[0, 0, head, 0] = side_key
        keys_ref[0, 0, head, 1] = side_value
        memory_t = mem_ref[0, head]
        score_side = dot_nt(query_low, side_key) * (SCORE * LOG2E) + side_ref[0]
        score_main = dot(query_low, memory_t[:WIDE]) * (SCORE * LOG2E) + main_ref[0]
        top = jnp.maximum(
            jnp.max(score_side, axis=-1, keepdims=True), jnp.max(score_main, axis=-1, keepdims=True)
        )
        weight_side = jnp.exp2(score_side - top)
        weight_main = jnp.exp2(score_main - top)
        total = jnp.sum(weight_side, axis=-1, keepdims=True) + jnp.sum(weight_main, axis=-1, keepdims=True)
        mixed = dot(weight_side.astype(BF16), side_value) + dot_nt(
            weight_main.astype(BF16), value_columns(memory_t)
        )
        outs.append(mixed / total + query)
        logs.append(top + jnp.log2(total))
    attended = jnp.concatenate(outs, axis=1).astype(BF16)
    att_ref[0, 0] = attended
    lane = lax.broadcasted_iota(jnp.int32, (ROWS, WIDE), 1)
    log_ref[0, 0] = jnp.where(lane == 0, logs[0], logs[1])
    part = dot(attended, proj_ref[0])[None]

    @pl.when(pair == 0)
    def _():
        branch[here] = part

    @pl.when(pair > 0)
    def _():
        branch[here] += part

    @pl.when(pair == pl.num_programs(0) - 1)
    def _():
        middle = x_rows[here][0].astype(F32) + branch[here][0]
        middle_ref[0] = middle
        unit, _ = norm_parts(middle)
        normed_two_ref[0] = (unit * gain_two_ref[...]).astype(BF16)


def mlp_kernel(
    normed_ref, cot_ref, first_ref, second_ref, middle_ref, gain_ref,
    out_ref, grad_ref, grad_low_ref, d_first_ref, d_second_ref, d_gain_ref,
    cot_rows, cot_t, normed_t, total, grad_normed, active, grad_hidden,
):
    tile = pl.program_id(0)
    clips = cot_ref.shape[0]
    wide = normed_ref.shape[1]

    @pl.when(tile == 0)
    def _():
        swap = reorder((ROWS, TPC), 0)

        @pl.loop(0, clips)
        def _(clip):
            here = pl.ds(pl.multiple_of(clip * ROWS, ROWS), ROWS)
            cot_rows[here, :] = dot(swap, cot_ref[clip]).astype(BF16)
            total[here, :] = middle_ref[here, :]
            grad_normed[here, :] = jnp.zeros((ROWS, wide), F32)

        for lanes in range(0, wide, WIDE):
            cot_t[lanes : lanes + WIDE, :] = cot_rows[:, lanes : lanes + WIDE].T
            normed_t[lanes : lanes + WIDE, :] = normed_ref[:, lanes : lanes + WIDE].T

    first = first_ref[...]
    second = second_ref[...]

    @pl.loop(0, clips)
    def _(clip):
        here = pl.ds(pl.multiple_of(clip * ROWS, ROWS), ROWS)
        hidden = dot(normed_ref[here, :], first)
        grad_active = dot_nt(cot_rows[here, :], second)
        bell = jnp.exp2(hidden * hidden * (-0.5 * LOG2E))
        step = 1.0 / (1.0 + (0.3275911 * math.sqrt(0.5)) * jnp.abs(hidden))
        tail = step * (0.5 * 1.061405429) + (0.5 * -1.453152027)
        tail = step * tail + (0.5 * 1.421413741)
        tail = step * tail + (0.5 * -0.284496736)
        tail = step * tail + (0.5 * 0.254829592)
        tail = step * tail * bell
        cumulative = jnp.where(hidden < 0.0, tail, 1.0 - tail)
        slope = cumulative + hidden * bell * 0.3989422804014327
        active_low = (hidden * cumulative).astype(BF16)
        hidden_low = (slope * grad_active).astype(BF16)
        active[here, :] = active_low
        grad_hidden[here, :] = hidden_low
        total[here, :] += dot(active_low, second)
        grad_normed[here, :] += dot_nt(hidden_low, first)

    d_first_ref[...] = dot(normed_t[...], grad_hidden[...]).astype(BF16)
    d_second_ref[...] = dot(cot_t[...], active[...]).astype(BF16).T

    @pl.when(tile == pl.num_programs(0) - 1)
    def _():
        back = reorder((TPC, ROWS), 1)
        d_gain_ref[...] = jnp.zeros_like(d_gain_ref)

        @pl.loop(0, clips)
        def _(clip):
            here = pl.ds(pl.multiple_of(clip * ROWS, ROWS), ROWS)
            out_ref[clip] = dot(back, total[here, :].astype(BF16)).astype(BF16)
            pulled, d_gain = norm_pull(middle_ref[here, :], gain_ref[...], grad_normed[here, :])
            grad = cot_rows[here, :].astype(F32) + pulled
            grad_ref[here, :] = grad
            grad_low_ref[here, :] = grad.astype(BF16)
            d_gain_ref[...] += d_gain


def backward_kernel(
    x_ref, w_ref, mem_ref, side_ref, main_ref, taps_ref, proj_ref, gain_ref,
    packed_ref, keys_ref, att_ref, log_ref, normed_ref, grad_ref, grad_low_ref,
    d_x_ref, d_w_ref, d_proj_ref, d_taps_ref, d_gain_ref,
    grad_normed,
):
    pair, clip = pl.program_id(0), pl.program_id(1)
    here = pl.ds(clip, 1)

    @pl.when(clip == 0)
    def _():
        d_w_ref[...] = jnp.zeros_like(d_w_ref)
        d_proj_ref[...] = jnp.zeros_like(d_proj_ref)
        d_taps_ref[...] = jnp.zeros_like(d_taps_ref)

    grad_branch = grad_low_ref[...]
    grad_out = dot_nt(grad_branch, proj_ref[0])
    d_proj_ref[0] += dot_tn(att_ref[0, 0], grad_branch)
    pieces = []
    for head in range(PAIR):
        base = 3 * WIDE * head
        query = packed_ref[0, 0, :, base : base + WIDE]
        key = packed_ref[0, 0, :, base + WIDE : base + 2 * WIDE].astype(F32)
        value = packed_ref[0, 0, :, base + 2 * WIDE : base + 3 * WIDE].astype(F32)
        out_grad = grad_out[:, WIDE * head : WIDE * (head + 1)].astype(BF16)
        taps = taps_ref[0, head]
        side_key = keys_ref[0, 0, head, 0]
        side_value = keys_ref[0, 0, head, 1]
        memory_t = mem_ref[0, head]
        log = log_ref[0, 0, :, head : head + 1]
        score_side = dot_nt(query, side_key) * (SCORE * LOG2E) + side_ref[0]
        score_main = dot(query, memory_t[:WIDE]) * (SCORE * LOG2E) + main_ref[0]
        weight_side = jnp.exp2(score_side - log)
        weight_main = jnp.exp2(score_main - log)
        grad_side = dot_nt(out_grad, side_value)
        grad_main = dot(out_grad, value_columns(memory_t))
        inner = jnp.sum(weight_side * grad_side, axis=-1, keepdims=True) + jnp.sum(
            weight_main * grad_main, axis=-1, keepdims=True
        )
        score_grad_side = (weight_side * (grad_side - inner)).astype(BF16)
        score_grad_main = (weight_main * (grad_main - inner)).astype(BF16)
        grad_query = (
            dot(score_grad_side, side_key) + dot_nt(score_grad_main, memory_t[:WIDE])
        ) * SCORE + out_grad.astype(F32)
        grad_key = dot_tn(score_grad_side, query)[:HALF] * SCORE
        grad_value = dot_tn(weight_side.astype(BF16), out_grad)[:HALF]
        pieces += [
            grad_query,
            jnp.concatenate([taps[0:1] * grad_key, taps[1:2] * grad_key], axis=0),
            jnp.concatenate([taps[2:3] * grad_value, taps[3:4] * grad_value], axis=0),
        ]
        d_taps_ref[0, head] += jnp.concatenate(
            [
                jnp.sum(part * grad, axis=0, keepdims=True)
                for part, grad in (
                    (key[:HALF], grad_key),
                    (key[HALF:], grad_key),
                    (value[:HALF], grad_value),
                    (value[HALF:], grad_value),
                )
            ],
            axis=0,
        )
    grad_packed = jnp.concatenate(pieces, axis=1).astype(BF16)
    d_w_ref[0] += dot_tn(grad_packed, normed_ref[0])
    part = dot(grad_packed, w_ref[0])[None]

    @pl.when(pair == 0)
    def _():
        grad_normed[here] = part

    @pl.when(pair > 0)
    def _():
        grad_normed[here] += part

    @pl.when(pair == pl.num_programs(0) - 1)
    def _():
        rows = dot(reorder((ROWS, TPC), 0), x_ref[0])
        pulled, d_gain = norm_pull(rows, gain_ref[...], grad_normed[here][0])
        d_x = (grad_ref[...] + pulled).astype(BF16)
        d_x_ref[0] = dot(reorder((TPC, ROWS), 1), d_x).astype(BF16)

        @pl.when(clip == 0)
        def _():
            d_gain_ref[...] = d_gain

        @pl.when(clip > 0)
        def _():
            d_gain_ref[...] += d_gain


VMEM_LIMIT = 60 << 20


def compiler_params(dims):
    return pltpu.CompilerParams(
        dimension_semantics=("arbitrary",) * dims, vmem_limit_bytes=VMEM_LIMIT
    )


def shaped(shape, dtype):
    return jax.ShapeDtypeStruct(shape, dtype)


def attention_forward(x, w, mem, tail, side, main, taps, proj, gain_one, gain_two):
    clips, pairs = x.shape[0], w.shape[0]
    width = x.shape[2]
    packed_width = w.shape[1]
    late = lambda p, c: jnp.where(p == pairs - 1, c, 0)
    early = lambda p, c: jnp.where(p == 0, c, clips - 1)
    per_step = lambda p, c: (p, c)
    return pl.pallas_call(
        forward_kernel,
        grid=(pairs, clips),
        in_specs=[
            pl.BlockSpec((1, TPC, width), lambda p, c: (early(p, c), 0, 0)),
            pl.BlockSpec((1, packed_width, width), lambda p, c: (p, 0, 0)),
            pl.BlockSpec((1, PAIR, 2 * HD, MAIN), lambda p, c: (c, p, 0, 0)),
            pl.BlockSpec((1, PAIR, 2, REST, WIDE), lambda p, c: (c, p, 0, 0, 0)),
            pl.BlockSpec((1, 1, SIDE), lambda p, c: (c, 0, 0)),
            pl.BlockSpec((1, 1, MAIN), lambda p, c: (c, 0, 0)),
            pl.BlockSpec((1, PAIR, 4, WIDE), lambda p, c: (p, 0, 0, 0)),
            pl.BlockSpec((1, PAIR * WIDE, width), lambda p, c: (p, 0, 0)),
            pl.BlockSpec((1, width), lambda p, c: (0, 0)),
            pl.BlockSpec((1, width), lambda p, c: (0, 0)),
        ],
        out_specs=[
            pl.BlockSpec((1, 1, ROWS, packed_width), lambda p, c: (p, c, 0, 0)),
            pl.BlockSpec((1, 1, PAIR, 2, SIDE, WIDE), lambda p, c: (p, c, 0, 0, 0, 0)),
            pl.BlockSpec((1, 1, ROWS, PAIR * WIDE), lambda p, c: (p, c, 0, 0)),
            pl.BlockSpec((1, 1, ROWS, WIDE), lambda p, c: (p, c, 0, 0)),
            pl.BlockSpec((1, ROWS, width), lambda p, c: (c, 0, 0)),
            pl.BlockSpec((1, ROWS, width), lambda p, c: (late(p, c), 0, 0)),
            pl.BlockSpec((1, ROWS, width), lambda p, c: (late(p, c), 0, 0)),
        ],
        out_shape=[
            shaped((pairs, clips, ROWS, packed_width), BF16),
            shaped((pairs, clips, PAIR, 2, SIDE, WIDE), BF16),
            shaped((pairs, clips, ROWS, PAIR * WIDE), BF16),
            shaped((pairs, clips, ROWS, WIDE), F32),
            shaped((clips, ROWS, width), BF16),
            shaped((clips, ROWS, width), F32),
            shaped((clips, ROWS, width), BF16),
        ],
        scratch_shapes=[
            pltpu.VMEM((clips, ROWS, width), BF16),
            pltpu.VMEM((clips, ROWS, width), BF16),
            pltpu.VMEM((clips, ROWS, width), F32),
        ],
        compiler_params=compiler_params(2),
        name="attention_forward",
    )(x, w, mem, tail, side, main, taps, proj, gain_one, gain_two)


def once(shape):
    return pl.BlockSpec(shape, lambda t: (0,) * len(shape), pipeline_mode=pl.Buffered(1))


def mlp(normed, cot, first, second, middle, gain):
    rows, width = normed.shape
    hidden = first.shape[1]
    clips = cot.shape[0]
    tile = 512
    return pl.pallas_call(
        mlp_kernel,
        grid=(hidden // tile,),
        in_specs=[
            once((rows, width)),
            once((clips, TPC, width)),
            pl.BlockSpec((width, tile), lambda t: (0, t)),
            pl.BlockSpec((tile, width), lambda t: (t, 0)),
            once((rows, width)),
            once((1, width)),
        ],
        out_specs=[
            once((clips, TPC, width)),
            once((rows, width)),
            once((rows, width)),
            pl.BlockSpec((width, tile), lambda t: (0, t)),
            pl.BlockSpec((tile, width), lambda t: (t, 0)),
            once((1, width)),
        ],
        out_shape=[
            shaped((clips, TPC, width), BF16),
            shaped((rows, width), F32),
            shaped((rows, width), BF16),
            shaped((width, hidden), BF16),
            shaped((hidden, width), BF16),
            shaped((1, width), F32),
        ],
        scratch_shapes=[
            pltpu.VMEM((rows, width), BF16),
            pltpu.VMEM((width, rows), BF16),
            pltpu.VMEM((width, rows), BF16),
            pltpu.VMEM((rows, width), F32),
            pltpu.VMEM((rows, width), F32),
            pltpu.VMEM((rows, tile), BF16),
            pltpu.VMEM((rows, tile), BF16),
        ],
        compiler_params=compiler_params(1),
        name="mlp",
    )(normed, cot, first, second, middle, gain)


def attention_backward(x, w, mem, side, main, taps, proj, gain, packed, keys, att, log, normed, grad, grad_low):
    clips, pairs = x.shape[0], w.shape[0]
    width = x.shape[2]
    packed_width = w.shape[1]
    late = lambda p, c: jnp.where(p == pairs - 1, c, 0)
    return pl.pallas_call(
        backward_kernel,
        grid=(pairs, clips),
        in_specs=[
            pl.BlockSpec((1, TPC, width), lambda p, c: (late(p, c), 0, 0)),
            pl.BlockSpec((1, packed_width, width), lambda p, c: (p, 0, 0)),
            pl.BlockSpec((1, PAIR, 2 * HD, MAIN), lambda p, c: (c, p, 0, 0)),
            pl.BlockSpec((1, 1, SIDE), lambda p, c: (c, 0, 0)),
            pl.BlockSpec((1, 1, MAIN), lambda p, c: (c, 0, 0)),
            pl.BlockSpec((1, PAIR, 4, WIDE), lambda p, c: (p, 0, 0, 0)),
            pl.BlockSpec((1, PAIR * WIDE, width), lambda p, c: (p, 0, 0)),
            pl.BlockSpec((1, width), lambda p, c: (0, 0)),
            pl.BlockSpec((1, 1, ROWS, packed_width), lambda p, c: (p, c, 0, 0)),
            pl.BlockSpec((1, 1, PAIR, 2, SIDE, WIDE), lambda p, c: (p, c, 0, 0, 0, 0)),
            pl.BlockSpec((1, 1, ROWS, PAIR * WIDE), lambda p, c: (p, c, 0, 0)),
            pl.BlockSpec((1, 1, ROWS, WIDE), lambda p, c: (p, c, 0, 0)),
            pl.BlockSpec((1, ROWS, width), lambda p, c: (c, 0, 0)),
            pl.BlockSpec((ROWS, width), lambda p, c: (late(p, c), 0)),
            pl.BlockSpec((ROWS, width), lambda p, c: (c, 0)),
        ],
        out_specs=[
            pl.BlockSpec((1, TPC, width), lambda p, c: (late(p, c), 0, 0)),
            pl.BlockSpec((1, packed_width, width), lambda p, c: (p, 0, 0)),
            pl.BlockSpec((1, PAIR * WIDE, width), lambda p, c: (p, 0, 0)),
            pl.BlockSpec((1, PAIR, 4, WIDE), lambda p, c: (p, 0, 0, 0)),
            pl.BlockSpec((1, width), lambda p, c: (0, 0)),
        ],
        out_shape=[
            shaped((clips, TPC, width), BF16),
            shaped((pairs, packed_width, width), F32),
            shaped((pairs, PAIR * WIDE, width), F32),
            shaped((pairs, PAIR, 4, WIDE), F32),
            shaped((1, width), F32),
        ],
        scratch_shapes=[pltpu.VMEM((clips, ROWS, width), F32)],
        compiler_params=compiler_params(2),
        name="attention_backward",
    )(x, w, mem, side, main, taps, proj, gain, packed, keys, att, log, normed, grad, grad_low)


def group_gather(own, heads, fetch=None):
    blocks = [fetch(own, 0) if fetch else own]
    for shift in range(1, heads):
        sent = fetch(own, -shift) if fetch else own
        blocks.append(lax.ppermute(sent, "head", [(src, (src - shift) % heads) for src in range(heads)]))
    return blocks


def group_sum(blocks, heads):
    total = blocks[0]
    for shift in range(1, heads):
        total = total + lax.ppermute(
            blocks[shift].astype(BF16), "head", [(src, (src + shift) % heads) for src in range(heads)]
        ).astype(F32)
    return total


def local(
    heads,
    inputs,
    qkv_weight,
    proj_weight,
    pool_weight,
    gain_one,
    gain_two,
    hidden_weight,
    output_weight,
    memory,
    clip_index,
    cotangent,
):
    width = inputs.shape[3]
    micro, own_clips = inputs.shape[:2]
    clips = micro * own_clips
    own_heads = qkv_weight.shape[1]
    all_heads = own_heads * heads
    pairs = all_heads // PAIR
    me = lax.axis_index("head")

    def mine(array, shift):
        start = lax.rem(me + shift + heads, heads) * own_clips
        return lax.dynamic_slice_in_dim(array, start, own_clips, axis=1)

    w_own = qkv_weight.transpose(1, 2, 0)
    w_all = jnp.concatenate(group_gather(w_own, heads), axis=0)
    proj_all = jnp.concatenate(group_gather(proj_weight, heads), axis=0)
    taps_all = jnp.concatenate(group_gather(pool_weight, heads), axis=0)
    memory_t = memory.transpose(0, 1, 3, 4, 2)
    mem_all = jnp.concatenate(group_gather(memory_t, heads, mine), axis=2)
    mem_all = mem_all.reshape(clips, all_heads, 2 * HD, TPC)

    first = lax.all_gather(hidden_weight, ("batch", "head"), axis=0, tiled=True)
    second = lax.all_gather(output_weight, ("batch", "head"), axis=0, tiled=True)

    pad = WIDE - HD
    w_all = jnp.pad(w_all.reshape(all_heads, 3, HD, width), ((0, 0), (0, 0), (0, pad), (0, 0)))
    w_all = w_all.reshape(pairs, PIECES * WIDE, width)
    proj_all = jnp.pad(proj_all, ((0, 0), (0, pad), (0, 0))).reshape(pairs, PAIR * WIDE, width)
    taps_all = jnp.pad(taps_all.astype(F32), ((0, 0), (0, 0), (0, pad))).reshape(pairs, PAIR, 4, WIDE)
    tail = mem_all[..., MAIN:].reshape(clips, all_heads, 2, HD, REST).swapaxes(3, 4)
    tail = jnp.pad(tail.astype(F32), ((0, 0),) * 4 + ((0, pad),))

    index = mine(clip_index, 0).reshape(clips, 1, 1)
    main_slot = lax.broadcasted_iota(jnp.int32, (1, 1, MAIN), 2) // PTOK
    main_mask = jnp.where(index > main_slot, 0.0, NEG).astype(F32)
    spot = lax.broadcasted_iota(jnp.int32, (1, 1, SIDE), 2)
    tail_open = (spot >= HALF) & (spot < HALF + REST) & (index > (TPC - 1) // PTOK)
    side_mask = jnp.where((spot < PTOK) | tail_open, 0.0, NEG).astype(F32)

    x = inputs.reshape(clips, TPC, width)
    gain_one = gain_one.reshape(1, width)
    gain_two = gain_two.reshape(1, width)
    packed, keys, att, log, normed, middle, normed_two = attention_forward(
        x, w_all, mem_all, tail, side_mask, main_mask, taps_all, proj_all, gain_one, gain_two
    )
    outputs, grad, grad_low, d_first, d_second, d_gain_two = mlp(
        normed_two.reshape(clips * ROWS, width),
        cotangent.reshape(clips, TPC, width),
        first,
        second,
        middle.reshape(clips * ROWS, width),
        gain_two,
    )
    d_x, d_w, d_proj, d_taps, d_gain_one = attention_backward(
        x, w_all, mem_all, side_mask, main_mask, taps_all, proj_all, gain_one,
        packed, keys, att, log, normed, grad, grad_low,
    )
    d_w = d_w.reshape(heads, own_heads, 3, WIDE, width)[:, :, :, :HD].reshape(heads, own_heads, 3 * HD, width)
    d_proj = d_proj.reshape(heads, own_heads, WIDE, width)[:, :, :HD]
    d_taps = d_taps.reshape(heads, own_heads, 4, WIDE)[..., :HD]
    d_w, d_proj, d_taps = (
        lax.psum(group_sum(list(grads), heads).astype(BF16), "batch").astype(F32)
        for grads in (d_w, d_proj, d_taps)
    )
    both = ("batch", "head")
    d_first = lax.psum_scatter(d_first, both, scatter_dimension=0, tiled=True).astype(F32)
    d_second = lax.psum_scatter(d_second, both, scatter_dimension=0, tiled=True).astype(F32)
    d_gains = lax.psum_scatter(
        jnp.concatenate([d_gain_one, d_gain_two], axis=0), both, scatter_dimension=1, tiled=True
    )
    return (
        outputs.reshape(inputs.shape),
        d_x.reshape(inputs.shape),
        d_w.transpose(2, 0, 1),
        d_proj,
        d_taps,
        d_gains[0],
        d_gains[1],
        d_first,
        d_second,
    )


def solution(mesh):
    return jax.shard_map(
        functools.partial(local, mesh.shape["head"]),
        mesh=mesh,
        in_specs=(
            P(None, ("batch", "head"), None, None),
            P(None, "head", None),
            P("head", None, None),
            P("head", None, None),
            P(),
            P(),
            P(("batch", "head"), None),
            P(("batch", "head"), None),
            P(None, "batch", None, "head", None),
            P(None, "batch"),
            P(None, ("batch", "head"), None, None),
        ),
        out_specs=(
            P(None, ("batch", "head"), None, None),
            P(None, ("batch", "head"), None, None),
            P(None, "head", None),
            P("head", None, None),
            P("head", None, None),
            P(("batch", "head")),
            P(("batch", "head")),
            P(("batch", "head"), None),
            P(("batch", "head"), None),
        ),
        check_vma=False,
    )
```

```python
import functools
import math

import jax
import jax.numpy as jnp
from jax import lax
from jax.experimental import pallas as pl
from jax.experimental.pallas import tpu as pltpu
from jax.sharding import PartitionSpec as P

HD = 96
WIDE = 128
FRAMES = 8
TPC = 392
PTOK = 196
SPOT = TPC // FRAMES
HALF = 200
ROWS = 2 * HALF
MAIN = 384
REST = TPC - MAIN
SIDE = 256
PAIR = 2
PIECES = 3 * PAIR

NORM_EPS = 1e-06
NEG = -1e30
LOG2E = 1.4426950408889634
SCORE = HD ** (-0.5)

F32 = jnp.float32
BF16 = jnp.bfloat16


def dot(a, b):
    return lax.dot_general(a, b, (((1,), (0,)), ((), ())), preferred_element_type=F32)


def dot_nt(a, b):
    return lax.dot_general(a, b, (((1,), (1,)), ((), ())), preferred_element_type=F32)


def dot_tn(a, b):
    return lax.dot_general(a, b, (((0,), (0,)), ((), ())), preferred_element_type=F32)


def reorder(shape, row_dim):
    rows = lax.broadcasted_iota(jnp.int32, shape, row_dim)
    tokens = lax.broadcasted_iota(jnp.int32, shape, 1 - row_dim)
    odd = (rows >= HALF).astype(jnp.int32)
    spot = rows - HALF * odd
    frame = sum((spot >= SPOT * step).astype(jnp.int32) for step in range(1, FRAMES // 2))
    return ((tokens == spot + SPOT * (frame + odd)) & (spot < PTOK)).astype(BF16)


def norm_parts(values):
    average = jnp.mean(values, axis=-1, keepdims=True)
    centered = values - average
    spread = lax.rsqrt(jnp.mean(centered * centered, axis=-1, keepdims=True) + NORM_EPS)
    return centered * spread, spread


def norm_pull(values, gain, grad):
    unit, spread = norm_parts(values)
    scaled = grad * gain
    inner = jnp.mean(scaled * unit, axis=-1, keepdims=True)
    pulled = spread * (scaled - jnp.mean(scaled, axis=-1, keepdims=True) - unit * inner)
    return pulled, jnp.sum(grad * unit, axis=0, keepdims=True)


def value_columns(memory_t):
    return jnp.concatenate([memory_t[HD:], jnp.zeros((WIDE - HD, memory_t.shape[1]), BF16)], axis=0)


def forward_kernel(
    x_ref, w_ref, mem_ref, tail_ref, side_ref, main_ref, taps_ref, gain_one_ref, gain_two_ref,
    packed_ref, keys_ref, att_ref, log_ref, normed_ref, middle_ref, normed_two_ref,
    x_rows, normed_rows, branch,
):
    forward_step(
        pl.program_id(0), pl.program_id(1), pl.num_programs(0),
        w_ref.at[0], mem_ref.at[0], tail_ref.at[0], taps_ref.at[0],
        x_ref, side_ref, main_ref, gain_one_ref, gain_two_ref,
        packed_ref, keys_ref, att_ref, log_ref, normed_ref, middle_ref, normed_two_ref,
        x_rows, normed_rows, branch,
    )


def forward_step(
    pair, clip, pairs,
    w_ref, mem_ref, tail_ref, taps_ref,
    x_ref, side_ref, main_ref, gain_one_ref, gain_two_ref,
    packed_ref, keys_ref, att_ref, log_ref, normed_ref, middle_ref, normed_two_ref,
    x_rows, normed_rows, branch,
):
    here = pl.ds(clip, 1)

    @pl.when(pair == 0)
    def _():
        rows = dot(reorder((ROWS, TPC), 0), x_ref[0])
        x_rows[here] = rows.astype(BF16)[None]
        unit, _ = norm_parts(rows)
        low = (unit * gain_one_ref[...]).astype(BF16)
        normed_rows[here] = low[None]
        normed_ref[0] = low

    normed = normed_rows[here][0]
    packed = dot_nt(normed, w_ref[: PIECES * WIDE])
    packed_ref[0, 0] = packed.astype(BF16)
    logs = []
    outs = []
    for head in range(PAIR):
        base = 3 * WIDE * head
        query = packed[:, base : base + WIDE]
        key = packed[:, base + WIDE : base + 2 * WIDE]
        value = packed[:, base + 2 * WIDE : base + 3 * WIDE]
        query_low = query.astype(BF16)
        taps = taps_ref[head]
        zeros = jnp.zeros((SIDE - HALF - REST, WIDE), F32)
        pooled_key = taps[0:1] * key[:HALF] + taps[1:2] * key[HALF:]
        pooled_value = taps[2:3] * value[:HALF] + taps[3:4] * value[HALF:]
        tail = tail_ref[head].astype(F32)
        side_key = jnp.concatenate([pooled_key, tail[:REST], zeros], axis=0).astype(BF16)
        side_value = jnp.concatenate([pooled_value, tail[REST:], zeros], axis=0).astype(BF16)
        keys_ref[0, 0, head, 0] = side_key
        keys_ref[0, 0, head, 1] = side_value
        memory_t = mem_ref[head]
        score_side = dot_nt(query_low, side_key) * (SCORE * LOG2E) + side_ref[0]
        score_main = dot(query_low, memory_t[:WIDE]) * (SCORE * LOG2E) + main_ref[0]
        top = jnp.maximum(
            jnp.max(score_side, axis=-1, keepdims=True), jnp.max(score_main, axis=-1, keepdims=True)
        )
        weight_side = jnp.exp2(score_side - top)
        weight_main = jnp.exp2(score_main - top)
        total = jnp.sum(weight_side, axis=-1, keepdims=True) + jnp.sum(weight_main, axis=-1, keepdims=True)
        mixed = dot(weight_side.astype(BF16), side_value) + dot_nt(
            weight_main.astype(BF16), value_columns(memory_t)
        )
        outs.append(mixed / total + query)
        logs.append(top + jnp.log2(total))
    attended = jnp.concatenate(outs, axis=1).astype(BF16)
    att_ref[0, 0] = attended
    lane = lax.broadcasted_iota(jnp.int32, (ROWS, WIDE), 1)
    log_ref[0, 0] = jnp.where(lane == 0, logs[0], logs[1])
    part = dot(attended, w_ref[PIECES * WIDE :])[None]

    @pl.when(pair == 0)
    def _():
        branch[here] = part

    @pl.when(pair > 0)
    def _():
        branch[here] += part

    @pl.when(pair == pairs - 1)
    def _():
        middle = x_rows[here][0].astype(F32) + branch[here][0]
        middle_ref[0] = middle
        unit, _ = norm_parts(middle)
        normed_two_ref[0] = (unit * gain_two_ref[...]).astype(BF16)


def mlp_kernel(
    normed_ref, cot_ref, first_ref, second_ref, middle_ref, gain_ref,
    out_ref, grad_ref, grad_low_ref, d_first_ref, d_second_ref, d_gain_ref,
    cot_rows, cot_t, normed_t, total, grad_normed, active, grad_hidden,
):
    tile = pl.program_id(0)
    clips = cot_ref.shape[0]
    wide = normed_ref.shape[1]

    @pl.when(tile == 0)
    def _():
        swap = reorder((ROWS, TPC), 0)

        @pl.loop(0, clips)
        def _(clip):
            here = pl.ds(pl.multiple_of(clip * ROWS, ROWS), ROWS)
            cot_rows[here, :] = dot(swap, cot_ref[clip]).astype(BF16)
            total[here, :] = middle_ref[here, :]
            grad_normed[here, :] = jnp.zeros((ROWS, wide), F32)

        for lanes in range(0, wide, WIDE):
            cot_t[lanes : lanes + WIDE, :] = cot_rows[:, lanes : lanes + WIDE].T
            normed_t[lanes : lanes + WIDE, :] = normed_ref[:, lanes : lanes + WIDE].T

    first = first_ref[...]
    second = second_ref[...]

    @pl.loop(0, clips)
    def _(clip):
        here = pl.ds(pl.multiple_of(clip * ROWS, ROWS), ROWS)
        hidden = dot(normed_ref[here, :], first)
        grad_active = dot_nt(cot_rows[here, :], second)
        bell = jnp.exp2(hidden * hidden * (-0.5 * LOG2E))
        step = 1.0 / (1.0 + (0.3275911 * math.sqrt(0.5)) * jnp.abs(hidden))
        tail = step * (0.5 * 1.061405429) + (0.5 * -1.453152027)
        tail = step * tail + (0.5 * 1.421413741)
        tail = step * tail + (0.5 * -0.284496736)
        tail = step * tail + (0.5 * 0.254829592)
        tail = step * tail * bell
        cumulative = jnp.where(hidden < 0.0, tail, 1.0 - tail)
        slope = cumulative + hidden * bell * 0.3989422804014327
        active_low = (hidden * cumulative).astype(BF16)
        hidden_low = (slope * grad_active).astype(BF16)
        active[here, :] = active_low
        grad_hidden[here, :] = hidden_low
        total[here, :] += dot(active_low, second)
        grad_normed[here, :] += dot_nt(hidden_low, first)

    d_first_ref[...] = dot(normed_t[...], grad_hidden[...]).astype(BF16)
    d_second_ref[...] = dot(cot_t[...], active[...]).astype(BF16).T

    @pl.when(tile == pl.num_programs(0) - 1)
    def _():
        back = reorder((TPC, ROWS), 1)
        d_gain_ref[...] = jnp.zeros_like(d_gain_ref)

        @pl.loop(0, clips)
        def _(clip):
            here = pl.ds(pl.multiple_of(clip * ROWS, ROWS), ROWS)
            out_ref[clip] = dot(back, total[here, :].astype(BF16)).astype(BF16)
            pulled, d_gain = norm_pull(middle_ref[here, :], gain_ref[...], grad_normed[here, :])
            grad = cot_rows[here, :].astype(F32) + pulled
            grad_ref[here, :] = grad
            grad_low_ref[here, :] = grad.astype(BF16)
            d_gain_ref[...] += d_gain


def backward_kernel(
    x_ref, w_ref, mem_ref, side_ref, main_ref, taps_ref, gain_ref,
    packed_ref, keys_ref, att_ref, log_ref, normed_ref, grad_ref, grad_low_ref,
    d_x_ref, d_w_ref, d_taps_ref, d_gain_ref,
    grad_normed,
):
    pair, clip = pl.program_id(0), pl.program_id(1)
    here = pl.ds(clip, 1)

    @pl.when(clip == 0)
    def _():
        d_w_ref[...] = jnp.zeros_like(d_w_ref)
        d_taps_ref[...] = jnp.zeros_like(d_taps_ref)

    grad_branch = grad_low_ref[...]
    grad_out = dot_nt(grad_branch, w_ref[0, PIECES * WIDE :])
    d_w_ref[0, PIECES * WIDE :] += dot_tn(att_ref[0, 0], grad_branch)
    pieces = []
    for head in range(PAIR):
        base = 3 * WIDE * head
        query = packed_ref[0, 0, :, base : base + WIDE]
        key = packed_ref[0, 0, :, base + WIDE : base + 2 * WIDE].astype(F32)
        value = packed_ref[0, 0, :, base + 2 * WIDE : base + 3 * WIDE].astype(F32)
        out_grad = grad_out[:, WIDE * head : WIDE * (head + 1)].astype(BF16)
        taps = taps_ref[0, head]
        side_key = keys_ref[0, 0, head, 0]
        side_value = keys_ref[0, 0, head, 1]
        memory_t = mem_ref[0, head]
        log = log_ref[0, 0, :, head : head + 1]
        score_side = dot_nt(query, side_key) * (SCORE * LOG2E) + side_ref[0]
        score_main = dot(query, memory_t[:WIDE]) * (SCORE * LOG2E) + main_ref[0]
        weight_side = jnp.exp2(score_side - log)
        weight_main = jnp.exp2(score_main - log)
        grad_side = dot_nt(out_grad, side_value)
        grad_main = dot(out_grad, value_columns(memory_t))
        inner = jnp.sum(weight_side * grad_side, axis=-1, keepdims=True) + jnp.sum(
            weight_main * grad_main, axis=-1, keepdims=True
        )
        score_grad_side = (weight_side * (grad_side - inner)).astype(BF16)
        score_grad_main = (weight_main * (grad_main - inner)).astype(BF16)
        grad_query = (
            dot(score_grad_side, side_key) + dot_nt(score_grad_main, memory_t[:WIDE])
        ) * SCORE + out_grad.astype(F32)
        grad_key = dot_tn(score_grad_side, query)[:HALF] * SCORE
        grad_value = dot_tn(weight_side.astype(BF16), out_grad)[:HALF]
        pieces += [
            grad_query,
            jnp.concatenate([taps[0:1] * grad_key, taps[1:2] * grad_key], axis=0),
            jnp.concatenate([taps[2:3] * grad_value, taps[3:4] * grad_value], axis=0),
        ]
        d_taps_ref[0, head] += jnp.concatenate(
            [
                jnp.sum(part * grad, axis=0, keepdims=True)
                for part, grad in (
                    (key[:HALF], grad_key),
                    (key[HALF:], grad_key),
                    (value[:HALF], grad_value),
                    (value[HALF:], grad_value),
                )
            ],
            axis=0,
        )
    grad_packed = jnp.concatenate(pieces, axis=1).astype(BF16)
    d_w_ref[0, : PIECES * WIDE] += dot_tn(grad_packed, normed_ref[0])
    part = dot(grad_packed, w_ref[0, : PIECES * WIDE])[None]

    @pl.when(pair == 0)
    def _():
        grad_normed[here] = part

    @pl.when(pair > 0)
    def _():
        grad_normed[here] += part

    @pl.when(pair == pl.num_programs(0) - 1)
    def _():
        rows = dot(reorder((ROWS, TPC), 0), x_ref[0])
        pulled, d_gain = norm_pull(rows, gain_ref[...], grad_normed[here][0])
        d_x = (grad_ref[...] + pulled).astype(BF16)
        d_x_ref[0] = dot(reorder((TPC, ROWS), 1), d_x).astype(BF16)

        @pl.when(clip == 0)
        def _():
            d_gain_ref[...] = d_gain

        @pl.when(clip > 0)
        def _():
            d_gain_ref[...] += d_gain


VMEM_LIMIT = 60 << 20


def compiler_params(dims):
    return pltpu.CompilerParams(
        dimension_semantics=("arbitrary",) * dims, vmem_limit_bytes=VMEM_LIMIT
    )


def shaped(shape, dtype):
    return jax.ShapeDtypeStruct(shape, dtype)


class Links:
    def __init__(self, send, recv):
        self.send, self.recv, self.made = send, recv, {}

    def add(self, name, src, dst, device):
        at = len(self.made)
        self.made[name] = (src, dst, device, at)

    def get(self, name):
        src, dst, device, at = self.made[name]
        return pltpu.make_async_remote_copy(
            src_ref=src,
            dst_ref=dst,
            send_sem=self.send.at[at],
            recv_sem=self.recv.at[at],
            device_id=device,
            device_id_type=pl.DeviceIdType.MESH,
        )

    def start(self, *names):
        for name in names:
            self.get(name).start()

    def arrived(self, *names):
        for name in names:
            self.get(name).wait_recv()

    def sent(self):
        for name in self.made:
            self.get(name).wait_send()


def place():
    batch, head = lax.axis_index("batch"), lax.axis_index("head")
    z, y, core = batch // 4, lax.rem(batch // 2, 2), lax.rem(batch, 2)

    def at(z, y, core, x):
        return {"batch": (z * 2 + y) * 2 + core, "head": x}

    return z, y, core, head, at


def greet(devices):
    barrier = pltpu.get_barrier_semaphore()
    for device in devices:
        pl.semaphore_signal(barrier, inc=1, device_id=device, device_id_type=pl.DeviceIdType.MESH)
    pl.semaphore_wait(barrier, len(devices))


def turn(z, shift):
    return lax.rem(z + shift + 4, 4)


FORWARD_COPIES = 48


def forward_links_kernel(
    x_ref, side_ref, main_ref, gain_one_ref, gain_two_ref,
    w_own, mem_own, tail_own, taps_own, hidden_own, output_own,
    packed_ref, keys_ref, att_ref, log_ref, normed_ref, middle_ref, normed_two_ref,
    first_all, second_all, w_out, mem_out, taps_out,
    x_rows, normed_rows, branch, w_all, mem_all, tail_all, taps_all,
    send, recv, near, save,
):
    step = pl.program_id(0)
    z, y, core, x, at = place()
    links = Links(send, recv)
    beside, above, sibling = at(z, y, core, 1 - x), at(z, 1 - y, core, x), at(z, y, 1 - core, x)
    along = [at(turn(z, shift), y, core, x) for shift in (1, 2, 3)]
    column = pl.ds(pl.multiple_of(core * MAIN, MAIN), MAIN)

    def slab(z, y):
        return (lax.div(2 * z + y, 4), pl.ds(pl.multiple_of(lax.rem(2 * z + y, 4) * 256, 256), 256), column)

    def w_far(z, y):
        pair, rows, lanes = slab(z, y)
        return w_all.at[2 + pair, rows, lanes]

    links.add("xw", w_own.at[slab(z, y)], w_far(z, y), beside)
    for shift in (1, 2, 3):
        links.add(f"zw{shift}", w_far(z, y), w_far(z, y), along[shift - 1])
    for shift in range(4):
        links.add(f"yw{shift}", w_far(turn(z, -shift), y), w_far(turn(z, -shift), y), above)
    far = w_all.at[pl.ds(2, 2), :, column]
    links.add("cw", far, far, sibling)
    me = ((z * 2 + y) * 2 + core) * 2 + x
    links.add("x0", hidden_own, first_all.at[me], beside)
    links.add("x1", output_own, second_all.at[me], beside)

    def group(which, z, y):
        return (first_all, second_all)[which].at[pl.ds(((z * 2 + y) * 2 + core) * 2, 2)]

    for which in (0, 1):
        for shift in (1, 2, 3):
            links.add(f"z{shift}{which}", group(which, z, y), group(which, z, y), along[shift - 1])
        for shift in range(4):
            from_z = turn(z, -shift)
            links.add(f"y{shift}{which}", group(which, from_z, y), group(which, from_z, y), above)
            links.add(f"c{shift}{which}", group(which, from_z, y), group(which, from_z, y), sibling)
            links.add(f"d{shift}{which}", group(which, from_z, 1 - y), group(which, from_z, 1 - y), sibling)
    clips = mem_own.shape[0]
    for clip in range(clips):
        links.add(f"m{clip}", mem_own.at[clip, 1 - x, :, :, pl.ds(0, MAIN)], mem_all.at[1, clip], beside)
    links.add("tail", tail_own.at[:, 1 - x], tail_all.at[1], beside)
    links.add("taps", taps_own, taps_all.at[pl.ds(2, 2)], beside)

    local = [
        (w_own, w_all.at[pl.ds(0, 2)]),
        (tail_own.at[:, x], tail_all.at[0]),
        (taps_own, taps_all.at[pl.ds(0, 2)]),
        (hidden_own, first_all.at[me]),
        (output_own, second_all.at[me]),
    ] + [(mem_own.at[clip, x, :, :, pl.ds(0, MAIN)], mem_all.at[0, clip]) for clip in range(clips)]
    local = [pltpu.make_async_copy(src, dst, near.at[i]) for i, (src, dst) in enumerate(local)]
    saved = [
        (w_all, w_out),
        (taps_all, taps_out),
        (mem_all.at[0], mem_out.at[0]),
        (mem_all.at[1], mem_out.at[1]),
    ]
    saved = [pltpu.make_async_copy(src, dst, save.at[i]) for i, (src, dst) in enumerate(saved)]

    @pl.when(step == 0)
    def _():
        greet([beside, above, sibling] + along)
        links.start("xw", "taps", "tail", "x0", "x1")
        for copy in local:
            copy.start()
        for copy in local:
            copy.wait()

    def both(*names):
        return [name + str(which) for name in names for which in (0, 1)]

    plan = {
        2: (["xw"], ["zw1", "zw2", "zw3", "yw0"]),
        3: (["x0", "x1"], both("z1", "z2", "z3", "y0", "c0") + ["m0", "m1"]),
        5: (["zw1", "zw2", "zw3"], ["yw1", "yw2", "yw3"]),
        6: ([], ["m2", "m3"]),
        7: (["yw0", "yw1", "yw2", "yw3"], ["cw"]),
        8: (["cw", "tail", "taps", "m0"], []),
        9: (both("z1"), both("y1", "c1")),
        10: (["m1"] + both("z2"), both("y2", "c2")),
        12: (["m2"], []),
        13: (both("y0", "y1"), both("d0", "d1")),
        14: (["m3"] + both("z3"), both("y3", "c3")),
    }
    for when, (awaited, started) in plan.items():

        @pl.when(step == when)
        def _(awaited=awaited, started=started):
            links.arrived(*awaited)
            links.start(*started)

    @pl.when(step == 14)
    def _():
        for copy in saved:
            copy.start()

    pair, clip = pair_of(step), clip_of(step)
    side = lax.div(pair, 2)
    heads = pl.ds(lax.rem(pair, 2) * PAIR, PAIR)
    forward_step(
        pair, clip, 4,
        w_all.at[pair], mem_all.at[side, clip, heads], tail_all.at[side, clip, heads], taps_all.at[pair],
        x_ref, side_ref, main_ref, gain_one_ref, gain_two_ref,
        packed_ref, keys_ref, att_ref, log_ref, normed_ref, middle_ref, normed_two_ref,
        x_rows, normed_rows, branch,
    )

    @pl.when(step == pl.num_programs(0) - 1)
    def _():
        links.arrived(*both("y2", "y3"))
        links.start(*both("d2", "d3"))
        for copy in saved:
            copy.wait()
        links.arrived(*both("c0", "c1", "c2", "c3", "d0", "d1", "d2", "d3"))
        links.sent()


def pair_of(step):
    return jnp.where(step < 8, lax.div(step, 4), 2 + lax.rem(step, 2))


def clip_of(step):
    return jnp.where(step < 8, lax.rem(step, 4), lax.div(step, 2) - 4)


def attention_forward_links(x, w, mem, tail, side, main, taps, gain_one, gain_two, hidden_weight, output_weight):
    clips, width = x.shape[0], x.shape[2]
    packed_width = PIECES * WIDE
    devices = 32
    early = lambda s: jnp.where(s < 4, s, clips - 1)
    late = lambda s: jnp.where(s < 8, 0, clip_of(s))
    anywhere = pl.BlockSpec(memory_space=pl.ANY)
    return pl.pallas_call(
        forward_links_kernel,
        grid=(4 * clips,),
        in_specs=[
            pl.BlockSpec((1, TPC, width), lambda s: (early(s), 0, 0)),
            pl.BlockSpec((1, 1, SIDE), lambda s: (clip_of(s), 0, 0)),
            pl.BlockSpec((1, 1, MAIN), lambda s: (clip_of(s), 0, 0)),
            pl.BlockSpec((1, width), lambda s: (0, 0)),
            pl.BlockSpec((1, width), lambda s: (0, 0)),
        ] + [anywhere] * 6,
        out_specs=[
            pl.BlockSpec((1, 1, ROWS, packed_width), lambda s: (pair_of(s), clip_of(s), 0, 0)),
            pl.BlockSpec((1, 1, PAIR, 2, SIDE, WIDE), lambda s: (pair_of(s), clip_of(s), 0, 0, 0, 0)),
            pl.BlockSpec((1, 1, ROWS, PAIR * WIDE), lambda s: (pair_of(s), clip_of(s), 0, 0)),
            pl.BlockSpec((1, 1, ROWS, WIDE), lambda s: (pair_of(s), clip_of(s), 0, 0)),
            pl.BlockSpec((1, ROWS, width), lambda s: (early(s), 0, 0)),
            pl.BlockSpec((1, ROWS, width), lambda s: (late(s), 0, 0)),
            pl.BlockSpec((1, ROWS, width), lambda s: (late(s), 0, 0)),
        ] + [anywhere] * 5,
        out_shape=[
            shaped((4, clips, ROWS, packed_width), BF16),
            shaped((4, clips, PAIR, 2, SIDE, WIDE), BF16),
            shaped((4, clips, ROWS, PAIR * WIDE), BF16),
            shaped((4, clips, ROWS, WIDE), F32),
            shaped((clips, ROWS, width), BF16),
            shaped((clips, ROWS, width), F32),
            shaped((clips, ROWS, width), BF16),
            shaped((devices,) + hidden_weight.shape, BF16),
            shaped((devices,) + output_weight.shape, BF16),
            shaped((4,) + w.shape[1:], BF16),
            shaped((2, clips, 4, 2 * HD, MAIN), BF16),
            shaped((4,) + taps.shape[1:], F32),
        ],
        scratch_shapes=[
            pltpu.VMEM((clips, ROWS, width), BF16),
            pltpu.VMEM((clips, ROWS, width), BF16),
            pltpu.VMEM((clips, ROWS, width), F32),
            pltpu.VMEM((4,) + w.shape[1:], BF16),
            pltpu.VMEM((2, clips, 4, 2 * HD, MAIN), BF16),
            pltpu.VMEM((2, clips, 4, 2 * REST, WIDE), BF16),
            pltpu.VMEM((4,) + taps.shape[1:], F32),
            pltpu.SemaphoreType.DMA((FORWARD_COPIES,)),
            pltpu.SemaphoreType.DMA((FORWARD_COPIES,)),
            pltpu.SemaphoreType.DMA((5 + clips,)),
            pltpu.SemaphoreType.DMA((4,)),
        ],
        compiler_params=pltpu.CompilerParams(
            dimension_semantics=("arbitrary",),
            vmem_limit_bytes=VMEM_LIMIT,
            collective_id=0,
            has_side_effects=True,
        ),
        name="attention_forward_links",
    )(x, side, main, gain_one, gain_two, w, mem, tail, taps, hidden_weight, output_weight)


def attention_forward(x, w, mem, tail, side, main, taps, gain_one, gain_two):
    clips, pairs = x.shape[0], w.shape[0]
    width = x.shape[2]
    packed_width = PIECES * WIDE
    weight_rows = w.shape[1]
    late = lambda p, c: jnp.where(p == pairs - 1, c, 0)
    early = lambda p, c: jnp.where(p == 0, c, clips - 1)
    per_step = lambda p, c: (p, c)
    return pl.pallas_call(
        forward_kernel,
        grid=(pairs, clips),
        in_specs=[
            pl.BlockSpec((1, TPC, width), lambda p, c: (early(p, c), 0, 0)),
            pl.BlockSpec((1, weight_rows, width), lambda p, c: (p, 0, 0)),
            pl.BlockSpec((1, PAIR, 2 * HD, MAIN), lambda p, c: (c, p, 0, 0)),
            pl.BlockSpec((1, PAIR, 2 * REST, WIDE), lambda p, c: (c, p, 0, 0)),
            pl.BlockSpec((1, 1, SIDE), lambda p, c: (c, 0, 0)),
            pl.BlockSpec((1, 1, MAIN), lambda p, c: (c, 0, 0)),
            pl.BlockSpec((1, PAIR, 4, WIDE), lambda p, c: (p, 0, 0, 0)),
            pl.BlockSpec((1, width), lambda p, c: (0, 0)),
            pl.BlockSpec((1, width), lambda p, c: (0, 0)),
        ],
        out_specs=[
            pl.BlockSpec((1, 1, ROWS, packed_width), lambda p, c: (p, c, 0, 0)),
            pl.BlockSpec((1, 1, PAIR, 2, SIDE, WIDE), lambda p, c: (p, c, 0, 0, 0, 0)),
            pl.BlockSpec((1, 1, ROWS, PAIR * WIDE), lambda p, c: (p, c, 0, 0)),
            pl.BlockSpec((1, 1, ROWS, WIDE), lambda p, c: (p, c, 0, 0)),
            pl.BlockSpec((1, ROWS, width), lambda p, c: (early(p, c), 0, 0)),
            pl.BlockSpec((1, ROWS, width), lambda p, c: (late(p, c), 0, 0)),
            pl.BlockSpec((1, ROWS, width), lambda p, c: (late(p, c), 0, 0)),
        ],
        out_shape=[
            shaped((pairs, clips, ROWS, packed_width), BF16),
            shaped((pairs, clips, PAIR, 2, SIDE, WIDE), BF16),
            shaped((pairs, clips, ROWS, PAIR * WIDE), BF16),
            shaped((pairs, clips, ROWS, WIDE), F32),
            shaped((clips, ROWS, width), BF16),
            shaped((clips, ROWS, width), F32),
            shaped((clips, ROWS, width), BF16),
        ],
        scratch_shapes=[
            pltpu.VMEM((clips, ROWS, width), BF16),
            pltpu.VMEM((clips, ROWS, width), BF16),
            pltpu.VMEM((clips, ROWS, width), F32),
        ],
        compiler_params=compiler_params(2),
        name="attention_forward",
    )(x, w, mem, tail, side, main, taps, gain_one, gain_two)


def once(shape):
    return pl.BlockSpec(shape, lambda t: (0,) * len(shape), pipeline_mode=pl.Buffered(1))


def mlp(normed, cot, first, second, middle, gain):
    rows, width = normed.shape
    hidden = first.shape[1]
    clips = cot.shape[0]
    tile = 512
    return pl.pallas_call(
        mlp_kernel,
        grid=(hidden // tile,),
        in_specs=[
            once((rows, width)),
            once((clips, TPC, width)),
            pl.BlockSpec((width, tile), lambda t: (0, t)),
            pl.BlockSpec((tile, width), lambda t: (t, 0)),
            once((rows, width)),
            once((1, width)),
        ],
        out_specs=[
            once((clips, TPC, width)),
            once((rows, width)),
            once((rows, width)),
            pl.BlockSpec((width, tile), lambda t: (0, t)),
            pl.BlockSpec((tile, width), lambda t: (t, 0)),
            once((1, width)),
        ],
        out_shape=[
            shaped((clips, TPC, width), BF16),
            shaped((rows, width), F32),
            shaped((rows, width), BF16),
            shaped((width, hidden), BF16),
            shaped((hidden, width), BF16),
            shaped((1, width), F32),
        ],
        scratch_shapes=[
            pltpu.VMEM((rows, width), BF16),
            pltpu.VMEM((width, rows), BF16),
            pltpu.VMEM((width, rows), BF16),
            pltpu.VMEM((rows, width), F32),
            pltpu.VMEM((rows, width), F32),
            pltpu.VMEM((rows, tile), BF16),
            pltpu.VMEM((rows, tile), BF16),
        ],
        compiler_params=compiler_params(1),
        name="mlp",
    )(normed, cot, first, second, middle, gain)


def attention_backward(x, w, mem, side, main, taps, gain, packed, keys, att, log, normed, grad, grad_low):
    clips, pairs = x.shape[0], w.shape[0]
    width = x.shape[2]
    packed_width = PIECES * WIDE
    weight_rows = w.shape[1]
    late = lambda p, c: jnp.where(p == pairs - 1, c, 0)
    return pl.pallas_call(
        backward_kernel,
        grid=(pairs, clips),
        in_specs=[
            pl.BlockSpec((1, TPC, width), lambda p, c: (late(p, c), 0, 0)),
            pl.BlockSpec((1, weight_rows, width), lambda p, c: (p, 0, 0)),
            pl.BlockSpec((1, PAIR, 2 * HD, MAIN), lambda p, c: (c, p, 0, 0))
            if mem.ndim == 4
            else pl.BlockSpec(
                (None, 1, PAIR, 2 * HD, MAIN), lambda p, c: (lax.div(p, 2), c, lax.rem(p, 2), 0, 0)
            ),
            pl.BlockSpec((1, 1, SIDE), lambda p, c: (c, 0, 0)),
            pl.BlockSpec((1, 1, MAIN), lambda p, c: (c, 0, 0)),
            pl.BlockSpec((1, PAIR, 4, WIDE), lambda p, c: (p, 0, 0, 0)),
            pl.BlockSpec((1, width), lambda p, c: (0, 0)),
            pl.BlockSpec((1, 1, ROWS, packed_width), lambda p, c: (p, c, 0, 0)),
            pl.BlockSpec((1, 1, PAIR, 2, SIDE, WIDE), lambda p, c: (p, c, 0, 0, 0, 0)),
            pl.BlockSpec((1, 1, ROWS, PAIR * WIDE), lambda p, c: (p, c, 0, 0)),
            pl.BlockSpec((1, 1, ROWS, WIDE), lambda p, c: (p, c, 0, 0)),
            pl.BlockSpec((1, ROWS, width), lambda p, c: (c, 0, 0)),
            pl.BlockSpec((ROWS, width), lambda p, c: (late(p, c), 0)),
            pl.BlockSpec((ROWS, width), lambda p, c: (c, 0)),
        ],
        out_specs=[
            pl.BlockSpec((1, TPC, width), lambda p, c: (late(p, c), 0, 0)),
            pl.BlockSpec((1, weight_rows, width), lambda p, c: (p, 0, 0)),
            pl.BlockSpec((1, PAIR, 4, WIDE), lambda p, c: (p, 0, 0, 0)),
            pl.BlockSpec((1, width), lambda p, c: (0, 0)),
        ],
        out_shape=[
            shaped((clips, TPC, width), BF16),
            shaped((pairs, weight_rows, width), F32),
            shaped((pairs, PAIR, 4, WIDE), F32),
            shaped((1, width), F32),
        ],
        scratch_shapes=[pltpu.VMEM((clips, ROWS, width), F32)],
        compiler_params=compiler_params(2),
        name="attention_backward",
    )(x, w, mem, side, main, taps, gain, packed, keys, att, log, normed, grad, grad_low)


def group_gather(own, heads, fetch=None):
    blocks = [fetch(own, 0) if fetch else own]
    for shift in range(1, heads):
        sent = fetch(own, -shift) if fetch else own
        blocks.append(lax.ppermute(sent, "head", [(src, (src - shift) % heads) for src in range(heads)]))
    return blocks


def group_sum(blocks, heads):
    total = blocks[0]
    for shift in range(1, heads):
        total = total + lax.ppermute(
            blocks[shift].astype(BF16), "head", [(src, (src + shift) % heads) for src in range(heads)]
        ).astype(F32)
    return total


def local(
    heads,
    batches,
    inputs,
    qkv_weight,
    proj_weight,
    pool_weight,
    gain_one,
    gain_two,
    hidden_weight,
    output_weight,
    memory,
    clip_index,
    cotangent,
):
    width = inputs.shape[3]
    micro, own_clips = inputs.shape[:2]
    clips = micro * own_clips
    own_heads = qkv_weight.shape[1]
    all_heads = own_heads * heads
    pairs = all_heads // PAIR
    me = lax.axis_index("head")
    linked = (heads, batches, micro, own_clips) == (2, 16, 4, 1)

    def mine(array, shift):
        start = lax.rem(me + shift + heads, heads) * own_clips
        return lax.dynamic_slice_in_dim(array, start, own_clips, axis=1)

    pad = WIDE - HD
    qkv_rows = jnp.pad(
        qkv_weight.transpose(1, 2, 0).reshape(own_heads, 3, HD, width), ((0, 0), (0, 0), (0, pad), (0, 0))
    )
    proj_rows = jnp.pad(proj_weight, ((0, 0), (0, pad), (0, 0)))
    taps_own = jnp.pad(pool_weight.astype(F32), ((0, 0), (0, 0), (0, pad)))
    memory_t = memory.transpose(0, 1, 3, 4, 2)
    tail_own = memory_t[..., MAIN:].reshape(memory_t.shape[:3] + (2, HD, REST)).swapaxes(4, 5)
    tail_own = jnp.pad(tail_own, ((0, 0),) * 5 + ((0, pad),)).reshape(memory_t.shape[:3] + (2 * REST, WIDE))

    index = mine(clip_index, 0).reshape(clips, 1, 1)
    main_slot = lax.broadcasted_iota(jnp.int32, (1, 1, MAIN), 2) // PTOK
    main_mask = jnp.where(index > main_slot, 0.0, NEG).astype(F32)
    spot = lax.broadcasted_iota(jnp.int32, (1, 1, SIDE), 2)
    tail_open = (spot >= HALF) & (spot < HALF + REST) & (index > (TPC - 1) // PTOK)
    side_mask = jnp.where((spot < PTOK) | tail_open, 0.0, NEG).astype(F32)

    x = inputs.reshape(clips, TPC, width)
    gain_one = gain_one.reshape(1, width)
    gain_two = gain_two.reshape(1, width)
    w_own = jnp.concatenate(
        [
            qkv_rows.reshape(-1, PIECES * WIDE, width),
            proj_rows.reshape(-1, PAIR * WIDE, width),
        ],
        axis=1,
    ) if own_heads % PAIR == 0 else None
    if linked:
        (packed, keys, att, log, normed, middle, normed_two, first, second, w_all, mem_all, taps_all) = (
            attention_forward_links(
                x, w_own, memory_t, tail_own, side_mask, main_mask,
                taps_own.reshape(-1, PAIR, 4, WIDE), gain_one, gain_two, hidden_weight, output_weight,
            )
        )
        first = first.reshape(width, -1)
        second = second.reshape(-1, width)
    else:
        qkv_all = jnp.concatenate(group_gather(qkv_rows, heads), axis=0)
        proj_all = jnp.concatenate(group_gather(proj_rows, heads), axis=0)
        w_all = jnp.concatenate(
            [
                qkv_all.reshape(pairs, PIECES * WIDE, width),
                proj_all.reshape(pairs, PAIR * WIDE, width),
            ],
            axis=1,
        )
        taps_all = jnp.concatenate(group_gather(taps_own, heads), axis=0).reshape(pairs, PAIR, 4, WIDE)
        mem_all = jnp.concatenate(group_gather(memory_t, heads, mine), axis=2)
        mem_all = mem_all.reshape(clips, all_heads, 2 * HD, TPC)
        tail = jnp.concatenate(group_gather(tail_own, heads, mine), axis=2)
        tail = tail.reshape(clips, all_heads, 2 * REST, WIDE)

        first = lax.all_gather(hidden_weight, ("batch", "head"), axis=0, tiled=True)
        second = lax.all_gather(output_weight, ("batch", "head"), axis=0, tiled=True)
        packed, keys, att, log, normed, middle, normed_two = attention_forward(
            x, w_all, mem_all, tail, side_mask, main_mask, taps_all, gain_one, gain_two
        )
    outputs, grad, grad_low, d_first, d_second, d_gain_two = mlp(
        normed_two.reshape(clips * ROWS, width),
        cotangent.reshape(clips, TPC, width),
        first,
        second,
        middle.reshape(clips * ROWS, width),
        gain_two,
    )
    d_x, d_w, d_taps, d_gain_one = attention_backward(
        x, w_all, mem_all, side_mask, main_mask, taps_all, gain_one,
        packed, keys, att, log, normed, grad, grad_low,
    )
    d_proj = d_w[:, PIECES * WIDE :].reshape(heads, own_heads, WIDE, width)[:, :, :HD]
    d_w = d_w[:, : PIECES * WIDE].reshape(heads, own_heads, 3, WIDE, width)[:, :, :, :HD]
    d_w = d_w.reshape(heads, own_heads, 3 * HD, width)
    d_taps = d_taps.reshape(heads, own_heads, 4, WIDE)[..., :HD]
    d_w, d_proj, d_taps = (
        lax.psum(group_sum(list(grads), heads).astype(BF16), "batch").astype(F32)
        for grads in (d_w, d_proj, d_taps)
    )
    both = ("batch", "head")
    d_first = lax.psum_scatter(d_first, both, scatter_dimension=0, tiled=True).astype(F32)
    d_second = lax.psum_scatter(d_second, both, scatter_dimension=0, tiled=True).astype(F32)
    d_gains = lax.psum_scatter(
        jnp.concatenate([d_gain_one, d_gain_two], axis=0), both, scatter_dimension=1, tiled=True
    )
    return (
        outputs.reshape(inputs.shape),
        d_x.reshape(inputs.shape),
        d_w.transpose(2, 0, 1),
        d_proj,
        d_taps,
        d_gains[0],
        d_gains[1],
        d_first,
        d_second,
    )


def solution(mesh):
    return jax.shard_map(
        functools.partial(local, mesh.shape["head"], mesh.shape["batch"]),
        mesh=mesh,
        in_specs=(
            P(None, ("batch", "head"), None, None),
            P(None, "head", None),
            P("head", None, None),
            P("head", None, None),
            P(),
            P(),
            P(("batch", "head"), None),
            P(("batch", "head"), None),
            P(None, "batch", None, "head", None),
            P(None, "batch"),
            P(None, ("batch", "head"), None, None),
        ),
        out_specs=(
            P(None, ("batch", "head"), None, None),
            P(None, ("batch", "head"), None, None),
            P(None, "head", None),
            P("head", None, None),
            P("head", None, None),
            P(("batch", "head")),
            P(("batch", "head")),
            P(("batch", "head"), None),
            P(("batch", "head"), None),
        ),
        check_vma=False,
    )
```

```python
import functools
import math

import jax
import jax.numpy as jnp
from jax import lax
from jax.experimental import pallas as pl
from jax.experimental.pallas import tpu as pltpu
from jax.sharding import PartitionSpec as P

HD = 96
WIDE = 128
FRAMES = 8
TPC = 392
PTOK = 196
SPOT = TPC // FRAMES
HALF = 200
ROWS = 2 * HALF
MAIN = 384
REST = TPC - MAIN
SIDE = 256
PAIR = 2
PIECES = 3 * PAIR

NORM_EPS = 1e-06
NEG = -1e30
LOG2E = 1.4426950408889634
SCORE = HD ** (-0.5)

F32 = jnp.float32
BF16 = jnp.bfloat16


def dot(a, b):
    return lax.dot_general(a, b, (((1,), (0,)), ((), ())), preferred_element_type=F32)


def dot_nt(a, b):
    return lax.dot_general(a, b, (((1,), (1,)), ((), ())), preferred_element_type=F32)


def dot_tn(a, b):
    return lax.dot_general(a, b, (((0,), (0,)), ((), ())), preferred_element_type=F32)


def reorder(shape, row_dim):
    rows = lax.broadcasted_iota(jnp.int32, shape, row_dim)
    tokens = lax.broadcasted_iota(jnp.int32, shape, 1 - row_dim)
    odd = (rows >= HALF).astype(jnp.int32)
    spot = rows - HALF * odd
    frame = sum((spot >= SPOT * step).astype(jnp.int32) for step in range(1, FRAMES // 2))
    return ((tokens == spot + SPOT * (frame + odd)) & (spot < PTOK)).astype(BF16)


def norm_parts(values):
    average = jnp.mean(values, axis=-1, keepdims=True)
    centered = values - average
    spread = lax.rsqrt(jnp.mean(centered * centered, axis=-1, keepdims=True) + NORM_EPS)
    return centered * spread, spread


def norm_pull(values, gain, grad):
    unit, spread = norm_parts(values)
    scaled = grad * gain
    inner = jnp.mean(scaled * unit, axis=-1, keepdims=True)
    pulled = spread * (scaled - jnp.mean(scaled, axis=-1, keepdims=True) - unit * inner)
    return pulled, jnp.sum(grad * unit, axis=0, keepdims=True)


def value_columns(memory_t):
    return jnp.concatenate([memory_t[HD:], jnp.zeros((WIDE - HD, memory_t.shape[1]), BF16)], axis=0)


def forward_kernel(
    x_ref, w_ref, mem_ref, tail_ref, side_ref, main_ref, taps_ref, gain_one_ref, gain_two_ref,
    packed_ref, keys_ref, att_ref, log_ref, normed_ref, middle_ref, normed_two_ref,
    x_rows, normed_rows, branch,
):
    forward_step(
        pl.program_id(0), pl.program_id(1), pl.num_programs(0),
        w_ref.at[0], mem_ref.at[0], tail_ref.at[0], taps_ref.at[0],
        x_ref, side_ref, main_ref, gain_one_ref, gain_two_ref,
        packed_ref, keys_ref, att_ref, log_ref, normed_ref, middle_ref, normed_two_ref,
        x_rows, normed_rows, branch,
    )


def forward_step(
    pair, clip, pairs,
    w_ref, mem_ref, tail_ref, taps_ref,
    x_ref, side_ref, main_ref, gain_one_ref, gain_two_ref,
    packed_ref, keys_ref, att_ref, log_ref, normed_ref, middle_ref, normed_two_ref,
    x_rows, normed_rows, branch,
):
    here = pl.ds(clip, 1)

    @pl.when(pair == 0)
    def _():
        rows = dot(reorder((ROWS, TPC), 0), x_ref[0])
        x_rows[here] = rows.astype(BF16)[None]
        unit, _ = norm_parts(rows)
        low = (unit * gain_one_ref[...]).astype(BF16)
        normed_rows[here] = low[None]
        normed_ref[0] = low

    normed = normed_rows[here][0]
    packed = dot_nt(normed, w_ref[: PIECES * WIDE])
    packed_ref[0, 0] = packed.astype(BF16)
    logs = []
    outs = []
    for head in range(PAIR):
        base = 3 * WIDE * head
        query = packed[:, base : base + WIDE]
        key = packed[:, base + WIDE : base + 2 * WIDE]
        value = packed[:, base + 2 * WIDE : base + 3 * WIDE]
        query_low = query.astype(BF16)
        taps = taps_ref[head]
        zeros = jnp.zeros((SIDE - HALF - REST, WIDE), F32)
        pooled_key = taps[0:1] * key[:HALF] + taps[1:2] * key[HALF:]
        pooled_value = taps[2:3] * value[:HALF] + taps[3:4] * value[HALF:]
        tail = tail_ref[head].astype(F32)
        side_key = jnp.concatenate([pooled_key, tail[:REST], zeros], axis=0).astype(BF16)
        side_value = jnp.concatenate([pooled_value, tail[REST:], zeros], axis=0).astype(BF16)
        keys_ref[0, 0, head, 0] = side_key
        keys_ref[0, 0, head, 1] = side_value
        memory_t = mem_ref[head]
        score_side = dot_nt(query_low, side_key) * (SCORE * LOG2E) + side_ref[0]
        score_main = dot(query_low, memory_t[:WIDE]) * (SCORE * LOG2E) + main_ref[0]
        top = jnp.maximum(
            jnp.max(score_side, axis=-1, keepdims=True), jnp.max(score_main, axis=-1, keepdims=True)
        )
        weight_side = jnp.exp2(score_side - top)
        weight_main = jnp.exp2(score_main - top)
        total = jnp.sum(weight_side, axis=-1, keepdims=True) + jnp.sum(weight_main, axis=-1, keepdims=True)
        mixed = dot(weight_side.astype(BF16), side_value) + dot_nt(
            weight_main.astype(BF16), value_columns(memory_t)
        )
        outs.append(mixed / total + query)
        logs.append(top + jnp.log2(total))
    attended = jnp.concatenate(outs, axis=1).astype(BF16)
    att_ref[0, 0] = attended
    lane = lax.broadcasted_iota(jnp.int32, (ROWS, WIDE), 1)
    log_ref[0, 0] = jnp.where(lane == 0, logs[0], logs[1])
    part = dot(attended, w_ref[PIECES * WIDE :])[None]

    @pl.when(pair == 0)
    def _():
        branch[here] = part

    @pl.when(pair > 0)
    def _():
        branch[here] += part

    @pl.when(pair == pairs - 1)
    def _():
        middle = x_rows[here][0].astype(F32) + branch[here][0]
        middle_ref[0] = middle
        unit, _ = norm_parts(middle)
        normed_two_ref[0] = (unit * gain_two_ref[...]).astype(BF16)


def mlp_kernel(
    normed_ref, cot_ref, first_ref, second_ref, middle_ref, gain_ref,
    out_ref, grad_ref, grad_low_ref, d_first_ref, d_second_ref, d_gain_ref,
    cot_rows, cot_t, normed_t, total, grad_normed, active, grad_hidden,
):
    tile = pl.program_id(0)
    clips = cot_ref.shape[0]
    wide = normed_ref.shape[1]

    @pl.when(tile == 0)
    def _():
        swap = reorder((ROWS, TPC), 0)

        @pl.loop(0, clips)
        def _(clip):
            here = pl.ds(pl.multiple_of(clip * ROWS, ROWS), ROWS)
            cot_rows[here, :] = dot(swap, cot_ref[clip]).astype(BF16)
            total[here, :] = middle_ref[here, :]
            grad_normed[here, :] = jnp.zeros((ROWS, wide), F32)

        for lanes in range(0, wide, WIDE):
            cot_t[lanes : lanes + WIDE, :] = cot_rows[:, lanes : lanes + WIDE].T
            normed_t[lanes : lanes + WIDE, :] = normed_ref[:, lanes : lanes + WIDE].T

    first = first_ref[...]
    second = second_ref[...]

    @pl.loop(0, clips)
    def _(clip):
        here = pl.ds(pl.multiple_of(clip * ROWS, ROWS), ROWS)
        hidden = dot(normed_ref[here, :], first)
        grad_active = dot_nt(cot_rows[here, :], second)
        bell = jnp.exp2(hidden * hidden * (-0.5 * LOG2E))
        step = 1.0 / (1.0 + (0.3275911 * math.sqrt(0.5)) * jnp.abs(hidden))
        tail = step * (0.5 * 1.061405429) + (0.5 * -1.453152027)
        tail = step * tail + (0.5 * 1.421413741)
        tail = step * tail + (0.5 * -0.284496736)
        tail = step * tail + (0.5 * 0.254829592)
        tail = step * tail * bell
        cumulative = jnp.where(hidden < 0.0, tail, 1.0 - tail)
        slope = cumulative + hidden * bell * 0.3989422804014327
        active_low = (hidden * cumulative).astype(BF16)
        hidden_low = (slope * grad_active).astype(BF16)
        active[here, :] = active_low
        grad_hidden[here, :] = hidden_low
        total[here, :] += dot(active_low, second)
        grad_normed[here, :] += dot_nt(hidden_low, first)

    d_first_ref[...] = dot(normed_t[...], grad_hidden[...]).astype(BF16)
    d_second_ref[...] = dot(cot_t[...], active[...]).astype(BF16).T

    @pl.when(tile == pl.num_programs(0) - 1)
    def _():
        back = reorder((TPC, ROWS), 1)
        d_gain_ref[...] = jnp.zeros_like(d_gain_ref)

        @pl.loop(0, clips)
        def _(clip):
            here = pl.ds(pl.multiple_of(clip * ROWS, ROWS), ROWS)
            out_ref[clip] = dot(back, total[here, :].astype(BF16)).astype(BF16)
            pulled, d_gain = norm_pull(middle_ref[here, :], gain_ref[...], grad_normed[here, :])
            grad = cot_rows[here, :].astype(F32) + pulled
            grad_ref[here, :] = grad
            grad_low_ref[here, :] = grad.astype(BF16)
            d_gain_ref[...] += d_gain


def backward_kernel(
    x_ref, w_ref, mem_ref, side_ref, main_ref, taps_ref, gain_ref,
    packed_ref, keys_ref, att_ref, log_ref, normed_ref, grad_ref, grad_low_ref,
    d_x_ref, d_w_ref, d_taps_ref, d_gain_ref,
    grad_normed,
):
    backward_step(
        pl.program_id(1), pl.program_id(0) == 0, pl.program_id(0) == pl.num_programs(0) - 1,
        w_ref.at[0], d_w_ref.at[0], d_taps_ref.at[0],
        x_ref, mem_ref, side_ref, main_ref, taps_ref, gain_ref,
        packed_ref, keys_ref, att_ref, log_ref, normed_ref, grad_ref, grad_low_ref,
        d_x_ref, d_gain_ref, grad_normed,
    )


def backward_step(
    clip, first_pair, last_pair,
    w_ref, d_w_ref, d_taps_ref,
    x_ref, mem_ref, side_ref, main_ref, taps_ref, gain_ref,
    packed_ref, keys_ref, att_ref, log_ref, normed_ref, grad_ref, grad_low_ref,
    d_x_ref, d_gain_ref, grad_normed,
):
    here = pl.ds(clip, 1)

    @pl.when(clip == 0)
    def _():
        d_w_ref[...] = jnp.zeros_like(d_w_ref)
        d_taps_ref[...] = jnp.zeros_like(d_taps_ref)

    grad_branch = grad_low_ref[...]
    grad_out = dot_nt(grad_branch, w_ref[PIECES * WIDE :])
    d_w_ref[PIECES * WIDE :] += dot_tn(att_ref[0, 0], grad_branch)
    pieces = []
    for head in range(PAIR):
        base = 3 * WIDE * head
        query = packed_ref[0, 0, :, base : base + WIDE]
        key = packed_ref[0, 0, :, base + WIDE : base + 2 * WIDE].astype(F32)
        value = packed_ref[0, 0, :, base + 2 * WIDE : base + 3 * WIDE].astype(F32)
        out_grad = grad_out[:, WIDE * head : WIDE * (head + 1)].astype(BF16)
        taps = taps_ref[0, head]
        side_key = keys_ref[0, 0, head, 0]
        side_value = keys_ref[0, 0, head, 1]
        memory_t = mem_ref[0, head]
        log = log_ref[0, 0, :, head : head + 1]
        score_side = dot_nt(query, side_key) * (SCORE * LOG2E) + side_ref[0]
        score_main = dot(query, memory_t[:WIDE]) * (SCORE * LOG2E) + main_ref[0]
        weight_side = jnp.exp2(score_side - log)
        weight_main = jnp.exp2(score_main - log)
        grad_side = dot_nt(out_grad, side_value)
        grad_main = dot(out_grad, value_columns(memory_t))
        inner = jnp.sum(weight_side * grad_side, axis=-1, keepdims=True) + jnp.sum(
            weight_main * grad_main, axis=-1, keepdims=True
        )
        score_grad_side = (weight_side * (grad_side - inner)).astype(BF16)
        score_grad_main = (weight_main * (grad_main - inner)).astype(BF16)
        grad_query = (
            dot(score_grad_side, side_key) + dot_nt(score_grad_main, memory_t[:WIDE])
        ) * SCORE + out_grad.astype(F32)
        grad_key = dot_tn(score_grad_side, query)[:HALF] * SCORE
        grad_value = dot_tn(weight_side.astype(BF16), out_grad)[:HALF]
        pieces += [
            grad_query,
            jnp.concatenate([taps[0:1] * grad_key, taps[1:2] * grad_key], axis=0),
            jnp.concatenate([taps[2:3] * grad_value, taps[3:4] * grad_value], axis=0),
        ]
        d_taps_ref[head] += jnp.concatenate(
            [
                jnp.sum(part * grad, axis=0, keepdims=True)
                for part, grad in (
                    (key[:HALF], grad_key),
                    (key[HALF:], grad_key),
                    (value[:HALF], grad_value),
                    (value[HALF:], grad_value),
                )
            ],
            axis=0,
        )
    grad_packed = jnp.concatenate(pieces, axis=1).astype(BF16)
    d_w_ref[: PIECES * WIDE] += dot_tn(grad_packed, normed_ref[0])
    part = dot(grad_packed, w_ref[: PIECES * WIDE])[None]

    @pl.when(first_pair)
    def _():
        grad_normed[here] = part

    @pl.when(jnp.logical_not(first_pair))
    def _():
        grad_normed[here] += part

    @pl.when(last_pair)
    def _():
        rows = dot(reorder((ROWS, TPC), 0), x_ref[0])
        pulled, d_gain = norm_pull(rows, gain_ref[...], grad_normed[here][0])
        d_x = (grad_ref[...] + pulled).astype(BF16)
        d_x_ref[0] = dot(reorder((TPC, ROWS), 1), d_x).astype(BF16)

        @pl.when(clip == 0)
        def _():
            d_gain_ref[...] = d_gain

        @pl.when(clip > 0)
        def _():
            d_gain_ref[...] += d_gain


class Scatter:
    def __init__(self, name, order, source, total, from_core, from_one, from_two, from_z, result, out, links, sem, here):
        self.name, self.order, self.links, self.here = name, order, links, here
        self.total, self.from_core, self.from_one, self.from_two, self.from_z = (
            total, from_core, from_one, from_two, from_z
        )
        self.result = result
        z, y, core, x, beside, above, sibling, along = here
        links.add(name + "c", source.at[:, :, 1 - core], from_core, sibling)
        self.own = pltpu.make_async_copy(source.at[:, :, core], total, sem.at[0])
        self.done = pltpu.make_async_copy(result, out, sem.at[1])
        if order == "xyz":
            links.add(name + "x", total.at[:, :, 1 - x], from_one, beside)
            links.add(name + "y", total.at[:, 1 - y, x], from_two, above)
            for shift in (1, 2, 3):
                links.add(f"{name}z{shift}", total.at[turn(z, shift), y, x], from_z.at[shift - 1], along[shift - 1])
        else:
            links.add(name + "y", total.at[:, 1 - y], from_one, above)
            for shift in (1, 2, 3):
                links.add(f"{name}z{shift}", total.at[turn(z, shift), y], from_z.at[shift - 1], along[shift - 1])
            links.add(name + "x", total.at[z, y, 1 - x], from_two, beside)

    def stage(self, axis):
        return [f"{self.name}z{shift}" for shift in (1, 2, 3)] if axis == "z" else [self.name + axis]

    def begin(self):
        self.links.start(self.name + "c")
        self.own.start()

    def step(self, at):
        z, y, core, x = self.here[:4]
        total = self.total
        axis = ("c" + self.order)[at]
        self.links.arrived(*self.stage(axis))
        if axis == "c":
            self.own.wait()

            @pl.loop(0, 4)
            def _(row):
                for column in (0, 1):
                    for head in (0, 1):
                        total[row, column, head] = add_low(total[row, column, head], self.from_core[row, column, head])

        elif at == 1:

            @pl.loop(0, 4)
            def _(row):
                for other in (0, 1):
                    spot = (row, other, x) if self.order == "xyz" else (row, y, other)
                    total[spot] = add_low(total[spot], self.from_one[row, other])

        elif axis == "y":

            @pl.loop(0, 4)
            def _(row):
                total[row, y, x] = add_low(total[row, y, x], self.from_two[row])

        elif axis == "z" and at == 2:
            for head in (0, 1):
                part = total[z, y, head].astype(F32)
                for shift in range(3):
                    part = part + self.from_z[shift, head].astype(F32)
                total[z, y, head] = part.astype(BF16)
        else:
            part = total[z, y, x].astype(F32)
            if axis == "z":
                for shift in range(3):
                    part = part + self.from_z[shift].astype(F32)
            else:
                part = part + self.from_two[...].astype(F32)
            self.result[...] = part
            self.done.start()
        if at < 3:
            self.links.start(*self.stage(self.order[at]))


def add_low(one, other):
    return (one.astype(F32) + other.astype(F32)).astype(BF16)


def unpad(ref, into, more=None):
    for piece in range(ref.shape[0] // WIDE):
        rows = ref[WIDE * piece : WIDE * piece + HD]
        narrow = slice(HD * piece, HD * (piece + 1))
        if more is not None:
            rows = rows + more[narrow].astype(F32)
        into[narrow] = rows.astype(BF16)


BACKWARD_COPIES = 48
THIRD = 384
PART = 96


def backward_links_kernel(
    x_ref, w_ref, mem_ref, side_ref, main_ref, taps_ref, gain_ref,
    packed_ref, keys_ref, att_ref, log_ref, normed_ref, grad_ref, grad_low_ref, gain_two_ref,
    d_first, d_second,
    d_x_ref, small_out, first_out, second_out, w_out,
    grad_normed, d_gain, d_w, d_taps,
    far_sent, far_got, own, own_core, own_y, own_z, whole,
    small_mine, small_far, small_x, small_core, small_y, small_z,
    first_total, first_core, first_one, first_two, first_z, first_result,
    second_total, second_core, second_one, second_two, second_z, second_result,
    send, recv, near,
):
    step = pl.program_id(0)
    last = pl.num_programs(0) - 1
    z, y, core, x, at = place()
    links = Links(send, recv)
    beside, above, sibling = at(z, y, core, 1 - x), at(z, 1 - y, core, x), at(z, y, 1 - core, x)
    along = [at(turn(z, shift), y, core, x) for shift in (1, 2, 3)]
    here = (z, y, core, x, beside, above, sibling, along)
    first = Scatter(
        "f", "xyz", d_first, first_total, first_core, first_one, first_two, first_z, first_result, first_out,
        links, near.at[pl.ds(0, 2)], here,
    )
    second = Scatter(
        "s", "yzx", d_second, second_total, second_core, second_one, second_two, second_z, second_result, second_out,
        links, near.at[pl.ds(2, 2)], here,
    )

    def lanes(core):
        return pl.ds(pl.multiple_of(core * THIRD, THIRD), THIRD)

    def rows(y, z):
        return pl.ds(pl.multiple_of(y * THIRD + z * PART, PART), PART)

    def half(y):
        return pl.ds(pl.multiple_of(y * THIRD, THIRD), THIRD)

    for i in (0, 1):
        links.add(f"far{i}", far_sent.at[i], far_got.at[i], beside)
        links.add(f"rc{i}", own.at[i, :, lanes(1 - core)], own_core.at[i], sibling)
        links.add(f"ry{i}", own.at[i, half(1 - y), lanes(core)], own_y.at[i], above)
        for shift in (1, 2, 3):
            links.add(
                f"rz{i}{shift}", own.at[i, rows(y, turn(z, shift)), lanes(core)], own_z.at[i, shift - 1], along[shift - 1]
            )
        piece = whole.at[i, rows(y, z), lanes(core)]
        for shift in (1, 2, 3):
            links.add(f"gz{i}{shift}", piece, piece, along[shift - 1])
        piece = whole.at[i, half(y), lanes(core)]
        links.add(f"gy{i}", piece, piece, above)
        piece = whole.at[i, :, lanes(core)]
        links.add(f"gc{i}", piece, piece, sibling)
    links.add("mx", small_far, small_x, beside)
    links.add("mc", small_mine, small_core, sibling)
    links.add("my", small_core, small_y, above)
    for shift in (1, 2, 3):
        links.add(f"mz{shift}", small_z.at[z], small_z.at[z], along[shift - 1])

    @pl.when(step == 0)
    def _():
        greet([beside, above, sibling] + along)
        first.begin()
        second.begin()

    backward_step(
        lax.rem(step, 4), step < 4, step >= 12,
        w_ref.at[0], d_w, d_taps.at[lax.div(step, 4)],
        x_ref, mem_ref, side_ref, main_ref, taps_ref, gain_ref,
        packed_ref, keys_ref, att_ref, log_ref, normed_ref, grad_ref, grad_low_ref,
        d_x_ref, d_gain, grad_normed,
    )

    def sum_core(i):
        links.arrived(f"rc{i}")
        own[i, :, lanes(core)] = add_low(own[i, :, lanes(core)], own_core[i])
        links.start(f"ry{i}")

    def sum_y(i):
        links.arrived(f"ry{i}")
        own[i, half(y), lanes(core)] = add_low(own[i, half(y), lanes(core)], own_y[i])
        links.start(*[f"rz{i}{shift}" for shift in (1, 2, 3)])

    def sum_z(i):
        links.arrived(*[f"rz{i}{shift}" for shift in (1, 2, 3)])
        part = own[i, rows(y, z), lanes(core)].astype(F32)
        for shift in range(3):
            part = part + own_z[i, shift].astype(F32)
        whole[i, rows(y, z), lanes(core)] = part.astype(BF16)
        links.start(*[f"gz{i}{shift}" for shift in (1, 2, 3)])

    def spread_y(i):
        links.arrived(*[f"gz{i}{shift}" for shift in (1, 2, 3)])
        links.start(f"gy{i}")

    def spread_core(i):
        links.arrived(f"gy{i}")
        links.start(f"gc{i}")

    def far(i):
        unpad(d_w, far_sent.at[i])
        links.start(f"far{i}")

    def mine(i):
        links.arrived(f"far{i}")
        unpad(d_w, own.at[i], far_got.at[i])
        links.start(f"rc{i}")

    plan = {
        1: [lambda: first.step(0)],
        2: [lambda: second.step(0)],
        3: [lambda: far(0)],
        7: [lambda: far(1), lambda: first.step(1)],
        8: [lambda: second.step(1)],
        10: [lambda: first.step(2)],
        11: [lambda: mine(0)],
        12: [lambda: sum_core(0)],
        13: [lambda: sum_y(0), lambda: first.step(3)],
        14: [lambda: sum_z(0), lambda: second.step(2)],
    }
    for when, acts in plan.items():

        @pl.when(step == when)
        def _(acts=acts):
            for act in acts:
                act()

    @pl.when(step == last)
    def _():
        mine(1)
        for i, target in ((2, small_mine), (0, small_far)):
            target[...] = jnp.zeros_like(target)
            target[0:1] = d_gain[...]
            target[1:2] = gain_two_ref[...]
            for j in (0, 1):
                target[8:16, WIDE * j : WIDE * (j + 1)] = d_taps[i + j].reshape(8, WIDE)
        links.start("mx")
        spread_y(0)
        sum_core(1)
        links.arrived("mx")
        small_mine[...] += small_x[...]
        links.start("mc")
        spread_core(0)
        sum_y(1)
        links.arrived("mc")
        small_core[...] += small_mine[...]
        links.start("my")
        second.step(3)
        sum_z(1)
        links.arrived("my")
        small_z[pl.ds(z, 1)] = (small_y[...] + small_core[...])[None]
        links.start("mz1", "mz2", "mz3")
        spread_y(1)
        spread_core(1)
        links.arrived("mz1", "mz2", "mz3")
        small_out[...] = (small_z[0] + small_z[1]) + (small_z[2] + small_z[3])
        links.arrived("gc0", "gc1")
        save = pltpu.make_async_copy(whole, w_out, near.at[4])
        save.start()
        save.wait()
        first.done.wait()
        second.done.wait()
        links.sent()


VMEM_LIMIT = 60 << 20


def compiler_params(dims):
    return pltpu.CompilerParams(
        dimension_semantics=("arbitrary",) * dims, vmem_limit_bytes=VMEM_LIMIT
    )


def shaped(shape, dtype):
    return jax.ShapeDtypeStruct(shape, dtype)


class Links:
    def __init__(self, send, recv):
        self.send, self.recv, self.made = send, recv, {}

    def add(self, name, src, dst, device):
        at = len(self.made)
        self.made[name] = (src, dst, device, at)

    def get(self, name):
        src, dst, device, at = self.made[name]
        return pltpu.make_async_remote_copy(
            src_ref=src,
            dst_ref=dst,
            send_sem=self.send.at[at],
            recv_sem=self.recv.at[at],
            device_id=device,
            device_id_type=pl.DeviceIdType.MESH,
        )

    def start(self, *names):
        for name in names:
            self.get(name).start()

    def arrived(self, *names):
        for name in names:
            self.get(name).wait_recv()

    def sent(self):
        for name in self.made:
            self.get(name).wait_send()


def place():
    batch, head = lax.axis_index("batch"), lax.axis_index("head")
    z, y, core = batch // 4, lax.rem(batch // 2, 2), lax.rem(batch, 2)

    def at(z, y, core, x):
        return {"batch": (z * 2 + y) * 2 + core, "head": x}

    return z, y, core, head, at


def greet(devices):
    barrier = pltpu.get_barrier_semaphore()
    for device in devices:
        pl.semaphore_signal(barrier, inc=1, device_id=device, device_id_type=pl.DeviceIdType.MESH)
    pl.semaphore_wait(barrier, len(devices))


def turn(z, shift):
    return lax.rem(z + shift + 4, 4)


FORWARD_COPIES = 48


def forward_links_kernel(
    x_ref, side_ref, main_ref, gain_one_ref, gain_two_ref,
    w_own, mem_own, tail_own, taps_own, hidden_own, output_own,
    packed_ref, keys_ref, att_ref, log_ref, normed_ref, middle_ref, normed_two_ref,
    first_all, second_all, w_out, mem_out, taps_out,
    x_rows, normed_rows, branch, w_all, mem_all, tail_all, taps_all,
    send, recv, near, save,
):
    step = pl.program_id(0)
    z, y, core, x, at = place()
    links = Links(send, recv)
    beside, above, sibling = at(z, y, core, 1 - x), at(z, 1 - y, core, x), at(z, y, 1 - core, x)
    along = [at(turn(z, shift), y, core, x) for shift in (1, 2, 3)]
    column = pl.ds(pl.multiple_of(core * MAIN, MAIN), MAIN)

    def slab(z, y):
        return (lax.div(2 * z + y, 4), pl.ds(pl.multiple_of(lax.rem(2 * z + y, 4) * 256, 256), 256), column)

    def w_far(z, y):
        pair, rows, lanes = slab(z, y)
        return w_all.at[2 + pair, rows, lanes]

    links.add("xw", w_own.at[slab(z, y)], w_far(z, y), beside)
    for shift in (1, 2, 3):
        links.add(f"zw{shift}", w_far(z, y), w_far(z, y), along[shift - 1])
    for shift in range(4):
        links.add(f"yw{shift}", w_far(turn(z, -shift), y), w_far(turn(z, -shift), y), above)
    far = w_all.at[pl.ds(2, 2), :, column]
    links.add("cw", far, far, sibling)
    me = ((z * 2 + y) * 2 + core) * 2 + x
    links.add("x0", hidden_own, first_all.at[me], beside)
    links.add("x1", output_own, second_all.at[me], beside)

    def group(which, z, y):
        return (first_all, second_all)[which].at[pl.ds(((z * 2 + y) * 2 + core) * 2, 2)]

    for which in (0, 1):
        for shift in (1, 2, 3):
            links.add(f"z{shift}{which}", group(which, z, y), group(which, z, y), along[shift - 1])
        for shift in range(4):
            from_z = turn(z, -shift)
            links.add(f"y{shift}{which}", group(which, from_z, y), group(which, from_z, y), above)
            links.add(f"c{shift}{which}", group(which, from_z, y), group(which, from_z, y), sibling)
            links.add(f"d{shift}{which}", group(which, from_z, 1 - y), group(which, from_z, 1 - y), sibling)
    clips = mem_own.shape[0]
    for clip in range(clips):
        links.add(f"m{clip}", mem_own.at[clip, 1 - x, :, :, pl.ds(0, MAIN)], mem_all.at[1, clip], beside)
    links.add("tail", tail_own.at[:, 1 - x], tail_all.at[1], beside)
    links.add("taps", taps_own, taps_all.at[pl.ds(2, 2)], beside)

    local = [
        (w_own, w_all.at[pl.ds(0, 2)]),
        (tail_own.at[:, x], tail_all.at[0]),
        (taps_own, taps_all.at[pl.ds(0, 2)]),
        (hidden_own, first_all.at[me]),
        (output_own, second_all.at[me]),
    ] + [(mem_own.at[clip, x, :, :, pl.ds(0, MAIN)], mem_all.at[0, clip]) for clip in range(clips)]
    local = [pltpu.make_async_copy(src, dst, near.at[i]) for i, (src, dst) in enumerate(local)]
    saved = [
        (w_all, w_out),
        (taps_all, taps_out),
        (mem_all.at[0], mem_out.at[0]),
        (mem_all.at[1], mem_out.at[1]),
    ]
    saved = [pltpu.make_async_copy(src, dst, save.at[i]) for i, (src, dst) in enumerate(saved)]

    @pl.when(step == 0)
    def _():
        greet([beside, above, sibling] + along)
        links.start("xw", "taps", "tail", "x0", "x1")
        for copy in local:
            copy.start()
        for copy in local:
            copy.wait()

    def both(*names):
        return [name + str(which) for name in names for which in (0, 1)]

    plan = {
        2: (["xw"], ["zw1", "zw2", "zw3", "yw0"]),
        3: (["x0", "x1"], both("z1", "z2", "z3", "y0", "c0") + ["m0", "m1"]),
        5: (["zw1", "zw2", "zw3"], ["yw1", "yw2", "yw3"]),
        6: ([], ["m2", "m3"]),
        7: (["yw0", "yw1", "yw2", "yw3"], ["cw"]),
        8: (["cw", "tail", "taps", "m0"], []),
        9: (both("z1"), both("y1", "c1")),
        10: (["m1"] + both("z2"), both("y2", "c2")),
        12: (["m2"], []),
        13: (both("y0", "y1"), both("d0", "d1")),
        14: (["m3"] + both("z3"), both("y3", "c3")),
    }
    for when, (awaited, started) in plan.items():

        @pl.when(step == when)
        def _(awaited=awaited, started=started):
            links.arrived(*awaited)
            links.start(*started)

    @pl.when(step == 14)
    def _():
        for copy in saved:
            copy.start()

    pair, clip = pair_of(step), clip_of(step)
    side = lax.div(pair, 2)
    heads = pl.ds(lax.rem(pair, 2) * PAIR, PAIR)
    forward_step(
        pair, clip, 4,
        w_all.at[pair], mem_all.at[side, clip, heads], tail_all.at[side, clip, heads], taps_all.at[pair],
        x_ref, side_ref, main_ref, gain_one_ref, gain_two_ref,
        packed_ref, keys_ref, att_ref, log_ref, normed_ref, middle_ref, normed_two_ref,
        x_rows, normed_rows, branch,
    )

    @pl.when(step == pl.num_programs(0) - 1)
    def _():
        links.arrived(*both("y2", "y3"))
        links.start(*both("d2", "d3"))
        for copy in saved:
            copy.wait()
        links.arrived(*both("c0", "c1", "c2", "c3", "d0", "d1", "d2", "d3"))
        links.sent()


def pair_of(step):
    return jnp.where(step < 8, lax.div(step, 4), 2 + lax.rem(step, 2))


def clip_of(step):
    return jnp.where(step < 8, lax.rem(step, 4), lax.div(step, 2) - 4)


def attention_forward_links(x, w, mem, tail, side, main, taps, gain_one, gain_two, hidden_weight, output_weight):
    clips, width = x.shape[0], x.shape[2]
    packed_width = PIECES * WIDE
    devices = 32
    early = lambda s: jnp.where(s < 4, s, clips - 1)
    late = lambda s: jnp.where(s < 8, 0, clip_of(s))
    anywhere = pl.BlockSpec(memory_space=pl.ANY)
    return pl.pallas_call(
        forward_links_kernel,
        grid=(4 * clips,),
        in_specs=[
            pl.BlockSpec((1, TPC, width), lambda s: (early(s), 0, 0)),
            pl.BlockSpec((1, 1, SIDE), lambda s: (clip_of(s), 0, 0)),
            pl.BlockSpec((1, 1, MAIN), lambda s: (clip_of(s), 0, 0)),
            pl.BlockSpec((1, width), lambda s: (0, 0)),
            pl.BlockSpec((1, width), lambda s: (0, 0)),
        ] + [anywhere] * 6,
        out_specs=[
            pl.BlockSpec((1, 1, ROWS, packed_width), lambda s: (pair_of(s), clip_of(s), 0, 0)),
            pl.BlockSpec((1, 1, PAIR, 2, SIDE, WIDE), lambda s: (pair_of(s), clip_of(s), 0, 0, 0, 0)),
            pl.BlockSpec((1, 1, ROWS, PAIR * WIDE), lambda s: (pair_of(s), clip_of(s), 0, 0)),
            pl.BlockSpec((1, 1, ROWS, WIDE), lambda s: (pair_of(s), clip_of(s), 0, 0)),
            pl.BlockSpec((1, ROWS, width), lambda s: (early(s), 0, 0)),
            pl.BlockSpec((1, ROWS, width), lambda s: (late(s), 0, 0)),
            pl.BlockSpec((1, ROWS, width), lambda s: (late(s), 0, 0)),
        ] + [anywhere] * 5,
        out_shape=[
            shaped((4, clips, ROWS, packed_width), BF16),
            shaped((4, clips, PAIR, 2, SIDE, WIDE), BF16),
            shaped((4, clips, ROWS, PAIR * WIDE), BF16),
            shaped((4, clips, ROWS, WIDE), F32),
            shaped((clips, ROWS, width), BF16),
            shaped((clips, ROWS, width), F32),
            shaped((clips, ROWS, width), BF16),
            shaped((devices,) + hidden_weight.shape, BF16),
            shaped((devices,) + output_weight.shape, BF16),
            shaped((4,) + w.shape[1:], BF16),
            shaped((2, clips, 4, 2 * HD, MAIN), BF16),
            shaped((4,) + taps.shape[1:], F32),
        ],
        scratch_shapes=[
            pltpu.VMEM((clips, ROWS, width), BF16),
            pltpu.VMEM((clips, ROWS, width), BF16),
            pltpu.VMEM((clips, ROWS, width), F32),
            pltpu.VMEM((4,) + w.shape[1:], BF16),
            pltpu.VMEM((2, clips, 4, 2 * HD, MAIN), BF16),
            pltpu.VMEM((2, clips, 4, 2 * REST, WIDE), BF16),
            pltpu.VMEM((4,) + taps.shape[1:], F32),
            pltpu.SemaphoreType.DMA((FORWARD_COPIES,)),
            pltpu.SemaphoreType.DMA((FORWARD_COPIES,)),
            pltpu.SemaphoreType.DMA((5 + clips,)),
            pltpu.SemaphoreType.DMA((4,)),
        ],
        compiler_params=pltpu.CompilerParams(
            dimension_semantics=("arbitrary",),
            vmem_limit_bytes=VMEM_LIMIT,
            collective_id=0,
            has_side_effects=True,
        ),
        name="attention_forward_links",
    )(x, side, main, gain_one, gain_two, w, mem, tail, taps, hidden_weight, output_weight)


def attention_forward(x, w, mem, tail, side, main, taps, gain_one, gain_two):
    clips, pairs = x.shape[0], w.shape[0]
    width = x.shape[2]
    packed_width = PIECES * WIDE
    weight_rows = w.shape[1]
    late = lambda p, c: jnp.where(p == pairs - 1, c, 0)
    early = lambda p, c: jnp.where(p == 0, c, clips - 1)
    per_step = lambda p, c: (p, c)
    return pl.pallas_call(
        forward_kernel,
        grid=(pairs, clips),
        in_specs=[
            pl.BlockSpec((1, TPC, width), lambda p, c: (early(p, c), 0, 0)),
            pl.BlockSpec((1, weight_rows, width), lambda p, c: (p, 0, 0)),
            pl.BlockSpec((1, PAIR, 2 * HD, MAIN), lambda p, c: (c, p, 0, 0)),
            pl.BlockSpec((1, PAIR, 2 * REST, WIDE), lambda p, c: (c, p, 0, 0)),
            pl.BlockSpec((1, 1, SIDE), lambda p, c: (c, 0, 0)),
            pl.BlockSpec((1, 1, MAIN), lambda p, c: (c, 0, 0)),
            pl.BlockSpec((1, PAIR, 4, WIDE), lambda p, c: (p, 0, 0, 0)),
            pl.BlockSpec((1, width), lambda p, c: (0, 0)),
            pl.BlockSpec((1, width), lambda p, c: (0, 0)),
        ],
        out_specs=[
            pl.BlockSpec((1, 1, ROWS, packed_width), lambda p, c: (p, c, 0, 0)),
            pl.BlockSpec((1, 1, PAIR, 2, SIDE, WIDE), lambda p, c: (p, c, 0, 0, 0, 0)),
            pl.BlockSpec((1, 1, ROWS, PAIR * WIDE), lambda p, c: (p, c, 0, 0)),
            pl.BlockSpec((1, 1, ROWS, WIDE), lambda p, c: (p, c, 0, 0)),
            pl.BlockSpec((1, ROWS, width), lambda p, c: (early(p, c), 0, 0)),
            pl.BlockSpec((1, ROWS, width), lambda p, c: (late(p, c), 0, 0)),
            pl.BlockSpec((1, ROWS, width), lambda p, c: (late(p, c), 0, 0)),
        ],
        out_shape=[
            shaped((pairs, clips, ROWS, packed_width), BF16),
            shaped((pairs, clips, PAIR, 2, SIDE, WIDE), BF16),
            shaped((pairs, clips, ROWS, PAIR * WIDE), BF16),
            shaped((pairs, clips, ROWS, WIDE), F32),
            shaped((clips, ROWS, width), BF16),
            shaped((clips, ROWS, width), F32),
            shaped((clips, ROWS, width), BF16),
        ],
        scratch_shapes=[
            pltpu.VMEM((clips, ROWS, width), BF16),
            pltpu.VMEM((clips, ROWS, width), BF16),
            pltpu.VMEM((clips, ROWS, width), F32),
        ],
        compiler_params=compiler_params(2),
        name="attention_forward",
    )(x, w, mem, tail, side, main, taps, gain_one, gain_two)


def once(shape):
    return pl.BlockSpec(shape, lambda t: (0,) * len(shape), pipeline_mode=pl.Buffered(1))


def mlp(normed, cot, first, second, middle, gain):
    rows, width = normed.shape
    hidden = first.shape[1]
    clips = cot.shape[0]
    tile = 512
    return pl.pallas_call(
        mlp_kernel,
        grid=(hidden // tile,),
        in_specs=[
            once((rows, width)),
            once((clips, TPC, width)),
            pl.BlockSpec((width, tile), lambda t: (0, t)),
            pl.BlockSpec((tile, width), lambda t: (t, 0)),
            once((rows, width)),
            once((1, width)),
        ],
        out_specs=[
            once((clips, TPC, width)),
            once((rows, width)),
            once((rows, width)),
            pl.BlockSpec((width, tile), lambda t: (0, t)),
            pl.BlockSpec((tile, width), lambda t: (t, 0)),
            once((1, width)),
        ],
        out_shape=[
            shaped((clips, TPC, width), BF16),
            shaped((rows, width), F32),
            shaped((rows, width), BF16),
            shaped((width, hidden), BF16),
            shaped((hidden, width), BF16),
            shaped((1, width), F32),
        ],
        scratch_shapes=[
            pltpu.VMEM((rows, width), BF16),
            pltpu.VMEM((width, rows), BF16),
            pltpu.VMEM((width, rows), BF16),
            pltpu.VMEM((rows, width), F32),
            pltpu.VMEM((rows, width), F32),
            pltpu.VMEM((rows, tile), BF16),
            pltpu.VMEM((rows, tile), BF16),
        ],
        compiler_params=compiler_params(1),
        name="mlp",
    )(normed, cot, first, second, middle, gain)


def attention_backward(x, w, mem, side, main, taps, gain, packed, keys, att, log, normed, grad, grad_low):
    clips, pairs = x.shape[0], w.shape[0]
    width = x.shape[2]
    packed_width = PIECES * WIDE
    weight_rows = w.shape[1]
    late = lambda p, c: jnp.where(p == pairs - 1, c, 0)
    return pl.pallas_call(
        backward_kernel,
        grid=(pairs, clips),
        in_specs=[
            pl.BlockSpec((1, TPC, width), lambda p, c: (late(p, c), 0, 0)),
            pl.BlockSpec((1, weight_rows, width), lambda p, c: (p, 0, 0)),
            pl.BlockSpec((1, PAIR, 2 * HD, MAIN), lambda p, c: (c, p, 0, 0))
            if mem.ndim == 4
            else pl.BlockSpec(
                (None, 1, PAIR, 2 * HD, MAIN), lambda p, c: (lax.div(p, 2), c, lax.rem(p, 2), 0, 0)
            ),
            pl.BlockSpec((1, 1, SIDE), lambda p, c: (c, 0, 0)),
            pl.BlockSpec((1, 1, MAIN), lambda p, c: (c, 0, 0)),
            pl.BlockSpec((1, PAIR, 4, WIDE), lambda p, c: (p, 0, 0, 0)),
            pl.BlockSpec((1, width), lambda p, c: (0, 0)),
            pl.BlockSpec((1, 1, ROWS, packed_width), lambda p, c: (p, c, 0, 0)),
            pl.BlockSpec((1, 1, PAIR, 2, SIDE, WIDE), lambda p, c: (p, c, 0, 0, 0, 0)),
            pl.BlockSpec((1, 1, ROWS, PAIR * WIDE), lambda p, c: (p, c, 0, 0)),
            pl.BlockSpec((1, 1, ROWS, WIDE), lambda p, c: (p, c, 0, 0)),
            pl.BlockSpec((1, ROWS, width), lambda p, c: (c, 0, 0)),
            pl.BlockSpec((ROWS, width), lambda p, c: (late(p, c), 0)),
            pl.BlockSpec((ROWS, width), lambda p, c: (c, 0)),
        ],
        out_specs=[
            pl.BlockSpec((1, TPC, width), lambda p, c: (late(p, c), 0, 0)),
            pl.BlockSpec((1, weight_rows, width), lambda p, c: (p, 0, 0)),
            pl.BlockSpec((1, PAIR, 4, WIDE), lambda p, c: (p, 0, 0, 0)),
            pl.BlockSpec((1, width), lambda p, c: (0, 0)),
        ],
        out_shape=[
            shaped((clips, TPC, width), BF16),
            shaped((pairs, weight_rows, width), F32),
            shaped((pairs, PAIR, 4, WIDE), F32),
            shaped((1, width), F32),
        ],
        scratch_shapes=[pltpu.VMEM((clips, ROWS, width), F32)],
        compiler_params=compiler_params(2),
        name="attention_backward",
    )(x, w, mem, side, main, taps, gain, packed, keys, att, log, normed, grad, grad_low)


def attention_backward_links(
    x, w, mem, side, main, taps, gain, packed, keys, att, log, normed, grad, grad_low, gain_two, d_first, d_second
):
    clips, width = x.shape[0], x.shape[2]
    packed_width = PIECES * WIDE
    weight_rows = w.shape[1]
    low_rows = weight_rows // WIDE * HD
    pair_at = lambda s: lax.rem(lax.div(s, 4) + 2, 4)
    clip_at = lambda s: lax.rem(s, 4)
    late = lambda s: jnp.where(s < 12, 0, s - 12)
    anywhere = pl.BlockSpec(memory_space=pl.ANY)
    per_step = lambda s: (pair_at(s), clip_at(s), 0, 0)
    small = (16, width)

    def scatter_scratch(shape, order):
        one, two, last = ((4, 2), (4,), (3,)) if order == "xyz" else ((4, 2), (), (3, 2))
        return [
            pltpu.VMEM(lead + shape, BF16) for lead in ((4, 2, 2), (4, 2, 2), one, two, last)
        ] + [pltpu.VMEM(shape, F32)]

    first_shape, second_shape = d_first.shape[4:], d_second.shape[4:]
    return pl.pallas_call(
        backward_links_kernel,
        grid=(4 * clips,),
        in_specs=[
            pl.BlockSpec((1, TPC, width), lambda s: (late(s), 0, 0)),
            pl.BlockSpec((1, weight_rows, width), lambda s: (pair_at(s), 0, 0)),
            pl.BlockSpec(
                (None, 1, PAIR, 2 * HD, MAIN),
                lambda s: (lax.div(pair_at(s), 2), clip_at(s), lax.rem(pair_at(s), 2), 0, 0),
            ),
            pl.BlockSpec((1, 1, SIDE), lambda s: (clip_at(s), 0, 0)),
            pl.BlockSpec((1, 1, MAIN), lambda s: (clip_at(s), 0, 0)),
            pl.BlockSpec((1, PAIR, 4, WIDE), lambda s: (pair_at(s), 0, 0, 0)),
            pl.BlockSpec((1, width), lambda s: (0, 0)),
            pl.BlockSpec((1, 1, ROWS, packed_width), per_step),
            pl.BlockSpec((1, 1, PAIR, 2, SIDE, WIDE), lambda s: per_step(s) + (0, 0)),
            pl.BlockSpec((1, 1, ROWS, PAIR * WIDE), per_step),
            pl.BlockSpec((1, 1, ROWS, WIDE), per_step),
            pl.BlockSpec((1, ROWS, width), lambda s: (clip_at(s), 0, 0)),
            pl.BlockSpec((ROWS, width), lambda s: (late(s), 0)),
            pl.BlockSpec((ROWS, width), lambda s: (clip_at(s), 0)),
            pl.BlockSpec((1, width), lambda s: (0, 0)),
            anywhere,
            anywhere,
        ],
        out_specs=[
            pl.BlockSpec((1, TPC, width), lambda s: (late(s), 0, 0)),
            pl.BlockSpec(small, lambda s: (0, 0)),
            anywhere,
            anywhere,
            anywhere,
        ],
        out_shape=[
            shaped((clips, TPC, width), BF16),
            shaped(small, F32),
            shaped(first_shape, F32),
            shaped(second_shape, F32),
            shaped((2, low_rows, width), BF16),
        ],
        scratch_shapes=[
            pltpu.VMEM((clips, ROWS, width), F32),
            pltpu.VMEM((1, width), F32),
            pltpu.VMEM((weight_rows, width), F32),
            pltpu.VMEM((4, PAIR, 4, WIDE), F32),
            pltpu.VMEM((2, low_rows, width), BF16),
            pltpu.VMEM((2, low_rows, width), BF16),
            pltpu.VMEM((2, low_rows, width), BF16),
            pltpu.VMEM((2, low_rows, THIRD), BF16),
            pltpu.VMEM((2, THIRD, THIRD), BF16),
            pltpu.VMEM((2, 3, PART, THIRD), BF16),
            pltpu.VMEM((2, low_rows, width), BF16),
        ]
        + [pltpu.VMEM(small, F32)] * 5
        + [pltpu.VMEM((4,) + small, F32)]
        + scatter_scratch(first_shape, "xyz")
        + scatter_scratch(second_shape, "yzx")
        + [
            pltpu.SemaphoreType.DMA((BACKWARD_COPIES,)),
            pltpu.SemaphoreType.DMA((BACKWARD_COPIES,)),
            pltpu.SemaphoreType.DMA((5,)),
        ],
        compiler_params=pltpu.CompilerParams(
            dimension_semantics=("arbitrary",),
            vmem_limit_bytes=VMEM_LIMIT,
            collective_id=1,
            has_side_effects=True,
        ),
        name="attention_backward_links",
    )(x, w, mem, side, main, taps, gain, packed, keys, att, log, normed, grad, grad_low, gain_two, d_first, d_second)


def group_gather(own, heads, fetch=None):
    blocks = [fetch(own, 0) if fetch else own]
    for shift in range(1, heads):
        sent = fetch(own, -shift) if fetch else own
        blocks.append(lax.ppermute(sent, "head", [(src, (src - shift) % heads) for src in range(heads)]))
    return blocks


def group_sum(blocks, heads):
    total = blocks[0]
    for shift in range(1, heads):
        total = total + lax.ppermute(
            blocks[shift].astype(BF16), "head", [(src, (src + shift) % heads) for src in range(heads)]
        ).astype(F32)
    return total


def local(
    heads,
    batches,
    inputs,
    qkv_weight,
    proj_weight,
    pool_weight,
    gain_one,
    gain_two,
    hidden_weight,
    output_weight,
    memory,
    clip_index,
    cotangent,
):
    width = inputs.shape[3]
    micro, own_clips = inputs.shape[:2]
    clips = micro * own_clips
    own_heads = qkv_weight.shape[1]
    all_heads = own_heads * heads
    pairs = all_heads // PAIR
    me = lax.axis_index("head")
    linked = (heads, batches, micro, own_clips) == (2, 16, 4, 1)

    def mine(array, shift):
        start = lax.rem(me + shift + heads, heads) * own_clips
        return lax.dynamic_slice_in_dim(array, start, own_clips, axis=1)

    pad = WIDE - HD
    qkv_rows = jnp.pad(
        qkv_weight.transpose(1, 2, 0).reshape(own_heads, 3, HD, width), ((0, 0), (0, 0), (0, pad), (0, 0))
    )
    proj_rows = jnp.pad(proj_weight, ((0, 0), (0, pad), (0, 0)))
    taps_own = jnp.pad(pool_weight.astype(F32), ((0, 0), (0, 0), (0, pad)))
    memory_t = memory.transpose(0, 1, 3, 4, 2)
    tail_own = memory_t[..., MAIN:].reshape(memory_t.shape[:3] + (2, HD, REST)).swapaxes(4, 5)
    tail_own = jnp.pad(tail_own, ((0, 0),) * 5 + ((0, pad),)).reshape(memory_t.shape[:3] + (2 * REST, WIDE))

    index = mine(clip_index, 0).reshape(clips, 1, 1)
    main_slot = lax.broadcasted_iota(jnp.int32, (1, 1, MAIN), 2) // PTOK
    main_mask = jnp.where(index > main_slot, 0.0, NEG).astype(F32)
    spot = lax.broadcasted_iota(jnp.int32, (1, 1, SIDE), 2)
    tail_open = (spot >= HALF) & (spot < HALF + REST) & (index > (TPC - 1) // PTOK)
    side_mask = jnp.where((spot < PTOK) | tail_open, 0.0, NEG).astype(F32)

    x = inputs.reshape(clips, TPC, width)
    gain_one = gain_one.reshape(1, width)
    gain_two = gain_two.reshape(1, width)
    w_own = jnp.concatenate(
        [
            qkv_rows.reshape(-1, PIECES * WIDE, width),
            proj_rows.reshape(-1, PAIR * WIDE, width),
        ],
        axis=1,
    ) if own_heads % PAIR == 0 else None
    if linked:
        (packed, keys, att, log, normed, middle, normed_two, first, second, w_all, mem_all, taps_all) = (
            attention_forward_links(
                x, w_own, memory_t, tail_own, side_mask, main_mask,
                taps_own.reshape(-1, PAIR, 4, WIDE), gain_one, gain_two, hidden_weight, output_weight,
            )
        )
        first = first.reshape(width, -1)
        second = second.reshape(-1, width)
    else:
        qkv_all = jnp.concatenate(group_gather(qkv_rows, heads), axis=0)
        proj_all = jnp.concatenate(group_gather(proj_rows, heads), axis=0)
        w_all = jnp.concatenate(
            [
                qkv_all.reshape(pairs, PIECES * WIDE, width),
                proj_all.reshape(pairs, PAIR * WIDE, width),
            ],
            axis=1,
        )
        taps_all = jnp.concatenate(group_gather(taps_own, heads), axis=0).reshape(pairs, PAIR, 4, WIDE)
        mem_all = jnp.concatenate(group_gather(memory_t, heads, mine), axis=2)
        mem_all = mem_all.reshape(clips, all_heads, 2 * HD, TPC)
        tail = jnp.concatenate(group_gather(tail_own, heads, mine), axis=2)
        tail = tail.reshape(clips, all_heads, 2 * REST, WIDE)

        first = lax.all_gather(hidden_weight, ("batch", "head"), axis=0, tiled=True)
        second = lax.all_gather(output_weight, ("batch", "head"), axis=0, tiled=True)
        packed, keys, att, log, normed, middle, normed_two = attention_forward(
            x, w_all, mem_all, tail, side_mask, main_mask, taps_all, gain_one, gain_two
        )
    outputs, grad, grad_low, d_first, d_second, d_gain_two = mlp(
        normed_two.reshape(clips * ROWS, width),
        cotangent.reshape(clips, TPC, width),
        first,
        second,
        middle.reshape(clips * ROWS, width),
        gain_two,
    )
    if linked:
        d_x, small, d_first, d_second, d_w = attention_backward_links(
            x, w_all, mem_all, side_mask, main_mask, taps_all, gain_one,
            packed, keys, att, log, normed, grad, grad_low, d_gain_two,
            d_first.reshape(4, 2, 2, 2, -1, d_first.shape[1]), d_second.reshape(4, 2, 2, 2, -1, width),
        )
        qkv_rows = PAIR * 3 * HD
        d_qkv = d_w[:, :qkv_rows].astype(F32).reshape(own_heads, 3 * HD, width)
        d_proj = d_w[:, qkv_rows:].astype(F32).reshape(own_heads, HD, width)
        d_taps = small[8:, : 2 * WIDE].reshape(PAIR, 4, 2, WIDE).transpose(2, 0, 1, 3)[..., :HD]
        share = width // (batches * heads)
        start = (lax.axis_index("batch") * heads + me) * share
        d_gains = lax.dynamic_slice_in_dim(small[:2], start, share, axis=1)
        return (
            outputs.reshape(inputs.shape),
            d_x.reshape(inputs.shape),
            d_qkv.transpose(2, 0, 1),
            d_proj,
            d_taps.reshape(own_heads, 4, HD),
            d_gains[0],
            d_gains[1],
            d_first,
            d_second,
        )
    d_x, d_w, d_taps, d_gain_one = attention_backward(
        x, w_all, mem_all, side_mask, main_mask, taps_all, gain_one,
        packed, keys, att, log, normed, grad, grad_low,
    )
    d_proj = d_w[:, PIECES * WIDE :].reshape(heads, own_heads, WIDE, width)[:, :, :HD]
    d_w = d_w[:, : PIECES * WIDE].reshape(heads, own_heads, 3, WIDE, width)[:, :, :, :HD]
    d_w = d_w.reshape(heads, own_heads, 3 * HD, width)
    d_taps = d_taps.reshape(heads, own_heads, 4, WIDE)[..., :HD]
    d_w, d_proj, d_taps = (
        lax.psum(group_sum(list(grads), heads).astype(BF16), "batch").astype(F32)
        for grads in (d_w, d_proj, d_taps)
    )
    both = ("batch", "head")
    d_first = lax.psum_scatter(d_first, both, scatter_dimension=0, tiled=True).astype(F32)
    d_second = lax.psum_scatter(d_second, both, scatter_dimension=0, tiled=True).astype(F32)
    d_gains = lax.psum_scatter(
        jnp.concatenate([d_gain_one, d_gain_two], axis=0), both, scatter_dimension=1, tiled=True
    )
    return (
        outputs.reshape(inputs.shape),
        d_x.reshape(inputs.shape),
        d_w.transpose(2, 0, 1),
        d_proj,
        d_taps,
        d_gains[0],
        d_gains[1],
        d_first,
        d_second,
    )


def solution(mesh):
    return jax.shard_map(
        functools.partial(local, mesh.shape["head"], mesh.shape["batch"]),
        mesh=mesh,
        in_specs=(
            P(None, ("batch", "head"), None, None),
            P(None, "head", None),
            P("head", None, None),
            P("head", None, None),
            P(),
            P(),
            P(("batch", "head"), None),
            P(("batch", "head"), None),
            P(None, "batch", None, "head", None),
            P(None, "batch"),
            P(None, ("batch", "head"), None, None),
        ),
        out_specs=(
            P(None, ("batch", "head"), None, None),
            P(None, ("batch", "head"), None, None),
            P(None, "head", None),
            P("head", None, None),
            P("head", None, None),
            P(("batch", "head")),
            P(("batch", "head")),
            P(("batch", "head"), None),
            P(("batch", "head"), None),
        ),
        check_vma=False,
    )
```

```python
import functools
import math

import jax
import jax.numpy as jnp
from jax import lax
from jax.experimental import pallas as pl
from jax.experimental.pallas import tpu as pltpu
from jax.sharding import PartitionSpec as P

HD = 96
WIDE = 128
FRAMES = 8
TPC = 392
PTOK = 196
SPOT = TPC // FRAMES
HALF = 200
ROWS = 2 * HALF
MAIN = 384
REST = TPC - MAIN
SIDE = 256
PAIR = 2
PIECES = 3 * PAIR

NORM_EPS = 1e-06
NEG = -1e30
LOG2E = 1.4426950408889634
SCORE = HD ** (-0.5)

F32 = jnp.float32
BF16 = jnp.bfloat16


def dot(a, b):
    return lax.dot_general(a, b, (((1,), (0,)), ((), ())), preferred_element_type=F32)


def dot_nt(a, b):
    return lax.dot_general(a, b, (((1,), (1,)), ((), ())), preferred_element_type=F32)


def dot_tn(a, b):
    return lax.dot_general(a, b, (((0,), (0,)), ((), ())), preferred_element_type=F32)


def reorder(shape, row_dim):
    rows = lax.broadcasted_iota(jnp.int32, shape, row_dim)
    tokens = lax.broadcasted_iota(jnp.int32, shape, 1 - row_dim)
    odd = (rows >= HALF).astype(jnp.int32)
    spot = rows - HALF * odd
    frame = sum((spot >= SPOT * step).astype(jnp.int32) for step in range(1, FRAMES // 2))
    return ((tokens == spot + SPOT * (frame + odd)) & (spot < PTOK)).astype(BF16)


def norm_parts(values):
    average = jnp.mean(values, axis=-1, keepdims=True)
    centered = values - average
    spread = lax.rsqrt(jnp.mean(centered * centered, axis=-1, keepdims=True) + NORM_EPS)
    return centered * spread, spread


def norm_pull(values, gain, grad):
    unit, spread = norm_parts(values)
    scaled = grad * gain
    inner = jnp.mean(scaled * unit, axis=-1, keepdims=True)
    pulled = spread * (scaled - jnp.mean(scaled, axis=-1, keepdims=True) - unit * inner)
    return pulled, jnp.sum(grad * unit, axis=0, keepdims=True)


def as_row(ref):
    return ref[...].reshape(1, -1)


def widen(taps):
    return jnp.concatenate([taps, jnp.zeros((taps.shape[0], WIDE - taps.shape[1]), F32)], axis=1)


def mask_rows(index):
    slot = lax.broadcasted_iota(jnp.int32, (1, MAIN), 1) // PTOK
    main = jnp.where(index > slot, 0.0, NEG)
    spot = lax.broadcasted_iota(jnp.int32, (1, SIDE), 1)
    tail_open = (spot >= HALF) & (spot < HALF + REST) & (index > (TPC - 1) // PTOK)
    return jnp.where((spot < PTOK) | tail_open, 0.0, NEG), main


def value_columns(memory_t):
    return jnp.concatenate([memory_t[HD:], jnp.zeros((WIDE - HD, memory_t.shape[1]), BF16)], axis=0)


def forward_kernel(
    x_ref, cot_ref, w_ref, mem_ref, tail_ref, side_ref, main_ref, taps_ref, gain_one_ref, gain_two_ref,
    packed_ref, keys_ref, att_ref, log_ref, normed_ref, middle_ref, normed_two_ref, cot_out,
    x_rows, normed_rows, branch, logs,
):
    forward_step(
        pl.program_id(0), pl.program_id(1), pl.num_programs(0), (side_ref[0], main_ref[0]),
        w_ref.at[0, : PIECES * WIDE], w_ref.at[0, PIECES * WIDE :], mem_ref.at[0], tail_ref.at[0], taps_ref.at[0],
        x_ref, cot_ref, gain_one_ref, gain_two_ref,
        packed_ref, keys_ref, att_ref, log_ref, normed_ref, middle_ref, normed_two_ref, cot_out,
        x_rows, normed_rows, branch, logs,
    )


def forward_step(
    pair, clip, pairs, masks,
    qkv_ref, proj_ref, mem_ref, tail_ref, taps_ref,
    x_ref, cot_ref, gain_one_ref, gain_two_ref,
    packed_ref, keys_ref, att_ref, log_ref, normed_ref, middle_ref, normed_two_ref, cot_out,
    x_rows, normed_rows, branch, log_rows,
):
    here = pl.ds(clip, 1)

    @pl.when(pair == 0)
    def _():
        rows = dot(reorder((ROWS, TPC), 0), x_ref[0])
        x_rows[here] = rows.astype(BF16)[None]
        unit, _ = norm_parts(rows)
        low = (unit * as_row(gain_one_ref)).astype(BF16)
        normed_rows[here] = low[None]
        normed_ref[0] = low
        log_rows[here] = jnp.zeros((1, ROWS, WIDE), F32)

    normed = normed_rows[here][0]
    packed = dot_nt(normed, qkv_ref[...].reshape(-1, normed.shape[1]))
    packed_ref[0, 0] = packed.astype(BF16)
    logs = []
    outs = []
    for head in range(PAIR):
        base = 3 * WIDE * head
        query = packed[:, base : base + WIDE]
        key = packed[:, base + WIDE : base + 2 * WIDE]
        value = packed[:, base + 2 * WIDE : base + 3 * WIDE]
        query_low = query.astype(BF16)
        taps = widen(taps_ref[head])
        zeros = jnp.zeros((SIDE - HALF - REST, WIDE), F32)
        pooled_key = taps[0:1] * key[:HALF] + taps[1:2] * key[HALF:]
        pooled_value = taps[2:3] * value[:HALF] + taps[3:4] * value[HALF:]
        tail = tail_ref[head].astype(F32)
        side_key = jnp.concatenate([pooled_key, tail[:REST], zeros], axis=0).astype(BF16)
        side_value = jnp.concatenate([pooled_value, tail[REST:], zeros], axis=0).astype(BF16)
        keys_ref[0, 0, head, 0] = side_key
        keys_ref[0, 0, head, 1] = side_value
        memory_t = mem_ref[head]
        score_side = dot_nt(query_low, side_key) * (SCORE * LOG2E) + masks[0]
        score_main = dot(query_low, memory_t[:WIDE]) * (SCORE * LOG2E) + masks[1]
        top = jnp.maximum(
            jnp.max(score_side, axis=-1, keepdims=True), jnp.max(score_main, axis=-1, keepdims=True)
        )
        weight_side = jnp.exp2(score_side - top)
        weight_main = jnp.exp2(score_main - top)
        total = jnp.sum(weight_side, axis=-1, keepdims=True) + jnp.sum(weight_main, axis=-1, keepdims=True)
        mixed = dot(weight_side.astype(BF16), side_value) + dot_nt(
            weight_main.astype(BF16), value_columns(memory_t)
        )
        outs.append(mixed / total + query)
        logs.append(top + jnp.log2(total))
    attended = jnp.concatenate(outs, axis=1).astype(BF16)
    att_ref[0, 0] = attended
    lane = lax.broadcasted_iota(jnp.int32, (ROWS, WIDE), 1) - PAIR * pair
    log_rows[here] = jnp.where(lane == 0, logs[0], jnp.where(lane == 1, logs[1], log_rows[here][0]))[None]
    part = dot(attended, proj_ref[...].reshape(-1, normed.shape[1]))[None]

    @pl.when(pair == 0)
    def _():
        branch[here] = part

    @pl.when(pair > 0)
    def _():
        branch[here] += part

    @pl.when(pair == pairs - 1)
    def _():
        middle = x_rows[here][0].astype(F32) + branch[here][0]
        middle_ref[0] = middle
        unit, _ = norm_parts(middle)
        normed_two_ref[0] = (unit * as_row(gain_two_ref)).astype(BF16)
        log_ref[0] = log_rows[here][0]
        cot_out[0] = dot(reorder((ROWS, TPC), 0), cot_ref[0]).astype(BF16)


def mlp_kernel(
    normed_ref, cot_ref, first_ref, second_ref, middle_ref, gain_ref,
    out_ref, grad_ref, d_first_ref, d_second_ref, d_gain_ref,
    middle, total, grad_normed, active, grad_hidden, near,
):
    step = pl.program_id(0)
    clips = middle.shape[0] // ROWS
    tiles = pl.num_programs(0) - clips
    fetch = pltpu.make_async_copy(middle_ref, middle, near.at[0])

    @pl.when(step == 0)
    def _():
        fetch.start()
        d_gain_ref[...] = jnp.zeros_like(d_gain_ref)

    @pl.when(step < tiles)
    def _():
        first = first_ref[...]
        second = second_ref[...]

        @pl.loop(0, middle.shape[0] // CHUNK)
        def _(chunk):
            here = pl.ds(pl.multiple_of(chunk * CHUNK, CHUNK), CHUNK)
            hidden = dot(normed_ref[here, :], first)
            grad_active = dot_nt(cot_ref[here, :], second)
            bell = jnp.exp2(hidden * hidden * (-0.5 * LOG2E))
            step_size = 1.0 / (1.0 + (0.3275911 * math.sqrt(0.5)) * jnp.abs(hidden))
            tail = step_size * (0.5 * 1.061405429) + (0.5 * -1.453152027)
            tail = step_size * tail + (0.5 * 1.421413741)
            tail = step_size * tail + (0.5 * -0.284496736)
            tail = step_size * tail + (0.5 * 0.254829592)
            tail = step_size * tail * bell
            cumulative = jnp.where(hidden < 0.0, tail, 1.0 - tail)
            slope = cumulative + hidden * bell * 0.3989422804014327
            active_low = (hidden * cumulative).astype(BF16)
            hidden_low = (slope * grad_active).astype(BF16)
            active[here, :] = active_low
            grad_hidden[here, :] = hidden_low
            fed = dot(active_low, second)
            back = dot_nt(hidden_low, first)

            @pl.when(step == 0)
            def _():
                total[here, :] = fed
                grad_normed[here, :] = back

            @pl.when(step > 0)
            def _():
                total[here, :] += fed
                grad_normed[here, :] += back

        d_first_ref[...] = dot_tn(normed_ref[...], grad_hidden[...]).astype(BF16)
        d_second_ref[...] = dot_tn(active[...], cot_ref[...]).astype(BF16)

    @pl.when(step == tiles)
    def _():
        fetch.wait()

    @pl.when(step >= tiles)
    def _():
        here = pl.ds(pl.multiple_of((step - tiles) * ROWS, ROWS), ROWS)
        values = middle[here, :]
        out = (values + total[here, :]).astype(BF16)
        out_ref[0] = dot(reorder((TPC, ROWS), 1), out).astype(BF16)
        pulled, d_gain = norm_pull(values, as_row(gain_ref), grad_normed[here, :])
        grad_ref[...] = (cot_ref[here, :].astype(F32) + pulled).astype(BF16)
        d_gain_ref[...] += d_gain


def backward_kernel(
    x_ref, w_ref, mem_ref, side_ref, main_ref, taps_ref, gain_ref,
    packed_ref, keys_ref, att_ref, log_ref, normed_ref, grad_ref,
    d_x_ref, d_w_ref, d_taps_ref, d_gain_ref,
    grad_normed,
):
    backward_step(
        pl.program_id(0), pl.program_id(1), pl.program_id(0) == 0, pl.program_id(0) == pl.num_programs(0) - 1,
        (side_ref[0], main_ref[0]),
        w_ref.at[0, : PIECES * WIDE], w_ref.at[0, PIECES * WIDE :], d_w_ref.at[0], d_taps_ref.at[0],
        x_ref, mem_ref, taps_ref, gain_ref,
        packed_ref, keys_ref, att_ref, log_ref, normed_ref, grad_ref,
        d_x_ref, d_gain_ref, grad_normed,
    )


def backward_step(
    pair, clip, first_pair, last_pair, masks,
    qkv_ref, proj_ref, d_w_ref, d_taps_ref,
    x_ref, mem_ref, taps_ref, gain_ref,
    packed_ref, keys_ref, att_ref, log_ref, normed_ref, grad_ref,
    d_x_ref, d_gain_ref, grad_normed,
):
    here = pl.ds(clip, 1)

    @pl.when(clip == 0)
    def _():
        d_w_ref[...] = jnp.zeros_like(d_w_ref)
        d_taps_ref[...] = jnp.zeros_like(d_taps_ref)

    grad_branch = grad_ref[...]
    lane = lax.broadcasted_iota(jnp.int32, (ROWS, WIDE), 1) - PAIR * pair
    width = grad_branch.shape[1]
    grad_out = dot_nt(grad_branch, proj_ref[...].reshape(-1, width))
    d_w_ref[PIECES * WIDE :] += dot_tn(att_ref[0, 0], grad_branch)
    pieces = []
    for head in range(PAIR):
        base = 3 * WIDE * head
        query = packed_ref[0, 0, :, base : base + WIDE]
        key = packed_ref[0, 0, :, base + WIDE : base + 2 * WIDE].astype(F32)
        value = packed_ref[0, 0, :, base + 2 * WIDE : base + 3 * WIDE].astype(F32)
        out_grad = grad_out[:, WIDE * head : WIDE * (head + 1)].astype(BF16)
        taps = widen(taps_ref[0, head])
        side_key = keys_ref[0, 0, head, 0]
        side_value = keys_ref[0, 0, head, 1]
        memory_t = mem_ref[0, head]
        log = jnp.sum(jnp.where(lane == head, log_ref[0], 0.0), axis=-1, keepdims=True)
        score_side = dot_nt(query, side_key) * (SCORE * LOG2E) + masks[0]
        score_main = dot(query, memory_t[:WIDE]) * (SCORE * LOG2E) + masks[1]
        weight_side = jnp.exp2(score_side - log)
        weight_main = jnp.exp2(score_main - log)
        grad_side = dot_nt(out_grad, side_value)
        grad_main = dot(out_grad, value_columns(memory_t))
        inner = jnp.sum(weight_side * grad_side, axis=-1, keepdims=True) + jnp.sum(
            weight_main * grad_main, axis=-1, keepdims=True
        )
        score_grad_side = (weight_side * (grad_side - inner)).astype(BF16)
        score_grad_main = (weight_main * (grad_main - inner)).astype(BF16)
        grad_query = (
            dot(score_grad_side, side_key) + dot_nt(score_grad_main, memory_t[:WIDE])
        ) * SCORE + out_grad.astype(F32)
        grad_key = dot_tn(score_grad_side, query)[:HALF] * SCORE
        grad_value = dot_tn(weight_side.astype(BF16), out_grad)[:HALF]
        pieces += [
            grad_query,
            jnp.concatenate([taps[0:1] * grad_key, taps[1:2] * grad_key], axis=0),
            jnp.concatenate([taps[2:3] * grad_value, taps[3:4] * grad_value], axis=0),
        ]
        d_taps_ref[head] += jnp.concatenate(
            [
                jnp.sum(part * grad, axis=0, keepdims=True)
                for part, grad in (
                    (key[:HALF], grad_key),
                    (key[HALF:], grad_key),
                    (value[:HALF], grad_value),
                    (value[HALF:], grad_value),
                )
            ],
            axis=0,
        )
    grad_packed = jnp.concatenate(pieces, axis=1).astype(BF16)
    d_w_ref[: PIECES * WIDE] += dot_tn(grad_packed, normed_ref[0])
    part = dot(grad_packed, qkv_ref[...].reshape(-1, width))[None]

    @pl.when(first_pair)
    def _():
        grad_normed[here] = part

    @pl.when(jnp.logical_not(first_pair))
    def _():
        grad_normed[here] += part

    @pl.when(last_pair)
    def _():
        rows = dot(reorder((ROWS, TPC), 0), x_ref[0])
        pulled, d_gain = norm_pull(rows, as_row(gain_ref), grad_normed[here][0])
        d_x = (grad_branch.astype(F32) + pulled).astype(BF16)
        d_x_ref[0] = dot(reorder((TPC, ROWS), 1), d_x).astype(BF16)

        @pl.when(clip == 0)
        def _():
            d_gain_ref[...] = d_gain

        @pl.when(clip > 0)
        def _():
            d_gain_ref[...] += d_gain


class Scatter:
    def __init__(self, name, order, source, total, from_core, from_one, from_two, from_z, result, out, links, sem, here):
        self.name, self.order, self.links, self.here = name, order, links, here
        self.total, self.from_core, self.from_one, self.from_two, self.from_z = (
            total, from_core, from_one, from_two, from_z
        )
        self.result = result
        z, y, core, x, beside, above, sibling, along = here
        links.add(name + "c", source.at[:, :, 1 - core], from_core, sibling)
        self.own = pltpu.make_async_copy(source.at[:, :, core], total, sem.at[0])
        self.done = pltpu.make_async_copy(result, out, sem.at[1])
        if order == "xyz":
            links.add(name + "x", total.at[:, :, 1 - x], from_one, beside)
            links.add(name + "y", total.at[:, 1 - y, x], from_two, above)
            for shift in (1, 2, 3):
                links.add(f"{name}z{shift}", total.at[turn(z, shift), y, x], from_z.at[shift - 1], along[shift - 1])
        else:
            links.add(name + "y", total.at[:, 1 - y], from_one, above)
            for shift in (1, 2, 3):
                links.add(f"{name}z{shift}", total.at[turn(z, shift), y], from_z.at[shift - 1], along[shift - 1])
            links.add(name + "x", total.at[z, y, 1 - x], from_two, beside)

    def stage(self, axis):
        return [f"{self.name}z{shift}" for shift in (1, 2, 3)] if axis == "z" else [self.name + axis]

    def begin(self):
        self.links.start(self.name + "c")
        self.own.start()

    def step(self, at):
        z, y, core, x = self.here[:4]
        total = self.total
        axis = ("c" + self.order)[at]
        self.links.arrived(*self.stage(axis))
        if axis == "c":
            self.own.wait()

            @pl.loop(0, 4)
            def _(row):
                for column in (0, 1):
                    for head in (0, 1):
                        total[row, column, head] = add_low(total[row, column, head], self.from_core[row, column, head])

        elif at == 1:

            @pl.loop(0, 4)
            def _(row):
                for other in (0, 1):
                    spot = (row, other, x) if self.order == "xyz" else (row, y, other)
                    total[spot] = add_low(total[spot], self.from_one[row, other])

        elif axis == "y":

            @pl.loop(0, 4)
            def _(row):
                total[row, y, x] = add_low(total[row, y, x], self.from_two[row])

        elif axis == "z" and at == 2:
            for head in (0, 1):
                part = total[z, y, head].astype(F32)
                for shift in range(3):
                    part = part + self.from_z[shift, head].astype(F32)
                total[z, y, head] = part.astype(BF16)
        else:
            part = total[z, y, x].astype(F32)
            if axis == "z":
                for shift in range(3):
                    part = part + self.from_z[shift].astype(F32)
            else:
                part = part + self.from_two[...].astype(F32)
            self.result[...] = part
            self.done.start()
        if at < 3:
            self.links.start(*self.stage(self.order[at]))


def add_low(one, other):
    return (one.astype(F32) + other.astype(F32)).astype(BF16)


def unpad(ref, into, more=None):
    for piece in range(ref.shape[0] // WIDE):
        rows = ref[WIDE * piece : WIDE * piece + HD]
        narrow = slice(HD * piece, HD * (piece + 1))
        if more is not None:
            rows = rows + more[narrow].astype(F32)
        into[narrow] = rows.astype(BF16)


BACKWARD_COPIES = 48
THIRD = 384
PART = 96


def backward_links_kernel(
    index_ref, x_ref, qkv_ref, proj_ref, mem_ref, taps_ref, gain_ref,
    packed_ref, keys_ref, att_ref, log_ref, normed_ref, grad_ref, gain_two_ref,
    d_first, d_second,
    d_x_ref, small_out, first_out, second_out, w_out,
    grad_normed, d_gain, d_w, d_taps,
    far_sent, far_got, own, own_core, own_y, own_z, whole,
    small_mine, small_far, small_x, small_core, small_y, small_z,
    first_total, first_core, first_one, first_two, first_z, first_result,
    second_total, second_core, second_one, second_two, second_z, second_result,
    send, recv, near,
):
    step = pl.program_id(0)
    last = pl.num_programs(0) - 1
    z, y, core, x, at = place()
    links = Links(send, recv)
    beside, above, sibling = at(z, y, core, 1 - x), at(z, 1 - y, core, x), at(z, y, 1 - core, x)
    along = [at(turn(z, shift), y, core, x) for shift in (1, 2, 3)]
    here = (z, y, core, x, beside, above, sibling, along)
    first = Scatter(
        "f", "xyz", d_first, first_total, first_core, first_one, first_two, first_z, first_result, first_out,
        links, near.at[pl.ds(0, 2)], here,
    )
    second = Scatter(
        "s", "yzx", d_second, second_total, second_core, second_one, second_two, second_z, second_result, second_out,
        links, near.at[pl.ds(2, 2)], here,
    )

    def lanes(core):
        return pl.ds(pl.multiple_of(core * THIRD, THIRD), THIRD)

    def rows(y, z):
        return pl.ds(pl.multiple_of(y * THIRD + z * PART, PART), PART)

    def half(y):
        return pl.ds(pl.multiple_of(y * THIRD, THIRD), THIRD)

    for i in (0, 1):
        links.add(f"far{i}", far_sent.at[i], far_got.at[i], beside)
        links.add(f"rc{i}", own.at[i, :, lanes(1 - core)], own_core.at[i], sibling)
        links.add(f"ry{i}", own.at[i, half(1 - y), lanes(core)], own_y.at[i], above)
        for shift in (1, 2, 3):
            links.add(
                f"rz{i}{shift}", own.at[i, rows(y, turn(z, shift)), lanes(core)], own_z.at[i, shift - 1], along[shift - 1]
            )
        piece = whole.at[i, rows(y, z), lanes(core)]
        for shift in (1, 2, 3):
            links.add(f"gz{i}{shift}", piece, piece, along[shift - 1])
        piece = whole.at[i, half(y), lanes(core)]
        links.add(f"gy{i}", piece, piece, above)
        piece = whole.at[i, :, lanes(core)]
        links.add(f"gc{i}", piece, piece, sibling)
    links.add("mx", small_far, small_x, beside)
    links.add("mc", small_mine, small_core, sibling)
    links.add("my", small_core, small_y, above)
    for shift in (1, 2, 3):
        links.add(f"mz{shift}", small_z.at[z], small_z.at[z], along[shift - 1])

    @pl.when(step == 0)
    def _():
        greet([beside, above, sibling] + along)
        first.begin()
        second.begin()

    backward_step(
        lax.rem(lax.div(step, 4) + 2, 4), lax.rem(step, 4), step < 4, step >= 12,
        mask_rows(index_ref[x, lax.rem(step, 4)]),
        qkv_ref.at[0], proj_ref.at[0], d_w, d_taps.at[lax.div(step, 4)],
        x_ref, mem_ref, taps_ref, gain_ref,
        packed_ref, keys_ref, att_ref, log_ref, normed_ref, grad_ref,
        d_x_ref, d_gain, grad_normed,
    )

    def sum_core(i):
        links.arrived(f"rc{i}")
        own[i, :, lanes(core)] = add_low(own[i, :, lanes(core)], own_core[i])
        links.start(f"ry{i}")

    def sum_y(i):
        links.arrived(f"ry{i}")
        own[i, half(y), lanes(core)] = add_low(own[i, half(y), lanes(core)], own_y[i])
        links.start(*[f"rz{i}{shift}" for shift in (1, 2, 3)])

    def sum_z(i):
        links.arrived(*[f"rz{i}{shift}" for shift in (1, 2, 3)])
        part = own[i, rows(y, z), lanes(core)].astype(F32)
        for shift in range(3):
            part = part + own_z[i, shift].astype(F32)
        whole[i, rows(y, z), lanes(core)] = part.astype(BF16)
        links.start(*[f"gz{i}{shift}" for shift in (1, 2, 3)])

    def spread_y(i):
        links.arrived(*[f"gz{i}{shift}" for shift in (1, 2, 3)])
        links.start(f"gy{i}")

    def spread_core(i):
        links.arrived(f"gy{i}")
        links.start(f"gc{i}")

    def far(i):
        unpad(d_w, far_sent.at[i])
        links.start(f"far{i}")

    def mine(i):
        links.arrived(f"far{i}")
        unpad(d_w, own.at[i], far_got.at[i])
        links.start(f"rc{i}")

    plan = {
        1: [lambda: first.step(0)],
        2: [lambda: second.step(0)],
        3: [lambda: far(0)],
        7: [lambda: far(1), lambda: first.step(1)],
        8: [lambda: second.step(1)],
        10: [lambda: first.step(2)],
        11: [lambda: mine(0)],
        12: [lambda: sum_core(0)],
        13: [lambda: sum_y(0), lambda: first.step(3)],
        14: [lambda: sum_z(0), lambda: second.step(2)],
    }
    for when, acts in plan.items():

        @pl.when(step == when)
        def _(acts=acts):
            for act in acts:
                act()

    @pl.when(step == last)
    def _():
        mine(1)
        for i, target in ((2, small_mine), (0, small_far)):
            target[...] = jnp.zeros_like(target)
            target[0:1] = d_gain[...]
            target[1:2] = gain_two_ref[...]
            for j in (0, 1):
                target[8:16, WIDE * j : WIDE * (j + 1)] = d_taps[i + j].reshape(8, WIDE)
        links.start("mx")
        spread_y(0)
        sum_core(1)
        links.arrived("mx")
        small_mine[...] += small_x[...]
        links.start("mc")
        spread_core(0)
        sum_y(1)
        links.arrived("mc")
        small_core[...] += small_mine[...]
        links.start("my")
        second.step(3)
        sum_z(1)
        links.arrived("my")
        small_z[pl.ds(z, 1)] = (small_y[...] + small_core[...])[None]
        links.start("mz1", "mz2", "mz3")
        spread_y(1)
        spread_core(1)
        links.arrived("mz1", "mz2", "mz3")
        small_out[...] = (small_z[0] + small_z[1]) + (small_z[2] + small_z[3])
        links.arrived("gc0", "gc1")
        save = pltpu.make_async_copy(whole, w_out, near.at[4])
        save.start()
        save.wait()
        first.done.wait()
        second.done.wait()
        links.sent()


VMEM_LIMIT = 60 << 20


def compiler_params(dims):
    return pltpu.CompilerParams(
        dimension_semantics=("arbitrary",) * dims, vmem_limit_bytes=VMEM_LIMIT
    )


def shaped(shape, dtype):
    return jax.ShapeDtypeStruct(shape, dtype)


class Links:
    def __init__(self, send, recv):
        self.send, self.recv, self.made = send, recv, {}

    def add(self, name, src, dst, device, send_if=None, recv_if=None):
        at = len(self.made)
        self.made[name] = (src, dst, device, at, send_if, recv_if)

    def get(self, name):
        src, dst, device, at = self.made[name][:4]
        return pltpu.make_async_remote_copy(
            src_ref=src,
            dst_ref=dst,
            send_sem=self.send.at[at],
            recv_sem=self.recv.at[at],
            device_id=device,
            device_id_type=pl.DeviceIdType.MESH,
        )

    def start(self, *names):
        for name in names:
            self.only(self.made[name][4], self.get(name).start)

    def arrived(self, *names):
        for name in names:
            self.only(self.made[name][5], self.get(name).wait_recv)

    def sent(self):
        for name in self.made:
            self.only(self.made[name][4], self.get(name).wait_send)

    def only(self, condition, act):
        if condition is None:
            act()
        else:
            pl.when(condition)(lambda: act())


def place():
    batch, head = lax.axis_index("batch"), lax.axis_index("head")
    z, y, core = batch // 4, lax.rem(batch // 2, 2), lax.rem(batch, 2)

    def at(z, y, core, x):
        return {"batch": (z * 2 + y) * 2 + core, "head": x}

    return z, y, core, head, at


def greet(devices):
    barrier = pltpu.get_barrier_semaphore()
    for device in devices:
        pl.semaphore_signal(barrier, inc=1, device_id=device, device_id_type=pl.DeviceIdType.MESH)
    pl.semaphore_wait(barrier, len(devices))


def turn(z, shift):
    return lax.rem(z + shift + 4, 4)


FORWARD_COPIES = 96
SPLIT = HD // 2


def forward_links_kernel(
    index_ref, x_ref, cot_ref, gain_one_ref, gain_two_ref,
    qkv_own, proj_own, mem_own, tail_own, taps_own, hidden_own, output_own,
    packed_ref, keys_ref, att_ref, log_ref, normed_ref, middle_ref, normed_two_ref, cot_out,
    first_all, second_all, qkv_out, proj_out, mem_out, taps_out,
    x_rows, normed_rows, branch, logs, qkv_all, proj_all, mem_all, tail_all, taps_all,
    send, recv, near, save,
):
    step = pl.program_id(0)
    z, y, core, x, at = place()
    links = Links(send, recv)
    beside, above, sibling = at(z, y, core, 1 - x), at(z, 1 - y, core, x), at(z, y, 1 - core, x)
    higher, lower = at(turn(z, 1), y, core, x), at(turn(z, -1), y, core, x)
    column = pl.ds(pl.multiple_of(core * MAIN, MAIN), MAIN)
    me = ((z * 2 + y) * 2 + core) * 2 + x
    clips = mem_own.shape[0]

    def split(z, y, *between):
        rows = pl.ds(pl.multiple_of(y * SPLIT, SPLIT), SPLIT)
        return (lax.div(z, 2), lax.rem(z, 2)) + between + (rows, column)

    def block(kind, z, y):
        if kind == "q":
            return qkv_all.at[pl.ds(2, 2)].at[split(z, y, slice(None))]
        if kind == "p":
            return proj_all.at[pl.ds(2, 2)].at[split(z, y)]
        return (first_all if kind == "0" else second_all).at[pl.ds(((z * 2 + y) * 2 + core) * 2, 2)]

    links.add("xq", qkv_own.at[split(z, y, slice(None))], block("q", z, y), beside)
    links.add("xp", proj_own.at[split(z, y)], block("p", z, y), beside)
    links.add("x0", hidden_own, first_all.at[me], beside)
    links.add("x1", output_own, second_all.at[me], beside)
    for kind in "qp01":
        mine = block(kind, z, y)
        links.add("y" + kind, mine, mine, above)
        if kind in "01":
            links.add("c" + kind, mine, mine, sibling)
            mine = block(kind, z, 1 - y)
            links.add("e" + kind, mine, mine, sibling)
        for hop in (1, 2, 3):
            below, beyond = z >= hop, z + hop <= 3
            passed = block(kind, turn(z, 1 - hop), y)
            links.add(f"u{hop}{kind}", passed, passed, higher, (z <= 2) & (z >= hop - 1), below)
            passed = block(kind, turn(z, hop - 1), y)
            links.add(f"d{hop}{kind}", passed, passed, lower, (z >= 1) & (z + hop <= 4), beyond)
            for side, shift, there in (("u", -hop, below), ("d", hop, beyond)):
                came = block(kind, turn(z, shift), y)
                links.add(f"y{side}{hop}{kind}", came, came, above, there, there)
                if kind in "01":
                    links.add(f"c{side}{hop}{kind}", came, came, sibling, there, there)
                    came = block(kind, turn(z, shift), 1 - y)
                    links.add(f"e{side}{hop}{kind}", came, came, sibling, there, there)
    far = qkv_all.at[pl.ds(2, 2), :, :, pl.ds(0, HD), column]
    links.add("cq", far, far, sibling)
    far = proj_all.at[pl.ds(2, 2), :, pl.ds(0, HD), column]
    links.add("cp", far, far, sibling)
    for clip in range(clips):
        links.add(f"m{clip}", mem_own.at[clip, 1 - x, :, :, pl.ds(0, MAIN)], mem_all.at[1, clip], beside)
    links.add("tail", tail_own.at[:, 1 - x], tail_all.at[1], beside)
    links.add("taps", taps_own, taps_all.at[pl.ds(2, 2)], beside)

    local = [
        (qkv_own, qkv_all.at[pl.ds(0, 2), :, :, pl.ds(0, HD)]),
        (proj_own, proj_all.at[pl.ds(0, 2), :, pl.ds(0, HD)]),
        (tail_own.at[:, x], tail_all.at[0]),
        (taps_own, taps_all.at[pl.ds(0, 2)]),
        (hidden_own, first_all.at[me]),
        (output_own, second_all.at[me]),
    ] + [(mem_own.at[clip, x, :, :, pl.ds(0, MAIN)], mem_all.at[0, clip]) for clip in range(clips)]
    local = [pltpu.make_async_copy(src, dst, near.at[i]) for i, (src, dst) in enumerate(local)]
    saved = [
        (qkv_all, qkv_out),
        (proj_all, proj_out),
        (taps_all, taps_out),
        (mem_all.at[0], mem_out.at[0]),
    ] + [(mem_all.at[1, clip], mem_out.at[1, clip]) for clip in range(clips)]
    saved = [pltpu.make_async_copy(src, dst, save.at[i]) for i, (src, dst) in enumerate(saved)]

    @pl.when(step == 0)
    def _():
        greet([beside, above, sibling, higher, lower])
        links.start("xq", "xp", "taps", "tail", "x0", "x1")
        for copy in local:
            copy.start()

        @pl.loop(0, 4)
        def _(pair):
            for head in range(PAIR):
                for piece in range(3):
                    qkv_all[pair, head, piece, HD:] = jnp.zeros((WIDE - HD, qkv_all.shape[-1]), BF16)
                proj_all[pair, head, HD:] = jnp.zeros((WIDE - HD, qkv_all.shape[-1]), BF16)

        for copy in local:
            copy.wait()

    def hop(number, kinds):
        for kind in kinds:
            links.arrived(f"u{number}{kind}", f"d{number}{kind}")
            if number < 3:
                links.start(f"u{number + 1}{kind}", f"d{number + 1}{kind}")
            links.start(f"yu{number}{kind}", f"yd{number}{kind}")
            if kind in "01":
                links.start(f"cu{number}{kind}", f"cd{number}{kind}")

    def begin(kinds):
        for kind in kinds:
            links.arrived("x" + kind)
            links.start("u1" + kind, "d1" + kind, "y" + kind)
            if kind in "01":
                links.start("c" + kind)

    def across(number, kinds):
        for kind in kinds:
            for side in ("u", "d") if number else ("",):
                name = f"{side}{number}{kind}" if number else kind
                links.arrived("y" + name)
                if kind in "01":
                    links.start("e" + name)

    def weights():
        for number in range(4):
            across(number, "qp")
        links.start("cq", "cp")
        links.arrived("cq", "cp", "tail", "taps")

    def memory(clip):
        links.arrived(f"m{clip}")
        saved[4 + clip].start()

    plan = {
        1: [saved[3].start],
        2: [lambda: begin("qp"), lambda: links.start("m0")],
        3: [lambda: begin("01"), lambda: links.start("m1")],
        4: [lambda: hop(1, "qp")],
        5: [lambda: links.start("m2")],
        6: [lambda: hop(2, "qp"), lambda: links.start("m3")],
        7: [lambda: hop(3, "qp")],
        8: [lambda: hop(1, "0"), weights, lambda: memory(0)],
        9: [lambda: hop(1, "1")] + [copy.start for copy in saved[:3]],
        10: [lambda: hop(2, "0"), lambda: memory(1)],
        11: [lambda: hop(2, "1"), lambda: across(0, "01")],
        12: [lambda: across(1, "0"), lambda: memory(2)],
        13: [lambda: hop(3, "0"), lambda: across(1, "1")],
        14: [lambda: hop(3, "1"), lambda: across(2, "0"), lambda: memory(3)],
    }
    for when, acts in plan.items():

        @pl.when(step == when)
        def _(acts=acts):
            for act in acts:
                act()

    pair, clip = pair_of(step), clip_of(step)
    side = lax.div(pair, 2)
    heads = pl.ds(lax.rem(pair, 2) * PAIR, PAIR)
    forward_step(
        pair, clip, 4, mask_rows(index_ref[x, clip]),
        qkv_all.at[pair], proj_all.at[pair],
        mem_all.at[side, clip, heads], tail_all.at[side, clip, heads], taps_all.at[pair],
        x_ref, cot_ref, gain_one_ref, gain_two_ref,
        packed_ref, keys_ref, att_ref, log_ref, normed_ref, middle_ref, normed_two_ref, cot_out,
        x_rows, normed_rows, branch, logs,
    )

    @pl.when(step == pl.num_programs(0) - 1)
    def _():
        across(2, "1")
        across(3, "01")
        for copy in saved:
            copy.wait()
        for kind in "01":
            links.arrived("c" + kind, "e" + kind)
            for number in (1, 2, 3):
                for side in "ud":
                    links.arrived(f"c{side}{number}{kind}", f"e{side}{number}{kind}")
        links.sent()


def pair_of(step):
    return jnp.where(step < 8, lax.div(step, 4), 2 + lax.rem(step, 2))


def clip_of(step):
    return jnp.where(step < 8, lax.rem(step, 4), lax.div(step, 2) - 4)


def attention_forward_links(
    index, x, cot, qkv, proj, mem, tail, taps, gain_one, gain_two, hidden_weight, output_weight
):
    clips, width = x.shape[0], x.shape[2]
    packed_width = PIECES * WIDE
    devices = 32
    early = lambda s: jnp.where(s < 4, s, clips - 1)
    late = lambda s: jnp.where(s < 8, 0, clip_of(s))
    anywhere = pl.BlockSpec(memory_space=pl.ANY)
    return pl.pallas_call(
        forward_links_kernel,
        grid=(4 * clips,),
        in_specs=[
            pl.BlockSpec(memory_space=pltpu.SMEM),
            pl.BlockSpec((1, TPC, width), lambda s: (early(s), 0, 0)),
            pl.BlockSpec((1, TPC, width), lambda s: (late(s), 0, 0)),
            pl.BlockSpec(gain_one.shape, lambda s: (0,)),
            pl.BlockSpec(gain_two.shape, lambda s: (0,)),
        ] + [anywhere] * 7,
        out_specs=[
            pl.BlockSpec((1, 1, ROWS, packed_width), lambda s: (pair_of(s), clip_of(s), 0, 0)),
            pl.BlockSpec((1, 1, PAIR, 2, SIDE, WIDE), lambda s: (pair_of(s), clip_of(s), 0, 0, 0, 0)),
            pl.BlockSpec((1, 1, ROWS, PAIR * WIDE), lambda s: (pair_of(s), clip_of(s), 0, 0)),
            pl.BlockSpec((1, ROWS, WIDE), lambda s: (late(s), 0, 0)),
            pl.BlockSpec((1, ROWS, width), lambda s: (early(s), 0, 0)),
            pl.BlockSpec((1, ROWS, width), lambda s: (late(s), 0, 0)),
            pl.BlockSpec((1, ROWS, width), lambda s: (late(s), 0, 0)),
            pl.BlockSpec((1, ROWS, width), lambda s: (late(s), 0, 0)),
        ] + [anywhere] * 6,
        out_shape=[
            shaped((4, clips, ROWS, packed_width), BF16),
            shaped((4, clips, PAIR, 2, SIDE, WIDE), BF16),
            shaped((4, clips, ROWS, PAIR * WIDE), BF16),
            shaped((clips, ROWS, WIDE), F32),
            shaped((clips, ROWS, width), BF16),
            shaped((clips, ROWS, width), F32),
            shaped((clips, ROWS, width), BF16),
            shaped((clips, ROWS, width), BF16),
            shaped((devices,) + hidden_weight.shape, BF16),
            shaped((devices,) + output_weight.shape, BF16),
            shaped((4, PAIR, 3, WIDE, width), BF16),
            shaped((4, PAIR, WIDE, width), BF16),
            shaped((2, clips, 4, 2 * HD, MAIN), BF16),
            shaped((4,) + taps.shape[1:], F32),
        ],
        scratch_shapes=[
            pltpu.VMEM((clips, ROWS, width), BF16),
            pltpu.VMEM((clips, ROWS, width), BF16),
            pltpu.VMEM((clips, ROWS, width), F32),
            pltpu.VMEM((clips, ROWS, WIDE), F32),
            pltpu.VMEM((4, PAIR, 3, WIDE, width), BF16),
            pltpu.VMEM((4, PAIR, WIDE, width), BF16),
            pltpu.VMEM((2, clips, 4, 2 * HD, MAIN), BF16),
            pltpu.VMEM((2, clips, 4, 2 * REST, WIDE), BF16),
            pltpu.VMEM((4,) + taps.shape[1:], F32),
            pltpu.SemaphoreType.DMA((FORWARD_COPIES,)),
            pltpu.SemaphoreType.DMA((FORWARD_COPIES,)),
            pltpu.SemaphoreType.DMA((6 + clips,)),
            pltpu.SemaphoreType.DMA((4 + clips,)),
        ],
        compiler_params=pltpu.CompilerParams(
            dimension_semantics=("arbitrary",),
            vmem_limit_bytes=VMEM_LIMIT,
            collective_id=0,
            has_side_effects=True,
        ),
        name="attention_forward_links",
    )(index, x, cot, gain_one, gain_two, qkv, proj, mem, tail, taps, hidden_weight, output_weight)


def attention_forward(x, cot, w, mem, tail, side, main, taps, gain_one, gain_two):
    clips, pairs = x.shape[0], w.shape[0]
    width = x.shape[2]
    packed_width = PIECES * WIDE
    weight_rows = w.shape[1]
    late = lambda p, c: jnp.where(p == pairs - 1, c, 0)
    early = lambda p, c: jnp.where(p == 0, c, clips - 1)
    per_step = lambda p, c: (p, c)
    return pl.pallas_call(
        forward_kernel,
        grid=(pairs, clips),
        in_specs=[
            pl.BlockSpec((1, TPC, width), lambda p, c: (early(p, c), 0, 0)),
            pl.BlockSpec((1, TPC, width), lambda p, c: (late(p, c), 0, 0)),
            pl.BlockSpec((1, weight_rows, width), lambda p, c: (p, 0, 0)),
            pl.BlockSpec((1, PAIR, 2 * HD, MAIN), lambda p, c: (c, p, 0, 0)),
            pl.BlockSpec((1, PAIR, 2 * REST, WIDE), lambda p, c: (c, p, 0, 0)),
            pl.BlockSpec((1, 1, SIDE), lambda p, c: (c, 0, 0)),
            pl.BlockSpec((1, 1, MAIN), lambda p, c: (c, 0, 0)),
            pl.BlockSpec((1, PAIR, 4, HD), lambda p, c: (p, 0, 0, 0)),
            pl.BlockSpec(gain_one.shape, lambda p, c: (0,)),
            pl.BlockSpec(gain_two.shape, lambda p, c: (0,)),
        ],
        out_specs=[
            pl.BlockSpec((1, 1, ROWS, packed_width), lambda p, c: (p, c, 0, 0)),
            pl.BlockSpec((1, 1, PAIR, 2, SIDE, WIDE), lambda p, c: (p, c, 0, 0, 0, 0)),
            pl.BlockSpec((1, 1, ROWS, PAIR * WIDE), lambda p, c: (p, c, 0, 0)),
            pl.BlockSpec((1, ROWS, WIDE), lambda p, c: (late(p, c), 0, 0)),
            pl.BlockSpec((1, ROWS, width), lambda p, c: (early(p, c), 0, 0)),
            pl.BlockSpec((1, ROWS, width), lambda p, c: (late(p, c), 0, 0)),
            pl.BlockSpec((1, ROWS, width), lambda p, c: (late(p, c), 0, 0)),
            pl.BlockSpec((1, ROWS, width), lambda p, c: (late(p, c), 0, 0)),
        ],
        out_shape=[
            shaped((pairs, clips, ROWS, packed_width), BF16),
            shaped((pairs, clips, PAIR, 2, SIDE, WIDE), BF16),
            shaped((pairs, clips, ROWS, PAIR * WIDE), BF16),
            shaped((clips, ROWS, WIDE), F32),
            shaped((clips, ROWS, width), BF16),
            shaped((clips, ROWS, width), F32),
            shaped((clips, ROWS, width), BF16),
            shaped((clips, ROWS, width), BF16),
        ],
        scratch_shapes=[
            pltpu.VMEM((clips, ROWS, width), BF16),
            pltpu.VMEM((clips, ROWS, width), BF16),
            pltpu.VMEM((clips, ROWS, width), F32),
            pltpu.VMEM((clips, ROWS, WIDE), F32),
        ],
        compiler_params=compiler_params(2),
        name="attention_forward",
    )(x, cot, w, mem, tail, side, main, taps, gain_one, gain_two)


def once(shape):
    return pl.BlockSpec(shape, lambda t: (0,) * len(shape), pipeline_mode=pl.Buffered(1))


CHUNK = 800
TILE = 768


def mlp(normed, cot, first, second, middle, gain):
    rows, width = normed.shape
    hidden = first.shape[1]
    clips = rows // ROWS
    tiles = hidden // TILE
    tile_at = lambda t: jnp.minimum(t, tiles - 1)
    clip_at = lambda t: jnp.maximum(t - tiles, 0)
    return pl.pallas_call(
        mlp_kernel,
        grid=(tiles + clips,),
        in_specs=[
            once((rows, width)),
            once((rows, width)),
            pl.BlockSpec((width, TILE), lambda t: (0, tile_at(t))),
            pl.BlockSpec((TILE, width), lambda t: (tile_at(t), 0)),
            pl.BlockSpec(memory_space=pl.ANY),
            pl.BlockSpec(gain.shape, lambda t: (0,)),
        ],
        out_specs=[
            pl.BlockSpec((1, TPC, width), lambda t: (clip_at(t), 0, 0)),
            pl.BlockSpec((ROWS, width), lambda t: (clip_at(t), 0)),
            pl.BlockSpec((width, TILE), lambda t: (0, tile_at(t))),
            pl.BlockSpec((TILE, width), lambda t: (tile_at(t), 0)),
            once((1, width)),
        ],
        out_shape=[
            shaped((clips, TPC, width), BF16),
            shaped((rows, width), BF16),
            shaped((width, hidden), BF16),
            shaped((hidden, width), BF16),
            shaped((1, width), F32),
        ],
        scratch_shapes=[
            pltpu.VMEM((rows, width), F32),
            pltpu.VMEM((rows, width), F32),
            pltpu.VMEM((rows, width), F32),
            pltpu.VMEM((rows, TILE), BF16),
            pltpu.VMEM((rows, TILE), BF16),
            pltpu.SemaphoreType.DMA((1,)),
        ],
        compiler_params=compiler_params(1),
        name="mlp",
    )(normed, cot, first, second, middle, gain)


def attention_backward(x, w, mem, side, main, taps, gain, packed, keys, att, log, normed, grad):
    clips, pairs = x.shape[0], w.shape[0]
    width = x.shape[2]
    packed_width = PIECES * WIDE
    weight_rows = w.shape[1]
    late = lambda p, c: jnp.where(p == pairs - 1, c, 0)
    return pl.pallas_call(
        backward_kernel,
        grid=(pairs, clips),
        in_specs=[
            pl.BlockSpec((1, TPC, width), lambda p, c: (late(p, c), 0, 0)),
            pl.BlockSpec((1, weight_rows, width), lambda p, c: (p, 0, 0)),
            pl.BlockSpec((1, PAIR, 2 * HD, MAIN), lambda p, c: (c, p, 0, 0)),
            pl.BlockSpec((1, 1, SIDE), lambda p, c: (c, 0, 0)),
            pl.BlockSpec((1, 1, MAIN), lambda p, c: (c, 0, 0)),
            pl.BlockSpec((1, PAIR, 4, HD), lambda p, c: (p, 0, 0, 0)),
            pl.BlockSpec(gain.shape, lambda p, c: (0,)),
            pl.BlockSpec((1, 1, ROWS, packed_width), lambda p, c: (p, c, 0, 0)),
            pl.BlockSpec((1, 1, PAIR, 2, SIDE, WIDE), lambda p, c: (p, c, 0, 0, 0, 0)),
            pl.BlockSpec((1, 1, ROWS, PAIR * WIDE), lambda p, c: (p, c, 0, 0)),
            pl.BlockSpec((1, ROWS, WIDE), lambda p, c: (c, 0, 0)),
            pl.BlockSpec((1, ROWS, width), lambda p, c: (c, 0, 0)),
            pl.BlockSpec((ROWS, width), lambda p, c: (c, 0)),
        ],
        out_specs=[
            pl.BlockSpec((1, TPC, width), lambda p, c: (late(p, c), 0, 0)),
            pl.BlockSpec((1, weight_rows, width), lambda p, c: (p, 0, 0)),
            pl.BlockSpec((1, PAIR, 4, WIDE), lambda p, c: (p, 0, 0, 0)),
            pl.BlockSpec((1, width), lambda p, c: (0, 0)),
        ],
        out_shape=[
            shaped((clips, TPC, width), BF16),
            shaped((pairs, weight_rows, width), F32),
            shaped((pairs, PAIR, 4, WIDE), F32),
            shaped((1, width), F32),
        ],
        scratch_shapes=[pltpu.VMEM((clips, ROWS, width), F32)],
        compiler_params=compiler_params(2),
        name="attention_backward",
    )(x, w, mem, side, main, taps, gain, packed, keys, att, log, normed, grad)


def attention_backward_links(
    index, x, qkv, proj, mem, taps, gain, packed, keys, att, log, normed, grad, gain_two, d_first, d_second
):
    clips, width = x.shape[0], x.shape[2]
    packed_width = PIECES * WIDE
    weight_rows = (PIECES + PAIR) * WIDE
    low_rows = weight_rows // WIDE * HD
    pair_at = lambda s: lax.rem(lax.div(s, 4) + 2, 4)
    clip_at = lambda s: lax.rem(s, 4)
    late = lambda s: jnp.where(s < 12, 0, s - 12)
    anywhere = pl.BlockSpec(memory_space=pl.ANY)
    per_step = lambda s: (pair_at(s), clip_at(s), 0, 0)
    small = (16, width)

    def scatter_scratch(shape, order):
        one, two, last = ((4, 2), (4,), (3,)) if order == "xyz" else ((4, 2), (), (3, 2))
        return [
            pltpu.VMEM(lead + shape, BF16) for lead in ((4, 2, 2), (4, 2, 2), one, two, last)
        ] + [pltpu.VMEM(shape, F32)]

    first_shape, second_shape = d_first.shape[4:], d_second.shape[4:]
    return pl.pallas_call(
        backward_links_kernel,
        grid=(4 * clips,),
        in_specs=[
            pl.BlockSpec(memory_space=pltpu.SMEM),
            pl.BlockSpec((1, TPC, width), lambda s: (late(s), 0, 0)),
            pl.BlockSpec((1,) + qkv.shape[1:], lambda s: (pair_at(s), 0, 0, 0, 0)),
            pl.BlockSpec((1,) + proj.shape[1:], lambda s: (pair_at(s), 0, 0, 0)),
            pl.BlockSpec(
                (None, 1, PAIR, 2 * HD, MAIN),
                lambda s: (lax.div(pair_at(s), 2), clip_at(s), lax.rem(pair_at(s), 2), 0, 0),
            ),
            pl.BlockSpec((1, PAIR, 4, HD), lambda s: (pair_at(s), 0, 0, 0)),
            pl.BlockSpec(gain.shape, lambda s: (0,)),
            pl.BlockSpec((1, 1, ROWS, packed_width), per_step),
            pl.BlockSpec((1, 1, PAIR, 2, SIDE, WIDE), lambda s: per_step(s) + (0, 0)),
            pl.BlockSpec((1, 1, ROWS, PAIR * WIDE), per_step),
            pl.BlockSpec((1, ROWS, WIDE), lambda s: (clip_at(s), 0, 0)),
            pl.BlockSpec((1, ROWS, width), lambda s: (clip_at(s), 0, 0)),
            pl.BlockSpec((ROWS, width), lambda s: (clip_at(s), 0)),
            pl.BlockSpec((1, width), lambda s: (0, 0)),
            anywhere,
            anywhere,
        ],
        out_specs=[
            pl.BlockSpec((1, TPC, width), lambda s: (late(s), 0, 0)),
            pl.BlockSpec(small, lambda s: (0, 0)),
            anywhere,
            anywhere,
            anywhere,
        ],
        out_shape=[
            shaped((clips, TPC, width), BF16),
            shaped(small, F32),
            shaped(first_shape, F32),
            shaped(second_shape, F32),
            shaped((2, low_rows, width), BF16),
        ],
        scratch_shapes=[
            pltpu.VMEM((clips, ROWS, width), F32),
            pltpu.VMEM((1, width), F32),
            pltpu.VMEM((weight_rows, width), F32),
            pltpu.VMEM((4, PAIR, 4, WIDE), F32),
            pltpu.VMEM((2, low_rows, width), BF16),
            pltpu.VMEM((2, low_rows, width), BF16),
            pltpu.VMEM((2, low_rows, width), BF16),
            pltpu.VMEM((2, low_rows, THIRD), BF16),
            pltpu.VMEM((2, THIRD, THIRD), BF16),
            pltpu.VMEM((2, 3, PART, THIRD), BF16),
            pltpu.VMEM((2, low_rows, width), BF16),
        ]
        + [pltpu.VMEM(small, F32)] * 5
        + [pltpu.VMEM((4,) + small, F32)]
        + scatter_scratch(first_shape, "xyz")
        + scatter_scratch(second_shape, "yzx")
        + [
            pltpu.SemaphoreType.DMA((BACKWARD_COPIES,)),
            pltpu.SemaphoreType.DMA((BACKWARD_COPIES,)),
            pltpu.SemaphoreType.DMA((5,)),
        ],
        compiler_params=pltpu.CompilerParams(
            dimension_semantics=("arbitrary",),
            vmem_limit_bytes=VMEM_LIMIT,
            collective_id=1,
            has_side_effects=True,
        ),
        name="attention_backward_links",
    )(
        index, x, qkv, proj, mem, taps, gain, packed, keys, att, log, normed, grad, gain_two, d_first, d_second
    )


def group_gather(own, heads, fetch=None):
    blocks = [fetch(own, 0) if fetch else own]
    for shift in range(1, heads):
        sent = fetch(own, -shift) if fetch else own
        blocks.append(lax.ppermute(sent, "head", [(src, (src - shift) % heads) for src in range(heads)]))
    return blocks


def group_sum(blocks, heads):
    total = blocks[0]
    for shift in range(1, heads):
        total = total + lax.ppermute(
            blocks[shift].astype(BF16), "head", [(src, (src + shift) % heads) for src in range(heads)]
        ).astype(F32)
    return total


def local(
    heads,
    batches,
    inputs,
    qkv_weight,
    proj_weight,
    pool_weight,
    gain_one,
    gain_two,
    hidden_weight,
    output_weight,
    memory,
    clip_index,
    cotangent,
):
    width = inputs.shape[3]
    micro, own_clips = inputs.shape[:2]
    clips = micro * own_clips
    own_heads = qkv_weight.shape[1]
    all_heads = own_heads * heads
    pairs = all_heads // PAIR
    me = lax.axis_index("head")
    linked = (heads, batches, micro, own_clips) == (2, 16, 4, 1)

    def mine(array, shift):
        start = lax.rem(me + shift + heads, heads) * own_clips
        return lax.dynamic_slice_in_dim(array, start, own_clips, axis=1)

    pad = WIDE - HD
    qkv_rows = jnp.pad(
        qkv_weight.transpose(1, 2, 0).reshape(own_heads, 3, HD, width), ((0, 0), (0, 0), (0, pad), (0, 0))
    )
    proj_rows = jnp.pad(proj_weight, ((0, 0), (0, pad), (0, 0)))
    taps_own = pool_weight.astype(F32)
    memory_t = memory.transpose(0, 1, 3, 4, 2)
    tail_own = memory_t[..., MAIN:].reshape(memory_t.shape[:3] + (2, HD, REST)).swapaxes(4, 5)
    tail_own = jnp.pad(tail_own, ((0, 0),) * 5 + ((0, pad),)).reshape(memory_t.shape[:3] + (2 * REST, WIDE))

    x = inputs.reshape(clips, TPC, width)
    cot = cotangent.reshape(clips, TPC, width)
    if linked:
        (packed, keys, att, log, normed, middle, normed_two, cot_rows, first, second, qkv_all, proj_all, mem_all, taps_all) = (
            attention_forward_links(
                clip_index.T, x, cot, qkv_weight.transpose(1, 2, 0).reshape(PAIR, PAIR, 3, HD, width),
                proj_weight.reshape(PAIR, PAIR, HD, width), memory_t, tail_own,
                taps_own.reshape(-1, PAIR, 4, HD), gain_one, gain_two, hidden_weight, output_weight,
            )
        )
        first = first.reshape(width, -1)
        second = second.reshape(-1, width)
    else:
        qkv_all = jnp.concatenate(group_gather(qkv_rows, heads), axis=0)
        proj_all = jnp.concatenate(group_gather(proj_rows, heads), axis=0)
        w_all = jnp.concatenate(
            [
                qkv_all.reshape(pairs, PIECES * WIDE, width),
                proj_all.reshape(pairs, PAIR * WIDE, width),
            ],
            axis=1,
        )
        taps_all = jnp.concatenate(group_gather(taps_own, heads), axis=0).reshape(pairs, PAIR, 4, HD)
        mem_all = jnp.concatenate(group_gather(memory_t, heads, mine), axis=2)
        mem_all = mem_all.reshape(clips, all_heads, 2 * HD, TPC)
        tail = jnp.concatenate(group_gather(tail_own, heads, mine), axis=2)
        tail = tail.reshape(clips, all_heads, 2 * REST, WIDE)

        first = lax.all_gather(hidden_weight, ("batch", "head"), axis=0, tiled=True)
        second = lax.all_gather(output_weight, ("batch", "head"), axis=0, tiled=True)
        index = mine(clip_index, 0).reshape(clips, 1, 1)
        side_mask, main_mask = mask_rows(index)
        side_mask, main_mask = side_mask.reshape(clips, 1, SIDE), main_mask.reshape(clips, 1, MAIN)
        packed, keys, att, log, normed, middle, normed_two, cot_rows = attention_forward(
            x, cot, w_all, mem_all, tail, side_mask, main_mask, taps_all, gain_one, gain_two
        )
    outputs, grad, d_first, d_second, d_gain_two = mlp(
        normed_two.reshape(clips * ROWS, width),
        cot_rows.reshape(clips * ROWS, width),
        first,
        second,
        middle.reshape(clips * ROWS, width),
        gain_two,
    )
    if linked:
        d_x, small, d_first, d_second, d_w = attention_backward_links(
            clip_index.T, x, qkv_all, proj_all, mem_all, taps_all, gain_one,
            packed, keys, att, log, normed, grad, d_gain_two,
            d_first.reshape(4, 2, 2, 2, -1, d_first.shape[1]), d_second.reshape(4, 2, 2, 2, -1, width),
        )
        qkv_rows = PAIR * 3 * HD
        d_qkv = d_w[:, :qkv_rows].astype(F32).reshape(own_heads, 3 * HD, width)
        d_proj = d_w[:, qkv_rows:].astype(F32).reshape(own_heads, HD, width)
        d_taps = small[8:, : 2 * WIDE].reshape(PAIR, 4, 2, WIDE).transpose(2, 0, 1, 3)[..., :HD]
        share = width // (batches * heads)
        start = (lax.axis_index("batch") * heads + me) * share
        d_gains = lax.dynamic_slice_in_dim(small[:2], start, share, axis=1)
        return (
            outputs.reshape(inputs.shape),
            d_x.reshape(inputs.shape),
            d_qkv.transpose(2, 0, 1),
            d_proj,
            d_taps.reshape(own_heads, 4, HD),
            d_gains[0],
            d_gains[1],
            d_first,
            d_second,
        )
    d_x, d_w, d_taps, d_gain_one = attention_backward(
        x, w_all, mem_all, side_mask, main_mask, taps_all, gain_one,
        packed, keys, att, log, normed, grad,
    )
    d_proj = d_w[:, PIECES * WIDE :].reshape(heads, own_heads, WIDE, width)[:, :, :HD]
    d_w = d_w[:, : PIECES * WIDE].reshape(heads, own_heads, 3, WIDE, width)[:, :, :, :HD]
    d_w = d_w.reshape(heads, own_heads, 3 * HD, width)
    d_taps = d_taps.reshape(heads, own_heads, 4, WIDE)[..., :HD]
    d_w, d_proj, d_taps = (
        lax.psum(group_sum(list(grads), heads).astype(BF16), "batch").astype(F32)
        for grads in (d_w, d_proj, d_taps)
    )
    both = ("batch", "head")
    d_first = lax.psum_scatter(d_first, both, scatter_dimension=0, tiled=True).astype(F32)
    d_second = lax.psum_scatter(d_second, both, scatter_dimension=0, tiled=True).astype(F32)
    d_gains = lax.psum_scatter(
        jnp.concatenate([d_gain_one, d_gain_two], axis=0), both, scatter_dimension=1, tiled=True
    )
    return (
        outputs.reshape(inputs.shape),
        d_x.reshape(inputs.shape),
        d_w.transpose(2, 0, 1),
        d_proj,
        d_taps,
        d_gains[0],
        d_gains[1],
        d_first,
        d_second,
    )


def solution(mesh):
    return jax.shard_map(
        functools.partial(local, mesh.shape["head"], mesh.shape["batch"]),
        mesh=mesh,
        in_specs=(
            P(None, ("batch", "head"), None, None),
            P(None, "head", None),
            P("head", None, None),
            P("head", None, None),
            P(),
            P(),
            P(("batch", "head"), None),
            P(("batch", "head"), None),
            P(None, "batch", None, "head", None),
            P(None, "batch"),
            P(None, ("batch", "head"), None, None),
        ),
        out_specs=(
            P(None, ("batch", "head"), None, None),
            P(None, ("batch", "head"), None, None),
            P(None, "head", None),
            P("head", None, None),
            P("head", None, None),
            P(("batch", "head")),
            P(("batch", "head")),
            P(("batch", "head"), None),
            P(("batch", "head"), None),
        ),
        check_vma=False,
    )
```

```python
import functools
import math

import jax
import jax.numpy as jnp
from jax import lax
from jax.experimental import pallas as pl
from jax.experimental.pallas import tpu as pltpu
from jax.sharding import PartitionSpec as P

HD = 96
WIDE = 128
FRAMES = 8
TPC = 392
PTOK = 196
SPOT = TPC // FRAMES
HALF = 200
ROWS = 2 * HALF
MAIN = 384
REST = TPC - MAIN
SIDE = 256
PAIR = 2
PIECES = 3 * PAIR

NORM_EPS = 1e-06
NEG = -1e30
LOG2E = 1.4426950408889634
SCORE = HD ** (-0.5)

F32 = jnp.float32
BF16 = jnp.bfloat16


def dot(a, b):
    return lax.dot_general(a, b, (((1,), (0,)), ((), ())), preferred_element_type=F32)


def dot_nt(a, b):
    return lax.dot_general(a, b, (((1,), (1,)), ((), ())), preferred_element_type=F32)


def dot_tn(a, b):
    return lax.dot_general(a, b, (((0,), (0,)), ((), ())), preferred_element_type=F32)


def reorder(shape, row_dim):
    rows = lax.broadcasted_iota(jnp.int32, shape, row_dim)
    tokens = lax.broadcasted_iota(jnp.int32, shape, 1 - row_dim)
    odd = (rows >= HALF).astype(jnp.int32)
    spot = rows - HALF * odd
    frame = sum((spot >= SPOT * step).astype(jnp.int32) for step in range(1, FRAMES // 2))
    return ((tokens == spot + SPOT * (frame + odd)) & (spot < PTOK)).astype(BF16)


def norm_parts(values):
    average = jnp.mean(values, axis=-1, keepdims=True)
    centered = values - average
    spread = lax.rsqrt(jnp.mean(centered * centered, axis=-1, keepdims=True) + NORM_EPS)
    return centered * spread, spread


def norm_pull(values, gain, grad):
    unit, spread = norm_parts(values)
    scaled = grad * gain
    inner = jnp.mean(scaled * unit, axis=-1, keepdims=True)
    pulled = spread * (scaled - jnp.mean(scaled, axis=-1, keepdims=True) - unit * inner)
    return pulled, jnp.sum(grad * unit, axis=0, keepdims=True)


def as_row(ref):
    return ref[...].reshape(1, -1)


def widen(taps):
    return jnp.concatenate([taps, jnp.zeros((taps.shape[0], WIDE - taps.shape[1]), F32)], axis=1)


def mask_rows(index):
    slot = lax.broadcasted_iota(jnp.int32, (1, MAIN), 1) // PTOK
    main = jnp.where(index > slot, 0.0, NEG)
    spot = lax.broadcasted_iota(jnp.int32, (1, SIDE), 1)
    tail_open = (spot >= HALF) & (spot < HALF + REST) & (index > (TPC - 1) // PTOK)
    return jnp.where((spot < PTOK) | tail_open, 0.0, NEG), main


def value_columns(memory_t):
    return jnp.concatenate([memory_t[HD:], jnp.zeros((WIDE - HD, memory_t.shape[1]), BF16)], axis=0)


def forward_kernel(
    x_ref, cot_ref, w_ref, mem_ref, tail_ref, side_ref, main_ref, taps_ref, gain_one_ref, gain_two_ref,
    packed_ref, keys_ref, att_ref, log_ref, normed_ref, middle_ref, normed_two_ref, cot_out,
    x_rows, normed_rows, branch, logs,
):
    forward_step(
        pl.program_id(0), pl.program_id(1), pl.num_programs(0), (side_ref[0], main_ref[0]),
        w_ref.at[0, : PIECES * WIDE], w_ref.at[0, PIECES * WIDE :], mem_ref.at[0], tail_ref.at[0], taps_ref.at[0],
        x_ref, cot_ref, gain_one_ref, gain_two_ref,
        packed_ref, keys_ref, att_ref, log_ref, normed_ref, middle_ref, normed_two_ref, cot_out,
        x_rows, normed_rows, branch, logs,
    )


def forward_step(
    pair, clip, pairs, masks,
    qkv_ref, proj_ref, mem_ref, tail_ref, taps_ref,
    x_ref, cot_ref, gain_one_ref, gain_two_ref,
    packed_ref, keys_ref, att_ref, log_ref, normed_ref, middle_ref, normed_two_ref, cot_out,
    x_rows, normed_rows, branch, log_rows,
):
    here = pl.ds(clip, 1)

    @pl.when(pair == 0)
    def _():
        rows = dot(reorder((ROWS, TPC), 0), x_ref[0])
        x_rows[here] = rows.astype(BF16)[None]
        unit, _ = norm_parts(rows)
        low = (unit * as_row(gain_one_ref)).astype(BF16)
        normed_rows[here] = low[None]
        normed_ref[0] = low
        log_rows[here] = jnp.zeros((1, ROWS, WIDE), F32)

    normed = normed_rows[here][0]
    packed = dot_nt(normed, qkv_ref[...].reshape(-1, normed.shape[1]))
    packed_ref[0, 0] = packed.astype(BF16)
    logs = []
    outs = []
    for head in range(PAIR):
        base = 3 * WIDE * head
        query = packed[:, base : base + WIDE]
        key = packed[:, base + WIDE : base + 2 * WIDE]
        value = packed[:, base + 2 * WIDE : base + 3 * WIDE]
        query_low = query.astype(BF16)
        taps = widen(taps_ref[head])
        zeros = jnp.zeros((SIDE - HALF - REST, WIDE), F32)
        pooled_key = taps[0:1] * key[:HALF] + taps[1:2] * key[HALF:]
        pooled_value = taps[2:3] * value[:HALF] + taps[3:4] * value[HALF:]
        tail = tail_ref[head].astype(F32)
        side_key = jnp.concatenate([pooled_key, tail[:REST], zeros], axis=0).astype(BF16)
        side_value = jnp.concatenate([pooled_value, tail[REST:], zeros], axis=0).astype(BF16)
        keys_ref[0, 0, head, 0] = side_key
        keys_ref[0, 0, head, 1] = side_value
        memory_t = mem_ref[head]
        score_side = dot_nt(query_low, side_key) * (SCORE * LOG2E) + masks[0]
        score_main = dot(query_low, memory_t[:WIDE]) * (SCORE * LOG2E) + masks[1]
        top = jnp.maximum(
            jnp.max(score_side, axis=-1, keepdims=True), jnp.max(score_main, axis=-1, keepdims=True)
        )
        weight_side = jnp.exp2(score_side - top)
        weight_main = jnp.exp2(score_main - top)
        total = jnp.sum(weight_side, axis=-1, keepdims=True) + jnp.sum(weight_main, axis=-1, keepdims=True)
        mixed = dot(weight_side.astype(BF16), side_value) + dot_nt(
            weight_main.astype(BF16), value_columns(memory_t)
        )
        outs.append(mixed / total + query)
        logs.append(top + jnp.log2(total))
    attended = jnp.concatenate(outs, axis=1).astype(BF16)
    att_ref[0, 0] = attended
    lane = lax.broadcasted_iota(jnp.int32, (ROWS, WIDE), 1) - PAIR * pair
    log_rows[here] = jnp.where(lane == 0, logs[0], jnp.where(lane == 1, logs[1], log_rows[here][0]))[None]
    part = dot(attended, proj_ref[...].reshape(-1, normed.shape[1]))[None]

    @pl.when(pair == 0)
    def _():
        branch[here] = part

    @pl.when(pair > 0)
    def _():
        branch[here] += part

    @pl.when(pair == pairs - 1)
    def _():
        middle = x_rows[here][0].astype(F32) + branch[here][0]
        middle_ref[0] = middle
        unit, _ = norm_parts(middle)
        normed_two_ref[0] = (unit * as_row(gain_two_ref)).astype(BF16)
        log_ref[0] = log_rows[here][0]
        cot_out[0] = dot(reorder((ROWS, TPC), 0), cot_ref[0]).astype(BF16)


def feed(step, chunk, normed_ref, cot_ref, first, second, total, grad_normed, active, grad_hidden):
    here = pl.ds(chunk * CHUNK, CHUNK)
    hidden = dot(normed_ref[here, :], first)
    grad_active = dot_nt(cot_ref[here, :], second)
    bell = jnp.exp2(hidden * hidden * (-0.5 * LOG2E))
    near = 1.0 / (1.0 + (0.3275911 * math.sqrt(0.5)) * jnp.abs(hidden))
    tail = near * (0.5 * 1.061405429) + (0.5 * -1.453152027)
    tail = near * tail + (0.5 * 1.421413741)
    tail = near * tail + (0.5 * -0.284496736)
    tail = near * tail + (0.5 * 0.254829592)
    tail = near * tail * bell
    cumulative = jnp.where(hidden < 0.0, tail, 1.0 - tail)
    slope = cumulative + hidden * bell * 0.3989422804014327
    active_low = (hidden * cumulative).astype(BF16)
    hidden_low = (slope * grad_active).astype(BF16)
    active[here, :] = active_low
    grad_hidden[here, :] = hidden_low
    fed = dot(active_low, second)
    back = dot_nt(hidden_low, first)

    @pl.when(step == 0)
    def _():
        total[here, :] = fed
        grad_normed[here, :] = back

    @pl.when(step > 0)
    def _():
        total[here, :] += fed
        grad_normed[here, :] += back


def mlp_kernel(*refs):
    mlp_step(None, *refs)


def mlp_links_kernel(
    normed_ref, cot_ref, first_ref, second_ref, middle_ref, gain_ref,
    out_ref, grad_ref, d_gain_ref, first_out, second_out, first_left, second_left,
    middle, total, grad_normed, active, grad_hidden, near, *rest,
):
    step = pl.program_id(0)
    here = place()
    z, y, core, x, at = here
    first_refs, second_refs = rest[:5], rest[5:10]
    first_keep, second_keep, first_result, second_result, send, recv, store = rest[10:]
    links = Links(send, recv)
    partners = Partners(here)
    sums, outs = [], []
    for tile in range(EARLY):
        sums.append(
            (
                Sum(f"f{tile}", "xy", None, [ref.at[tile] for ref in first_refs], links, partners),
                Sum(f"s{tile}", "yx", tile, [ref.at[tile] for ref in second_refs], links, partners),
            )
        )
        outs.append(
            (
                pltpu.make_async_copy(
                    first_result.at[tile], first_out.at[:, pl.ds(tile * TILE, TILE)], store.at[2 * tile]
                ),
                pltpu.make_async_copy(second_result, second_out, store.at[2 * tile + 1]),
            )
        )
    kept = [
        [
            pltpu.make_async_copy(left.at[tile], out.at[tile], store.at[2 * (EARLY + tile) + i])
            for i, (left, out) in enumerate(((first_keep, first_left), (second_keep, second_left)))
        ]
        for tile in range(TILES - EARLY)
    ]

    def store_grads(d_first, d_second):
        for tile in range(TILES):

            @pl.when(step == tile)
            def _(tile=tile):
                early = tile < EARLY
                for early_ref, keep_ref, grad in (
                    (first_refs[0], first_keep, d_first),
                    (second_refs[0], second_keep, d_second),
                ):
                    into = early_ref if early else keep_ref
                    into[tile if early else tile - EARLY] = grad.reshape(into.shape[1:]).astype(BF16)
                if not early:
                    for copy in kept[tile - EARLY]:
                        copy.start()

    def finish(tile):
        one, two = sums[tile]
        one.finish(first_result.at[tile])
        outs[tile][0].start()

        @pl.when(z == tile)
        def _():
            two.finish(second_result)
            outs[tile][1].start()

    def act(moment):
        for tile, (one, two) in enumerate(sums):
            plan = {
                (tile + 1, 0): [one.begin, two.begin],
                (tile + 1, 1): [one.core, two.core],
                (tile + 2, 0): [one.first, two.first],
                (tile + 2, 1): [one.second, two.second],
                (tile + 3, 0): [lambda: finish(tile)],
            }
            for (when, which), acts in plan.items():
                if which != moment:
                    continue

                @pl.when(step == when)
                def _(acts=acts):
                    for one_act in acts:
                        one_act()

    @pl.when(step == 0)
    def _():
        greet(partners.all())

    mlp_step(
        act, normed_ref, cot_ref, first_ref, second_ref, middle_ref, gain_ref,
        out_ref, grad_ref, store_grads, None, d_gain_ref,
        middle, total, grad_normed, active, grad_hidden, near,
    )

    @pl.when(step == pl.num_programs(0) - 1)
    def _():
        links.sent()
        for copies in kept:
            for copy in copies:
                copy.wait()
        for tile, (one, two) in enumerate(outs):
            one.wait()
            pl.when(z == tile)(lambda two=two: two.wait())


class Partners:
    def __init__(self, here):
        self.place = here
        z, y, core, x, at = here
        self.x, self.y, self.core = at(z, y, core, 1 - x), at(z, 1 - y, core, x), at(z, y, 1 - core, x)
        self.along = [at(turn(z, shift), y, core, x) for shift in (1, 2, 3)]

    def all(self):
        return [self.x, self.y, self.core] + self.along


class Sum:
    def __init__(self, name, order, owner, refs, links, partners):
        self.name, self.order, self.owner, self.links = name, order, owner, links
        self.data, self.from_core, self.from_one, self.from_two, self.from_z = refs
        self.place = z, y, core, x, at = partners.place
        data = self.data
        self.planes = data.shape[0]
        self.names = [name + "c", name + "a", name + "b"] + [f"{name}z{shift}" for shift in (1, 2, 3)]
        links.add(name + "c", data.at[:, :, 1 - core], self.from_core, partners.core)
        if order == "xy":
            links.add(name + "a", data.at[:, :, core, 1 - x], self.from_one, partners.x)
            links.add(name + "b", data.at[:, 1 - y, core, x], self.from_two, partners.y)
        else:
            links.add(name + "a", data.at[:, 1 - y, core], self.from_one, partners.y)
            links.add(name + "b", data.at[:, y, core, 1 - x], self.from_two, partners.x)
        for shift in (1, 2, 3):
            into = self.from_z.at[shift - 1]
            if owner is None:
                source = data.at[turn(z, shift), y, core, x]
                links.add(f"{name}z{shift}", source, into, partners.along[shift - 1])
            else:
                links.add(
                    f"{name}z{shift}", data.at[0, y, core, x], into, at(owner, y, core, x),
                    z == (owner + shift) % 4, z == owner,
                )

    def begin(self):
        self.links.start(self.name + "c")

    def core(self):
        z, y, core, x, at = self.place
        self.links.arrived(self.name + "c")

        @pl.loop(0, self.planes)
        def _(plane):
            for column in (0, 1):
                for head in (0, 1):
                    self.data[plane, column, core, head] = add_low(
                        self.data[plane, column, core, head], self.from_core[plane, column, head]
                    )

        self.links.start(self.name + "a")

    def first(self):
        z, y, core, x, at = self.place
        self.links.arrived(self.name + "a")

        @pl.loop(0, self.planes)
        def _(plane):
            for other in (0, 1):
                spot = (plane, other, core, x) if self.order == "xy" else (plane, y, core, other)
                self.data[spot] = add_low(self.data[spot], self.from_one[plane, other])

        self.links.start(self.name + "b")

    def second(self):
        z, y, core, x, at = self.place
        self.links.arrived(self.name + "b")

        @pl.loop(0, self.planes)
        def _(plane):
            self.data[plane, y, core, x] = add_low(self.data[plane, y, core, x], self.from_two[plane])

        self.links.start(*self.names[3:])

    def finish(self, result):
        z, y, core, x, at = self.place
        for name in self.names[3:]:
            self.links.get(name).wait_recv()
        part = self.data[z if self.owner is None else 0, y, core, x].astype(F32)
        for shift in range(3):
            part = part + self.from_z[shift].astype(F32)
        result[...] = part


def mlp_step(
    act, normed_ref, cot_ref, first_ref, second_ref, middle_ref, gain_ref,
    out_ref, grad_ref, d_first_ref, d_second_ref, d_gain_ref,
    middle, total, grad_normed, active, grad_hidden, near,
):
    step = pl.program_id(0)
    clips = middle.shape[0] // ROWS
    tiles = pl.num_programs(0) - clips
    chunks = middle.shape[0] // CHUNK
    fetch = pltpu.make_async_copy(middle_ref, middle, near.at[0])

    @pl.when(step == 0)
    def _():
        fetch.start()
        d_gain_ref[...] = jnp.zeros_like(d_gain_ref)

    if act is not None:
        act(0)

    @pl.when(step < tiles)
    def _():
        first = first_ref[...]
        second = second_ref[...]
        for chunk in range(chunks):
            if act is not None and chunk == 1:
                act(1)
            feed(step, chunk, normed_ref, cot_ref, first, second, total, grad_normed, active, grad_hidden)
        if act is not None:
            act(2)
        d_first = dot_tn(normed_ref[...], grad_hidden[...])
        d_second = dot_tn(active[...], cot_ref[...])
        if act is not None:
            d_first_ref(d_first, d_second)
        else:
            d_first_ref[...] = d_first.astype(BF16)
            d_second_ref[...] = d_second.astype(BF16)

    @pl.when(step == tiles)
    def _():
        fetch.wait()

    @pl.when(step >= tiles)
    def _():
        here = pl.ds(pl.multiple_of((step - tiles) * ROWS, ROWS), ROWS)
        values = middle[here, :]
        out = (values + total[here, :]).astype(BF16)
        out_ref[0] = dot(reorder((TPC, ROWS), 1), out).astype(BF16)
        pulled, d_gain = norm_pull(values, as_row(gain_ref), grad_normed[here, :])
        grad_ref[...] = (cot_ref[here, :].astype(F32) + pulled).astype(BF16)
        d_gain_ref[...] += d_gain


def backward_kernel(
    x_ref, w_ref, mem_ref, side_ref, main_ref, taps_ref, gain_ref,
    packed_ref, keys_ref, att_ref, log_ref, normed_ref, grad_ref,
    d_x_ref, d_w_ref, d_taps_ref, d_gain_ref,
    grad_normed,
):
    pair, clip = pl.program_id(0), pl.program_id(1)
    here = pl.ds(clip, 1)

    @pl.when(clip == 0)
    def _():
        d_w_ref[...] = jnp.zeros_like(d_w_ref)
        d_taps_ref[...] = jnp.zeros_like(d_taps_ref)

    grad_packed = backward_attention(
        pair, (side_ref[0], main_ref[0]), w_ref.at[0, PIECES * WIDE :], d_taps_ref.at[0],
        mem_ref.at[0], taps_ref.at[0], packed_ref.at[0, 0], keys_ref.at[0, 0], att_ref.at[0, 0], log_ref, grad_ref,
    )
    d_w_ref[0, PIECES * WIDE :] += dot_tn(att_ref[0, 0], grad_ref[...])
    d_w_ref[0, : PIECES * WIDE] += dot_tn(grad_packed, normed_ref[0])
    part = dot(grad_packed, w_ref[0, : PIECES * WIDE])[None]

    @pl.when(pair == 0)
    def _():
        grad_normed[here] = part

    @pl.when(pair > 0)
    def _():
        grad_normed[here] += part

    @pl.when(pair == pl.num_programs(0) - 1)
    def _():
        d_x_ref[0], d_gain = input_grad(x_ref[0], grad_normed[here][0], gain_ref, grad_ref[...])

        @pl.when(clip == 0)
        def _():
            d_gain_ref[...] = d_gain

        @pl.when(clip > 0)
        def _():
            d_gain_ref[...] += d_gain


def input_grad(x, grad_normed, gain_ref, grad_branch):
    rows = dot(reorder((ROWS, TPC), 0), x)
    pulled, d_gain = norm_pull(rows, as_row(gain_ref), grad_normed)
    d_x = (grad_branch.astype(F32) + pulled).astype(BF16)
    return dot(reorder((TPC, ROWS), 1), d_x).astype(BF16), d_gain


def backward_attention(
    pair, masks, proj_ref, d_taps_ref, mem_ref, taps_ref, packed_ref, keys_ref, att_ref, log_ref, grad_ref
):
    lane = lax.broadcasted_iota(jnp.int32, (ROWS, WIDE), 1) - PAIR * pair
    grad_out = dot_nt(grad_ref[...], proj_ref[...].reshape(PAIR * WIDE, -1))
    pieces = []
    for head in range(PAIR):
        base = 3 * WIDE * head
        query = packed_ref[:, base : base + WIDE]
        key = packed_ref[:, base + WIDE : base + 2 * WIDE].astype(F32)
        value = packed_ref[:, base + 2 * WIDE : base + 3 * WIDE].astype(F32)
        out_grad = grad_out[:, WIDE * head : WIDE * (head + 1)].astype(BF16)
        taps = widen(taps_ref[head])
        side_key = keys_ref[head, 0]
        side_value = keys_ref[head, 1]
        memory_t = mem_ref[head]
        log = jnp.sum(jnp.where(lane == head, log_ref[0], 0.0), axis=-1, keepdims=True)
        score_side = dot_nt(query, side_key) * (SCORE * LOG2E) + masks[0]
        score_main = dot(query, memory_t[:WIDE]) * (SCORE * LOG2E) + masks[1]
        weight_side = jnp.exp2(score_side - log)
        weight_main = jnp.exp2(score_main - log)
        grad_side = dot_nt(out_grad, side_value)
        grad_main = dot(out_grad, value_columns(memory_t))
        mixed = att_ref[:, WIDE * head : WIDE * (head + 1)].astype(F32) - query.astype(F32)
        inner = jnp.sum(out_grad.astype(F32) * mixed, axis=-1, keepdims=True)
        score_grad_side = (weight_side * (grad_side - inner)).astype(BF16)
        score_grad_main = (weight_main * (grad_main - inner)).astype(BF16)
        grad_query = (
            dot(score_grad_side, side_key) + dot_nt(score_grad_main, memory_t[:WIDE])
        ) * SCORE + out_grad.astype(F32)
        grad_key = dot_tn(score_grad_side, query)[:HALF] * SCORE
        grad_value = dot_tn(weight_side.astype(BF16), out_grad)[:HALF]
        pieces += [
            grad_query,
            jnp.concatenate([taps[0:1] * grad_key, taps[1:2] * grad_key], axis=0),
            jnp.concatenate([taps[2:3] * grad_value, taps[3:4] * grad_value], axis=0),
        ]
        d_taps_ref[head] += jnp.concatenate(
            [
                jnp.sum(part * grad, axis=0, keepdims=True)
                for part, grad in (
                    (key[:HALF], grad_key),
                    (key[HALF:], grad_key),
                    (value[:HALF], grad_value),
                    (value[HALF:], grad_value),
                )
            ],
            axis=0,
        )
    return jnp.concatenate(pieces, axis=1).astype(BF16)


def add_low(one, other):
    return (one.astype(F32) + other.astype(F32)).astype(BF16)


def unpad(ref, into, more=None):
    for piece in range(ref.shape[0] // WIDE):
        rows = ref[WIDE * piece : WIDE * piece + HD]
        narrow = slice(HD * piece, HD * (piece + 1))
        if more is not None:
            rows = rows + more[narrow].astype(F32)
        into[narrow] = rows.astype(BF16)


BACKWARD_COPIES = 96
CORE_LANES = 384
UNITS = (("p", 384, 384), ("0", 576, 640), ("1", 576, 640))


class AllReduce:
    def __init__(self, name, refs, links, partners):
        self.name, self.links = name, links
        self.own, self.core, self.y, self.z, self.whole = refs
        self.place = z, y, core, x, at = partners.place
        self.count = self.own.shape[0]
        links.add("rc" + name, self.own.at[:, half_lanes(1 - core)], self.core, partners.core)
        links.add("ry" + name, self.own.at[self.half(1 - y), half_lanes(core)], self.y, partners.y)
        for shift in (1, 2, 3):
            source = self.own.at[self.part(y, turn(z, shift)), half_lanes(core)]
            links.add(f"rz{shift}{name}", source, self.z.at[shift - 1], partners.along[shift - 1])
            piece = self.whole.at[self.part(y, z), half_lanes(core)]
            links.add(f"gz{shift}{name}", piece, piece, partners.along[shift - 1])
        piece = self.whole.at[self.half(y), half_lanes(core)]
        links.add("gy" + name, piece, piece, partners.y)
        piece = self.whole.at[:, half_lanes(core)]
        links.add("gc" + name, piece, piece, partners.core)

    def half(self, y):
        return pl.ds(pl.multiple_of(y * (self.count // 2), self.count // 2), self.count // 2)

    def part(self, y, z):
        size = self.count // 8
        return pl.ds(pl.multiple_of((4 * y + z) * size, size), size)

    def over_z(self, stage):
        return [f"{stage}{shift}{self.name}" for shift in (1, 2, 3)]

    def begin(self):
        self.links.start("rc" + self.name)

    def sum_core(self, far):
        lanes = half_lanes(self.place[2])
        self.links.arrived("rc" + self.name, "hx" + self.name)
        rows = far.got.shape[0]
        total = self.own[:rows, lanes].astype(F32) + self.core[:rows].astype(F32) + far.got[...].astype(F32)
        self.own[:rows, lanes] = total.astype(BF16)
        self.links.start("ry" + self.name)

    def sum_y(self):
        z, y, core, x, at = self.place
        self.links.arrived("ry" + self.name)
        spot = (self.half(y), half_lanes(core))
        self.own[spot] = add_low(self.own[spot], self.y[...])
        self.links.start(*self.over_z("rz"))

    def sum_z(self):
        z, y, core, x, at = self.place
        self.links.arrived(*self.over_z("rz"))
        spot = (self.part(y, z), half_lanes(core))
        part = self.own[spot].astype(F32)
        for shift in range(3):
            part = part + self.z[shift].astype(F32)
        self.whole[spot] = part.astype(BF16)
        self.links.start(*self.over_z("gz"))

    def spread_y(self):
        self.links.arrived(*self.over_z("gz"))
        self.links.start("gy" + self.name)

    def spread_core(self):
        self.links.arrived("gy" + self.name)
        self.links.start("gc" + self.name)

    def done(self):
        self.links.arrived("gc" + self.name)


class Far:
    def __init__(self, name, refs, links, partners):
        self.name, self.links = name, links
        self.sent, self.core, self.got = refs
        self.place = z, y, core, x, at = partners.place
        links.add("hc" + name, self.sent.at[:, half_lanes(1 - core)], self.core, partners.core)
        links.add("hx" + name, self.sent.at[:, half_lanes(core)], self.got, partners.x)

    def begin(self):
        self.links.start("hc" + self.name)

    def pass_on(self):
        lanes = half_lanes(self.place[2])
        self.links.arrived("hc" + self.name)
        self.sent[:, lanes] = add_low(self.sent[:, lanes], self.core[...])
        self.links.start("hx" + self.name)


def half_lanes(core):
    return pl.ds(pl.multiple_of(core * CORE_LANES, CORE_LANES), CORE_LANES)


def narrow(value, into, first):
    for piece in range(value.shape[0] // WIDE):
        rows = value[WIDE * piece : WIDE * piece + HD]
        spot = slice(first + HD * piece, first + HD * (piece + 1))
        into[spot] = rows.astype(BF16)


def backward_links_kernel(
    index_ref, x_ref, qkv_ref, proj_ref, mem_ref, taps_ref, gain_ref,
    packed_ref, keys_ref, att_ref, log_ref, normed_ref, grad_ref, gain_two_ref,
    d_first, d_second,
    d_x_ref, small_out, first_out, second_out, proj_out, qkv_out,
    grad_packed, d_gain, d_taps,
    small_mine, small_far, small_x, small_core, small_y, small_z,
    first_result, second_result, send, recv, near, *rest,
):
    step = pl.program_id(0)
    last = pl.num_programs(0) - 1
    z, y, core, x, at = place()
    links = Links(send, recv)
    partners = Partners((z, y, core, x, at))
    late = TILES - EARLY
    first_refs, second_refs, rest = rest[:5], rest[5:10], rest[10:]
    loads = [
        pltpu.make_async_copy(d_first, first_refs[0], near.at[0]),
        pltpu.make_async_copy(d_second, second_refs[0], near.at[1]),
    ]
    sums = [
        (
            Sum(f"f{tile}", "xy", None, [ref.at[tile] for ref in first_refs], links, partners),
            Sum(f"s{tile}", "yx", EARLY + tile, [ref.at[tile] for ref in second_refs], links, partners),
        )
        for tile in range(late)
    ]
    first_done = [
        pltpu.make_async_copy(first_result.at[tile], first_out.at[:, pl.ds(tile * TILE, TILE)], near.at[2 + tile])
        for tile in range(late)
    ]
    second_done = pltpu.make_async_copy(second_result, second_out, near.at[2 + late])
    units, far = {}, {}
    for i, (name, rows, _) in enumerate(UNITS):
        refs = rest[8 * i : 8 * i + 8]
        units[name] = AllReduce(name, refs[:5], links, partners)
        far[name] = Far(name, refs[5:], links, partners)
    save = [
        pltpu.make_async_copy(units[name].whole.at[pl.ds(0, rows)], out, near.at[3 + late + i])
        for i, ((name, rows, _), out) in enumerate(zip(UNITS, (proj_out, qkv_out.at[0], qkv_out.at[1])))
    ]
    links.add("mx", small_far, small_x, partners.x)
    links.add("mc", small_mine, small_core, partners.core)
    links.add("my", small_core, small_y, partners.y)
    for shift in (1, 2, 3):
        links.add(f"mz{shift}", small_z.at[z], small_z.at[z], partners.along[shift - 1])

    def proj_grads():
        grad = grad_ref[...].reshape(-1, grad_ref.shape[2])
        return [dot_tn(att_ref[pair].reshape(-1, PAIR * WIDE), grad) for pair in (0, 1)]

    def far_proj():
        for pair, value in enumerate(proj_grads()):
            narrow(value, far["p"].sent, 192 * pair)
        far["p"].begin()

    def own_proj():
        for pair, value in enumerate(proj_grads()):
            narrow(value, units["p"].own, 192 * pair)
        units["p"].begin()

    def qkv_grad():
        width = normed_ref.shape[2]
        grad = grad_packed[lax.div(step, 4)].reshape(-1, PIECES * WIDE)
        return dot_tn(grad, normed_ref[...].reshape(-1, width))

    def far_qkv(name):
        narrow(qkv_grad(), far[name].sent, 0)
        far[name].begin()

    def own_qkv(name):
        narrow(qkv_grad(), units[name].own, 0)
        units[name].begin()

    def begin():
        greet(partners.all())
        for copy in loads:
            copy.start()
        d_gain[...] = jnp.zeros_like(d_gain)
        d_taps[...] = jnp.zeros_like(d_taps)
        for name in ("0", "1"):
            padding = units[name].own.shape[0] - 576
            units[name].own[576:] = jnp.zeros((padding, units[name].own.shape[1]), BF16)

    def begin_sums():
        for copy in loads:
            copy.wait()
        for pair in sums:
            for one in pair:
                one.begin()

    def all_sums(stage):
        for pair in sums:
            for one in pair:
                getattr(one, stage)()

    def finish():
        for tile, (one, two) in enumerate(sums):
            one.finish(first_result.at[tile])
            first_done[tile].start()

            @pl.when(z == EARLY + tile)
            def _(two=two):
                two.finish(second_result)
                second_done.start()

    def at_steps(plan):
        for when, acts in plan.items():

            @pl.when(step == when)
            def _(acts=acts):
                for act in acts:
                    act()

    at_steps({0: [begin, far_proj], 8: [own_proj]})

    @pl.when(step < 16)
    def _():
        pair = lax.rem(lax.div(step, 4) + 2, 4)
        clip = lax.rem(step, 4)
        here = pl.ds(clip, 1)
        grad_packed[lax.div(step, 4), here] = backward_attention(
            pair, mask_rows(index_ref[x, clip]), proj_ref.at[0], d_taps.at[lax.div(step, 4)],
            mem_ref.at[0], taps_ref.at[0], packed_ref.at[0, 0], keys_ref.at[0, 0], att_ref.at[lax.rem(pair, 2), clip], log_ref,
            grad_ref.at[clip],
        )[None]

    @pl.when(step >= 16)
    def _():
        clip = step - 16
        grad = [
            dot(grad_packed[slot, clip], qkv_ref[(slot + 2) % 4].reshape(PIECES * WIDE, -1)) for slot in range(4)
        ]
        grad = (grad[0] + grad[1]) + (grad[2] + grad[3])
        d_x_ref[0], gain = input_grad(x_ref[0], grad, gain_ref, grad_ref[clip])
        d_gain[...] += gain

    p, zero, one = (units[name] for name, _, _ in UNITS)
    at_steps(
        {
            0: [begin_sums],
            1: [far["p"].pass_on],
            2: [lambda: all_sums("core")],
            3: [lambda: far_qkv("0")],
            4: [far["0"].pass_on],
            5: [lambda: all_sums("first")],
            7: [lambda: far_qkv("1"), lambda: all_sums("second")],
            8: [far["1"].pass_on],
            9: [lambda: p.sum_core(far["p"])],
            10: [finish],
            11: [lambda: own_qkv("0"), p.sum_y],
            12: [lambda: zero.sum_core(far["0"])],
            13: [p.sum_z],
            14: [zero.sum_y, p.spread_y],
            15: [lambda: own_qkv("1"), zero.sum_z, p.spread_core],
            16: [lambda: one.sum_core(far["1"])],
            17: [zero.spread_y, p.done, save[0].start],
        }
    )

    @pl.when(step == last)
    def _():
        for i, target in ((2, small_mine), (0, small_far)):
            target[...] = jnp.zeros_like(target)
            target[0:1] = d_gain[...]
            target[1:2] = gain_two_ref[...]
            for j in (0, 1):
                target[8:16, WIDE * j : WIDE * (j + 1)] = d_taps[i + j].reshape(8, WIDE)
        links.start("mx")
        one.sum_y()
        links.arrived("mx")
        small_mine[...] += small_x[...]
        links.start("mc")
        zero.spread_core()
        links.arrived("mc")
        small_core[...] += small_mine[...]
        links.start("my")
        one.sum_z()
        links.arrived("my")
        small_z[pl.ds(z, 1)] = (small_y[...] + small_core[...])[None]
        links.start("mz1", "mz2", "mz3")
        zero.done()
        save[1].start()
        one.spread_y()
        links.arrived("mz1", "mz2", "mz3")
        small_out[...] = (small_z[0] + small_z[1]) + (small_z[2] + small_z[3])
        one.spread_core()
        one.done()
        save[2].start()
        for copy in save + first_done:
            copy.wait()
        for tile in range(late):
            pl.when(z == EARLY + tile)(lambda: second_done.wait())
        links.sent()


VMEM_LIMIT = 60 << 20
CHUNK = 800
TILE = 768
TILES = 4
EARLY = 2


def compiler_params(dims):
    return pltpu.CompilerParams(
        dimension_semantics=("arbitrary",) * dims, vmem_limit_bytes=VMEM_LIMIT
    )


def shaped(shape, dtype):
    return jax.ShapeDtypeStruct(shape, dtype)


class Links:
    def __init__(self, send, recv):
        self.send, self.recv, self.made = send, recv, {}

    def add(self, name, src, dst, device, send_if=None, recv_if=None):
        at = len(self.made)
        self.made[name] = (src, dst, device, at, send_if, recv_if)

    def get(self, name):
        src, dst, device, at = self.made[name][:4]
        return pltpu.make_async_remote_copy(
            src_ref=src,
            dst_ref=dst,
            send_sem=self.send.at[at],
            recv_sem=self.recv.at[at],
            device_id=device,
            device_id_type=pl.DeviceIdType.MESH,
        )

    def start(self, *names):
        for name in names:
            self.only(self.made[name][4], self.get(name).start)

    def arrived(self, *names):
        for name in names:
            self.only(self.made[name][5], self.get(name).wait_recv)

    def sent(self):
        for name in self.made:
            self.only(self.made[name][4], self.get(name).wait_send)

    def only(self, condition, act):
        if condition is None:
            act()
        else:
            pl.when(condition)(lambda: act())


def place():
    batch, head = lax.axis_index("batch"), lax.axis_index("head")
    z, y, core = batch // 4, lax.rem(batch // 2, 2), lax.rem(batch, 2)

    def at(z, y, core, x):
        return {"batch": (z * 2 + y) * 2 + core, "head": x}

    return z, y, core, head, at


def greet(devices):
    barrier = pltpu.get_barrier_semaphore()
    for device in devices:
        pl.semaphore_signal(barrier, inc=1, device_id=device, device_id_type=pl.DeviceIdType.MESH)
    pl.semaphore_wait(barrier, len(devices))


def turn(z, shift):
    return lax.rem(z + shift + 4, 4)


FORWARD_COPIES = 96
SPLIT = HD // 2


def forward_links_kernel(
    index_ref, x_ref, cot_ref, gain_one_ref, gain_two_ref,
    qkv_own, proj_own, mem_own, tail_own, taps_own, hidden_own, output_own,
    packed_ref, keys_ref, att_ref, log_ref, normed_ref, middle_ref, normed_two_ref, cot_out,
    first_all, second_all, qkv_out, proj_out, mem_out, taps_out,
    x_rows, normed_rows, branch, logs, qkv_all, proj_all, mem_all, tail_all, taps_all,
    send, recv, near, save,
):
    step = pl.program_id(0)
    z, y, core, x, at = place()
    links = Links(send, recv)
    beside, above, sibling = at(z, y, core, 1 - x), at(z, 1 - y, core, x), at(z, y, 1 - core, x)
    higher, lower = at(turn(z, 1), y, core, x), at(turn(z, -1), y, core, x)
    column = pl.ds(pl.multiple_of(core * MAIN, MAIN), MAIN)
    me = ((z * 2 + y) * 2 + core) * 2 + x
    clips = mem_own.shape[0]

    def split(z, y, *between):
        rows = pl.ds(pl.multiple_of(y * SPLIT, SPLIT), SPLIT)
        return (lax.div(z, 2), lax.rem(z, 2)) + between + (rows, column)

    def block(kind, z, y):
        if kind == "q":
            return qkv_all.at[pl.ds(2, 2)].at[split(z, y, slice(None))]
        if kind == "p":
            return proj_all.at[pl.ds(2, 2)].at[split(z, y)]
        return (first_all if kind == "0" else second_all).at[pl.ds(((z * 2 + y) * 2 + core) * 2, 2)]

    links.add("xq", qkv_own.at[split(z, y, slice(None))], block("q", z, y), beside)
    links.add("xp", proj_own.at[split(z, y)], block("p", z, y), beside)
    links.add("x0", hidden_own, first_all.at[me], beside)
    links.add("x1", output_own, second_all.at[me], beside)
    for kind in "qp01":
        mine = block(kind, z, y)
        links.add("y" + kind, mine, mine, above)
        if kind in "01":
            links.add("c" + kind, mine, mine, sibling)
            mine = block(kind, z, 1 - y)
            links.add("e" + kind, mine, mine, sibling)
        for hop in (1, 2, 3):
            below, beyond = z >= hop, z + hop <= 3
            passed = block(kind, turn(z, 1 - hop), y)
            links.add(f"u{hop}{kind}", passed, passed, higher, (z <= 2) & (z >= hop - 1), below)
            passed = block(kind, turn(z, hop - 1), y)
            links.add(f"d{hop}{kind}", passed, passed, lower, (z >= 1) & (z + hop <= 4), beyond)
            for side, shift, there in (("u", -hop, below), ("d", hop, beyond)):
                came = block(kind, turn(z, shift), y)
                links.add(f"y{side}{hop}{kind}", came, came, above, there, there)
                if kind in "01":
                    links.add(f"c{side}{hop}{kind}", came, came, sibling, there, there)
                    came = block(kind, turn(z, shift), 1 - y)
                    links.add(f"e{side}{hop}{kind}", came, came, sibling, there, there)
    far = qkv_all.at[pl.ds(2, 2), :, :, pl.ds(0, HD), column]
    links.add("cq", far, far, sibling)
    far = proj_all.at[pl.ds(2, 2), :, pl.ds(0, HD), column]
    links.add("cp", far, far, sibling)
    for clip in range(clips):
        links.add(f"m{clip}", mem_own.at[clip, 1 - x, :, :, pl.ds(0, MAIN)], mem_all.at[1, clip], beside)
    links.add("tail", tail_own.at[:, 1 - x], tail_all.at[1], beside)
    links.add("taps", taps_own, taps_all.at[pl.ds(2, 2)], beside)

    local = [
        (qkv_own, qkv_all.at[pl.ds(0, 2), :, :, pl.ds(0, HD)]),
        (proj_own, proj_all.at[pl.ds(0, 2), :, pl.ds(0, HD)]),
        (tail_own.at[:, x], tail_all.at[0]),
        (taps_own, taps_all.at[pl.ds(0, 2)]),
        (mem_own.at[0, x, :, :, pl.ds(0, MAIN)], mem_all.at[0, 0]),
        (hidden_own, first_all.at[me]),
        (output_own, second_all.at[me]),
    ] + [(mem_own.at[clip, x, :, :, pl.ds(0, MAIN)], mem_all.at[0, clip]) for clip in range(1, clips)]
    local = [pltpu.make_async_copy(src, dst, near.at[i]) for i, (src, dst) in enumerate(local)]
    saved = [
        (qkv_all, qkv_out),
        (proj_all, proj_out),
        (taps_all, taps_out),
        (mem_all.at[0], mem_out.at[0]),
    ] + [(mem_all.at[1, clip], mem_out.at[1, clip]) for clip in range(clips)]
    saved = [pltpu.make_async_copy(src, dst, save.at[i]) for i, (src, dst) in enumerate(saved)]

    @pl.when(step == 0)
    def _():
        greet([beside, above, sibling, higher, lower])
        links.start("xq", "xp", "taps", "tail", "x0", "x1")
        for copy in local:
            copy.start()

        @pl.loop(0, 4)
        def _(pair):
            for head in range(PAIR):
                for piece in range(3):
                    qkv_all[pair, head, piece, HD:] = jnp.zeros((WIDE - HD, qkv_all.shape[-1]), BF16)
                proj_all[pair, head, HD:] = jnp.zeros((WIDE - HD, qkv_all.shape[-1]), BF16)

        for copy in local[:5]:
            copy.wait()

    def settle():
        for copy in local[5:]:
            copy.wait()
        saved[3].start()

    def hop(number, kinds):
        for kind in kinds:
            links.arrived(f"u{number}{kind}", f"d{number}{kind}")
            if number < 3:
                links.start(f"u{number + 1}{kind}", f"d{number + 1}{kind}")
            links.start(f"yu{number}{kind}", f"yd{number}{kind}")
            if kind in "01":
                links.start(f"cu{number}{kind}", f"cd{number}{kind}")

    def begin(kinds):
        for kind in kinds:
            links.arrived("x" + kind)
            links.start("u1" + kind, "d1" + kind, "y" + kind)
            if kind in "01":
                links.start("c" + kind)

    def across(number, kinds):
        for kind in kinds:
            for side in ("u", "d") if number else ("",):
                name = f"{side}{number}{kind}" if number else kind
                links.arrived("y" + name)
                if kind in "01":
                    links.start("e" + name)

    def weights():
        for number in range(4):
            across(number, "qp")
        links.start("cq", "cp")
        links.arrived("cq", "cp", "tail", "taps")

    def memory(clip):
        links.arrived(f"m{clip}")
        saved[4 + clip].start()

    plan = {
        1: [settle],
        2: [lambda: begin("qp"), lambda: links.start("m0")],
        3: [lambda: begin("01"), lambda: links.start("m1")],
        4: [lambda: hop(1, "qp")],
        5: [lambda: links.start("m2")],
        6: [lambda: hop(2, "qp"), lambda: links.start("m3")],
        7: [lambda: hop(3, "qp")],
        8: [lambda: hop(1, "0"), weights, lambda: memory(0)],
        9: [lambda: hop(1, "1")] + [copy.start for copy in saved[:3]],
        10: [lambda: hop(2, "0"), lambda: memory(1)],
        11: [lambda: hop(2, "1"), lambda: across(0, "01")],
        12: [lambda: across(1, "0"), lambda: memory(2)],
        13: [lambda: hop(3, "0"), lambda: across(1, "1")],
        14: [lambda: hop(3, "1"), lambda: across(2, "0"), lambda: memory(3)],
    }
    for when, acts in plan.items():

        @pl.when(step == when)
        def _(acts=acts):
            for act in acts:
                act()

    pair, clip = pair_of(step), clip_of(step)
    side = lax.div(pair, 2)
    heads = pl.ds(lax.rem(pair, 2) * PAIR, PAIR)
    forward_step(
        pair, clip, 4, mask_rows(index_ref[x, clip]),
        qkv_all.at[pair], proj_all.at[pair],
        mem_all.at[side, clip, heads], tail_all.at[side, clip, heads], taps_all.at[pair],
        x_ref, cot_ref, gain_one_ref, gain_two_ref,
        packed_ref, keys_ref, att_ref, log_ref, normed_ref, middle_ref, normed_two_ref, cot_out,
        x_rows, normed_rows, branch, logs,
    )

    @pl.when(step == pl.num_programs(0) - 1)
    def _():
        across(2, "1")
        across(3, "01")
        for copy in saved:
            copy.wait()
        for kind in "01":
            links.arrived("c" + kind, "e" + kind)
            for number in (1, 2, 3):
                for side in "ud":
                    links.arrived(f"c{side}{number}{kind}", f"e{side}{number}{kind}")
        links.sent()


def pair_of(step):
    return jnp.where(step < 8, lax.div(step, 4), 2 + lax.rem(step, 2))


def clip_of(step):
    return jnp.where(step < 8, lax.rem(step, 4), lax.div(step, 2) - 4)


def attention_forward_links(
    index, x, cot, qkv, proj, mem, tail, taps, gain_one, gain_two, hidden_weight, output_weight
):
    clips, width = x.shape[0], x.shape[2]
    packed_width = PIECES * WIDE
    devices = 32
    early = lambda s: jnp.where(s < 4, s, clips - 1)
    late = lambda s: jnp.where(s < 8, 0, clip_of(s))
    anywhere = pl.BlockSpec(memory_space=pl.ANY)
    return pl.pallas_call(
        forward_links_kernel,
        grid=(4 * clips,),
        in_specs=[
            pl.BlockSpec(memory_space=pltpu.SMEM),
            pl.BlockSpec((1, TPC, width), lambda s: (early(s), 0, 0)),
            pl.BlockSpec((1, TPC, width), lambda s: (late(s), 0, 0)),
            pl.BlockSpec(gain_one.shape, lambda s: (0,)),
            pl.BlockSpec(gain_two.shape, lambda s: (0,)),
        ] + [anywhere] * 5 + [
            pl.BlockSpec(hidden_weight.shape, lambda s: (0, 0)),
            pl.BlockSpec(output_weight.shape, lambda s: (0, 0)),
        ],
        out_specs=[
            pl.BlockSpec((1, 1, ROWS, packed_width), lambda s: (pair_of(s), clip_of(s), 0, 0)),
            pl.BlockSpec((1, 1, PAIR, 2, SIDE, WIDE), lambda s: (pair_of(s), clip_of(s), 0, 0, 0, 0)),
            pl.BlockSpec((1, 1, ROWS, PAIR * WIDE), lambda s: (pair_of(s), clip_of(s), 0, 0)),
            pl.BlockSpec((1, ROWS, WIDE), lambda s: (late(s), 0, 0)),
            pl.BlockSpec((1, ROWS, width), lambda s: (early(s), 0, 0)),
            pl.BlockSpec((1, ROWS, width), lambda s: (late(s), 0, 0)),
            pl.BlockSpec((1, ROWS, width), lambda s: (late(s), 0, 0)),
            pl.BlockSpec((1, ROWS, width), lambda s: (late(s), 0, 0)),
        ] + [anywhere] * 6,
        out_shape=[
            shaped((4, clips, ROWS, packed_width), BF16),
            shaped((4, clips, PAIR, 2, SIDE, WIDE), BF16),
            shaped((4, clips, ROWS, PAIR * WIDE), BF16),
            shaped((clips, ROWS, WIDE), F32),
            shaped((clips, ROWS, width), BF16),
            shaped((clips, ROWS, width), F32),
            shaped((clips, ROWS, width), BF16),
            shaped((clips, ROWS, width), BF16),
            shaped((devices,) + hidden_weight.shape, BF16),
            shaped((devices,) + output_weight.shape, BF16),
            shaped((4, PAIR, 3, WIDE, width), BF16),
            shaped((4, PAIR, WIDE, width), BF16),
            shaped((2, clips, 4, 2 * HD, MAIN), BF16),
            shaped((4,) + taps.shape[1:], F32),
        ],
        scratch_shapes=[
            pltpu.VMEM((clips, ROWS, width), BF16),
            pltpu.VMEM((clips, ROWS, width), BF16),
            pltpu.VMEM((clips, ROWS, width), F32),
            pltpu.VMEM((clips, ROWS, WIDE), F32),
            pltpu.VMEM((4, PAIR, 3, WIDE, width), BF16),
            pltpu.VMEM((4, PAIR, WIDE, width), BF16),
            pltpu.VMEM((2, clips, 4, 2 * HD, MAIN), BF16),
            pltpu.VMEM((2, clips, 4, 2 * REST, WIDE), BF16),
            pltpu.VMEM((4,) + taps.shape[1:], F32),
            pltpu.SemaphoreType.DMA((FORWARD_COPIES,)),
            pltpu.SemaphoreType.DMA((FORWARD_COPIES,)),
            pltpu.SemaphoreType.DMA((6 + clips,)),
            pltpu.SemaphoreType.DMA((4 + clips,)),
        ],
        compiler_params=pltpu.CompilerParams(
            dimension_semantics=("arbitrary",),
            vmem_limit_bytes=VMEM_LIMIT,
            collective_id=0,
            has_side_effects=True,
        ),
        name="attention_forward_links",
    )(index, x, cot, gain_one, gain_two, qkv, proj, mem, tail, taps, hidden_weight, output_weight)


def attention_forward(x, cot, w, mem, tail, side, main, taps, gain_one, gain_two):
    clips, pairs = x.shape[0], w.shape[0]
    width = x.shape[2]
    packed_width = PIECES * WIDE
    weight_rows = w.shape[1]
    late = lambda p, c: jnp.where(p == pairs - 1, c, 0)
    early = lambda p, c: jnp.where(p == 0, c, clips - 1)
    per_step = lambda p, c: (p, c)
    return pl.pallas_call(
        forward_kernel,
        grid=(pairs, clips),
        in_specs=[
            pl.BlockSpec((1, TPC, width), lambda p, c: (early(p, c), 0, 0)),
            pl.BlockSpec((1, TPC, width), lambda p, c: (late(p, c), 0, 0)),
            pl.BlockSpec((1, weight_rows, width), lambda p, c: (p, 0, 0)),
            pl.BlockSpec((1, PAIR, 2 * HD, MAIN), lambda p, c: (c, p, 0, 0)),
            pl.BlockSpec((1, PAIR, 2 * REST, WIDE), lambda p, c: (c, p, 0, 0)),
            pl.BlockSpec((1, 1, SIDE), lambda p, c: (c, 0, 0)),
            pl.BlockSpec((1, 1, MAIN), lambda p, c: (c, 0, 0)),
            pl.BlockSpec((1, PAIR, 4, HD), lambda p, c: (p, 0, 0, 0)),
            pl.BlockSpec(gain_one.shape, lambda p, c: (0,)),
            pl.BlockSpec(gain_two.shape, lambda p, c: (0,)),
        ],
        out_specs=[
            pl.BlockSpec((1, 1, ROWS, packed_width), lambda p, c: (p, c, 0, 0)),
            pl.BlockSpec((1, 1, PAIR, 2, SIDE, WIDE), lambda p, c: (p, c, 0, 0, 0, 0)),
            pl.BlockSpec((1, 1, ROWS, PAIR * WIDE), lambda p, c: (p, c, 0, 0)),
            pl.BlockSpec((1, ROWS, WIDE), lambda p, c: (late(p, c), 0, 0)),
            pl.BlockSpec((1, ROWS, width), lambda p, c: (early(p, c), 0, 0)),
            pl.BlockSpec((1, ROWS, width), lambda p, c: (late(p, c), 0, 0)),
            pl.BlockSpec((1, ROWS, width), lambda p, c: (late(p, c), 0, 0)),
            pl.BlockSpec((1, ROWS, width), lambda p, c: (late(p, c), 0, 0)),
        ],
        out_shape=[
            shaped((pairs, clips, ROWS, packed_width), BF16),
            shaped((pairs, clips, PAIR, 2, SIDE, WIDE), BF16),
            shaped((pairs, clips, ROWS, PAIR * WIDE), BF16),
            shaped((clips, ROWS, WIDE), F32),
            shaped((clips, ROWS, width), BF16),
            shaped((clips, ROWS, width), F32),
            shaped((clips, ROWS, width), BF16),
            shaped((clips, ROWS, width), BF16),
        ],
        scratch_shapes=[
            pltpu.VMEM((clips, ROWS, width), BF16),
            pltpu.VMEM((clips, ROWS, width), BF16),
            pltpu.VMEM((clips, ROWS, width), F32),
            pltpu.VMEM((clips, ROWS, WIDE), F32),
        ],
        compiler_params=compiler_params(2),
        name="attention_forward",
    )(x, cot, w, mem, tail, side, main, taps, gain_one, gain_two)


def once(shape):
    return pl.BlockSpec(shape, lambda t: (0,) * len(shape), pipeline_mode=pl.Buffered(1))


def mlp(normed, cot, first, second, middle, gain):
    rows, width = normed.shape
    hidden = first.shape[1]
    clips = rows // ROWS
    tiles = hidden // TILE
    tile_at = lambda t: jnp.minimum(t, tiles - 1)
    clip_at = lambda t: jnp.maximum(t - tiles, 0)
    return pl.pallas_call(
        mlp_kernel,
        grid=(tiles + clips,),
        in_specs=[
            once((rows, width)),
            once((rows, width)),
            pl.BlockSpec((width, TILE), lambda t: (0, tile_at(t))),
            pl.BlockSpec((TILE, width), lambda t: (tile_at(t), 0)),
            pl.BlockSpec(memory_space=pl.ANY),
            pl.BlockSpec(gain.shape, lambda t: (0,)),
        ],
        out_specs=[
            pl.BlockSpec((1, TPC, width), lambda t: (clip_at(t), 0, 0)),
            pl.BlockSpec((ROWS, width), lambda t: (clip_at(t), 0)),
            pl.BlockSpec((width, TILE), lambda t: (0, tile_at(t))),
            pl.BlockSpec((TILE, width), lambda t: (tile_at(t), 0)),
            once((1, width)),
        ],
        out_shape=[
            shaped((clips, TPC, width), BF16),
            shaped((rows, width), BF16),
            shaped((width, hidden), BF16),
            shaped((hidden, width), BF16),
            shaped((1, width), F32),
        ],
        scratch_shapes=[
            pltpu.VMEM((rows, width), F32),
            pltpu.VMEM((rows, width), F32),
            pltpu.VMEM((rows, width), F32),
            pltpu.VMEM((rows, TILE), BF16),
            pltpu.VMEM((rows, TILE), BF16),
            pltpu.SemaphoreType.DMA((1,)),
        ],
        compiler_params=compiler_params(1),
        name="mlp",
    )(normed, cot, first, second, middle, gain)


def sum_scratch(lead, planes, shape):
    return [
        pltpu.VMEM(lead + dims + shape, BF16)
        for dims in ((planes, 2, 2, 2), (planes, 2, 2), (planes, 2), (planes,), (3,))
    ]


def mlp_links(normed, cot, first, second, middle, gain):
    rows, width = normed.shape
    hidden = first.shape[1]
    clips = rows // ROWS
    tile_at = lambda t: jnp.minimum(t, TILES - 1)
    clip_at = lambda t: jnp.maximum(t - TILES, 0)
    first_rows, second_rows = width // 32, hidden // 32
    anywhere = pl.BlockSpec(memory_space=pl.ANY)
    return pl.pallas_call(
        mlp_links_kernel,
        grid=(TILES + clips,),
        in_specs=[
            once((rows, width)),
            once((rows, width)),
            pl.BlockSpec((width, TILE), lambda t: (0, tile_at(t))),
            pl.BlockSpec((TILE, width), lambda t: (tile_at(t), 0)),
            anywhere,
            pl.BlockSpec(gain.shape, lambda t: (0,)),
        ],
        out_specs=[
            pl.BlockSpec((1, TPC, width), lambda t: (clip_at(t), 0, 0)),
            pl.BlockSpec((ROWS, width), lambda t: (clip_at(t), 0)),
            once((1, width)),
        ] + [anywhere] * 4,
        out_shape=[
            shaped((clips, TPC, width), BF16),
            shaped((rows, width), BF16),
            shaped((1, width), F32),
            shaped((first_rows, EARLY * TILE), F32),
            shaped((second_rows, width), F32),
            shaped((TILES - EARLY, 4, 2, 2, 2, first_rows, TILE), BF16),
            shaped((TILES - EARLY, 1, 2, 2, 2, second_rows, width), BF16),
        ],
        scratch_shapes=[
            pltpu.VMEM((rows, width), F32),
            pltpu.VMEM((rows, width), F32),
            pltpu.VMEM((rows, width), F32),
            pltpu.VMEM((rows, TILE), BF16),
            pltpu.VMEM((rows, TILE), BF16),
            pltpu.SemaphoreType.DMA((1,)),
        ]
        + sum_scratch((EARLY,), 4, (first_rows, TILE))
        + sum_scratch((EARLY,), 1, (second_rows, width))
        + [
            pltpu.VMEM((TILES - EARLY, 4, 2, 2, 2, first_rows, TILE), BF16),
            pltpu.VMEM((TILES - EARLY, 1, 2, 2, 2, second_rows, width), BF16),
            pltpu.VMEM((EARLY, first_rows, TILE), F32),
            pltpu.VMEM((second_rows, width), F32),
            pltpu.SemaphoreType.DMA((12 * EARLY,)),
            pltpu.SemaphoreType.DMA((12 * EARLY,)),
            pltpu.SemaphoreType.DMA((2 * TILES,)),
        ],
        compiler_params=pltpu.CompilerParams(
            dimension_semantics=("arbitrary",),
            vmem_limit_bytes=VMEM_LIMIT,
            collective_id=2,
            has_side_effects=True,
        ),
        name="mlp_links",
    )(normed, cot, first, second, middle, gain)


def attention_backward(x, w, mem, side, main, taps, gain, packed, keys, att, log, normed, grad):
    clips, pairs = x.shape[0], w.shape[0]
    width = x.shape[2]
    packed_width = PIECES * WIDE
    weight_rows = w.shape[1]
    late = lambda p, c: jnp.where(p == pairs - 1, c, 0)
    return pl.pallas_call(
        backward_kernel,
        grid=(pairs, clips),
        in_specs=[
            pl.BlockSpec((1, TPC, width), lambda p, c: (late(p, c), 0, 0)),
            pl.BlockSpec((1, weight_rows, width), lambda p, c: (p, 0, 0)),
            pl.BlockSpec((1, PAIR, 2 * HD, MAIN), lambda p, c: (c, p, 0, 0)),
            pl.BlockSpec((1, 1, SIDE), lambda p, c: (c, 0, 0)),
            pl.BlockSpec((1, 1, MAIN), lambda p, c: (c, 0, 0)),
            pl.BlockSpec((1, PAIR, 4, HD), lambda p, c: (p, 0, 0, 0)),
            pl.BlockSpec(gain.shape, lambda p, c: (0,)),
            pl.BlockSpec((1, 1, ROWS, packed_width), lambda p, c: (p, c, 0, 0)),
            pl.BlockSpec((1, 1, PAIR, 2, SIDE, WIDE), lambda p, c: (p, c, 0, 0, 0, 0)),
            pl.BlockSpec((1, 1, ROWS, PAIR * WIDE), lambda p, c: (p, c, 0, 0)),
            pl.BlockSpec((1, ROWS, WIDE), lambda p, c: (c, 0, 0)),
            pl.BlockSpec((1, ROWS, width), lambda p, c: (c, 0, 0)),
            pl.BlockSpec((ROWS, width), lambda p, c: (c, 0)),
        ],
        out_specs=[
            pl.BlockSpec((1, TPC, width), lambda p, c: (late(p, c), 0, 0)),
            pl.BlockSpec((1, weight_rows, width), lambda p, c: (p, 0, 0)),
            pl.BlockSpec((1, PAIR, 4, WIDE), lambda p, c: (p, 0, 0, 0)),
            pl.BlockSpec((1, width), lambda p, c: (0, 0)),
        ],
        out_shape=[
            shaped((clips, TPC, width), BF16),
            shaped((pairs, weight_rows, width), F32),
            shaped((pairs, PAIR, 4, WIDE), F32),
            shaped((1, width), F32),
        ],
        scratch_shapes=[pltpu.VMEM((clips, ROWS, width), F32)],
        compiler_params=compiler_params(2),
        name="attention_backward",
    )(x, w, mem, side, main, taps, gain, packed, keys, att, log, normed, grad)


def attention_backward_links(
    index, x, qkv, proj, mem, taps, gain, packed, keys, att, log, normed, grad, gain_two, d_first, d_second
):
    clips, width = x.shape[0], x.shape[2]
    packed_width = PIECES * WIDE
    steps = 4 * clips
    early = lambda s: jnp.minimum(s, steps - 1)
    pair_at = lambda s: lax.rem(lax.div(early(s), clips) + 2, 4)
    clip_at = lambda s: lax.rem(early(s), clips)
    late = lambda s: jnp.maximum(s - steps, 0)
    anywhere = pl.BlockSpec(memory_space=pl.ANY)
    per_step = lambda s: (pair_at(s), clip_at(s), 0, 0)
    small = (16, width)
    left = d_first.shape[0]
    first_shape, second_shape = d_first.shape[-2:], d_second.shape[-2:]
    units = []
    for _, rows, padded in UNITS:
        units += [
            pltpu.VMEM(shape, BF16)
            for shape in (
                (padded, width), (padded, CORE_LANES), (padded // 2, CORE_LANES), (3, padded // 8, CORE_LANES), (padded, width),
                (rows, width), (rows, CORE_LANES), (rows, CORE_LANES),
            )
        ]
    return pl.pallas_call(
        backward_links_kernel,
        grid=(steps + clips,),
        in_specs=[
            pl.BlockSpec(memory_space=pltpu.SMEM),
            pl.BlockSpec((1, TPC, width), lambda s: (late(s), 0, 0)),
            once(qkv.shape),
            pl.BlockSpec((1,) + proj.shape[1:], lambda s: (pair_at(s), 0, 0, 0)),
            pl.BlockSpec(
                (None, 1, PAIR, 2 * HD, MAIN),
                lambda s: (lax.div(pair_at(s), 2), clip_at(s), lax.rem(pair_at(s), 2), 0, 0),
            ),
            pl.BlockSpec((1, PAIR, 4, HD), lambda s: (pair_at(s), 0, 0, 0)),
            pl.BlockSpec(gain.shape, lambda s: (0,)),
            pl.BlockSpec((1, 1, ROWS, packed_width), per_step),
            pl.BlockSpec((1, 1, PAIR, 2, SIDE, WIDE), lambda s: per_step(s) + (0, 0)),
            pl.BlockSpec((2, clips, ROWS, PAIR * WIDE), lambda s: (lax.div(pair_at(s), 2), 0, 0, 0)),
            pl.BlockSpec((1, ROWS, WIDE), lambda s: (clip_at(s), 0, 0)),
            once((clips, ROWS, width)),
            once((clips, ROWS, width)),
            pl.BlockSpec((1, width), lambda s: (0, 0)),
            anywhere,
            anywhere,
        ],
        out_specs=[
            pl.BlockSpec((1, TPC, width), lambda s: (late(s), 0, 0)),
            pl.BlockSpec(small, lambda s: (0, 0)),
        ] + [anywhere] * 4,
        out_shape=[
            shaped((clips, TPC, width), BF16),
            shaped(small, F32),
            shaped((first_shape[0], left * TILE), F32),
            shaped(second_shape, F32),
            shaped((UNITS[0][1], width), BF16),
            shaped((2, UNITS[1][1], width), BF16),
        ],
        scratch_shapes=[
            pltpu.VMEM((4, clips, ROWS, packed_width), BF16),
            pltpu.VMEM((1, width), F32),
            pltpu.VMEM((4, PAIR, 4, WIDE), F32),
        ]
        + [pltpu.VMEM(small, F32)] * 5
        + [
            pltpu.VMEM((4,) + small, F32),
            pltpu.VMEM((left,) + first_shape, F32),
            pltpu.VMEM(second_shape, F32),
            pltpu.SemaphoreType.DMA((BACKWARD_COPIES,)),
            pltpu.SemaphoreType.DMA((BACKWARD_COPIES,)),
            pltpu.SemaphoreType.DMA((6 + left,)),
        ]
        + sum_scratch((left,), 4, first_shape)
        + sum_scratch((left,), 1, second_shape)
        + units,
        compiler_params=pltpu.CompilerParams(
            dimension_semantics=("arbitrary",),
            vmem_limit_bytes=VMEM_LIMIT,
            collective_id=1,
            has_side_effects=True,
        ),
        name="attention_backward_links",
    )(index, x, qkv, proj, mem, taps, gain, packed, keys, att, log, normed, grad, gain_two, d_first, d_second)


def group_gather(own, heads, fetch=None):
    blocks = [fetch(own, 0) if fetch else own]
    for shift in range(1, heads):
        sent = fetch(own, -shift) if fetch else own
        blocks.append(lax.ppermute(sent, "head", [(src, (src - shift) % heads) for src in range(heads)]))
    return blocks


def group_sum(blocks, heads):
    total = blocks[0]
    for shift in range(1, heads):
        total = total + lax.ppermute(
            blocks[shift].astype(BF16), "head", [(src, (src + shift) % heads) for src in range(heads)]
        ).astype(F32)
    return total


def local(
    heads,
    batches,
    inputs,
    qkv_weight,
    proj_weight,
    pool_weight,
    gain_one,
    gain_two,
    hidden_weight,
    output_weight,
    memory,
    clip_index,
    cotangent,
):
    width = inputs.shape[3]
    micro, own_clips = inputs.shape[:2]
    clips = micro * own_clips
    own_heads = qkv_weight.shape[1]
    all_heads = own_heads * heads
    pairs = all_heads // PAIR
    me = lax.axis_index("head")
    linked = (heads, batches, micro, own_clips) == (2, 16, 4, 1)

    def mine(array, shift):
        start = lax.rem(me + shift + heads, heads) * own_clips
        return lax.dynamic_slice_in_dim(array, start, own_clips, axis=1)

    pad = WIDE - HD
    qkv_rows = jnp.pad(
        qkv_weight.transpose(1, 2, 0).reshape(own_heads, 3, HD, width), ((0, 0), (0, 0), (0, pad), (0, 0))
    )
    proj_rows = jnp.pad(proj_weight, ((0, 0), (0, pad), (0, 0)))
    taps_own = pool_weight.astype(F32)
    memory_t = memory.transpose(0, 1, 3, 4, 2)
    tail_own = memory_t[..., MAIN:].reshape(memory_t.shape[:3] + (2, HD, REST)).swapaxes(4, 5)
    tail_own = jnp.pad(tail_own, ((0, 0),) * 5 + ((0, pad),)).reshape(memory_t.shape[:3] + (2 * REST, WIDE))

    x = inputs.reshape(clips, TPC, width)
    cot = cotangent.reshape(clips, TPC, width)
    if linked:
        (packed, keys, att, log, normed, middle, normed_two, cot_rows, first, second, qkv_all, proj_all, mem_all, taps_all) = (
            attention_forward_links(
                clip_index.T, x, cot, qkv_weight.transpose(1, 2, 0).reshape(PAIR, PAIR, 3, HD, width),
                proj_weight.reshape(PAIR, PAIR, HD, width), memory_t, tail_own,
                taps_own.reshape(-1, PAIR, 4, HD), gain_one, gain_two, hidden_weight, output_weight,
            )
        )
        first = first.reshape(width, -1)
        second = second.reshape(-1, width)
    else:
        qkv_all = jnp.concatenate(group_gather(qkv_rows, heads), axis=0)
        proj_all = jnp.concatenate(group_gather(proj_rows, heads), axis=0)
        w_all = jnp.concatenate(
            [
                qkv_all.reshape(pairs, PIECES * WIDE, width),
                proj_all.reshape(pairs, PAIR * WIDE, width),
            ],
            axis=1,
        )
        taps_all = jnp.concatenate(group_gather(taps_own, heads), axis=0).reshape(pairs, PAIR, 4, HD)
        mem_all = jnp.concatenate(group_gather(memory_t, heads, mine), axis=2)
        mem_all = mem_all.reshape(clips, all_heads, 2 * HD, TPC)
        tail = jnp.concatenate(group_gather(tail_own, heads, mine), axis=2)
        tail = tail.reshape(clips, all_heads, 2 * REST, WIDE)

        first = lax.all_gather(hidden_weight, ("batch", "head"), axis=0, tiled=True)
        second = lax.all_gather(output_weight, ("batch", "head"), axis=0, tiled=True)
        index = mine(clip_index, 0).reshape(clips, 1, 1)
        side_mask, main_mask = mask_rows(index)
        side_mask, main_mask = side_mask.reshape(clips, 1, SIDE), main_mask.reshape(clips, 1, MAIN)
        packed, keys, att, log, normed, middle, normed_two, cot_rows = attention_forward(
            x, cot, w_all, mem_all, tail, side_mask, main_mask, taps_all, gain_one, gain_two
        )
    rows = clips * ROWS
    mlp_args = (
        normed_two.reshape(rows, width), cot_rows.reshape(rows, width), first, second, middle.reshape(rows, width), gain_two
    )
    if linked:
        outputs, grad, d_gain_two, d_first, d_second, first_left, second_left = mlp_links(*mlp_args)
    else:
        outputs, grad, d_first, d_second, d_gain_two = mlp(*mlp_args)
    if linked:
        d_x, small, last_first, last_second, d_proj, d_qkv = attention_backward_links(
            clip_index.T, x, qkv_all, proj_all, mem_all, taps_all, gain_one,
            packed, keys, att, log, normed, grad.reshape(clips, ROWS, width), d_gain_two,
            first_left, second_left,
        )
        d_first = jnp.concatenate([d_first, last_first], axis=1)
        d_second = jnp.where(lax.axis_index("batch") // (batches // TILES) >= EARLY, last_second, d_second)
        d_qkv = d_qkv.astype(F32).reshape(own_heads, 3 * HD, width)
        d_proj = d_proj.astype(F32).reshape(own_heads, HD, width)
        d_taps = small[8:, : 2 * WIDE].reshape(PAIR, 4, 2, WIDE).transpose(2, 0, 1, 3)[..., :HD]
        share = width // (batches * heads)
        start = (lax.axis_index("batch") * heads + me) * share
        d_gains = lax.dynamic_slice_in_dim(small[:2], start, share, axis=1)
        return (
            outputs.reshape(inputs.shape),
            d_x.reshape(inputs.shape),
            d_qkv.transpose(2, 0, 1),
            d_proj,
            d_taps.reshape(own_heads, 4, HD),
            d_gains[0],
            d_gains[1],
            d_first,
            d_second,
        )
    d_x, d_w, d_taps, d_gain_one = attention_backward(
        x, w_all, mem_all, side_mask, main_mask, taps_all, gain_one,
        packed, keys, att, log, normed, grad,
    )
    d_proj = d_w[:, PIECES * WIDE :].reshape(heads, own_heads, WIDE, width)[:, :, :HD]
    d_w = d_w[:, : PIECES * WIDE].reshape(heads, own_heads, 3, WIDE, width)[:, :, :, :HD]
    d_w = d_w.reshape(heads, own_heads, 3 * HD, width)
    d_taps = d_taps.reshape(heads, own_heads, 4, WIDE)[..., :HD]
    d_w, d_proj, d_taps = (
        lax.psum(group_sum(list(grads), heads).astype(BF16), "batch").astype(F32)
        for grads in (d_w, d_proj, d_taps)
    )
    both = ("batch", "head")
    d_first = lax.psum_scatter(d_first, both, scatter_dimension=0, tiled=True).astype(F32)
    d_second = lax.psum_scatter(d_second, both, scatter_dimension=0, tiled=True).astype(F32)
    d_gains = lax.psum_scatter(
        jnp.concatenate([d_gain_one, d_gain_two], axis=0), both, scatter_dimension=1, tiled=True
    )
    return (
        outputs.reshape(inputs.shape),
        d_x.reshape(inputs.shape),
        d_w.transpose(2, 0, 1),
        d_proj,
        d_taps,
        d_gains[0],
        d_gains[1],
        d_first,
        d_second,
    )


def solution(mesh):
    return jax.shard_map(
        functools.partial(local, mesh.shape["head"], mesh.shape["batch"]),
        mesh=mesh,
        in_specs=(
            P(None, ("batch", "head"), None, None),
            P(None, "head", None),
            P("head", None, None),
            P("head", None, None),
            P(),
            P(),
            P(("batch", "head"), None),
            P(("batch", "head"), None),
            P(None, "batch", None, "head", None),
            P(None, "batch"),
            P(None, ("batch", "head"), None, None),
        ),
        out_specs=(
            P(None, ("batch", "head"), None, None),
            P(None, ("batch", "head"), None, None),
            P(None, "head", None),
            P("head", None, None),
            P("head", None, None),
            P(("batch", "head")),
            P(("batch", "head")),
            P(("batch", "head"), None),
            P(("batch", "head"), None),
        ),
        check_vma=False,
    )
```

```python
import functools
import math

import jax
import jax.numpy as jnp
from jax import lax
from jax.experimental import pallas as pl
from jax.experimental.pallas import tpu as pltpu
from jax.sharding import PartitionSpec as P

HD = 96
WIDE = 128
FRAMES = 8
TPC = 392
PTOK = 196
SPOT = TPC // FRAMES
HALF = 200
ROWS = 2 * HALF
MAIN = 384
REST = TPC - MAIN
SIDE = 256
PAIR = 2
PIECES = 3 * PAIR

NORM_EPS = 1e-06
NEG = -1e30
LOG2E = 1.4426950408889634
SCORE = HD ** (-0.5)

F32 = jnp.float32
BF16 = jnp.bfloat16


def dot(a, b):
    return lax.dot_general(a, b, (((1,), (0,)), ((), ())), preferred_element_type=F32)


def dot_nt(a, b):
    return lax.dot_general(a, b, (((1,), (1,)), ((), ())), preferred_element_type=F32)


def dot_tn(a, b):
    return lax.dot_general(a, b, (((0,), (0,)), ((), ())), preferred_element_type=F32)


def reorder(shape, row_dim):
    rows = lax.broadcasted_iota(jnp.int32, shape, row_dim)
    tokens = lax.broadcasted_iota(jnp.int32, shape, 1 - row_dim)
    odd = (rows >= HALF).astype(jnp.int32)
    spot = rows - HALF * odd
    frame = sum((spot >= SPOT * step).astype(jnp.int32) for step in range(1, FRAMES // 2))
    return ((tokens == spot + SPOT * (frame + odd)) & (spot < PTOK)).astype(BF16)


def norm_parts(values):
    average = jnp.mean(values, axis=-1, keepdims=True)
    centered = values - average
    spread = lax.rsqrt(jnp.mean(centered * centered, axis=-1, keepdims=True) + NORM_EPS)
    return centered * spread, spread


def norm_pull(values, gain, grad):
    unit, spread = norm_parts(values)
    scaled = grad * gain
    inner = jnp.mean(scaled * unit, axis=-1, keepdims=True)
    pulled = spread * (scaled - jnp.mean(scaled, axis=-1, keepdims=True) - unit * inner)
    return pulled, jnp.sum(grad * unit, axis=0, keepdims=True)


def as_row(ref):
    return ref[...].reshape(1, -1)


def widen(taps):
    return jnp.concatenate([taps, jnp.zeros((taps.shape[0], WIDE - taps.shape[1]), F32)], axis=1)


def mask_rows(index):
    slot = lax.broadcasted_iota(jnp.int32, (1, MAIN), 1) // PTOK
    main = jnp.where(index > slot, 0.0, NEG)
    spot = lax.broadcasted_iota(jnp.int32, (1, SIDE), 1)
    tail_open = (spot >= HALF) & (spot < HALF + REST) & (index > (TPC - 1) // PTOK)
    return jnp.where((spot < PTOK) | tail_open, 0.0, NEG), main


def value_columns(memory_t):
    return jnp.concatenate([memory_t[HD:], jnp.zeros((WIDE - HD, memory_t.shape[1]), BF16)], axis=0)


def forward_kernel(
    x_ref, cot_ref, w_ref, mem_ref, tail_ref, side_ref, main_ref, taps_ref, gain_one_ref, gain_two_ref,
    packed_ref, keys_ref, att_ref, log_ref, normed_ref, middle_ref, normed_two_ref, cot_out,
    x_rows, normed_rows, branch, logs,
):
    forward_step(
        pl.program_id(0), pl.program_id(1), pl.num_programs(0), (side_ref[0], main_ref[0]),
        w_ref.at[0, : PIECES * WIDE], w_ref.at[0, PIECES * WIDE :], mem_ref.at[0], tail_ref.at[0], taps_ref.at[0],
        x_ref, cot_ref, gain_one_ref, gain_two_ref,
        packed_ref, keys_ref, att_ref, log_ref, normed_ref, middle_ref, normed_two_ref, cot_out,
        x_rows, normed_rows, branch, logs,
    )


def forward_step(
    pair, clip, pairs, masks,
    qkv_ref, proj_ref, mem_ref, tail_ref, taps_ref,
    x_ref, cot_ref, gain_one_ref, gain_two_ref,
    packed_ref, keys_ref, att_ref, log_ref, normed_ref, middle_ref, normed_two_ref, cot_out,
    x_rows, normed_rows, branch, log_rows,
):
    here = pl.ds(clip, 1)

    @pl.when(pair == 0)
    def _():
        rows = dot(reorder((ROWS, TPC), 0), x_ref[0])
        x_rows[here] = rows.astype(BF16)[None]
        unit, _ = norm_parts(rows)
        low = (unit * as_row(gain_one_ref)).astype(BF16)
        normed_rows[here] = low[None]
        normed_ref[0] = low
        log_rows[here] = jnp.zeros((1, ROWS, WIDE), F32)

    normed = normed_rows[here][0]
    packed = dot_nt(normed, qkv_ref[...].reshape(-1, normed.shape[1]))
    packed_ref[0, 0] = packed.astype(BF16)
    logs = []
    outs = []
    for head in range(PAIR):
        base = 3 * WIDE * head
        query = packed[:, base : base + WIDE]
        key = packed[:, base + WIDE : base + 2 * WIDE]
        value = packed[:, base + 2 * WIDE : base + 3 * WIDE]
        query_low = query.astype(BF16)
        taps = widen(taps_ref[head])
        zeros = jnp.zeros((SIDE - HALF - REST, WIDE), F32)
        pooled_key = taps[0:1] * key[:HALF] + taps[1:2] * key[HALF:]
        pooled_value = taps[2:3] * value[:HALF] + taps[3:4] * value[HALF:]
        tail = tail_ref[head].astype(F32)
        side_key = jnp.concatenate([pooled_key, tail[:REST], zeros], axis=0).astype(BF16)
        side_value = jnp.concatenate([pooled_value, tail[REST:], zeros], axis=0).astype(BF16)
        keys_ref[0, 0, head, 0] = side_key
        keys_ref[0, 0, head, 1] = side_value
        memory_t = mem_ref[head]
        score_side = dot_nt(query_low, side_key) * (SCORE * LOG2E) + masks[0]
        score_main = dot(query_low, memory_t[:WIDE]) * (SCORE * LOG2E) + masks[1]
        top = jnp.maximum(
            jnp.max(score_side, axis=-1, keepdims=True), jnp.max(score_main, axis=-1, keepdims=True)
        )
        weight_side = jnp.exp2(score_side - top)
        weight_main = jnp.exp2(score_main - top)
        total = jnp.sum(weight_side, axis=-1, keepdims=True) + jnp.sum(weight_main, axis=-1, keepdims=True)
        mixed = dot(weight_side.astype(BF16), side_value) + dot_nt(
            weight_main.astype(BF16), value_columns(memory_t)
        )
        outs.append(mixed / total + query)
        logs.append(top + jnp.log2(total))
    attended = jnp.concatenate(outs, axis=1).astype(BF16)
    att_ref[0, 0] = attended
    lane = lax.broadcasted_iota(jnp.int32, (ROWS, WIDE), 1) - PAIR * pair
    log_rows[here] = jnp.where(lane == 0, logs[0], jnp.where(lane == 1, logs[1], log_rows[here][0]))[None]
    part = dot(attended, proj_ref[...].reshape(-1, normed.shape[1]))[None]

    @pl.when(pair == 0)
    def _():
        branch[here] = part

    @pl.when(pair > 0)
    def _():
        branch[here] += part

    @pl.when(pair == pairs - 1)
    def _():
        middle = x_rows[here][0].astype(F32) + branch[here][0]
        middle_ref[0] = middle
        unit, _ = norm_parts(middle)
        normed_two_ref[0] = (unit * as_row(gain_two_ref)).astype(BF16)
        log_ref[0] = log_rows[here][0]
        cot_out[0] = dot(reorder((ROWS, TPC), 0), cot_ref[0]).astype(BF16)


def feed(step, chunk, normed_ref, cot_ref, first, second, total, grad_normed, active, grad_hidden):
    here = pl.ds(chunk * CHUNK, CHUNK)
    hidden = dot(normed_ref[here, :], first)
    grad_active = dot_nt(cot_ref[here, :], second)
    bell = jnp.exp2(hidden * hidden * (-0.5 * LOG2E))
    near = 1.0 / (1.0 + (0.3275911 * math.sqrt(0.5)) * jnp.abs(hidden))
    tail = near * (0.5 * 1.061405429) + (0.5 * -1.453152027)
    tail = near * tail + (0.5 * 1.421413741)
    tail = near * tail + (0.5 * -0.284496736)
    tail = near * tail + (0.5 * 0.254829592)
    tail = near * tail * bell
    cumulative = jnp.where(hidden < 0.0, tail, 1.0 - tail)
    slope = cumulative + hidden * bell * 0.3989422804014327
    active_low = (hidden * cumulative).astype(BF16)
    hidden_low = (slope * grad_active).astype(BF16)
    active[here, :] = active_low
    grad_hidden[here, :] = hidden_low
    fed = dot(active_low, second)
    back = dot_nt(hidden_low, first)

    @pl.when(step == 0)
    def _():
        total[here, :] = fed
        grad_normed[here, :] = back

    @pl.when(step > 0)
    def _():
        total[here, :] += fed
        grad_normed[here, :] += back


def mlp_kernel(*refs):
    mlp_step(None, *refs)


def mlp_links_kernel(
    normed_ref, cot_ref, first_ref, second_ref, middle_ref, gain_ref,
    out_ref, grad_ref, d_gain_ref, first_out, second_out, first_left, second_left,
    middle, total, grad_normed, active, grad_hidden, near, *rest,
):
    step = pl.program_id(0)
    here = place()
    z, y, core, x, at = here
    first_refs, second_refs = rest[:5], rest[5:10]
    first_keep, second_keep, first_result, second_result, send, recv, store = rest[10:]
    links = Links(send, recv)
    partners = Partners(here)
    sums, outs = [], []
    for tile in range(EARLY):
        sums.append(
            (
                Sum(f"f{tile}", "xy", None, [ref.at[tile] for ref in first_refs], links, partners),
                Sum(f"s{tile}", "yx", tile, [ref.at[tile] for ref in second_refs], links, partners),
            )
        )
        outs.append(
            (
                pltpu.make_async_copy(
                    first_result.at[tile], first_out.at[:, pl.ds(tile * TILE, TILE)], store.at[2 * tile]
                ),
                pltpu.make_async_copy(second_result, second_out, store.at[2 * tile + 1]),
            )
        )
    kept = [
        [
            pltpu.make_async_copy(left.at[tile], out.at[tile], store.at[2 * (EARLY + tile) + i])
            for i, (left, out) in enumerate(((first_keep, first_left), (second_keep, second_left)))
        ]
        for tile in range(TILES - EARLY)
    ]

    def store_grads(d_first, d_second):
        for tile in range(TILES):

            @pl.when(step == tile)
            def _(tile=tile):
                early = tile < EARLY
                for early_ref, keep_ref, grad in (
                    (first_refs[0], first_keep, d_first),
                    (second_refs[0], second_keep, d_second),
                ):
                    into = early_ref if early else keep_ref
                    into[tile if early else tile - EARLY] = grad.reshape(into.shape[1:]).astype(BF16)
                if not early:
                    for copy in kept[tile - EARLY]:
                        copy.start()

    def finish(tile):
        one, two = sums[tile]
        one.finish(first_result.at[tile])
        outs[tile][0].start()

        @pl.when(z == tile)
        def _():
            two.finish(second_result)
            outs[tile][1].start()

    def act(moment):
        for tile, (one, two) in enumerate(sums):
            plan = {
                (tile + 1, 0): [one.begin, two.begin],
                (tile + 1, 1): [one.core, two.core],
                (tile + 2, 0): [one.first, two.first],
                (tile + 2, 1): [one.second, two.second],
                (tile + 3, 0): [lambda: finish(tile)],
            }
            for (when, which), acts in plan.items():
                if which != moment:
                    continue

                @pl.when(step == when)
                def _(acts=acts):
                    for one_act in acts:
                        one_act()

    @pl.when(step == 0)
    def _():
        greet(partners.all())

    mlp_step(
        act, normed_ref, cot_ref, first_ref, second_ref, middle_ref, gain_ref,
        out_ref, grad_ref, store_grads, None, d_gain_ref,
        middle, total, grad_normed, active, grad_hidden, near,
    )

    @pl.when(step == pl.num_programs(0) - 1)
    def _():
        links.sent()
        for copies in kept:
            for copy in copies:
                copy.wait()
        for tile, (one, two) in enumerate(outs):
            one.wait()
            pl.when(z == tile)(lambda two=two: two.wait())


class Partners:
    def __init__(self, here):
        self.place = here
        z, y, core, x, at = here
        self.x, self.y, self.core = at(z, y, core, 1 - x), at(z, 1 - y, core, x), at(z, y, 1 - core, x)
        self.along = [at(turn(z, shift), y, core, x) for shift in (1, 2, 3)]

    def all(self):
        return [self.x, self.y, self.core] + self.along


class Sum:
    def __init__(self, name, order, owner, refs, links, partners):
        self.name, self.order, self.owner, self.links = name, order, owner, links
        self.data, self.from_core, self.from_one, self.from_two, self.from_z = refs
        self.place = z, y, core, x, at = partners.place
        data = self.data
        self.planes = data.shape[0]
        self.names = [name + "c", name + "a", name + "b"] + [f"{name}z{shift}" for shift in (1, 2, 3)]
        links.add(name + "c", data.at[:, :, 1 - core], self.from_core, partners.core)
        if order == "xy":
            links.add(name + "a", data.at[:, :, core, 1 - x], self.from_one, partners.x)
            links.add(name + "b", data.at[:, 1 - y, core, x], self.from_two, partners.y)
        else:
            links.add(name + "a", data.at[:, 1 - y, core], self.from_one, partners.y)
            links.add(name + "b", data.at[:, y, core, 1 - x], self.from_two, partners.x)
        for shift in (1, 2, 3):
            into = self.from_z.at[shift - 1]
            if owner is None:
                source = data.at[turn(z, shift), y, core, x]
                links.add(f"{name}z{shift}", source, into, partners.along[shift - 1])
            else:
                links.add(
                    f"{name}z{shift}", data.at[0, y, core, x], into, at(owner, y, core, x),
                    z == (owner + shift) % 4, z == owner,
                )

    def begin(self):
        self.links.start(self.name + "c")

    def core(self):
        z, y, core, x, at = self.place
        self.links.arrived(self.name + "c")

        @pl.loop(0, self.planes)
        def _(plane):
            for column in (0, 1):
                for head in (0, 1):
                    self.data[plane, column, core, head] = add_low(
                        self.data[plane, column, core, head], self.from_core[plane, column, head]
                    )

        self.links.start(self.name + "a")

    def first(self):
        z, y, core, x, at = self.place
        self.links.arrived(self.name + "a")

        @pl.loop(0, self.planes)
        def _(plane):
            for other in (0, 1):
                spot = (plane, other, core, x) if self.order == "xy" else (plane, y, core, other)
                self.data[spot] = add_low(self.data[spot], self.from_one[plane, other])

        self.links.start(self.name + "b")

    def second(self):
        z, y, core, x, at = self.place
        self.links.arrived(self.name + "b")

        @pl.loop(0, self.planes)
        def _(plane):
            self.data[plane, y, core, x] = add_low(self.data[plane, y, core, x], self.from_two[plane])

        self.links.start(*self.names[3:])

    def finish(self, result):
        z, y, core, x, at = self.place
        for name in self.names[3:]:
            self.links.get(name).wait_recv()
        part = self.data[z if self.owner is None else 0, y, core, x].astype(F32)
        for shift in range(3):
            part = part + self.from_z[shift].astype(F32)
        result[...] = part


def mlp_step(
    act, normed_ref, cot_ref, first_ref, second_ref, middle_ref, gain_ref,
    out_ref, grad_ref, d_first_ref, d_second_ref, d_gain_ref,
    middle, total, grad_normed, active, grad_hidden, near,
):
    step = pl.program_id(0)
    clips = middle.shape[0] // ROWS
    tiles = pl.num_programs(0) - clips
    chunks = middle.shape[0] // CHUNK
    fetch = pltpu.make_async_copy(middle_ref, middle, near.at[0])

    @pl.when(step == 0)
    def _():
        fetch.start()
        d_gain_ref[...] = jnp.zeros_like(d_gain_ref)

    if act is not None:
        act(0)

    @pl.when(step < tiles)
    def _():
        first = first_ref[...]
        second = second_ref[...]
        for chunk in range(chunks):
            if act is not None and chunk == 1:
                act(1)
            feed(step, chunk, normed_ref, cot_ref, first, second, total, grad_normed, active, grad_hidden)
        if act is not None:
            act(2)
        d_first = dot_tn(normed_ref[...], grad_hidden[...])
        d_second = dot_tn(active[...], cot_ref[...])
        if act is not None:
            d_first_ref(d_first, d_second)
        else:
            d_first_ref[...] = d_first.astype(BF16)
            d_second_ref[...] = d_second.astype(BF16)

    @pl.when(step == tiles)
    def _():
        fetch.wait()

    @pl.when(step >= tiles)
    def _():
        here = pl.ds(pl.multiple_of((step - tiles) * ROWS, ROWS), ROWS)
        values = middle[here, :]
        out = (values + total[here, :]).astype(BF16)
        out_ref[0] = dot(reorder((TPC, ROWS), 1), out).astype(BF16)
        pulled, d_gain = norm_pull(values, as_row(gain_ref), grad_normed[here, :])
        grad_ref[...] = (cot_ref[here, :].astype(F32) + pulled).astype(BF16)
        d_gain_ref[...] += d_gain


def backward_kernel(
    x_ref, w_ref, mem_ref, side_ref, main_ref, taps_ref, gain_ref,
    packed_ref, keys_ref, att_ref, log_ref, normed_ref, grad_ref,
    d_x_ref, d_w_ref, d_taps_ref, d_gain_ref,
    grad_normed,
):
    pair, clip = pl.program_id(0), pl.program_id(1)
    here = pl.ds(clip, 1)

    @pl.when(clip == 0)
    def _():
        d_w_ref[...] = jnp.zeros_like(d_w_ref)
        d_taps_ref[...] = jnp.zeros_like(d_taps_ref)

    grad_packed = backward_attention(
        pair, (side_ref[0], main_ref[0]), w_ref.at[0, PIECES * WIDE :], d_taps_ref.at[0],
        mem_ref.at[0], taps_ref.at[0], packed_ref.at[0, 0], keys_ref.at[0, 0], att_ref.at[0, 0], log_ref, grad_ref,
    )
    d_w_ref[0, PIECES * WIDE :] += dot_tn(att_ref[0, 0], grad_ref[...])
    d_w_ref[0, : PIECES * WIDE] += dot_tn(grad_packed, normed_ref[0])
    part = dot(grad_packed, w_ref[0, : PIECES * WIDE])[None]

    @pl.when(pair == 0)
    def _():
        grad_normed[here] = part

    @pl.when(pair > 0)
    def _():
        grad_normed[here] += part

    @pl.when(pair == pl.num_programs(0) - 1)
    def _():
        d_x_ref[0], d_gain = input_grad(x_ref[0], grad_normed[here][0], gain_ref, grad_ref[...])

        @pl.when(clip == 0)
        def _():
            d_gain_ref[...] = d_gain

        @pl.when(clip > 0)
        def _():
            d_gain_ref[...] += d_gain


def input_grad(x, grad_normed, gain_ref, grad_branch):
    rows = dot(reorder((ROWS, TPC), 0), x)
    pulled, d_gain = norm_pull(rows, as_row(gain_ref), grad_normed)
    d_x = (grad_branch.astype(F32) + pulled).astype(BF16)
    return dot(reorder((TPC, ROWS), 1), d_x).astype(BF16), d_gain


def backward_attention(
    pair, masks, proj_ref, d_taps_ref, mem_ref, taps_ref, packed_ref, keys_ref, att_ref, log_ref, grad_ref
):
    lane = lax.broadcasted_iota(jnp.int32, (ROWS, WIDE), 1) - PAIR * pair
    grad_out = dot_nt(grad_ref[...], proj_ref[...].reshape(PAIR * WIDE, -1))
    pieces = []
    for head in range(PAIR):
        base = 3 * WIDE * head
        query = packed_ref[:, base : base + WIDE]
        key = packed_ref[:, base + WIDE : base + 2 * WIDE].astype(F32)
        value = packed_ref[:, base + 2 * WIDE : base + 3 * WIDE].astype(F32)
        out_grad = grad_out[:, WIDE * head : WIDE * (head + 1)].astype(BF16)
        taps = widen(taps_ref[head])
        side_key = keys_ref[head, 0]
        side_value = keys_ref[head, 1]
        memory_t = mem_ref[head]
        log = jnp.sum(jnp.where(lane == head, log_ref[0], 0.0), axis=-1, keepdims=True)
        score_side = dot_nt(query, side_key) * (SCORE * LOG2E) + masks[0]
        score_main = dot(query, memory_t[:WIDE]) * (SCORE * LOG2E) + masks[1]
        weight_side = jnp.exp2(score_side - log)
        weight_main = jnp.exp2(score_main - log)
        grad_side = dot_nt(out_grad, side_value)
        grad_main = dot(out_grad, value_columns(memory_t))
        mixed = att_ref[:, WIDE * head : WIDE * (head + 1)].astype(F32) - query.astype(F32)
        inner = jnp.sum(out_grad.astype(F32) * mixed, axis=-1, keepdims=True)
        score_grad_side = (weight_side * (grad_side - inner)).astype(BF16)
        score_grad_main = (weight_main * (grad_main - inner)).astype(BF16)
        grad_query = (
            dot(score_grad_side, side_key) + dot_nt(score_grad_main, memory_t[:WIDE])
        ) * SCORE + out_grad.astype(F32)
        grad_key = dot_tn(score_grad_side, query)[:HALF] * SCORE
        grad_value = dot_tn(weight_side.astype(BF16), out_grad)[:HALF]
        pieces += [
            grad_query,
            jnp.concatenate([taps[0:1] * grad_key, taps[1:2] * grad_key], axis=0),
            jnp.concatenate([taps[2:3] * grad_value, taps[3:4] * grad_value], axis=0),
        ]
        d_taps_ref[head] += jnp.concatenate(
            [
                jnp.sum(part * grad, axis=0, keepdims=True)
                for part, grad in (
                    (key[:HALF], grad_key),
                    (key[HALF:], grad_key),
                    (value[:HALF], grad_value),
                    (value[HALF:], grad_value),
                )
            ],
            axis=0,
        )
    return jnp.concatenate(pieces, axis=1).astype(BF16)


def add_low(one, other):
    return (one.astype(F32) + other.astype(F32)).astype(BF16)


def unpad(ref, into, more=None):
    for piece in range(ref.shape[0] // WIDE):
        rows = ref[WIDE * piece : WIDE * piece + HD]
        narrow = slice(HD * piece, HD * (piece + 1))
        if more is not None:
            rows = rows + more[narrow].astype(F32)
        into[narrow] = rows.astype(BF16)


BACKWARD_COPIES = 112
CORE_LANES = 384
UNITS = (("p", 384, 384, "yz"), ("0", 576, 640, "yz"), ("1", 384, 384, "yz"), ("2", 192, 256, "zy"))
FAR = (("p", 384), ("0", 576), ("1", 576))


class AllReduce:
    def __init__(self, name, order, refs, links, partners):
        self.name, self.order, self.links = name, order, links
        self.own, self.core, self.got_y, self.got_z, self.whole = refs
        self.place = z, y, core, x, at = partners.place
        self.count = self.own.shape[0]
        mine, lanes = self.part(y, z), half_lanes(core)
        links.add("rc" + name, self.own.at[:, half_lanes(1 - core)], self.core, partners.core)
        if order == "yz":
            to_y, to_z = self.rows(1 - y, 2), [self.part(y, turn(z, shift)) for shift in (1, 2, 3)]
            spread = self.rows(y, 2)
        else:
            to_y, to_z = self.part(1 - y, z), [self.rows(turn(z, shift), 4) for shift in (1, 2, 3)]
            spread = self.rows(z, 4)
        links.add("ry" + name, self.own.at[to_y, lanes], self.got_y, partners.y)
        back_z, back_y = (mine, spread) if order == "yz" else (spread, mine)
        piece = self.whole.at[back_y, lanes]
        links.add("gy" + name, piece, piece, partners.y)
        for shift in (1, 2, 3):
            links.add(
                f"rz{shift}{name}", self.own.at[to_z[shift - 1], lanes], self.got_z.at[shift - 1], partners.along[shift - 1]
            )
            piece = self.whole.at[back_z, lanes]
            links.add(f"gz{shift}{name}", piece, piece, partners.along[shift - 1])
        piece = self.whole.at[:, lanes]
        links.add("gc" + name, piece, piece, partners.core)

    def rows(self, at, parts):
        size = self.count // parts
        return pl.ds(pl.multiple_of(at * size, size), size)

    def part(self, y, z):
        return self.rows(4 * y + z if self.order == "yz" else 2 * z + y, 8)

    def stage(self, which, axis):
        return [f"{which}z{shift}{self.name}" for shift in (1, 2, 3)] if axis == "z" else [which + "y" + self.name]

    def begin(self):
        self.links.start("rc" + self.name)

    def sum_core(self, far):
        lanes = half_lanes(self.place[2])
        self.links.arrived("rc" + self.name)
        rows = far.shape[0]
        total = self.own[:rows, lanes].astype(F32) + self.core[:rows].astype(F32) + far[...].astype(F32)
        self.own[:rows, lanes] = total.astype(BF16)
        self.links.start(*self.stage("r", self.order[0]))

    def taken(self, axis, rows):
        part = self.own[rows, half_lanes(self.place[2])].astype(F32)
        for got in [self.got_y] if axis == "y" else [self.got_z.at[shift] for shift in range(3)]:
            part = part + got[...].astype(F32)
        return part.astype(BF16)

    def sum_one(self):
        z, y, core, x, at = self.place
        axis = self.order[0]
        self.links.arrived(*self.stage("r", axis))
        rows = self.rows(y, 2) if axis == "y" else self.rows(z, 4)
        self.own[rows, half_lanes(core)] = self.taken(axis, rows)
        self.links.start(*self.stage("r", self.order[1]))

    def sum_two(self):
        z, y, core, x, at = self.place
        axis = self.order[1]
        self.links.arrived(*self.stage("r", axis))
        rows = self.part(y, z)
        self.whole[rows, half_lanes(core)] = self.taken(axis, rows)
        self.links.start(*self.stage("g", axis))

    def spread_one(self):
        self.links.arrived(*self.stage("g", self.order[1]))
        self.links.start(*self.stage("g", self.order[0]))

    def spread_core(self):
        self.links.arrived(*self.stage("g", self.order[0]))
        self.links.start("gc" + self.name)

    def done(self):
        self.links.arrived("gc" + self.name)


class Far:
    def __init__(self, name, refs, links, partners):
        self.name, self.links = name, links
        self.sent, self.core, self.got = refs
        self.place = z, y, core, x, at = partners.place
        links.add("hc" + name, self.sent.at[:, half_lanes(1 - core)], self.core, partners.core)
        links.add("hx" + name, self.sent.at[:, half_lanes(core)], self.got, partners.x)

    def begin(self):
        self.links.start("hc" + self.name)

    def pass_on(self):
        lanes = half_lanes(self.place[2])
        self.links.arrived("hc" + self.name)
        self.sent[:, lanes] = add_low(self.sent[:, lanes], self.core[...])
        self.links.start("hx" + self.name)


def half_lanes(core):
    return pl.ds(pl.multiple_of(core * CORE_LANES, CORE_LANES), CORE_LANES)


def narrow(value, into, first):
    for piece in range(value.shape[0] // WIDE):
        rows = value[WIDE * piece : WIDE * piece + HD]
        spot = slice(first + HD * piece, first + HD * (piece + 1))
        into[spot] = rows.astype(BF16)


def backward_links_kernel(
    index_ref, x_ref, qkv_ref, proj_ref, mem_ref, taps_ref, gain_ref,
    packed_ref, keys_ref, att_ref, log_ref, normed_ref, grad_ref, gain_two_ref,
    d_first, d_second,
    d_x_ref, small_out, first_out, second_out, proj_out, qkv_out,
    grad_packed, d_gain, d_taps,
    small_mine, small_far, small_got, small_all,
    first_result, second_result, send, recv, near, *rest,
):
    step = pl.program_id(0)
    last = pl.num_programs(0) - 1
    z, y, core, x, at = place()
    links = Links(send, recv)
    partners = Partners((z, y, core, x, at))
    late = TILES - EARLY
    first_refs, second_refs, rest = rest[:5], rest[5:10], rest[10:]
    loads = [
        pltpu.make_async_copy(d_first, first_refs[0], near.at[0]),
        pltpu.make_async_copy(d_second, second_refs[0], near.at[1]),
    ]
    sums = [
        (
            Sum(f"f{tile}", "xy", None, [ref.at[tile] for ref in first_refs], links, partners),
            Sum(f"s{tile}", "yx", EARLY + tile, [ref.at[tile] for ref in second_refs], links, partners),
        )
        for tile in range(late)
    ]
    first_done = [
        pltpu.make_async_copy(first_result.at[tile], first_out.at[:, pl.ds(tile * TILE, TILE)], near.at[2 + tile])
        for tile in range(late)
    ]
    second_done = pltpu.make_async_copy(second_result, second_out, near.at[2 + late])
    units, far = {}, {}
    for i, (name, _, _, order) in enumerate(UNITS):
        units[name] = AllReduce(name, order, rest[5 * i : 5 * i + 5], links, partners)
    rest = rest[5 * len(UNITS) :]
    for i, (name, _) in enumerate(FAR):
        far[name] = Far(name, rest[3 * i : 3 * i + 3], links, partners)
    targets = (proj_out, qkv_out.at[0], qkv_out.at[1, pl.ds(0, 384)], qkv_out.at[1, pl.ds(384, 192)])
    save = [
        pltpu.make_async_copy(units[name].whole.at[pl.ds(0, rows)], out, near.at[3 + late + i])
        for i, ((name, rows, _, _), out) in enumerate(zip(UNITS, targets))
    ]
    diagonal = at(z, y, 1 - core, 1 - x)
    links.add("mx", small_far, small_got.at[0], partners.x)
    links.add("md", small_far, small_got.at[1], diagonal)
    links.add("mc", small_mine, small_got.at[2], partners.core)
    spot = 2 * z + y
    others = []
    for shift in range(4):
        for flip in (0, 1):
            if shift or flip:
                other = at(turn(z, shift), y + flip - 2 * y * flip, core, x)
                links.add(f"ms{shift}{flip}", small_all.at[spot], small_all.at[spot], other)
                others.append(other)
    spread_small = [f"ms{shift}{flip}" for shift in range(4) for flip in (0, 1) if shift or flip]

    def proj_grads():
        grad = grad_ref[...].reshape(-1, grad_ref.shape[2])
        return [dot_tn(att_ref[pair].reshape(-1, PAIR * WIDE), grad) for pair in (0, 1)]

    p, zero, one, two = (units[unit[0]] for unit in UNITS)

    def sum_core(name, *parts):
        links.arrived("hx" + name)
        first = 0
        for part, rows in zip(parts, (384, 192) if len(parts) > 1 else (far[name].got.shape[0],)):
            part.sum_core(far[name].got.at[pl.ds(first, rows)])
            first += rows

    def far_proj():
        for pair, value in enumerate(proj_grads()):
            narrow(value, far["p"].sent, 192 * pair)
        far["p"].begin()

    def own_proj():
        for pair, value in enumerate(proj_grads()):
            narrow(value, units["p"].own, 192 * pair)
        units["p"].begin()

    def qkv_grad():
        width = normed_ref.shape[2]
        grad = grad_packed[lax.div(step, 4)].reshape(-1, PIECES * WIDE)
        return dot_tn(grad, normed_ref[...].reshape(-1, width))

    def far_qkv(name):
        narrow(qkv_grad(), far[name].sent, 0)
        far[name].begin()

    def own_qkv(name):
        grad = qkv_grad()
        if name == "0":
            narrow(grad, zero.own, 0)
            zero.begin()
        else:
            narrow(grad[: 4 * WIDE], one.own, 0)
            narrow(grad[4 * WIDE :], two.own, 0)
            one.begin()
            two.begin()

    def begin():
        greet([partners.x, partners.core, diagonal] + others)
        for copy in loads:
            copy.start()
        d_gain[...] = jnp.zeros_like(d_gain)
        d_taps[...] = jnp.zeros_like(d_taps)
        for name, rows, padded, _ in UNITS:
            if padded > rows:
                units[name].own[rows:] = jnp.zeros((padded - rows, units[name].own.shape[1]), BF16)

    def begin_sums():
        for copy in loads:
            copy.wait()
        for pair in sums:
            for one in pair:
                one.begin()

    def all_sums(stage):
        for pair in sums:
            for one in pair:
                getattr(one, stage)()

    def finish():
        for tile, (one, two) in enumerate(sums):
            one.finish(first_result.at[tile])
            first_done[tile].start()

            @pl.when(z == EARLY + tile)
            def _(two=two):
                two.finish(second_result)
                second_done.start()

    def at_steps(plan):
        for when, acts in plan.items():

            @pl.when(step == when)
            def _(acts=acts):
                for act in acts:
                    act()

    at_steps({0: [begin, far_proj], 8: [own_proj]})

    @pl.when(step < 16)
    def _():
        pair = lax.rem(lax.div(step, 4) + 2, 4)
        clip = lax.rem(step, 4)
        here = pl.ds(clip, 1)
        grad_packed[lax.div(step, 4), here] = backward_attention(
            pair, mask_rows(index_ref[x, clip]), proj_ref.at[0], d_taps.at[lax.div(step, 4)],
            mem_ref.at[0], taps_ref.at[0], packed_ref.at[0, 0], keys_ref.at[0, 0], att_ref.at[lax.rem(pair, 2), clip], log_ref,
            grad_ref.at[clip],
        )[None]

    @pl.when(step >= 16)
    def _():
        clip = step - 16
        grad = [
            dot(grad_packed[slot, clip], qkv_ref[(slot + 2) % 4].reshape(PIECES * WIDE, -1)) for slot in range(4)
        ]
        grad = (grad[0] + grad[1]) + (grad[2] + grad[3])
        d_x_ref[0], gain = input_grad(x_ref[0], grad, gain_ref, grad_ref[clip])
        d_gain[...] += gain

    at_steps(
        {
            0: [begin_sums],
            1: [far["p"].pass_on],
            2: [lambda: all_sums("core")],
            3: [lambda: far_qkv("0")],
            4: [far["0"].pass_on],
            5: [lambda: all_sums("first")],
            7: [lambda: far_qkv("1")],
            8: [far["1"].pass_on, lambda: all_sums("second")],
            9: [lambda: sum_core("p", p)],
            11: [lambda: own_qkv("0"), p.sum_one],
            12: [lambda: sum_core("0", zero), finish],
            13: [p.sum_two],
            14: [zero.sum_one, p.spread_one],
            15: [lambda: own_qkv("1"), zero.sum_two, p.spread_core],
            16: [lambda: sum_core("1", one, two), zero.spread_one],
            17: [one.sum_one, two.sum_one, p.done, save[0].start],
            18: [one.sum_two, two.sum_two, zero.spread_core],
        }
    )

    @pl.when(step == last)
    def _():
        for i, target in ((2, small_mine), (0, small_far)):
            target[...] = jnp.zeros_like(target)
            target[0:1] = d_gain[...]
            target[1:2] = gain_two_ref[...]
            for j in (0, 1):
                target[8:16, WIDE * j : WIDE * (j + 1)] = d_taps[i + j].reshape(8, WIDE)
        links.start("mx", "md", "mc")
        one.spread_one()
        two.spread_one()
        links.arrived("mx", "md", "mc")
        small_all[pl.ds(spot, 1)] = ((small_mine[...] + small_got[2]) + (small_got[0] + small_got[1]))[None]
        links.start(*spread_small)
        zero.done()
        save[1].start()
        one.spread_core()
        two.spread_core()
        links.arrived(*spread_small)
        total = small_all[0]
        for i in range(1, 8):
            total = total + small_all[i]
        small_out[...] = total
        one.done()
        two.done()
        save[2].start()
        save[3].start()
        for copy in save + first_done:
            copy.wait()
        for tile in range(late):
            pl.when(z == EARLY + tile)(lambda: second_done.wait())
        links.sent()


VMEM_LIMIT = 60 << 20
CHUNK = 800
TILE = 768
TILES = 4
EARLY = 2


def compiler_params(dims):
    return pltpu.CompilerParams(
        dimension_semantics=("arbitrary",) * dims, vmem_limit_bytes=VMEM_LIMIT
    )


def shaped(shape, dtype):
    return jax.ShapeDtypeStruct(shape, dtype)


class Links:
    def __init__(self, send, recv):
        self.send, self.recv, self.made = send, recv, {}

    def add(self, name, src, dst, device, send_if=None, recv_if=None):
        at = len(self.made)
        self.made[name] = (src, dst, device, at, send_if, recv_if)

    def get(self, name):
        src, dst, device, at = self.made[name][:4]
        return pltpu.make_async_remote_copy(
            src_ref=src,
            dst_ref=dst,
            send_sem=self.send.at[at],
            recv_sem=self.recv.at[at],
            device_id=device,
            device_id_type=pl.DeviceIdType.MESH,
        )

    def start(self, *names):
        for name in names:
            self.only(self.made[name][4], self.get(name).start)

    def arrived(self, *names):
        for name in names:
            self.only(self.made[name][5], self.get(name).wait_recv)

    def sent(self):
        for name in self.made:
            self.only(self.made[name][4], self.get(name).wait_send)

    def only(self, condition, act):
        if condition is None:
            act()
        else:
            pl.when(condition)(lambda: act())


def place():
    batch, head = lax.axis_index("batch"), lax.axis_index("head")
    z, y, core = batch // 4, lax.rem(batch // 2, 2), lax.rem(batch, 2)

    def at(z, y, core, x):
        return {"batch": (z * 2 + y) * 2 + core, "head": x}

    return z, y, core, head, at


def greet(devices):
    barrier = pltpu.get_barrier_semaphore()
    for device in devices:
        pl.semaphore_signal(barrier, inc=1, device_id=device, device_id_type=pl.DeviceIdType.MESH)
    pl.semaphore_wait(barrier, len(devices))


def turn(z, shift):
    return lax.rem(z + shift + 4, 4)


FORWARD_COPIES = 96
SPLIT = HD // 2


def forward_links_kernel(
    index_ref, x_ref, cot_ref, gain_one_ref, gain_two_ref,
    qkv_own, proj_own, mem_own, tail_own, taps_own, hidden_own, output_own,
    packed_ref, keys_ref, att_ref, log_ref, normed_ref, middle_ref, normed_two_ref, cot_out,
    first_all, second_all, qkv_out, proj_out, mem_out, taps_out,
    x_rows, normed_rows, branch, logs, qkv_all, proj_all, mem_all, tail_all, taps_all,
    send, recv, near, save,
):
    step = pl.program_id(0)
    z, y, core, x, at = place()
    links = Links(send, recv)
    beside, above, sibling = at(z, y, core, 1 - x), at(z, 1 - y, core, x), at(z, y, 1 - core, x)
    higher, lower = at(turn(z, 1), y, core, x), at(turn(z, -1), y, core, x)
    column = pl.ds(pl.multiple_of(core * MAIN, MAIN), MAIN)
    me = ((z * 2 + y) * 2 + core) * 2 + x
    clips = mem_own.shape[0]

    def split(z, y, *between):
        rows = pl.ds(pl.multiple_of(y * SPLIT, SPLIT), SPLIT)
        return (lax.div(z, 2), lax.rem(z, 2)) + between + (rows, column)

    def block(kind, z, y):
        if kind == "q":
            return qkv_all.at[pl.ds(2, 2)].at[split(z, y, slice(None))]
        if kind == "p":
            return proj_all.at[pl.ds(2, 2)].at[split(z, y)]
        return (first_all if kind == "0" else second_all).at[pl.ds(((z * 2 + y) * 2 + core) * 2, 2)]

    links.add("xq", qkv_own.at[split(z, y, slice(None))], block("q", z, y), beside)
    links.add("xp", proj_own.at[split(z, y)], block("p", z, y), beside)
    links.add("x0", hidden_own, first_all.at[me], beside)
    links.add("x1", output_own, second_all.at[me], beside)
    for kind in "qp01":
        mine = block(kind, z, y)
        links.add("y" + kind, mine, mine, above)
        if kind in "01":
            links.add("c" + kind, mine, mine, sibling)
            mine = block(kind, z, 1 - y)
            links.add("e" + kind, mine, mine, sibling)
        for hop in (1, 2, 3):
            below, beyond = z >= hop, z + hop <= 3
            passed = block(kind, turn(z, 1 - hop), y)
            links.add(f"u{hop}{kind}", passed, passed, higher, (z <= 2) & (z >= hop - 1), below)
            passed = block(kind, turn(z, hop - 1), y)
            links.add(f"d{hop}{kind}", passed, passed, lower, (z >= 1) & (z + hop <= 4), beyond)
            for side, shift, there in (("u", -hop, below), ("d", hop, beyond)):
                came = block(kind, turn(z, shift), y)
                links.add(f"y{side}{hop}{kind}", came, came, above, there, there)
                if kind in "01":
                    links.add(f"c{side}{hop}{kind}", came, came, sibling, there, there)
                    came = block(kind, turn(z, shift), 1 - y)
                    links.add(f"e{side}{hop}{kind}", came, came, sibling, there, there)
    far = qkv_all.at[pl.ds(2, 2), :, :, pl.ds(0, HD), column]
    links.add("cq", far, far, sibling)
    far = proj_all.at[pl.ds(2, 2), :, pl.ds(0, HD), column]
    links.add("cp", far, far, sibling)
    for clip in range(clips):
        links.add(f"m{clip}", mem_own.at[clip, 1 - x, :, :, pl.ds(0, MAIN)], mem_all.at[1, clip], beside)
    links.add("tail", tail_own.at[:, 1 - x], tail_all.at[1], beside)
    links.add("taps", taps_own, taps_all.at[pl.ds(2, 2)], beside)

    local = [
        (qkv_own, qkv_all.at[pl.ds(0, 2), :, :, pl.ds(0, HD)]),
        (proj_own, proj_all.at[pl.ds(0, 2), :, pl.ds(0, HD)]),
        (tail_own.at[:, x], tail_all.at[0]),
        (taps_own, taps_all.at[pl.ds(0, 2)]),
        (mem_own.at[0, x, :, :, pl.ds(0, MAIN)], mem_all.at[0, 0]),
        (hidden_own, first_all.at[me]),
        (output_own, second_all.at[me]),
    ] + [(mem_own.at[clip, x, :, :, pl.ds(0, MAIN)], mem_all.at[0, clip]) for clip in range(1, clips)]
    local = [pltpu.make_async_copy(src, dst, near.at[i]) for i, (src, dst) in enumerate(local)]
    saved = [
        (qkv_all, qkv_out),
        (proj_all, proj_out),
        (taps_all, taps_out),
        (mem_all.at[0], mem_out.at[0]),
    ] + [(mem_all.at[1, clip], mem_out.at[1, clip]) for clip in range(clips)]
    saved = [pltpu.make_async_copy(src, dst, save.at[i]) for i, (src, dst) in enumerate(saved)]

    @pl.when(step == 0)
    def _():
        greet([beside, above, sibling, higher, lower])
        links.start("xq", "xp", "taps", "tail", "x0", "x1")
        for copy in local:
            copy.start()

        @pl.loop(0, 4)
        def _(pair):
            for head in range(PAIR):
                for piece in range(3):
                    qkv_all[pair, head, piece, HD:] = jnp.zeros((WIDE - HD, qkv_all.shape[-1]), BF16)
                proj_all[pair, head, HD:] = jnp.zeros((WIDE - HD, qkv_all.shape[-1]), BF16)

        for copy in local[:5]:
            copy.wait()

    def settle():
        for copy in local[5:]:
            copy.wait()
        saved[3].start()

    def hop(number, kinds):
        for kind in kinds:
            links.arrived(f"u{number}{kind}", f"d{number}{kind}")
            if number < 3:
                links.start(f"u{number + 1}{kind}", f"d{number + 1}{kind}")
            links.start(f"yu{number}{kind}", f"yd{number}{kind}")
            if kind in "01":
                links.start(f"cu{number}{kind}", f"cd{number}{kind}")

    def begin(kinds):
        for kind in kinds:
            links.arrived("x" + kind)
            links.start("u1" + kind, "d1" + kind, "y" + kind)
            if kind in "01":
                links.start("c" + kind)

    def across(number, kinds):
        for kind in kinds:
            for side in ("u", "d") if number else ("",):
                name = f"{side}{number}{kind}" if number else kind
                links.arrived("y" + name)
                if kind in "01":
                    links.start("e" + name)

    def weights():
        for number in range(4):
            across(number, "qp")
        links.start("cq", "cp")
        links.arrived("cq", "cp", "tail", "taps")

    def memory(clip):
        links.arrived(f"m{clip}")
        if clip + 2 < clips:
            links.start(f"m{clip + 2}")
        saved[4 + clip].start()

    plan = {
        1: [settle, lambda: begin("qp"), lambda: links.start("m0")],
        2: [lambda: begin("01")],
        3: [lambda: hop(1, "qp")],
        5: [lambda: hop(2, "qp"), lambda: links.start("m1")],
        6: [lambda: hop(3, "qp")],
        7: [lambda: hop(1, "0")],
        8: [weights, lambda: hop(1, "1"), lambda: memory(0)],
        9: [copy.start for copy in saved[:3]],
        10: [lambda: hop(2, "0"), lambda: memory(1)],
        11: [lambda: hop(2, "1"), lambda: across(0, "01")],
        12: [lambda: across(1, "0"), lambda: memory(2)],
        13: [lambda: hop(3, "0"), lambda: across(1, "1")],
        14: [lambda: hop(3, "1"), lambda: across(2, "0"), lambda: memory(3)],
    }
    for when, acts in plan.items():

        @pl.when(step == when)
        def _(acts=acts):
            for act in acts:
                act()

    pair, clip = pair_of(step), clip_of(step)
    side = lax.div(pair, 2)
    heads = pl.ds(lax.rem(pair, 2) * PAIR, PAIR)
    forward_step(
        pair, clip, 4, mask_rows(index_ref[x, clip]),
        qkv_all.at[pair], proj_all.at[pair],
        mem_all.at[side, clip, heads], tail_all.at[side, clip, heads], taps_all.at[pair],
        x_ref, cot_ref, gain_one_ref, gain_two_ref,
        packed_ref, keys_ref, att_ref, log_ref, normed_ref, middle_ref, normed_two_ref, cot_out,
        x_rows, normed_rows, branch, logs,
    )

    @pl.when(step == pl.num_programs(0) - 1)
    def _():
        across(2, "1")
        across(3, "01")
        for copy in saved:
            copy.wait()
        for kind in "01":
            links.arrived("c" + kind, "e" + kind)
            for number in (1, 2, 3):
                for side in "ud":
                    links.arrived(f"c{side}{number}{kind}", f"e{side}{number}{kind}")
        links.sent()


def pair_of(step):
    return jnp.where(step < 8, lax.div(step, 4), 2 + lax.rem(step, 2))


def clip_of(step):
    return jnp.where(step < 8, lax.rem(step, 4), lax.div(step, 2) - 4)


def attention_forward_links(
    index, x, cot, qkv, proj, mem, tail, taps, gain_one, gain_two, hidden_weight, output_weight
):
    clips, width = x.shape[0], x.shape[2]
    packed_width = PIECES * WIDE
    devices = 32
    early = lambda s: jnp.where(s < 4, s, clips - 1)
    late = lambda s: jnp.where(s < 8, 0, clip_of(s))
    anywhere = pl.BlockSpec(memory_space=pl.ANY)
    return pl.pallas_call(
        forward_links_kernel,
        grid=(4 * clips,),
        in_specs=[
            pl.BlockSpec(memory_space=pltpu.SMEM),
            pl.BlockSpec((1, TPC, width), lambda s: (early(s), 0, 0)),
            pl.BlockSpec((1, TPC, width), lambda s: (late(s), 0, 0)),
            pl.BlockSpec(gain_one.shape, lambda s: (0,)),
            pl.BlockSpec(gain_two.shape, lambda s: (0,)),
        ] + [anywhere] * 5 + [
            pl.BlockSpec(hidden_weight.shape, lambda s: (0, 0)),
            pl.BlockSpec(output_weight.shape, lambda s: (0, 0)),
        ],
        out_specs=[
            pl.BlockSpec((1, 1, ROWS, packed_width), lambda s: (pair_of(s), clip_of(s), 0, 0)),
            pl.BlockSpec((1, 1, PAIR, 2, SIDE, WIDE), lambda s: (pair_of(s), clip_of(s), 0, 0, 0, 0)),
            pl.BlockSpec((1, 1, ROWS, PAIR * WIDE), lambda s: (pair_of(s), clip_of(s), 0, 0)),
            pl.BlockSpec((1, ROWS, WIDE), lambda s: (late(s), 0, 0)),
            pl.BlockSpec((1, ROWS, width), lambda s: (early(s), 0, 0)),
            pl.BlockSpec((1, ROWS, width), lambda s: (late(s), 0, 0)),
            pl.BlockSpec((1, ROWS, width), lambda s: (late(s), 0, 0)),
            pl.BlockSpec((1, ROWS, width), lambda s: (late(s), 0, 0)),
        ] + [anywhere] * 6,
        out_shape=[
            shaped((4, clips, ROWS, packed_width), BF16),
            shaped((4, clips, PAIR, 2, SIDE, WIDE), BF16),
            shaped((4, clips, ROWS, PAIR * WIDE), BF16),
            shaped((clips, ROWS, WIDE), F32),
            shaped((clips, ROWS, width), BF16),
            shaped((clips, ROWS, width), F32),
            shaped((clips, ROWS, width), BF16),
            shaped((clips, ROWS, width), BF16),
            shaped((devices,) + hidden_weight.shape, BF16),
            shaped((devices,) + output_weight.shape, BF16),
            shaped((4, PAIR, 3, WIDE, width), BF16),
            shaped((4, PAIR, WIDE, width), BF16),
            shaped((2, clips, 4, 2 * HD, MAIN), BF16),
            shaped((4,) + taps.shape[1:], F32),
        ],
        scratch_shapes=[
            pltpu.VMEM((clips, ROWS, width), BF16),
            pltpu.VMEM((clips, ROWS, width), BF16),
            pltpu.VMEM((clips, ROWS, width), F32),
            pltpu.VMEM((clips, ROWS, WIDE), F32),
            pltpu.VMEM((4, PAIR, 3, WIDE, width), BF16),
            pltpu.VMEM((4, PAIR, WIDE, width), BF16),
            pltpu.VMEM((2, clips, 4, 2 * HD, MAIN), BF16),
            pltpu.VMEM((2, clips, 4, 2 * REST, WIDE), BF16),
            pltpu.VMEM((4,) + taps.shape[1:], F32),
            pltpu.SemaphoreType.DMA((FORWARD_COPIES,)),
            pltpu.SemaphoreType.DMA((FORWARD_COPIES,)),
            pltpu.SemaphoreType.DMA((6 + clips,)),
            pltpu.SemaphoreType.DMA((4 + clips,)),
        ],
        compiler_params=pltpu.CompilerParams(
            dimension_semantics=("arbitrary",),
            vmem_limit_bytes=VMEM_LIMIT,
            collective_id=0,
            has_side_effects=True,
        ),
        name="attention_forward_links",
    )(index, x, cot, gain_one, gain_two, qkv, proj, mem, tail, taps, hidden_weight, output_weight)


def attention_forward(x, cot, w, mem, tail, side, main, taps, gain_one, gain_two):
    clips, pairs = x.shape[0], w.shape[0]
    width = x.shape[2]
    packed_width = PIECES * WIDE
    weight_rows = w.shape[1]
    late = lambda p, c: jnp.where(p == pairs - 1, c, 0)
    early = lambda p, c: jnp.where(p == 0, c, clips - 1)
    per_step = lambda p, c: (p, c)
    return pl.pallas_call(
        forward_kernel,
        grid=(pairs, clips),
        in_specs=[
            pl.BlockSpec((1, TPC, width), lambda p, c: (early(p, c), 0, 0)),
            pl.BlockSpec((1, TPC, width), lambda p, c: (late(p, c), 0, 0)),
            pl.BlockSpec((1, weight_rows, width), lambda p, c: (p, 0, 0)),
            pl.BlockSpec((1, PAIR, 2 * HD, MAIN), lambda p, c: (c, p, 0, 0)),
            pl.BlockSpec((1, PAIR, 2 * REST, WIDE), lambda p, c: (c, p, 0, 0)),
            pl.BlockSpec((1, 1, SIDE), lambda p, c: (c, 0, 0)),
            pl.BlockSpec((1, 1, MAIN), lambda p, c: (c, 0, 0)),
            pl.BlockSpec((1, PAIR, 4, HD), lambda p, c: (p, 0, 0, 0)),
            pl.BlockSpec(gain_one.shape, lambda p, c: (0,)),
            pl.BlockSpec(gain_two.shape, lambda p, c: (0,)),
        ],
        out_specs=[
            pl.BlockSpec((1, 1, ROWS, packed_width), lambda p, c: (p, c, 0, 0)),
            pl.BlockSpec((1, 1, PAIR, 2, SIDE, WIDE), lambda p, c: (p, c, 0, 0, 0, 0)),
            pl.BlockSpec((1, 1, ROWS, PAIR * WIDE), lambda p, c: (p, c, 0, 0)),
            pl.BlockSpec((1, ROWS, WIDE), lambda p, c: (late(p, c), 0, 0)),
            pl.BlockSpec((1, ROWS, width), lambda p, c: (early(p, c), 0, 0)),
            pl.BlockSpec((1, ROWS, width), lambda p, c: (late(p, c), 0, 0)),
            pl.BlockSpec((1, ROWS, width), lambda p, c: (late(p, c), 0, 0)),
            pl.BlockSpec((1, ROWS, width), lambda p, c: (late(p, c), 0, 0)),
        ],
        out_shape=[
            shaped((pairs, clips, ROWS, packed_width), BF16),
            shaped((pairs, clips, PAIR, 2, SIDE, WIDE), BF16),
            shaped((pairs, clips, ROWS, PAIR * WIDE), BF16),
            shaped((clips, ROWS, WIDE), F32),
            shaped((clips, ROWS, width), BF16),
            shaped((clips, ROWS, width), F32),
            shaped((clips, ROWS, width), BF16),
            shaped((clips, ROWS, width), BF16),
        ],
        scratch_shapes=[
            pltpu.VMEM((clips, ROWS, width), BF16),
            pltpu.VMEM((clips, ROWS, width), BF16),
            pltpu.VMEM((clips, ROWS, width), F32),
            pltpu.VMEM((clips, ROWS, WIDE), F32),
        ],
        compiler_params=compiler_params(2),
        name="attention_forward",
    )(x, cot, w, mem, tail, side, main, taps, gain_one, gain_two)


def once(shape):
    return pl.BlockSpec(shape, lambda t: (0,) * len(shape), pipeline_mode=pl.Buffered(1))


def mlp(normed, cot, first, second, middle, gain):
    rows, width = normed.shape
    hidden = first.shape[1]
    clips = rows // ROWS
    tiles = hidden // TILE
    tile_at = lambda t: jnp.minimum(t, tiles - 1)
    clip_at = lambda t: jnp.maximum(t - tiles, 0)
    return pl.pallas_call(
        mlp_kernel,
        grid=(tiles + clips,),
        in_specs=[
            once((rows, width)),
            once((rows, width)),
            pl.BlockSpec((width, TILE), lambda t: (0, tile_at(t))),
            pl.BlockSpec((TILE, width), lambda t: (tile_at(t), 0)),
            pl.BlockSpec(memory_space=pl.ANY),
            pl.BlockSpec(gain.shape, lambda t: (0,)),
        ],
        out_specs=[
            pl.BlockSpec((1, TPC, width), lambda t: (clip_at(t), 0, 0)),
            pl.BlockSpec((ROWS, width), lambda t: (clip_at(t), 0)),
            pl.BlockSpec((width, TILE), lambda t: (0, tile_at(t))),
            pl.BlockSpec((TILE, width), lambda t: (tile_at(t), 0)),
            once((1, width)),
        ],
        out_shape=[
            shaped((clips, TPC, width), BF16),
            shaped((rows, width), BF16),
            shaped((width, hidden), BF16),
            shaped((hidden, width), BF16),
            shaped((1, width), F32),
        ],
        scratch_shapes=[
            pltpu.VMEM((rows, width), F32),
            pltpu.VMEM((rows, width), F32),
            pltpu.VMEM((rows, width), F32),
            pltpu.VMEM((rows, TILE), BF16),
            pltpu.VMEM((rows, TILE), BF16),
            pltpu.SemaphoreType.DMA((1,)),
        ],
        compiler_params=compiler_params(1),
        name="mlp",
    )(normed, cot, first, second, middle, gain)


def sum_scratch(lead, planes, shape):
    return [
        pltpu.VMEM(lead + dims + shape, BF16)
        for dims in ((planes, 2, 2, 2), (planes, 2, 2), (planes, 2), (planes,), (3,))
    ]


def mlp_links(normed, cot, first, second, middle, gain):
    rows, width = normed.shape
    hidden = first.shape[1]
    clips = rows // ROWS
    tile_at = lambda t: jnp.minimum(t, TILES - 1)
    clip_at = lambda t: jnp.maximum(t - TILES, 0)
    first_rows, second_rows = width // 32, hidden // 32
    anywhere = pl.BlockSpec(memory_space=pl.ANY)
    return pl.pallas_call(
        mlp_links_kernel,
        grid=(TILES + clips,),
        in_specs=[
            once((rows, width)),
            once((rows, width)),
            pl.BlockSpec((width, TILE), lambda t: (0, tile_at(t))),
            pl.BlockSpec((TILE, width), lambda t: (tile_at(t), 0)),
            anywhere,
            pl.BlockSpec(gain.shape, lambda t: (0,)),
        ],
        out_specs=[
            pl.BlockSpec((1, TPC, width), lambda t: (clip_at(t), 0, 0)),
            pl.BlockSpec((ROWS, width), lambda t: (clip_at(t), 0)),
            once((1, width)),
        ] + [anywhere] * 4,
        out_shape=[
            shaped((clips, TPC, width), BF16),
            shaped((rows, width), BF16),
            shaped((1, width), F32),
            shaped((first_rows, EARLY * TILE), F32),
            shaped((second_rows, width), F32),
            shaped((TILES - EARLY, 4, 2, 2, 2, first_rows, TILE), BF16),
            shaped((TILES - EARLY, 1, 2, 2, 2, second_rows, width), BF16),
        ],
        scratch_shapes=[
            pltpu.VMEM((rows, width), F32),
            pltpu.VMEM((rows, width), F32),
            pltpu.VMEM((rows, width), F32),
            pltpu.VMEM((rows, TILE), BF16),
            pltpu.VMEM((rows, TILE), BF16),
            pltpu.SemaphoreType.DMA((1,)),
        ]
        + sum_scratch((EARLY,), 4, (first_rows, TILE))
        + sum_scratch((EARLY,), 1, (second_rows, width))
        + [
            pltpu.VMEM((TILES - EARLY, 4, 2, 2, 2, first_rows, TILE), BF16),
            pltpu.VMEM((TILES - EARLY, 1, 2, 2, 2, second_rows, width), BF16),
            pltpu.VMEM((EARLY, first_rows, TILE), F32),
            pltpu.VMEM((second_rows, width), F32),
            pltpu.SemaphoreType.DMA((12 * EARLY,)),
            pltpu.SemaphoreType.DMA((12 * EARLY,)),
            pltpu.SemaphoreType.DMA((2 * TILES,)),
        ],
        compiler_params=pltpu.CompilerParams(
            dimension_semantics=("arbitrary",),
            vmem_limit_bytes=VMEM_LIMIT,
            collective_id=2,
            has_side_effects=True,
        ),
        name="mlp_links",
    )(normed, cot, first, second, middle, gain)


def attention_backward(x, w, mem, side, main, taps, gain, packed, keys, att, log, normed, grad):
    clips, pairs = x.shape[0], w.shape[0]
    width = x.shape[2]
    packed_width = PIECES * WIDE
    weight_rows = w.shape[1]
    late = lambda p, c: jnp.where(p == pairs - 1, c, 0)
    return pl.pallas_call(
        backward_kernel,
        grid=(pairs, clips),
        in_specs=[
            pl.BlockSpec((1, TPC, width), lambda p, c: (late(p, c), 0, 0)),
            pl.BlockSpec((1, weight_rows, width), lambda p, c: (p, 0, 0)),
            pl.BlockSpec((1, PAIR, 2 * HD, MAIN), lambda p, c: (c, p, 0, 0)),
            pl.BlockSpec((1, 1, SIDE), lambda p, c: (c, 0, 0)),
            pl.BlockSpec((1, 1, MAIN), lambda p, c: (c, 0, 0)),
            pl.BlockSpec((1, PAIR, 4, HD), lambda p, c: (p, 0, 0, 0)),
            pl.BlockSpec(gain.shape, lambda p, c: (0,)),
            pl.BlockSpec((1, 1, ROWS, packed_width), lambda p, c: (p, c, 0, 0)),
            pl.BlockSpec((1, 1, PAIR, 2, SIDE, WIDE), lambda p, c: (p, c, 0, 0, 0, 0)),
            pl.BlockSpec((1, 1, ROWS, PAIR * WIDE), lambda p, c: (p, c, 0, 0)),
            pl.BlockSpec((1, ROWS, WIDE), lambda p, c: (c, 0, 0)),
            pl.BlockSpec((1, ROWS, width), lambda p, c: (c, 0, 0)),
            pl.BlockSpec((ROWS, width), lambda p, c: (c, 0)),
        ],
        out_specs=[
            pl.BlockSpec((1, TPC, width), lambda p, c: (late(p, c), 0, 0)),
            pl.BlockSpec((1, weight_rows, width), lambda p, c: (p, 0, 0)),
            pl.BlockSpec((1, PAIR, 4, WIDE), lambda p, c: (p, 0, 0, 0)),
            pl.BlockSpec((1, width), lambda p, c: (0, 0)),
        ],
        out_shape=[
            shaped((clips, TPC, width), BF16),
            shaped((pairs, weight_rows, width), F32),
            shaped((pairs, PAIR, 4, WIDE), F32),
            shaped((1, width), F32),
        ],
        scratch_shapes=[pltpu.VMEM((clips, ROWS, width), F32)],
        compiler_params=compiler_params(2),
        name="attention_backward",
    )(x, w, mem, side, main, taps, gain, packed, keys, att, log, normed, grad)


def attention_backward_links(
    index, x, qkv, proj, mem, taps, gain, packed, keys, att, log, normed, grad, gain_two, d_first, d_second
):
    clips, width = x.shape[0], x.shape[2]
    packed_width = PIECES * WIDE
    steps = 4 * clips
    early = lambda s: jnp.minimum(s, steps - 1)
    pair_at = lambda s: lax.rem(lax.div(early(s), clips) + 2, 4)
    clip_at = lambda s: lax.rem(early(s), clips)
    late = lambda s: jnp.maximum(s - steps, 0)
    anywhere = pl.BlockSpec(memory_space=pl.ANY)
    per_step = lambda s: (pair_at(s), clip_at(s), 0, 0)
    small = (16, width)
    left = d_first.shape[0]
    first_shape, second_shape = d_first.shape[-2:], d_second.shape[-2:]
    units = []
    for _, _, padded, order in UNITS:
        one, three = (2, 8) if order == "yz" else (8, 4)
        units += [
            pltpu.VMEM(shape, BF16)
            for shape in (
                (padded, width), (padded, CORE_LANES), (padded // one, CORE_LANES), (3, padded // three, CORE_LANES),
                (padded, width),
            )
        ]
    for _, rows in FAR:
        units += [pltpu.VMEM(shape, BF16) for shape in ((rows, width), (rows, CORE_LANES), (rows, CORE_LANES))]
    return pl.pallas_call(
        backward_links_kernel,
        grid=(steps + clips,),
        in_specs=[
            pl.BlockSpec(memory_space=pltpu.SMEM),
            pl.BlockSpec((1, TPC, width), lambda s: (late(s), 0, 0)),
            once(qkv.shape),
            pl.BlockSpec((1,) + proj.shape[1:], lambda s: (pair_at(s), 0, 0, 0)),
            pl.BlockSpec(
                (None, 1, PAIR, 2 * HD, MAIN),
                lambda s: (lax.div(pair_at(s), 2), clip_at(s), lax.rem(pair_at(s), 2), 0, 0),
            ),
            pl.BlockSpec((1, PAIR, 4, HD), lambda s: (pair_at(s), 0, 0, 0)),
            pl.BlockSpec(gain.shape, lambda s: (0,)),
            pl.BlockSpec((1, 1, ROWS, packed_width), per_step),
            pl.BlockSpec((1, 1, PAIR, 2, SIDE, WIDE), lambda s: per_step(s) + (0, 0)),
            pl.BlockSpec((2, clips, ROWS, PAIR * WIDE), lambda s: (lax.div(pair_at(s), 2), 0, 0, 0)),
            pl.BlockSpec((1, ROWS, WIDE), lambda s: (clip_at(s), 0, 0)),
            once((clips, ROWS, width)),
            once((clips, ROWS, width)),
            pl.BlockSpec((1, width), lambda s: (0, 0)),
            anywhere,
            anywhere,
        ],
        out_specs=[
            pl.BlockSpec((1, TPC, width), lambda s: (late(s), 0, 0)),
            pl.BlockSpec(small, lambda s: (0, 0)),
        ] + [anywhere] * 4,
        out_shape=[
            shaped((clips, TPC, width), BF16),
            shaped(small, F32),
            shaped((first_shape[0], left * TILE), F32),
            shaped(second_shape, F32),
            shaped((UNITS[0][1], width), BF16),
            shaped((2, UNITS[1][1], width), BF16),
        ],
        scratch_shapes=[
            pltpu.VMEM((4, clips, ROWS, packed_width), BF16),
            pltpu.VMEM((1, width), F32),
            pltpu.VMEM((4, PAIR, 4, WIDE), F32),
        ]
        + [pltpu.VMEM(small, F32)] * 2
        + [
            pltpu.VMEM((3,) + small, F32),
            pltpu.VMEM((8,) + small, F32),
            pltpu.VMEM((left,) + first_shape, F32),
            pltpu.VMEM(second_shape, F32),
            pltpu.SemaphoreType.DMA((BACKWARD_COPIES,)),
            pltpu.SemaphoreType.DMA((BACKWARD_COPIES,)),
            pltpu.SemaphoreType.DMA((7 + left,)),
        ]
        + sum_scratch((left,), 4, first_shape)
        + sum_scratch((left,), 1, second_shape)
        + units,
        compiler_params=pltpu.CompilerParams(
            dimension_semantics=("arbitrary",),
            vmem_limit_bytes=VMEM_LIMIT,
            collective_id=1,
            has_side_effects=True,
        ),
        name="attention_backward_links",
    )(index, x, qkv, proj, mem, taps, gain, packed, keys, att, log, normed, grad, gain_two, d_first, d_second)


def group_gather(own, heads, fetch=None):
    blocks = [fetch(own, 0) if fetch else own]
    for shift in range(1, heads):
        sent = fetch(own, -shift) if fetch else own
        blocks.append(lax.ppermute(sent, "head", [(src, (src - shift) % heads) for src in range(heads)]))
    return blocks


def group_sum(blocks, heads):
    total = blocks[0]
    for shift in range(1, heads):
        total = total + lax.ppermute(
            blocks[shift].astype(BF16), "head", [(src, (src + shift) % heads) for src in range(heads)]
        ).astype(F32)
    return total


def local(
    heads,
    batches,
    inputs,
    qkv_weight,
    proj_weight,
    pool_weight,
    gain_one,
    gain_two,
    hidden_weight,
    output_weight,
    memory,
    clip_index,
    cotangent,
):
    width = inputs.shape[3]
    micro, own_clips = inputs.shape[:2]
    clips = micro * own_clips
    own_heads = qkv_weight.shape[1]
    all_heads = own_heads * heads
    pairs = all_heads // PAIR
    me = lax.axis_index("head")
    linked = (heads, batches, micro, own_clips) == (2, 16, 4, 1)

    def mine(array, shift):
        start = lax.rem(me + shift + heads, heads) * own_clips
        return lax.dynamic_slice_in_dim(array, start, own_clips, axis=1)

    pad = WIDE - HD
    qkv_rows = jnp.pad(
        qkv_weight.transpose(1, 2, 0).reshape(own_heads, 3, HD, width), ((0, 0), (0, 0), (0, pad), (0, 0))
    )
    proj_rows = jnp.pad(proj_weight, ((0, 0), (0, pad), (0, 0)))
    taps_own = pool_weight.astype(F32)
    memory_t = memory.transpose(0, 1, 3, 4, 2)
    tail_own = memory_t[..., MAIN:].reshape(memory_t.shape[:3] + (2, HD, REST)).swapaxes(4, 5)
    tail_own = jnp.pad(tail_own, ((0, 0),) * 5 + ((0, pad),)).reshape(memory_t.shape[:3] + (2 * REST, WIDE))

    x = inputs.reshape(clips, TPC, width)
    cot = cotangent.reshape(clips, TPC, width)
    if linked:
        (packed, keys, att, log, normed, middle, normed_two, cot_rows, first, second, qkv_all, proj_all, mem_all, taps_all) = (
            attention_forward_links(
                clip_index.T, x, cot, qkv_weight.transpose(1, 2, 0).reshape(PAIR, PAIR, 3, HD, width),
                proj_weight.reshape(PAIR, PAIR, HD, width), memory_t, tail_own,
                taps_own.reshape(-1, PAIR, 4, HD), gain_one, gain_two, hidden_weight, output_weight,
            )
        )
        first = first.reshape(width, -1)
        second = second.reshape(-1, width)
    else:
        qkv_all = jnp.concatenate(group_gather(qkv_rows, heads), axis=0)
        proj_all = jnp.concatenate(group_gather(proj_rows, heads), axis=0)
        w_all = jnp.concatenate(
            [
                qkv_all.reshape(pairs, PIECES * WIDE, width),
                proj_all.reshape(pairs, PAIR * WIDE, width),
            ],
            axis=1,
        )
        taps_all = jnp.concatenate(group_gather(taps_own, heads), axis=0).reshape(pairs, PAIR, 4, HD)
        mem_all = jnp.concatenate(group_gather(memory_t, heads, mine), axis=2)
        mem_all = mem_all.reshape(clips, all_heads, 2 * HD, TPC)
        tail = jnp.concatenate(group_gather(tail_own, heads, mine), axis=2)
        tail = tail.reshape(clips, all_heads, 2 * REST, WIDE)

        first = lax.all_gather(hidden_weight, ("batch", "head"), axis=0, tiled=True)
        second = lax.all_gather(output_weight, ("batch", "head"), axis=0, tiled=True)
        index = mine(clip_index, 0).reshape(clips, 1, 1)
        side_mask, main_mask = mask_rows(index)
        side_mask, main_mask = side_mask.reshape(clips, 1, SIDE), main_mask.reshape(clips, 1, MAIN)
        packed, keys, att, log, normed, middle, normed_two, cot_rows = attention_forward(
            x, cot, w_all, mem_all, tail, side_mask, main_mask, taps_all, gain_one, gain_two
        )
    rows = clips * ROWS
    mlp_args = (
        normed_two.reshape(rows, width), cot_rows.reshape(rows, width), first, second, middle.reshape(rows, width), gain_two
    )
    if linked:
        outputs, grad, d_gain_two, d_first, d_second, first_left, second_left = mlp_links(*mlp_args)
    else:
        outputs, grad, d_first, d_second, d_gain_two = mlp(*mlp_args)
    if linked:
        d_x, small, last_first, last_second, d_proj, d_qkv = attention_backward_links(
            clip_index.T, x, qkv_all, proj_all, mem_all, taps_all, gain_one,
            packed, keys, att, log, normed, grad.reshape(clips, ROWS, width), d_gain_two,
            first_left, second_left,
        )
        d_first = jnp.concatenate([d_first, last_first], axis=1)
        d_second = jnp.where(lax.axis_index("batch") // (batches // TILES) >= EARLY, last_second, d_second)
        d_qkv = d_qkv.astype(F32).reshape(own_heads, 3 * HD, width)
        d_proj = d_proj.astype(F32).reshape(own_heads, HD, width)
        d_taps = small[8:, : 2 * WIDE].reshape(PAIR, 4, 2, WIDE).transpose(2, 0, 1, 3)[..., :HD]
        share = width // (batches * heads)
        start = (lax.axis_index("batch") * heads + me) * share
        d_gains = lax.dynamic_slice_in_dim(small[:2], start, share, axis=1)
        return (
            outputs.reshape(inputs.shape),
            d_x.reshape(inputs.shape),
            d_qkv.transpose(2, 0, 1),
            d_proj,
            d_taps.reshape(own_heads, 4, HD),
            d_gains[0],
            d_gains[1],
            d_first,
            d_second,
        )
    d_x, d_w, d_taps, d_gain_one = attention_backward(
        x, w_all, mem_all, side_mask, main_mask, taps_all, gain_one,
        packed, keys, att, log, normed, grad,
    )
    d_proj = d_w[:, PIECES * WIDE :].reshape(heads, own_heads, WIDE, width)[:, :, :HD]
    d_w = d_w[:, : PIECES * WIDE].reshape(heads, own_heads, 3, WIDE, width)[:, :, :, :HD]
    d_w = d_w.reshape(heads, own_heads, 3 * HD, width)
    d_taps = d_taps.reshape(heads, own_heads, 4, WIDE)[..., :HD]
    d_w, d_proj, d_taps = (
        lax.psum(group_sum(list(grads), heads).astype(BF16), "batch").astype(F32)
        for grads in (d_w, d_proj, d_taps)
    )
    both = ("batch", "head")
    d_first = lax.psum_scatter(d_first, both, scatter_dimension=0, tiled=True).astype(F32)
    d_second = lax.psum_scatter(d_second, both, scatter_dimension=0, tiled=True).astype(F32)
    d_gains = lax.psum_scatter(
        jnp.concatenate([d_gain_one, d_gain_two], axis=0), both, scatter_dimension=1, tiled=True
    )
    return (
        outputs.reshape(inputs.shape),
        d_x.reshape(inputs.shape),
        d_w.transpose(2, 0, 1),
        d_proj,
        d_taps,
        d_gains[0],
        d_gains[1],
        d_first,
        d_second,
    )


def solution(mesh):
    return jax.shard_map(
        functools.partial(local, mesh.shape["head"], mesh.shape["batch"]),
        mesh=mesh,
        in_specs=(
            P(None, ("batch", "head"), None, None),
            P(None, "head", None),
            P("head", None, None),
            P("head", None, None),
            P(),
            P(),
            P(("batch", "head"), None),
            P(("batch", "head"), None),
            P(None, "batch", None, "head", None),
            P(None, "batch"),
            P(None, ("batch", "head"), None, None),
        ),
        out_specs=(
            P(None, ("batch", "head"), None, None),
            P(None, ("batch", "head"), None, None),
            P(None, "head", None),
            P("head", None, None),
            P("head", None, None),
            P(("batch", "head")),
            P(("batch", "head")),
            P(("batch", "head"), None),
            P(("batch", "head"), None),
        ),
        check_vma=False,
    )
```

```python
import functools
import math

import jax
import jax.numpy as jnp
from jax import lax
from jax.experimental import pallas as pl
from jax.experimental.pallas import tpu as pltpu
from jax.sharding import PartitionSpec as P

HD = 96
WIDE = 128
FRAMES = 8
TPC = 392
PTOK = 196
SPOT = TPC // FRAMES
HALF = 200
ROWS = 2 * HALF
MAIN = 384
REST = TPC - MAIN
SIDE = 256
PAIR = 2
PIECES = 3 * PAIR

NORM_EPS = 1e-06
NEG = -1e30
LOG2E = 1.4426950408889634
SCORE = HD ** (-0.5)

F32 = jnp.float32
BF16 = jnp.bfloat16


def dot(a, b):
    return lax.dot_general(a, b, (((1,), (0,)), ((), ())), preferred_element_type=F32)


def dot_nt(a, b):
    return lax.dot_general(a, b, (((1,), (1,)), ((), ())), preferred_element_type=F32)


def dot_tn(a, b):
    return lax.dot_general(a, b, (((0,), (0,)), ((), ())), preferred_element_type=F32)


def reorder(shape, row_dim):
    rows = lax.broadcasted_iota(jnp.int32, shape, row_dim)
    tokens = lax.broadcasted_iota(jnp.int32, shape, 1 - row_dim)
    odd = (rows >= HALF).astype(jnp.int32)
    spot = rows - HALF * odd
    frame = sum((spot >= SPOT * step).astype(jnp.int32) for step in range(1, FRAMES // 2))
    return ((tokens == spot + SPOT * (frame + odd)) & (spot < PTOK)).astype(BF16)


def norm_parts(values):
    average = jnp.mean(values, axis=-1, keepdims=True)
    centered = values - average
    spread = lax.rsqrt(jnp.mean(centered * centered, axis=-1, keepdims=True) + NORM_EPS)
    return centered * spread, spread


def norm_pull(values, gain, grad):
    unit, spread = norm_parts(values)
    scaled = grad * gain
    inner = jnp.mean(scaled * unit, axis=-1, keepdims=True)
    pulled = spread * (scaled - jnp.mean(scaled, axis=-1, keepdims=True) - unit * inner)
    return pulled, jnp.sum(grad * unit, axis=0, keepdims=True)


def as_row(ref):
    return ref[...].reshape(1, -1)


def widen(taps):
    return jnp.concatenate([taps, jnp.zeros((taps.shape[0], WIDE - taps.shape[1]), F32)], axis=1)


def mask_rows(index):
    slot = lax.broadcasted_iota(jnp.int32, (1, MAIN), 1) // PTOK
    main = jnp.where(index > slot, 0.0, NEG)
    spot = lax.broadcasted_iota(jnp.int32, (1, SIDE), 1)
    tail_open = (spot >= HALF) & (spot < HALF + REST) & (index > (TPC - 1) // PTOK)
    return jnp.where((spot < PTOK) | tail_open, 0.0, NEG), main


def value_columns(memory_t):
    return jnp.concatenate([memory_t[HD:], jnp.zeros((WIDE - HD, memory_t.shape[1]), BF16)], axis=0)


def forward_kernel(
    x_ref, cot_ref, w_ref, mem_ref, tail_ref, side_ref, main_ref, taps_ref, gain_one_ref, gain_two_ref,
    packed_ref, keys_ref, att_ref, log_ref, normed_ref, middle_ref, normed_two_ref, cot_out,
    x_rows, normed_rows, branch, logs,
):
    forward_step(
        pl.program_id(0), pl.program_id(1), pl.num_programs(0), (side_ref[0], main_ref[0]),
        w_ref.at[0, : PIECES * WIDE], w_ref.at[0, PIECES * WIDE :], mem_ref.at[0], tail_ref.at[0], taps_ref.at[0],
        x_ref, cot_ref, gain_one_ref, gain_two_ref,
        packed_ref, keys_ref, att_ref, log_ref, normed_ref, middle_ref, normed_two_ref, cot_out,
        x_rows, normed_rows, branch, logs,
    )


def forward_step(
    pair, clip, pairs, masks,
    qkv_ref, proj_ref, mem_ref, tail_ref, taps_ref,
    x_ref, cot_ref, gain_one_ref, gain_two_ref,
    packed_ref, keys_ref, att_ref, log_ref, normed_ref, middle_ref, normed_two_ref, cot_out,
    x_rows, normed_rows, branch, log_rows,
):
    here = pl.ds(clip, 1)

    @pl.when(pair == 0)
    def _():
        rows = dot(reorder((ROWS, TPC), 0), x_ref[0])
        x_rows[here] = rows.astype(BF16)[None]
        unit, _ = norm_parts(rows)
        low = (unit * as_row(gain_one_ref)).astype(BF16)
        normed_rows[here] = low[None]
        normed_ref[0] = low
        log_rows[here] = jnp.zeros((1, ROWS, WIDE), F32)

    normed = normed_rows[here][0]
    packed = dot_nt(normed, qkv_ref[...].reshape(-1, normed.shape[1]))
    packed_ref[0, 0] = packed.astype(BF16)
    logs = []
    outs = []
    for head in range(PAIR):
        base = 3 * WIDE * head
        query = packed[:, base : base + WIDE]
        key = packed[:, base + WIDE : base + 2 * WIDE]
        value = packed[:, base + 2 * WIDE : base + 3 * WIDE]
        query_low = query.astype(BF16)
        taps = widen(taps_ref[head])
        zeros = jnp.zeros((SIDE - HALF - REST, WIDE), F32)
        pooled_key = taps[0:1] * key[:HALF] + taps[1:2] * key[HALF:]
        pooled_value = taps[2:3] * value[:HALF] + taps[3:4] * value[HALF:]
        tail = tail_ref[head].astype(F32)
        side_key = jnp.concatenate([pooled_key, tail[:REST], zeros], axis=0).astype(BF16)
        side_value = jnp.concatenate([pooled_value, tail[REST:], zeros], axis=0).astype(BF16)
        keys_ref[0, 0, head, 0] = side_key
        keys_ref[0, 0, head, 1] = side_value
        memory_t = mem_ref[head]
        score_side = dot_nt(query_low, side_key) * (SCORE * LOG2E) + masks[0]
        score_main = dot(query_low, memory_t[:WIDE]) * (SCORE * LOG2E) + masks[1]
        top = jnp.maximum(
            jnp.max(score_side, axis=-1, keepdims=True), jnp.max(score_main, axis=-1, keepdims=True)
        )
        weight_side = jnp.exp2(score_side - top)
        weight_main = jnp.exp2(score_main - top)
        total = jnp.sum(weight_side, axis=-1, keepdims=True) + jnp.sum(weight_main, axis=-1, keepdims=True)
        mixed = dot(weight_side.astype(BF16), side_value) + dot_nt(
            weight_main.astype(BF16), value_columns(memory_t)
        )
        outs.append(mixed / total + query)
        logs.append(top + jnp.log2(total))
    attended = jnp.concatenate(outs, axis=1).astype(BF16)
    att_ref[0, 0] = attended
    lane = lax.broadcasted_iota(jnp.int32, (ROWS, WIDE), 1) - PAIR * pair
    log_rows[here] = jnp.where(lane == 0, logs[0], jnp.where(lane == 1, logs[1], log_rows[here][0]))[None]
    part = dot(attended, proj_ref[...].reshape(-1, normed.shape[1]))[None]

    @pl.when(pair == 0)
    def _():
        branch[here] = part

    @pl.when(pair > 0)
    def _():
        branch[here] += part

    @pl.when(pair == pairs - 1)
    def _():
        middle = x_rows[here][0].astype(F32) + branch[here][0]
        middle_ref[0] = middle
        unit, _ = norm_parts(middle)
        normed_two_ref[0] = (unit * as_row(gain_two_ref)).astype(BF16)
        log_ref[0] = log_rows[here][0]
        cot_out[0] = dot(reorder((ROWS, TPC), 0), cot_ref[0]).astype(BF16)


def feed(step, chunk, normed_ref, cot_ref, first, second, total, grad_normed, active, grad_hidden):
    here = pl.ds(chunk * CHUNK, CHUNK)
    hidden = dot(normed_ref[here, :], first)
    grad_active = dot_nt(cot_ref[here, :], second)
    bell = jnp.exp2(hidden * hidden * (-0.5 * LOG2E))
    near = 1.0 / (1.0 + (0.3275911 * math.sqrt(0.5)) * jnp.abs(hidden))
    tail = near * (0.5 * 1.061405429) + (0.5 * -1.453152027)
    tail = near * tail + (0.5 * 1.421413741)
    tail = near * tail + (0.5 * -0.284496736)
    tail = near * tail + (0.5 * 0.254829592)
    tail = near * tail * bell
    cumulative = jnp.where(hidden < 0.0, tail, 1.0 - tail)
    slope = cumulative + hidden * bell * 0.3989422804014327
    active_low = (hidden * cumulative).astype(BF16)
    hidden_low = (slope * grad_active).astype(BF16)
    active[here, :] = active_low
    grad_hidden[here, :] = hidden_low
    fed = dot(active_low, second)
    back = dot_nt(hidden_low, first)

    @pl.when(step == 0)
    def _():
        total[here, :] = fed
        grad_normed[here, :] = back

    @pl.when(step > 0)
    def _():
        total[here, :] += fed
        grad_normed[here, :] += back


def mlp_kernel(*refs):
    mlp_step(None, *refs)


def mlp_links_kernel(
    normed_ref, cot_ref, first_ref, second_ref, middle_ref, gain_ref,
    out_ref, grad_ref, d_gain_ref, first_out, second_out, first_left, second_left,
    middle, total, grad_normed, active, grad_hidden, near, *rest,
):
    step = pl.program_id(0)
    here = place()
    z, y, core, x, at = here
    first_refs, second_refs = rest[:5], rest[5:10]
    first_keep, second_keep, first_result, second_result, send, recv, store = rest[10:]
    links = Links(send, recv)
    partners = Partners(here)
    sums, outs = [], []
    for tile in range(EARLY):
        sums.append(
            (
                Sum(f"f{tile}", "xy", None, [ref.at[tile] for ref in first_refs], links, partners),
                Sum(f"s{tile}", "yx", tile, [ref.at[tile] for ref in second_refs], links, partners),
            )
        )
        outs.append(
            (
                pltpu.make_async_copy(
                    first_result.at[tile], first_out.at[:, pl.ds(tile * TILE, TILE)], store.at[2 * tile]
                ),
                pltpu.make_async_copy(second_result, second_out, store.at[2 * tile + 1]),
            )
        )
    kept = [
        [
            pltpu.make_async_copy(left.at[tile], out.at[tile], store.at[2 * (EARLY + tile) + i])
            for i, (left, out) in enumerate(((first_keep, first_left), (second_keep, second_left)))
        ]
        for tile in range(TILES - EARLY)
    ]

    def store_grads(d_first, d_second):
        for tile in range(TILES):

            @pl.when(step == tile)
            def _(tile=tile):
                early = tile < EARLY
                for early_ref, keep_ref, grad in (
                    (first_refs[0], first_keep, d_first),
                    (second_refs[0], second_keep, d_second),
                ):
                    into = early_ref if early else keep_ref
                    into[tile if early else tile - EARLY] = grad.reshape(into.shape[1:]).astype(BF16)
                if not early:
                    for copy in kept[tile - EARLY]:
                        copy.start()

    def finish(tile):
        one, two = sums[tile]
        one.finish(first_result.at[tile])
        outs[tile][0].start()

        @pl.when(z == tile)
        def _():
            two.finish(second_result)
            outs[tile][1].start()

    def act(moment):
        for tile, (one, two) in enumerate(sums):
            plan = {
                (tile + 1, 0): [one.begin, two.begin],
                (tile + 1, 1): [one.core, two.core],
                (tile + 2, 0): [one.first, two.first],
                (tile + 2, 1): [one.second, two.second],
                (tile + 3, 0): [lambda: finish(tile)],
            }
            for (when, which), acts in plan.items():
                if which != moment:
                    continue

                @pl.when(step == when)
                def _(acts=acts):
                    for one_act in acts:
                        one_act()

    @pl.when(step == 0)
    def _():
        greet(partners.all())

    mlp_step(
        act, normed_ref, cot_ref, first_ref, second_ref, middle_ref, gain_ref,
        out_ref, grad_ref, store_grads, None, d_gain_ref,
        middle, total, grad_normed, active, grad_hidden, near,
    )

    @pl.when(step == pl.num_programs(0) - 1)
    def _():
        links.sent()
        for copies in kept:
            for copy in copies:
                copy.wait()
        for tile, (one, two) in enumerate(outs):
            one.wait()
            pl.when(z == tile)(lambda two=two: two.wait())


class Partners:
    def __init__(self, here):
        self.place = here
        z, y, core, x, at = here
        self.x, self.y, self.core = at(z, y, core, 1 - x), at(z, 1 - y, core, x), at(z, y, 1 - core, x)
        self.along = [at(turn(z, shift), y, core, x) for shift in (1, 2, 3)]

    def all(self):
        return [self.x, self.y, self.core] + self.along


class Sum:
    def __init__(self, name, order, owner, refs, links, partners):
        self.name, self.order, self.owner, self.links = name, order, owner, links
        self.data, self.from_core, self.from_one, self.from_two, self.from_z = refs
        self.place = z, y, core, x, at = partners.place
        data = self.data
        self.planes = data.shape[0]
        self.names = [name + "c", name + "a", name + "b"] + [f"{name}z{shift}" for shift in (1, 2, 3)]
        links.add(name + "c", data.at[:, :, 1 - core], self.from_core, partners.core)
        if order == "xy":
            links.add(name + "a", data.at[:, :, core, 1 - x], self.from_one, partners.x)
            links.add(name + "b", data.at[:, 1 - y, core, x], self.from_two, partners.y)
        else:
            links.add(name + "a", data.at[:, 1 - y, core], self.from_one, partners.y)
            links.add(name + "b", data.at[:, y, core, 1 - x], self.from_two, partners.x)
        for shift in (1, 2, 3):
            into = self.from_z.at[shift - 1]
            if owner is None:
                source = data.at[turn(z, shift), y, core, x]
                links.add(f"{name}z{shift}", source, into, partners.along[shift - 1])
            else:
                links.add(
                    f"{name}z{shift}", data.at[0, y, core, x], into, at(owner, y, core, x),
                    z == (owner + shift) % 4, z == owner,
                )

    def begin(self):
        self.links.start(self.name + "c")

    def core(self):
        z, y, core, x, at = self.place
        self.links.arrived(self.name + "c")

        @pl.loop(0, self.planes)
        def _(plane):
            for column in (0, 1):
                for head in (0, 1):
                    self.data[plane, column, core, head] = add_low(
                        self.data[plane, column, core, head], self.from_core[plane, column, head]
                    )

        self.links.start(self.name + "a")

    def first(self):
        z, y, core, x, at = self.place
        self.links.arrived(self.name + "a")

        @pl.loop(0, self.planes)
        def _(plane):
            for other in (0, 1):
                spot = (plane, other, core, x) if self.order == "xy" else (plane, y, core, other)
                self.data[spot] = add_low(self.data[spot], self.from_one[plane, other])

        self.links.start(self.name + "b")

    def second(self):
        z, y, core, x, at = self.place
        self.links.arrived(self.name + "b")

        @pl.loop(0, self.planes)
        def _(plane):
            self.data[plane, y, core, x] = add_low(self.data[plane, y, core, x], self.from_two[plane])

        self.links.start(*self.names[3:])

    def finish(self, result):
        z, y, core, x, at = self.place
        for name in self.names[3:]:
            self.links.get(name).wait_recv()
        part = self.data[z if self.owner is None else 0, y, core, x].astype(F32)
        for shift in range(3):
            part = part + self.from_z[shift].astype(F32)
        result[...] = part


def mlp_step(
    act, normed_ref, cot_ref, first_ref, second_ref, middle_ref, gain_ref,
    out_ref, grad_ref, d_first_ref, d_second_ref, d_gain_ref,
    middle, total, grad_normed, active, grad_hidden, near,
):
    step = pl.program_id(0)
    clips = middle.shape[0] // ROWS
    tiles = pl.num_programs(0) - clips
    chunks = middle.shape[0] // CHUNK
    fetch = pltpu.make_async_copy(middle_ref, middle, near.at[0])

    @pl.when(step == 0)
    def _():
        fetch.start()
        d_gain_ref[...] = jnp.zeros_like(d_gain_ref)

    if act is not None:
        act(0)

    @pl.when(step < tiles)
    def _():
        first = first_ref[...]
        second = second_ref[...]
        for chunk in range(chunks):
            if act is not None and chunk == 1:
                act(1)
            feed(step, chunk, normed_ref, cot_ref, first, second, total, grad_normed, active, grad_hidden)
        if act is not None:
            act(2)
        d_first = dot_tn(normed_ref[...], grad_hidden[...])
        d_second = dot_tn(active[...], cot_ref[...])
        if act is not None:
            d_first_ref(d_first, d_second)
        else:
            d_first_ref[...] = d_first.astype(BF16)
            d_second_ref[...] = d_second.astype(BF16)

    @pl.when(step == tiles)
    def _():
        fetch.wait()

    @pl.when(step >= tiles)
    def _():
        here = pl.ds(pl.multiple_of((step - tiles) * ROWS, ROWS), ROWS)
        values = middle[here, :]
        out = (values + total[here, :]).astype(BF16)
        out_ref[0] = dot(reorder((TPC, ROWS), 1), out).astype(BF16)
        pulled, d_gain = norm_pull(values, as_row(gain_ref), grad_normed[here, :])
        grad_ref[...] = (cot_ref[here, :].astype(F32) + pulled).astype(BF16)
        d_gain_ref[...] += d_gain


def backward_kernel(
    x_ref, w_ref, mem_ref, side_ref, main_ref, taps_ref, gain_ref,
    packed_ref, keys_ref, att_ref, log_ref, normed_ref, grad_ref,
    d_x_ref, d_w_ref, d_taps_ref, d_gain_ref,
    grad_normed,
):
    pair, clip = pl.program_id(0), pl.program_id(1)
    here = pl.ds(clip, 1)

    @pl.when(clip == 0)
    def _():
        d_w_ref[...] = jnp.zeros_like(d_w_ref)
        d_taps_ref[...] = jnp.zeros_like(d_taps_ref)

    grad_packed = backward_attention(
        pair, (side_ref[0], main_ref[0]), w_ref.at[0, PIECES * WIDE :], d_taps_ref.at[0],
        mem_ref.at[0], taps_ref.at[0], packed_ref.at[0, 0], keys_ref.at[0, 0], att_ref.at[0, 0], log_ref, grad_ref,
    )
    d_w_ref[0, PIECES * WIDE :] += dot_tn(att_ref[0, 0], grad_ref[...])
    d_w_ref[0, : PIECES * WIDE] += dot_tn(grad_packed, normed_ref[0])
    part = dot(grad_packed, w_ref[0, : PIECES * WIDE])[None]

    @pl.when(pair == 0)
    def _():
        grad_normed[here] = part

    @pl.when(pair > 0)
    def _():
        grad_normed[here] += part

    @pl.when(pair == pl.num_programs(0) - 1)
    def _():
        d_x_ref[0], d_gain = input_grad(x_ref[0], grad_normed[here][0], gain_ref, grad_ref[...])

        @pl.when(clip == 0)
        def _():
            d_gain_ref[...] = d_gain

        @pl.when(clip > 0)
        def _():
            d_gain_ref[...] += d_gain


def input_grad(x, grad_normed, gain_ref, grad_branch):
    rows = dot(reorder((ROWS, TPC), 0), x)
    pulled, d_gain = norm_pull(rows, as_row(gain_ref), grad_normed)
    d_x = (grad_branch.astype(F32) + pulled).astype(BF16)
    return dot(reorder((TPC, ROWS), 1), d_x).astype(BF16), d_gain


def backward_attention(
    pair, masks, proj_ref, d_taps_ref, mem_ref, taps_ref, packed_ref, keys_ref, att_ref, log_ref, grad_ref
):
    lane = lax.broadcasted_iota(jnp.int32, (ROWS, WIDE), 1) - PAIR * pair
    grad_out = dot_nt(grad_ref[...], proj_ref[...].reshape(PAIR * WIDE, -1))
    pieces = []
    for head in range(PAIR):
        base = 3 * WIDE * head
        query = packed_ref[:, base : base + WIDE]
        key = packed_ref[:, base + WIDE : base + 2 * WIDE].astype(F32)
        value = packed_ref[:, base + 2 * WIDE : base + 3 * WIDE].astype(F32)
        out_grad = grad_out[:, WIDE * head : WIDE * (head + 1)].astype(BF16)
        taps = widen(taps_ref[head])
        side_key = keys_ref[head, 0]
        side_value = keys_ref[head, 1]
        memory_t = mem_ref[head]
        log = jnp.sum(jnp.where(lane == head, log_ref[0], 0.0), axis=-1, keepdims=True)
        score_side = dot_nt(query, side_key) * (SCORE * LOG2E) + masks[0]
        score_main = dot(query, memory_t[:WIDE]) * (SCORE * LOG2E) + masks[1]
        weight_side = jnp.exp2(score_side - log)
        weight_main = jnp.exp2(score_main - log)
        grad_side = dot_nt(out_grad, side_value)
        grad_main = dot(out_grad, value_columns(memory_t))
        mixed = att_ref[:, WIDE * head : WIDE * (head + 1)].astype(F32) - query.astype(F32)
        inner = jnp.sum(out_grad.astype(F32) * mixed, axis=-1, keepdims=True)
        score_grad_side = (weight_side * (grad_side - inner)).astype(BF16)
        score_grad_main = (weight_main * (grad_main - inner)).astype(BF16)
        grad_query = (
            dot(score_grad_side, side_key) + dot_nt(score_grad_main, memory_t[:WIDE])
        ) * SCORE + out_grad.astype(F32)
        grad_key = dot_tn(score_grad_side, query)[:HALF] * SCORE
        grad_value = dot_tn(weight_side.astype(BF16), out_grad)[:HALF]
        pieces += [
            grad_query,
            jnp.concatenate([taps[0:1] * grad_key, taps[1:2] * grad_key], axis=0),
            jnp.concatenate([taps[2:3] * grad_value, taps[3:4] * grad_value], axis=0),
        ]
        d_taps_ref[head] += jnp.concatenate(
            [
                jnp.sum(part * grad, axis=0, keepdims=True)
                for part, grad in (
                    (key[:HALF], grad_key),
                    (key[HALF:], grad_key),
                    (value[:HALF], grad_value),
                    (value[HALF:], grad_value),
                )
            ],
            axis=0,
        )
    return jnp.concatenate(pieces, axis=1).astype(BF16)


def add_low(one, other):
    return (one.astype(F32) + other.astype(F32)).astype(BF16)


def unpad(ref, into, more=None):
    for piece in range(ref.shape[0] // WIDE):
        rows = ref[WIDE * piece : WIDE * piece + HD]
        narrow = slice(HD * piece, HD * (piece + 1))
        if more is not None:
            rows = rows + more[narrow].astype(F32)
        into[narrow] = rows.astype(BF16)


BACKWARD_COPIES = 112
CORE_LANES = 384
UNITS = (("p", 384, 384, "yz"), ("0", 576, 640, "yz"), ("1", 384, 384, "yz"), ("2", 192, 256, "zy"))
FAR = (("p", 384), ("0", 576), ("1", 576))


class AllReduce:
    def __init__(self, name, order, refs, links, partners):
        self.name, self.order, self.links = name, order, links
        self.own, self.core, self.got_y, self.got_z, self.whole = refs
        self.place = z, y, core, x, at = partners.place
        self.count = self.own.shape[0]
        mine, lanes = self.part(y, z), half_lanes(core)
        links.add("rc" + name, self.own.at[:, half_lanes(1 - core)], self.core, partners.core)
        if order == "yz":
            to_y, to_z = self.rows(1 - y, 2), [self.part(y, turn(z, shift)) for shift in (1, 2, 3)]
            spread = self.rows(y, 2)
        else:
            to_y, to_z = self.part(1 - y, z), [self.rows(turn(z, shift), 4) for shift in (1, 2, 3)]
            spread = self.rows(z, 4)
        links.add("ry" + name, self.own.at[to_y, lanes], self.got_y, partners.y)
        back_z, back_y = (mine, spread) if order == "yz" else (spread, mine)
        piece = self.whole.at[back_y, lanes]
        links.add("gy" + name, piece, piece, partners.y)
        for shift in (1, 2, 3):
            links.add(
                f"rz{shift}{name}", self.own.at[to_z[shift - 1], lanes], self.got_z.at[shift - 1], partners.along[shift - 1]
            )
            piece = self.whole.at[back_z, lanes]
            links.add(f"gz{shift}{name}", piece, piece, partners.along[shift - 1])
        piece = self.whole.at[:, lanes]
        links.add("gc" + name, piece, piece, partners.core)

    def rows(self, at, parts):
        size = self.count // parts
        return pl.ds(pl.multiple_of(at * size, size), size)

    def part(self, y, z):
        return self.rows(4 * y + z if self.order == "yz" else 2 * z + y, 8)

    def stage(self, which, axis):
        return [f"{which}z{shift}{self.name}" for shift in (1, 2, 3)] if axis == "z" else [which + "y" + self.name]

    def begin(self):
        self.links.start("rc" + self.name)

    def sum_core(self, far):
        lanes = half_lanes(self.place[2])
        self.links.arrived("rc" + self.name)
        rows = far.shape[0]
        total = self.own[:rows, lanes].astype(F32) + self.core[:rows].astype(F32) + far[...].astype(F32)
        self.own[:rows, lanes] = total.astype(BF16)
        self.links.start(*self.stage("r", self.order[0]))

    def taken(self, axis, rows):
        part = self.own[rows, half_lanes(self.place[2])].astype(F32)
        for got in [self.got_y] if axis == "y" else [self.got_z.at[shift] for shift in range(3)]:
            part = part + got[...].astype(F32)
        return part.astype(BF16)

    def sum_one(self):
        z, y, core, x, at = self.place
        axis = self.order[0]
        self.links.arrived(*self.stage("r", axis))
        rows = self.rows(y, 2) if axis == "y" else self.rows(z, 4)
        self.own[rows, half_lanes(core)] = self.taken(axis, rows)
        self.links.start(*self.stage("r", self.order[1]))

    def sum_two(self):
        z, y, core, x, at = self.place
        axis = self.order[1]
        self.links.arrived(*self.stage("r", axis))
        rows = self.part(y, z)
        self.whole[rows, half_lanes(core)] = self.taken(axis, rows)
        self.links.start(*self.stage("g", axis))

    def spread_one(self):
        self.links.arrived(*self.stage("g", self.order[1]))
        self.links.start(*self.stage("g", self.order[0]))

    def spread_core(self):
        self.links.arrived(*self.stage("g", self.order[0]))
        self.links.start("gc" + self.name)

    def done(self):
        self.links.arrived("gc" + self.name)


class Far:
    def __init__(self, name, refs, links, partners):
        self.name, self.links = name, links
        self.sent, self.core, self.got = refs
        self.place = z, y, core, x, at = partners.place
        links.add("hc" + name, self.sent.at[:, half_lanes(1 - core)], self.core, partners.core)
        links.add("hx" + name, self.sent.at[:, half_lanes(core)], self.got, partners.x)

    def begin(self):
        self.links.start("hc" + self.name)

    def pass_on(self):
        lanes = half_lanes(self.place[2])
        self.links.arrived("hc" + self.name)
        self.sent[:, lanes] = add_low(self.sent[:, lanes], self.core[...])
        self.links.start("hx" + self.name)


def half_lanes(core):
    return pl.ds(pl.multiple_of(core * CORE_LANES, CORE_LANES), CORE_LANES)


def narrow(value, into, first):
    for piece in range(value.shape[0] // WIDE):
        rows = value[WIDE * piece : WIDE * piece + HD]
        spot = slice(first + HD * piece, first + HD * (piece + 1))
        into[spot] = rows.astype(BF16)


def backward_links_kernel(
    index_ref, x_ref, qkv_ref, proj_ref, mem_ref, taps_ref, gain_ref,
    packed_ref, keys_ref, att_ref, log_ref, normed_ref, grad_ref, gain_two_ref,
    d_first, d_second,
    d_x_ref, small_out, taps_out, first_out, second_out, proj_out, qkv_out,
    grad_packed, d_gain, d_taps,
    small_mine, small_far, small_got, small_all,
    first_result, second_result, send, recv, near, *rest,
):
    step = pl.program_id(0)
    last = pl.num_programs(0) - 1
    z, y, core, x, at = place()
    links = Links(send, recv)
    partners = Partners((z, y, core, x, at))
    late = TILES - EARLY
    first_refs, second_refs, rest = rest[:5], rest[5:10], rest[10:]
    loads = [
        pltpu.make_async_copy(d_first, first_refs[0], near.at[0]),
        pltpu.make_async_copy(d_second, second_refs[0], near.at[1]),
    ]
    sums = [
        (
            Sum(f"f{tile}", "xy", None, [ref.at[tile] for ref in first_refs], links, partners),
            Sum(f"s{tile}", "yx", EARLY + tile, [ref.at[tile] for ref in second_refs], links, partners),
        )
        for tile in range(late)
    ]
    first_done = [
        pltpu.make_async_copy(first_result.at[tile], first_out.at[:, pl.ds(tile * TILE, TILE)], near.at[2 + tile])
        for tile in range(late)
    ]
    second_done = pltpu.make_async_copy(second_result, second_out, near.at[2 + late])
    units, far = {}, {}
    for i, (name, _, _, order) in enumerate(UNITS):
        units[name] = AllReduce(name, order, rest[5 * i : 5 * i + 5], links, partners)
    rest = rest[5 * len(UNITS) :]
    for i, (name, _) in enumerate(FAR):
        far[name] = Far(name, rest[3 * i : 3 * i + 3], links, partners)
    targets = (proj_out, qkv_out.at[0], qkv_out.at[1, pl.ds(0, 384)], qkv_out.at[1, pl.ds(384, 192)])
    save = [
        pltpu.make_async_copy(units[name].whole.at[pl.ds(0, rows)], out, near.at[3 + late + i])
        for i, ((name, rows, _, _), out) in enumerate(zip(UNITS, targets))
    ]
    diagonal = at(z, y, 1 - core, 1 - x)
    links.add("mx", small_far, small_got.at[0], partners.x)
    links.add("md", small_far, small_got.at[1], diagonal)
    links.add("mc", small_mine, small_got.at[2], partners.core)
    spot = 2 * z + y
    others = []
    for shift in range(4):
        for flip in (0, 1):
            if shift or flip:
                other = at(turn(z, shift), y + flip - 2 * y * flip, core, x)
                links.add(f"ms{shift}{flip}", small_all.at[spot], small_all.at[spot], other)
                others.append(other)
    spread_small = [f"ms{shift}{flip}" for shift in range(4) for flip in (0, 1) if shift or flip]

    def proj_grads():
        grad = grad_ref[...].reshape(-1, grad_ref.shape[2])
        return [dot_tn(att_ref[pair].reshape(-1, PAIR * WIDE), grad) for pair in (0, 1)]

    p, zero, one, two = (units[unit[0]] for unit in UNITS)

    def sum_core(name, *parts):
        links.arrived("hx" + name)
        first = 0
        for part, rows in zip(parts, (384, 192) if len(parts) > 1 else (far[name].got.shape[0],)):
            part.sum_core(far[name].got.at[pl.ds(first, rows)])
            first += rows

    def far_proj():
        for pair, value in enumerate(proj_grads()):
            narrow(value, far["p"].sent, 192 * pair)
        far["p"].begin()

    def own_proj():
        for pair, value in enumerate(proj_grads()):
            narrow(value, units["p"].own, 192 * pair)
        units["p"].begin()

    def pair_lanes():
        pair = lax.rem(lax.div(step, 4) + 2, 4)
        return pl.ds(pl.multiple_of(pair * (PIECES * WIDE), PIECES * WIDE), PIECES * WIDE)

    def qkv_grad():
        width = normed_ref.shape[2]
        grad = grad_packed[:, :, pair_lanes()].reshape(-1, PIECES * WIDE)
        return dot_tn(grad, normed_ref[...].reshape(-1, width))

    def far_qkv(name):
        narrow(qkv_grad(), far[name].sent, 0)
        far[name].begin()

    def own_qkv(name):
        grad = qkv_grad()
        if name == "0":
            narrow(grad, zero.own, 0)
            zero.begin()
        else:
            narrow(grad[: 4 * WIDE], one.own, 0)
            narrow(grad[4 * WIDE :], two.own, 0)
            one.begin()
            two.begin()

    def begin():
        greet([partners.x, partners.core, diagonal] + others)
        for copy in loads:
            copy.start()
        d_gain[...] = jnp.zeros_like(d_gain)
        d_taps[...] = jnp.zeros_like(d_taps)
        for name, rows, padded, _ in UNITS:
            if padded > rows:
                units[name].own[rows:] = jnp.zeros((padded - rows, units[name].own.shape[1]), BF16)

    def begin_sums():
        for copy in loads:
            copy.wait()
        for pair in sums:
            for one in pair:
                one.begin()

    def all_sums(stage):
        for pair in sums:
            for one in pair:
                getattr(one, stage)()

    def finish():
        for tile, (one, two) in enumerate(sums):
            one.finish(first_result.at[tile])
            first_done[tile].start()

            @pl.when(z == EARLY + tile)
            def _(two=two):
                two.finish(second_result)
                second_done.start()

    def at_steps(plan):
        for when, acts in plan.items():

            @pl.when(step == when)
            def _(acts=acts):
                for act in acts:
                    act()

    at_steps({0: [begin, far_proj], 8: [own_proj]})

    @pl.when(step < 16)
    def _():
        pair = lax.rem(lax.div(step, 4) + 2, 4)
        clip = lax.rem(step, 4)
        here = pl.ds(clip, 1)
        grad_packed[here, :, pair_lanes()] = backward_attention(
            pair, mask_rows(index_ref[x, clip]), proj_ref.at[0], d_taps.at[lax.div(step, 4)],
            mem_ref.at[0], taps_ref.at[0], packed_ref.at[0, 0], keys_ref.at[0, 0], att_ref.at[lax.rem(pair, 2), clip], log_ref,
            grad_ref.at[clip],
        )[None]

    @pl.when(step >= 16)
    def _():
        clip = step - 16
        grad = dot(grad_packed[clip], qkv_ref[...].reshape(4 * PIECES * WIDE, -1))
        d_x_ref[0], gain = input_grad(x_ref[0], grad, gain_ref, grad_ref[clip])
        d_gain[...] += gain

    at_steps(
        {
            0: [begin_sums],
            1: [far["p"].pass_on],
            2: [lambda: all_sums("core")],
            3: [lambda: far_qkv("0")],
            4: [far["0"].pass_on],
            5: [lambda: all_sums("first")],
            7: [lambda: far_qkv("1")],
            8: [far["1"].pass_on, lambda: all_sums("second")],
            9: [lambda: sum_core("p", p)],
            11: [lambda: own_qkv("0"), p.sum_one],
            12: [lambda: sum_core("0", zero), finish],
            13: [p.sum_two],
            14: [zero.sum_one, p.spread_one],
            15: [lambda: own_qkv("1"), zero.sum_two, p.spread_core],
            16: [lambda: sum_core("1", one, two), zero.spread_one],
            17: [one.sum_one, two.sum_one, p.done, save[0].start],
            18: [one.sum_two, two.sum_two, zero.spread_core],
        }
    )

    @pl.when(step == last)
    def _():
        for i, target in ((2, small_mine), (0, small_far)):
            target[...] = jnp.zeros_like(target)
            target[0:1] = d_gain[...]
            target[1:2] = gain_two_ref[...]
            for j in (0, 1):
                target[8:16, WIDE * j : WIDE * (j + 1)] = d_taps[i + j].reshape(8, WIDE)
        links.start("mx", "md", "mc")
        one.spread_one()
        two.spread_one()
        links.arrived("mx", "md", "mc")
        small_all[pl.ds(spot, 1)] = ((small_mine[...] + small_got[2]) + (small_got[0] + small_got[1]))[None]
        links.start(*spread_small)
        zero.done()
        save[1].start()
        one.spread_core()
        two.spread_core()
        links.arrived(*spread_small)
        total = small_all[0]
        for i in range(1, 8):
            total = total + small_all[i]
        small_out[...] = total
        for pair in (0, 1):
            for head in range(PAIR):
                rows = slice(8 + 4 * head, 12 + 4 * head)
                taps_out[PAIR * pair + head] = total[rows, WIDE * pair : WIDE * pair + HD]
        one.done()
        two.done()
        save[2].start()
        save[3].start()
        for copy in save + first_done:
            copy.wait()
        for tile in range(late):
            pl.when(z == EARLY + tile)(lambda: second_done.wait())
        links.sent()


VMEM_LIMIT = 60 << 20
CHUNK = 800
TILE = 768
TILES = 4
EARLY = 2


def compiler_params(dims):
    return pltpu.CompilerParams(
        dimension_semantics=("arbitrary",) * dims, vmem_limit_bytes=VMEM_LIMIT
    )


def shaped(shape, dtype):
    return jax.ShapeDtypeStruct(shape, dtype)


class Links:
    def __init__(self, send, recv):
        self.send, self.recv, self.made = send, recv, {}

    def add(self, name, src, dst, device, send_if=None, recv_if=None):
        at = len(self.made)
        self.made[name] = (src, dst, device, at, send_if, recv_if)

    def get(self, name):
        src, dst, device, at = self.made[name][:4]
        return pltpu.make_async_remote_copy(
            src_ref=src,
            dst_ref=dst,
            send_sem=self.send.at[at],
            recv_sem=self.recv.at[at],
            device_id=device,
            device_id_type=pl.DeviceIdType.MESH,
        )

    def start(self, *names):
        for name in names:
            self.only(self.made[name][4], self.get(name).start)

    def arrived(self, *names):
        for name in names:
            self.only(self.made[name][5], self.get(name).wait_recv)

    def sent(self):
        for name in self.made:
            self.only(self.made[name][4], self.get(name).wait_send)

    def only(self, condition, act):
        if condition is None:
            act()
        else:
            pl.when(condition)(lambda: act())


def place():
    batch, head = lax.axis_index("batch"), lax.axis_index("head")
    z, y, core = batch // 4, lax.rem(batch // 2, 2), lax.rem(batch, 2)

    def at(z, y, core, x):
        return {"batch": (z * 2 + y) * 2 + core, "head": x}

    return z, y, core, head, at


def greet(devices):
    barrier = pltpu.get_barrier_semaphore()
    for device in devices:
        pl.semaphore_signal(barrier, inc=1, device_id=device, device_id_type=pl.DeviceIdType.MESH)
    pl.semaphore_wait(barrier, len(devices))


def turn(z, shift):
    return lax.rem(z + shift + 4, 4)


FORWARD_COPIES = 96
SPLIT = HD // 2


def forward_links_kernel(
    index_ref, x_ref, cot_ref, gain_one_ref, gain_two_ref,
    qkv_own, proj_own, mem_own, tail_own, taps_own, hidden_own, output_own,
    packed_ref, keys_ref, att_ref, log_ref, normed_ref, middle_ref, normed_two_ref, cot_out,
    first_all, second_all, qkv_out, proj_out, mem_out, taps_out,
    x_rows, normed_rows, branch, logs, qkv_all, proj_all, mem_all, tail_all, taps_all,
    send, recv, near, save,
):
    step = pl.program_id(0)
    z, y, core, x, at = place()
    links = Links(send, recv)
    beside, above, sibling = at(z, y, core, 1 - x), at(z, 1 - y, core, x), at(z, y, 1 - core, x)
    higher, lower = at(turn(z, 1), y, core, x), at(turn(z, -1), y, core, x)
    column = pl.ds(pl.multiple_of(core * MAIN, MAIN), MAIN)
    me = ((z * 2 + y) * 2 + core) * 2 + x
    clips = mem_own.shape[0]

    def split(z, y, *between):
        rows = pl.ds(pl.multiple_of(y * SPLIT, SPLIT), SPLIT)
        return (lax.div(z, 2), lax.rem(z, 2)) + between + (rows, column)

    def block(kind, z, y):
        if kind == "q":
            return qkv_all.at[pl.ds(2, 2)].at[split(z, y, slice(None))]
        if kind == "p":
            return proj_all.at[pl.ds(2, 2)].at[split(z, y)]
        return (first_all if kind == "0" else second_all).at[pl.ds(((z * 2 + y) * 2 + core) * 2, 2)]

    links.add("xq", qkv_own.at[split(z, y, slice(None))], block("q", z, y), beside)
    links.add("xp", proj_own.at[split(z, y)], block("p", z, y), beside)
    links.add("x0", hidden_own, first_all.at[me], beside)
    links.add("x1", output_own, second_all.at[me], beside)
    for kind in "qp01":
        mine = block(kind, z, y)
        links.add("y" + kind, mine, mine, above)
        if kind in "01":
            links.add("c" + kind, mine, mine, sibling)
            mine = block(kind, z, 1 - y)
            links.add("e" + kind, mine, mine, sibling)
        for hop in (1, 2, 3):
            below, beyond = z >= hop, z + hop <= 3
            passed = block(kind, turn(z, 1 - hop), y)
            links.add(f"u{hop}{kind}", passed, passed, higher, (z <= 2) & (z >= hop - 1), below)
            passed = block(kind, turn(z, hop - 1), y)
            links.add(f"d{hop}{kind}", passed, passed, lower, (z >= 1) & (z + hop <= 4), beyond)
            for side, shift, there in (("u", -hop, below), ("d", hop, beyond)):
                came = block(kind, turn(z, shift), y)
                links.add(f"y{side}{hop}{kind}", came, came, above, there, there)
                if kind in "01":
                    links.add(f"c{side}{hop}{kind}", came, came, sibling, there, there)
                    came = block(kind, turn(z, shift), 1 - y)
                    links.add(f"e{side}{hop}{kind}", came, came, sibling, there, there)
    far = qkv_all.at[pl.ds(2, 2), :, :, pl.ds(0, HD), column]
    links.add("cq", far, far, sibling)
    far = proj_all.at[pl.ds(2, 2), :, pl.ds(0, HD), column]
    links.add("cp", far, far, sibling)
    for clip in range(clips):
        links.add(f"m{clip}", mem_own.at[clip, 1 - x, :, :, pl.ds(0, MAIN)], mem_all.at[1, clip], beside)
    links.add("tail", tail_own.at[:, 1 - x], tail_all.at[1], beside)
    links.add("taps", taps_own, taps_all.at[pl.ds(2, 2)], beside)

    local = [
        (qkv_own, qkv_all.at[pl.ds(0, 2), :, :, pl.ds(0, HD)]),
        (proj_own, proj_all.at[pl.ds(0, 2), :, pl.ds(0, HD)]),
        (tail_own.at[:, x], tail_all.at[0]),
        (taps_own, taps_all.at[pl.ds(0, 2)]),
        (mem_own.at[0, x, :, :, pl.ds(0, MAIN)], mem_all.at[0, 0]),
        (hidden_own, first_all.at[me]),
        (output_own, second_all.at[me]),
    ] + [(mem_own.at[clip, x, :, :, pl.ds(0, MAIN)], mem_all.at[0, clip]) for clip in range(1, clips)]
    local = [pltpu.make_async_copy(src, dst, near.at[i]) for i, (src, dst) in enumerate(local)]
    saved = [
        (qkv_all, qkv_out),
        (proj_all, proj_out),
        (taps_all, taps_out),
        (mem_all.at[0], mem_out.at[0]),
    ] + [(mem_all.at[1, clip], mem_out.at[1, clip]) for clip in range(clips)]
    saved = [pltpu.make_async_copy(src, dst, save.at[i]) for i, (src, dst) in enumerate(saved)]

    @pl.when(step == 0)
    def _():
        greet([beside, above, sibling, higher, lower])
        links.start("xq", "xp", "taps", "tail", "x0", "x1")
        for copy in local:
            copy.start()

        @pl.loop(0, 4)
        def _(pair):
            for head in range(PAIR):
                for piece in range(3):
                    qkv_all[pair, head, piece, HD:] = jnp.zeros((WIDE - HD, qkv_all.shape[-1]), BF16)
                proj_all[pair, head, HD:] = jnp.zeros((WIDE - HD, qkv_all.shape[-1]), BF16)

        for copy in local[:5]:
            copy.wait()

    def settle():
        for copy in local[5:]:
            copy.wait()
        saved[3].start()

    def hop(number, kinds):
        for kind in kinds:
            links.arrived(f"u{number}{kind}", f"d{number}{kind}")
            if number < 3:
                links.start(f"u{number + 1}{kind}", f"d{number + 1}{kind}")
            links.start(f"yu{number}{kind}", f"yd{number}{kind}")
            if kind in "01":
                links.start(f"cu{number}{kind}", f"cd{number}{kind}")

    def begin(kinds):
        for kind in kinds:
            links.arrived("x" + kind)
            links.start("u1" + kind, "d1" + kind, "y" + kind)
            if kind in "01":
                links.start("c" + kind)

    def across(number, kinds):
        for kind in kinds:
            for side in ("u", "d") if number else ("",):
                name = f"{side}{number}{kind}" if number else kind
                links.arrived("y" + name)
                if kind in "01":
                    links.start("e" + name)

    def weights():
        for number in range(4):
            across(number, "qp")
        links.start("cq", "cp")
        links.arrived("cq", "cp", "tail", "taps")

    def memory(clip):
        links.arrived(f"m{clip}")
        if clip + 2 < clips:
            links.start(f"m{clip + 2}")
        saved[4 + clip].start()

    plan = {
        1: [settle, lambda: begin("qp"), lambda: links.start("m0")],
        2: [lambda: begin("01")],
        3: [lambda: hop(1, "qp")],
        5: [lambda: hop(2, "qp"), lambda: links.start("m1")],
        6: [lambda: hop(3, "qp")],
        7: [lambda: hop(1, "0")],
        8: [weights, lambda: hop(1, "1"), lambda: memory(0)],
        9: [copy.start for copy in saved[:3]],
        10: [lambda: hop(2, "0"), lambda: memory(1)],
        11: [lambda: hop(2, "1"), lambda: across(0, "01")],
        12: [lambda: across(1, "0"), lambda: memory(2)],
        13: [lambda: hop(3, "0"), lambda: across(1, "1")],
        14: [lambda: hop(3, "1"), lambda: across(2, "0"), lambda: memory(3)],
    }
    for when, acts in plan.items():

        @pl.when(step == when)
        def _(acts=acts):
            for act in acts:
                act()

    pair, clip = pair_of(step), clip_of(step)
    side = lax.div(pair, 2)
    heads = pl.ds(lax.rem(pair, 2) * PAIR, PAIR)
    forward_step(
        pair, clip, 4, mask_rows(index_ref[x, clip]),
        qkv_all.at[pair], proj_all.at[pair],
        mem_all.at[side, clip, heads], tail_all.at[side, clip, heads], taps_all.at[pair],
        x_ref, cot_ref, gain_one_ref, gain_two_ref,
        packed_ref, keys_ref, att_ref, log_ref, normed_ref, middle_ref, normed_two_ref, cot_out,
        x_rows, normed_rows, branch, logs,
    )

    @pl.when(step == pl.num_programs(0) - 1)
    def _():
        across(2, "1")
        across(3, "01")
        for copy in saved:
            copy.wait()
        for kind in "01":
            links.arrived("c" + kind, "e" + kind)
            for number in (1, 2, 3):
                for side in "ud":
                    links.arrived(f"c{side}{number}{kind}", f"e{side}{number}{kind}")
        links.sent()


def pair_of(step):
    return jnp.where(step < 8, lax.div(step, 4), 2 + lax.rem(step, 2))


def clip_of(step):
    return jnp.where(step < 8, lax.rem(step, 4), lax.div(step, 2) - 4)


def attention_forward_links(
    index, x, cot, qkv, proj, mem, tail, taps, gain_one, gain_two, hidden_weight, output_weight
):
    clips, width = x.shape[0], x.shape[2]
    packed_width = PIECES * WIDE
    devices = 32
    early = lambda s: jnp.where(s < 4, s, clips - 1)
    late = lambda s: jnp.where(s < 8, 0, clip_of(s))
    anywhere = pl.BlockSpec(memory_space=pl.ANY)
    return pl.pallas_call(
        forward_links_kernel,
        grid=(4 * clips,),
        in_specs=[
            pl.BlockSpec(memory_space=pltpu.SMEM),
            pl.BlockSpec((1, TPC, width), lambda s: (early(s), 0, 0)),
            pl.BlockSpec((1, TPC, width), lambda s: (late(s), 0, 0)),
            pl.BlockSpec(gain_one.shape, lambda s: (0,)),
            pl.BlockSpec(gain_two.shape, lambda s: (0,)),
        ] + [anywhere] * 5 + [
            pl.BlockSpec(hidden_weight.shape, lambda s: (0, 0)),
            pl.BlockSpec(output_weight.shape, lambda s: (0, 0)),
        ],
        out_specs=[
            pl.BlockSpec((1, 1, ROWS, packed_width), lambda s: (pair_of(s), clip_of(s), 0, 0)),
            pl.BlockSpec((1, 1, PAIR, 2, SIDE, WIDE), lambda s: (pair_of(s), clip_of(s), 0, 0, 0, 0)),
            pl.BlockSpec((1, 1, ROWS, PAIR * WIDE), lambda s: (pair_of(s), clip_of(s), 0, 0)),
            pl.BlockSpec((1, ROWS, WIDE), lambda s: (late(s), 0, 0)),
            pl.BlockSpec((1, ROWS, width), lambda s: (early(s), 0, 0)),
            pl.BlockSpec((1, ROWS, width), lambda s: (late(s), 0, 0)),
            pl.BlockSpec((1, ROWS, width), lambda s: (late(s), 0, 0)),
            pl.BlockSpec((1, ROWS, width), lambda s: (late(s), 0, 0)),
        ] + [anywhere] * 6,
        out_shape=[
            shaped((4, clips, ROWS, packed_width), BF16),
            shaped((4, clips, PAIR, 2, SIDE, WIDE), BF16),
            shaped((4, clips, ROWS, PAIR * WIDE), BF16),
            shaped((clips, ROWS, WIDE), F32),
            shaped((clips, ROWS, width), BF16),
            shaped((clips, ROWS, width), F32),
            shaped((clips, ROWS, width), BF16),
            shaped((clips, ROWS, width), BF16),
            shaped((devices,) + hidden_weight.shape, BF16),
            shaped((devices,) + output_weight.shape, BF16),
            shaped((4, PAIR, 3, WIDE, width), BF16),
            shaped((4, PAIR, WIDE, width), BF16),
            shaped((2, clips, 4, 2 * HD, MAIN), BF16),
            shaped((4,) + taps.shape[1:], F32),
        ],
        scratch_shapes=[
            pltpu.VMEM((clips, ROWS, width), BF16),
            pltpu.VMEM((clips, ROWS, width), BF16),
            pltpu.VMEM((clips, ROWS, width), F32),
            pltpu.VMEM((clips, ROWS, WIDE), F32),
            pltpu.VMEM((4, PAIR, 3, WIDE, width), BF16),
            pltpu.VMEM((4, PAIR, WIDE, width), BF16),
            pltpu.VMEM((2, clips, 4, 2 * HD, MAIN), BF16),
            pltpu.VMEM((2, clips, 4, 2 * REST, WIDE), BF16),
            pltpu.VMEM((4,) + taps.shape[1:], F32),
            pltpu.SemaphoreType.DMA((FORWARD_COPIES,)),
            pltpu.SemaphoreType.DMA((FORWARD_COPIES,)),
            pltpu.SemaphoreType.DMA((6 + clips,)),
            pltpu.SemaphoreType.DMA((4 + clips,)),
        ],
        compiler_params=pltpu.CompilerParams(
            dimension_semantics=("arbitrary",),
            vmem_limit_bytes=VMEM_LIMIT,
            collective_id=0,
            has_side_effects=True,
        ),
        name="attention_forward_links",
    )(index, x, cot, gain_one, gain_two, qkv, proj, mem, tail, taps, hidden_weight, output_weight)


def attention_forward(x, cot, w, mem, tail, side, main, taps, gain_one, gain_two):
    clips, pairs = x.shape[0], w.shape[0]
    width = x.shape[2]
    packed_width = PIECES * WIDE
    weight_rows = w.shape[1]
    late = lambda p, c: jnp.where(p == pairs - 1, c, 0)
    early = lambda p, c: jnp.where(p == 0, c, clips - 1)
    per_step = lambda p, c: (p, c)
    return pl.pallas_call(
        forward_kernel,
        grid=(pairs, clips),
        in_specs=[
            pl.BlockSpec((1, TPC, width), lambda p, c: (early(p, c), 0, 0)),
            pl.BlockSpec((1, TPC, width), lambda p, c: (late(p, c), 0, 0)),
            pl.BlockSpec((1, weight_rows, width), lambda p, c: (p, 0, 0)),
            pl.BlockSpec((1, PAIR, 2 * HD, MAIN), lambda p, c: (c, p, 0, 0)),
            pl.BlockSpec((1, PAIR, 2 * REST, WIDE), lambda p, c: (c, p, 0, 0)),
            pl.BlockSpec((1, 1, SIDE), lambda p, c: (c, 0, 0)),
            pl.BlockSpec((1, 1, MAIN), lambda p, c: (c, 0, 0)),
            pl.BlockSpec((1, PAIR, 4, HD), lambda p, c: (p, 0, 0, 0)),
            pl.BlockSpec(gain_one.shape, lambda p, c: (0,)),
            pl.BlockSpec(gain_two.shape, lambda p, c: (0,)),
        ],
        out_specs=[
            pl.BlockSpec((1, 1, ROWS, packed_width), lambda p, c: (p, c, 0, 0)),
            pl.BlockSpec((1, 1, PAIR, 2, SIDE, WIDE), lambda p, c: (p, c, 0, 0, 0, 0)),
            pl.BlockSpec((1, 1, ROWS, PAIR * WIDE), lambda p, c: (p, c, 0, 0)),
            pl.BlockSpec((1, ROWS, WIDE), lambda p, c: (late(p, c), 0, 0)),
            pl.BlockSpec((1, ROWS, width), lambda p, c: (early(p, c), 0, 0)),
            pl.BlockSpec((1, ROWS, width), lambda p, c: (late(p, c), 0, 0)),
            pl.BlockSpec((1, ROWS, width), lambda p, c: (late(p, c), 0, 0)),
            pl.BlockSpec((1, ROWS, width), lambda p, c: (late(p, c), 0, 0)),
        ],
        out_shape=[
            shaped((pairs, clips, ROWS, packed_width), BF16),
            shaped((pairs, clips, PAIR, 2, SIDE, WIDE), BF16),
            shaped((pairs, clips, ROWS, PAIR * WIDE), BF16),
            shaped((clips, ROWS, WIDE), F32),
            shaped((clips, ROWS, width), BF16),
            shaped((clips, ROWS, width), F32),
            shaped((clips, ROWS, width), BF16),
            shaped((clips, ROWS, width), BF16),
        ],
        scratch_shapes=[
            pltpu.VMEM((clips, ROWS, width), BF16),
            pltpu.VMEM((clips, ROWS, width), BF16),
            pltpu.VMEM((clips, ROWS, width), F32),
            pltpu.VMEM((clips, ROWS, WIDE), F32),
        ],
        compiler_params=compiler_params(2),
        name="attention_forward",
    )(x, cot, w, mem, tail, side, main, taps, gain_one, gain_two)


def once(shape):
    return pl.BlockSpec(shape, lambda t: (0,) * len(shape), pipeline_mode=pl.Buffered(1))


def mlp(normed, cot, first, second, middle, gain):
    rows, width = normed.shape
    hidden = first.shape[1]
    clips = rows // ROWS
    tiles = hidden // TILE
    tile_at = lambda t: jnp.minimum(t, tiles - 1)
    clip_at = lambda t: jnp.maximum(t - tiles, 0)
    return pl.pallas_call(
        mlp_kernel,
        grid=(tiles + clips,),
        in_specs=[
            once((rows, width)),
            once((rows, width)),
            pl.BlockSpec((width, TILE), lambda t: (0, tile_at(t))),
            pl.BlockSpec((TILE, width), lambda t: (tile_at(t), 0)),
            pl.BlockSpec(memory_space=pl.ANY),
            pl.BlockSpec(gain.shape, lambda t: (0,)),
        ],
        out_specs=[
            pl.BlockSpec((1, TPC, width), lambda t: (clip_at(t), 0, 0)),
            pl.BlockSpec((ROWS, width), lambda t: (clip_at(t), 0)),
            pl.BlockSpec((width, TILE), lambda t: (0, tile_at(t))),
            pl.BlockSpec((TILE, width), lambda t: (tile_at(t), 0)),
            once((1, width)),
        ],
        out_shape=[
            shaped((clips, TPC, width), BF16),
            shaped((rows, width), BF16),
            shaped((width, hidden), BF16),
            shaped((hidden, width), BF16),
            shaped((1, width), F32),
        ],
        scratch_shapes=[
            pltpu.VMEM((rows, width), F32),
            pltpu.VMEM((rows, width), F32),
            pltpu.VMEM((rows, width), F32),
            pltpu.VMEM((rows, TILE), BF16),
            pltpu.VMEM((rows, TILE), BF16),
            pltpu.SemaphoreType.DMA((1,)),
        ],
        compiler_params=compiler_params(1),
        name="mlp",
    )(normed, cot, first, second, middle, gain)


def sum_scratch(lead, planes, shape):
    return [
        pltpu.VMEM(lead + dims + shape, BF16)
        for dims in ((planes, 2, 2, 2), (planes, 2, 2), (planes, 2), (planes,), (3,))
    ]


def mlp_links(normed, cot, first, second, middle, gain):
    rows, width = normed.shape
    hidden = first.shape[1]
    clips = rows // ROWS
    tile_at = lambda t: jnp.minimum(t, TILES - 1)
    clip_at = lambda t: jnp.maximum(t - TILES, 0)
    first_rows, second_rows = width // 32, hidden // 32
    anywhere = pl.BlockSpec(memory_space=pl.ANY)
    return pl.pallas_call(
        mlp_links_kernel,
        grid=(TILES + clips,),
        in_specs=[
            once((rows, width)),
            once((rows, width)),
            pl.BlockSpec((width, TILE), lambda t: (0, tile_at(t))),
            pl.BlockSpec((TILE, width), lambda t: (tile_at(t), 0)),
            anywhere,
            pl.BlockSpec(gain.shape, lambda t: (0,)),
        ],
        out_specs=[
            pl.BlockSpec((1, TPC, width), lambda t: (clip_at(t), 0, 0)),
            pl.BlockSpec((ROWS, width), lambda t: (clip_at(t), 0)),
            once((1, width)),
        ] + [anywhere] * 4,
        out_shape=[
            shaped((clips, TPC, width), BF16),
            shaped((rows, width), BF16),
            shaped((1, width), F32),
            shaped((first_rows, EARLY * TILE), F32),
            shaped((second_rows, width), F32),
            shaped((TILES - EARLY, 4, 2, 2, 2, first_rows, TILE), BF16),
            shaped((TILES - EARLY, 1, 2, 2, 2, second_rows, width), BF16),
        ],
        scratch_shapes=[
            pltpu.VMEM((rows, width), F32),
            pltpu.VMEM((rows, width), F32),
            pltpu.VMEM((rows, width), F32),
            pltpu.VMEM((rows, TILE), BF16),
            pltpu.VMEM((rows, TILE), BF16),
            pltpu.SemaphoreType.DMA((1,)),
        ]
        + sum_scratch((EARLY,), 4, (first_rows, TILE))
        + sum_scratch((EARLY,), 1, (second_rows, width))
        + [
            pltpu.VMEM((TILES - EARLY, 4, 2, 2, 2, first_rows, TILE), BF16),
            pltpu.VMEM((TILES - EARLY, 1, 2, 2, 2, second_rows, width), BF16),
            pltpu.VMEM((EARLY, first_rows, TILE), F32),
            pltpu.VMEM((second_rows, width), F32),
            pltpu.SemaphoreType.DMA((12 * EARLY,)),
            pltpu.SemaphoreType.DMA((12 * EARLY,)),
            pltpu.SemaphoreType.DMA((2 * TILES,)),
        ],
        compiler_params=pltpu.CompilerParams(
            dimension_semantics=("arbitrary",),
            vmem_limit_bytes=VMEM_LIMIT,
            collective_id=2,
            has_side_effects=True,
        ),
        name="mlp_links",
    )(normed, cot, first, second, middle, gain)


def attention_backward(x, w, mem, side, main, taps, gain, packed, keys, att, log, normed, grad):
    clips, pairs = x.shape[0], w.shape[0]
    width = x.shape[2]
    packed_width = PIECES * WIDE
    weight_rows = w.shape[1]
    late = lambda p, c: jnp.where(p == pairs - 1, c, 0)
    return pl.pallas_call(
        backward_kernel,
        grid=(pairs, clips),
        in_specs=[
            pl.BlockSpec((1, TPC, width), lambda p, c: (late(p, c), 0, 0)),
            pl.BlockSpec((1, weight_rows, width), lambda p, c: (p, 0, 0)),
            pl.BlockSpec((1, PAIR, 2 * HD, MAIN), lambda p, c: (c, p, 0, 0)),
            pl.BlockSpec((1, 1, SIDE), lambda p, c: (c, 0, 0)),
            pl.BlockSpec((1, 1, MAIN), lambda p, c: (c, 0, 0)),
            pl.BlockSpec((1, PAIR, 4, HD), lambda p, c: (p, 0, 0, 0)),
            pl.BlockSpec(gain.shape, lambda p, c: (0,)),
            pl.BlockSpec((1, 1, ROWS, packed_width), lambda p, c: (p, c, 0, 0)),
            pl.BlockSpec((1, 1, PAIR, 2, SIDE, WIDE), lambda p, c: (p, c, 0, 0, 0, 0)),
            pl.BlockSpec((1, 1, ROWS, PAIR * WIDE), lambda p, c: (p, c, 0, 0)),
            pl.BlockSpec((1, ROWS, WIDE), lambda p, c: (c, 0, 0)),
            pl.BlockSpec((1, ROWS, width), lambda p, c: (c, 0, 0)),
            pl.BlockSpec((ROWS, width), lambda p, c: (c, 0)),
        ],
        out_specs=[
            pl.BlockSpec((1, TPC, width), lambda p, c: (late(p, c), 0, 0)),
            pl.BlockSpec((1, weight_rows, width), lambda p, c: (p, 0, 0)),
            pl.BlockSpec((1, PAIR, 4, WIDE), lambda p, c: (p, 0, 0, 0)),
            pl.BlockSpec((1, width), lambda p, c: (0, 0)),
        ],
        out_shape=[
            shaped((clips, TPC, width), BF16),
            shaped((pairs, weight_rows, width), F32),
            shaped((pairs, PAIR, 4, WIDE), F32),
            shaped((1, width), F32),
        ],
        scratch_shapes=[pltpu.VMEM((clips, ROWS, width), F32)],
        compiler_params=compiler_params(2),
        name="attention_backward",
    )(x, w, mem, side, main, taps, gain, packed, keys, att, log, normed, grad)


def attention_backward_links(
    index, x, qkv, proj, mem, taps, gain, packed, keys, att, log, normed, grad, gain_two, d_first, d_second
):
    clips, width = x.shape[0], x.shape[2]
    packed_width = PIECES * WIDE
    steps = 4 * clips
    early = lambda s: jnp.minimum(s, steps - 1)
    pair_at = lambda s: lax.rem(lax.div(early(s), clips) + 2, 4)
    clip_at = lambda s: lax.rem(early(s), clips)
    late = lambda s: jnp.maximum(s - steps, 0)
    anywhere = pl.BlockSpec(memory_space=pl.ANY)
    per_step = lambda s: (pair_at(s), clip_at(s), 0, 0)
    small = (16, width)
    left = d_first.shape[0]
    first_shape, second_shape = d_first.shape[-2:], d_second.shape[-2:]
    units = []
    for _, _, padded, order in UNITS:
        one, three = (2, 8) if order == "yz" else (8, 4)
        units += [
            pltpu.VMEM(shape, BF16)
            for shape in (
                (padded, width), (padded, CORE_LANES), (padded // one, CORE_LANES), (3, padded // three, CORE_LANES),
                (padded, width),
            )
        ]
    for _, rows in FAR:
        units += [pltpu.VMEM(shape, BF16) for shape in ((rows, width), (rows, CORE_LANES), (rows, CORE_LANES))]
    return pl.pallas_call(
        backward_links_kernel,
        grid=(steps + clips,),
        in_specs=[
            pl.BlockSpec(memory_space=pltpu.SMEM),
            pl.BlockSpec((1, TPC, width), lambda s: (late(s), 0, 0)),
            once(qkv.shape),
            pl.BlockSpec((1,) + proj.shape[1:], lambda s: (pair_at(s), 0, 0, 0)),
            pl.BlockSpec(
                (None, 1, PAIR, 2 * HD, MAIN),
                lambda s: (lax.div(pair_at(s), 2), clip_at(s), lax.rem(pair_at(s), 2), 0, 0),
            ),
            pl.BlockSpec((1, PAIR, 4, HD), lambda s: (pair_at(s), 0, 0, 0)),
            pl.BlockSpec(gain.shape, lambda s: (0,)),
            pl.BlockSpec((1, 1, ROWS, packed_width), per_step),
            pl.BlockSpec((1, 1, PAIR, 2, SIDE, WIDE), lambda s: per_step(s) + (0, 0)),
            pl.BlockSpec((2, clips, ROWS, PAIR * WIDE), lambda s: (lax.div(pair_at(s), 2), 0, 0, 0)),
            pl.BlockSpec((1, ROWS, WIDE), lambda s: (clip_at(s), 0, 0)),
            once((clips, ROWS, width)),
            once((clips, ROWS, width)),
            pl.BlockSpec((1, width), lambda s: (0, 0)),
            anywhere,
            anywhere,
        ],
        out_specs=[
            pl.BlockSpec((1, TPC, width), lambda s: (late(s), 0, 0)),
            pl.BlockSpec(small, lambda s: (0, 0)),
            pl.BlockSpec((4, 4, HD), lambda s: (0, 0, 0)),
        ] + [anywhere] * 4,
        out_shape=[
            shaped((clips, TPC, width), BF16),
            shaped(small, F32),
            shaped((4, 4, HD), F32),
            shaped((first_shape[0], left * TILE), F32),
            shaped(second_shape, F32),
            shaped((UNITS[0][1], width), BF16),
            shaped((2, UNITS[1][1], width), BF16),
        ],
        scratch_shapes=[
            pltpu.VMEM((clips, ROWS, 4 * packed_width), BF16),
            pltpu.VMEM((1, width), F32),
            pltpu.VMEM((4, PAIR, 4, WIDE), F32),
        ]
        + [pltpu.VMEM(small, F32)] * 2
        + [
            pltpu.VMEM((3,) + small, F32),
            pltpu.VMEM((8,) + small, F32),
            pltpu.VMEM((left,) + first_shape, F32),
            pltpu.VMEM(second_shape, F32),
            pltpu.SemaphoreType.DMA((BACKWARD_COPIES,)),
            pltpu.SemaphoreType.DMA((BACKWARD_COPIES,)),
            pltpu.SemaphoreType.DMA((7 + left,)),
        ]
        + sum_scratch((left,), 4, first_shape)
        + sum_scratch((left,), 1, second_shape)
        + units,
        compiler_params=pltpu.CompilerParams(
            dimension_semantics=("arbitrary",),
            vmem_limit_bytes=VMEM_LIMIT,
            collective_id=1,
            has_side_effects=True,
        ),
        name="attention_backward_links",
    )(index, x, qkv, proj, mem, taps, gain, packed, keys, att, log, normed, grad, gain_two, d_first, d_second)


def group_gather(own, heads, fetch=None):
    blocks = [fetch(own, 0) if fetch else own]
    for shift in range(1, heads):
        sent = fetch(own, -shift) if fetch else own
        blocks.append(lax.ppermute(sent, "head", [(src, (src - shift) % heads) for src in range(heads)]))
    return blocks


def group_sum(blocks, heads):
    total = blocks[0]
    for shift in range(1, heads):
        total = total + lax.ppermute(
            blocks[shift].astype(BF16), "head", [(src, (src + shift) % heads) for src in range(heads)]
        ).astype(F32)
    return total


def local(
    heads,
    batches,
    inputs,
    qkv_weight,
    proj_weight,
    pool_weight,
    gain_one,
    gain_two,
    hidden_weight,
    output_weight,
    memory,
    clip_index,
    cotangent,
):
    width = inputs.shape[3]
    micro, own_clips = inputs.shape[:2]
    clips = micro * own_clips
    own_heads = qkv_weight.shape[1]
    all_heads = own_heads * heads
    pairs = all_heads // PAIR
    me = lax.axis_index("head")
    linked = (heads, batches, micro, own_clips) == (2, 16, 4, 1)

    def mine(array, shift):
        start = lax.rem(me + shift + heads, heads) * own_clips
        return lax.dynamic_slice_in_dim(array, start, own_clips, axis=1)

    pad = WIDE - HD
    qkv_rows = jnp.pad(
        qkv_weight.transpose(1, 2, 0).reshape(own_heads, 3, HD, width), ((0, 0), (0, 0), (0, pad), (0, 0))
    )
    proj_rows = jnp.pad(proj_weight, ((0, 0), (0, pad), (0, 0)))
    taps_own = pool_weight.astype(F32)
    memory_t = memory.transpose(0, 1, 3, 4, 2)
    tail_own = memory_t[..., MAIN:].reshape(memory_t.shape[:3] + (2, HD, REST)).swapaxes(4, 5)
    tail_own = jnp.pad(tail_own, ((0, 0),) * 5 + ((0, pad),)).reshape(memory_t.shape[:3] + (2 * REST, WIDE))

    x = inputs.reshape(clips, TPC, width)
    cot = cotangent.reshape(clips, TPC, width)
    if linked:
        (packed, keys, att, log, normed, middle, normed_two, cot_rows, first, second, qkv_all, proj_all, mem_all, taps_all) = (
            attention_forward_links(
                clip_index.T, x, cot, qkv_weight.transpose(1, 2, 0).reshape(PAIR, PAIR, 3, HD, width),
                proj_weight.reshape(PAIR, PAIR, HD, width), memory_t, tail_own,
                taps_own.reshape(-1, PAIR, 4, HD), gain_one, gain_two, hidden_weight, output_weight,
            )
        )
        first = first.reshape(width, -1)
        second = second.reshape(-1, width)
    else:
        qkv_all = jnp.concatenate(group_gather(qkv_rows, heads), axis=0)
        proj_all = jnp.concatenate(group_gather(proj_rows, heads), axis=0)
        w_all = jnp.concatenate(
            [
                qkv_all.reshape(pairs, PIECES * WIDE, width),
                proj_all.reshape(pairs, PAIR * WIDE, width),
            ],
            axis=1,
        )
        taps_all = jnp.concatenate(group_gather(taps_own, heads), axis=0).reshape(pairs, PAIR, 4, HD)
        mem_all = jnp.concatenate(group_gather(memory_t, heads, mine), axis=2)
        mem_all = mem_all.reshape(clips, all_heads, 2 * HD, TPC)
        tail = jnp.concatenate(group_gather(tail_own, heads, mine), axis=2)
        tail = tail.reshape(clips, all_heads, 2 * REST, WIDE)

        first = lax.all_gather(hidden_weight, ("batch", "head"), axis=0, tiled=True)
        second = lax.all_gather(output_weight, ("batch", "head"), axis=0, tiled=True)
        index = mine(clip_index, 0).reshape(clips, 1, 1)
        side_mask, main_mask = mask_rows(index)
        side_mask, main_mask = side_mask.reshape(clips, 1, SIDE), main_mask.reshape(clips, 1, MAIN)
        packed, keys, att, log, normed, middle, normed_two, cot_rows = attention_forward(
            x, cot, w_all, mem_all, tail, side_mask, main_mask, taps_all, gain_one, gain_two
        )
    rows = clips * ROWS
    mlp_args = (
        normed_two.reshape(rows, width), cot_rows.reshape(rows, width), first, second, middle.reshape(rows, width), gain_two
    )
    if linked:
        outputs, grad, d_gain_two, d_first, d_second, first_left, second_left = mlp_links(*mlp_args)
    else:
        outputs, grad, d_first, d_second, d_gain_two = mlp(*mlp_args)
    if linked:
        d_x, small, d_taps, last_first, last_second, d_proj, d_qkv = attention_backward_links(
            clip_index.T, x, qkv_all, proj_all, mem_all, taps_all, gain_one,
            packed, keys, att, log, normed, grad.reshape(clips, ROWS, width), d_gain_two,
            first_left, second_left,
        )
        d_first = jnp.concatenate([d_first, last_first], axis=1)
        d_second = jnp.where(lax.axis_index("batch") // (batches // TILES) >= EARLY, last_second, d_second)
        d_qkv = d_qkv.astype(F32).reshape(own_heads, 3 * HD, width)
        d_proj = d_proj.astype(F32).reshape(own_heads, HD, width)
        share = width // (batches * heads)
        start = (lax.axis_index("batch") * heads + me) * share
        d_gains = lax.dynamic_slice_in_dim(small[:2], start, share, axis=1)
        return (
            outputs.reshape(inputs.shape),
            d_x.reshape(inputs.shape),
            d_qkv.transpose(2, 0, 1),
            d_proj,
            d_taps,
            d_gains[0],
            d_gains[1],
            d_first,
            d_second,
        )
    d_x, d_w, d_taps, d_gain_one = attention_backward(
        x, w_all, mem_all, side_mask, main_mask, taps_all, gain_one,
        packed, keys, att, log, normed, grad,
    )
    d_proj = d_w[:, PIECES * WIDE :].reshape(heads, own_heads, WIDE, width)[:, :, :HD]
    d_w = d_w[:, : PIECES * WIDE].reshape(heads, own_heads, 3, WIDE, width)[:, :, :, :HD]
    d_w = d_w.reshape(heads, own_heads, 3 * HD, width)
    d_taps = d_taps.reshape(heads, own_heads, 4, WIDE)[..., :HD]
    d_w, d_proj, d_taps = (
        lax.psum(group_sum(list(grads), heads).astype(BF16), "batch").astype(F32)
        for grads in (d_w, d_proj, d_taps)
    )
    both = ("batch", "head")
    d_first = lax.psum_scatter(d_first, both, scatter_dimension=0, tiled=True).astype(F32)
    d_second = lax.psum_scatter(d_second, both, scatter_dimension=0, tiled=True).astype(F32)
    d_gains = lax.psum_scatter(
        jnp.concatenate([d_gain_one, d_gain_two], axis=0), both, scatter_dimension=1, tiled=True
    )
    return (
        outputs.reshape(inputs.shape),
        d_x.reshape(inputs.shape),
        d_w.transpose(2, 0, 1),
        d_proj,
        d_taps,
        d_gains[0],
        d_gains[1],
        d_first,
        d_second,
    )


def solution(mesh):
    return jax.shard_map(
        functools.partial(local, mesh.shape["head"], mesh.shape["batch"]),
        mesh=mesh,
        in_specs=(
            P(None, ("batch", "head"), None, None),
            P(None, "head", None),
            P("head", None, None),
            P("head", None, None),
            P(),
            P(),
            P(("batch", "head"), None),
            P(("batch", "head"), None),
            P(None, "batch", None, "head", None),
            P(None, "batch"),
            P(None, ("batch", "head"), None, None),
        ),
        out_specs=(
            P(None, ("batch", "head"), None, None),
            P(None, ("batch", "head"), None, None),
            P(None, "head", None),
            P("head", None, None),
            P("head", None, None),
            P(("batch", "head")),
            P(("batch", "head")),
            P(("batch", "head"), None),
            P(("batch", "head"), None),
        ),
        check_vma=False,
    )
```
